32 devices in a mesh: fsdp: 4 (over y, core), ctx: 2 (over x), tp: 4 (over z).
Axes of the slice: x: 2, y: 2, z: 4, core: 2. Of those that a mesh axis runs over, the one named last changes fastest.
Arguments:
- hidden_in: bfloat16 [1024, 16, 768], P(('ctx', 'tp'), 'fsdp'), may hold values from -6 to 6
- rand_blocks: int32 [16, 16, 12, 3], P('fsdp', None, 'tp'), may hold values from 0 to 15, as said below
- w_in: float32 [768, 12, 192], P('fsdp', 'tp'), may hold values from -0.21875 to 0.21875
- qv_bias: float32 [2, 768], P(None, ('tp', 'fsdp')), may hold values from -1.2 to 1.2
- w_out: float32 [768, 768], P('tp', 'fsdp'), may hold values from -1.75 to 1.75
- out_bias: float32 [2, 768], P(None, 'fsdp'), may hold values from -3 to 3
- norm_gain: float32 [2, 768], P(None, 'fsdp'), may hold values from 0.1 to 1.9
- norm_bias: float32 [2, 768], P(None, 'fsdp'), may hold values from -3 to 3
- w_up: float32 [768, 3072], P('fsdp', 'tp'), may hold values from -0.21875 to 0.21875
- up_bias: float32 [3072], P(('tp', 'fsdp')), may hold values from -3 to 3
- w_down: float32 [3072, 768], P('tp', 'fsdp'), may hold values from -0.15625 to 0.15625
- cotangent: bfloat16 [1024, 16, 768], P(('ctx', 'tp'), 'fsdp'), may hold values from -6 to 6
Outputs:
- layer_out: bfloat16 [1024, 16, 768], P(('ctx', 'tp'), 'fsdp')
- grad_in: bfloat16 [1024, 16, 768], P(('ctx', 'tp'), 'fsdp')
- grad_w_in: float32 [768, 12, 192], P('fsdp', 'tp')
- grad_qv_bias: float32 [2, 768], P(None, ('tp', 'fsdp'))
- grad_w_out: float32 [768, 768], P('tp', 'fsdp')
- grad_out_bias: float32 [2, 768], P(None, 'fsdp')
- grad_norm_gain: float32 [2, 768], P(None, 'fsdp')
- grad_norm_bias: float32 [2, 768], P(None, 'fsdp')
- grad_w_up: float32 [768, 3072], P('fsdp', 'tp')
- grad_up_bias: float32 [3072], P(('tp', 'fsdp'))
- grad_w_down: float32 [3072, 768], P('tp', 'fsdp')
The draws below stay inside these ranges and needn't reach their ends.
Inputs may be any that keep to these rules, and one draw needn't show every extreme that they name: `rand_blocks`: for each sequence, head, pick and position p in 0..7 there is one k such that the random block of query block b = j * 8 + p lies in blocks ((j + k) mod (2)) * 8 to that plus 8 - 1, for every j. Over the 4 sequences of one index of fsdp, the heads of one index of tp, the picks and the positions, every k in 0..1 is taken equally often.
All inputs are finite; a program needn't handle non-finite values.
Results may differ from the reference program's by a relative error of at most 0.015.
The reference program's roundings to bfloat16 on the way count: a program that leaves them out, or rounds other values in their place, can miss the bound.
Values may be sent and summed in bfloat16 or wider, within the bound.
A program may use at most 192 MiB of HBM per device.

```python
import jax
import jax.numpy as jnp
from jax import lax

D = 768
H = 12
HD = 64
FF = 3072
BLK = 64
RAND = 3
SEQ = 1024
NB = 16
SEQ_DEV = 4
SEQS = 16
N_FSDP = 4
N_CTX = 2
N_TP = 4


def draw_rand_blocks(key, part):
    key = jax.random.fold_in(key, 11)
    per_dev = SEQ // (BLK * N_CTX)
    heads_local = H // N_TP
    units = SEQ_DEV * heads_local * RAND * per_dev
    shard_keys = jax.random.split(jax.random.fold_in(key, 1), N_FSDP * N_TP)

    def shuffled(subkey):
        return jax.random.permutation(subkey, units)
    orders = jax.vmap(shuffled)(shard_keys)
    offsets = (orders % N_CTX).reshape(N_FSDP, N_TP, SEQ_DEV, heads_local, RAND, per_dev)
    offsets = offsets.transpose(0, 2, 1, 3, 4, 5).reshape(SEQS, H, RAND, 1, per_dev)
    devices = jnp.arange(N_CTX).reshape(1, 1, 1, N_CTX, 1)
    within = jax.random.randint(jax.random.fold_in(key, 2), (SEQS, H, RAND, N_CTX, per_dev), 0, per_dev)
    chosen = (devices + offsets) % N_CTX * per_dev + within
    return chosen.reshape(SEQS, H, RAND, NB).transpose(0, 3, 1, 2).astype(jnp.int32)


def levels(key, extent, cuts, least, high):
    factor_of, own = 1.0, jax.random.fold_in(key, 6)
    for axis_at, parts in cuts:
        steps = jnp.exp(jax.random.uniform(jax.random.fold_in(own, axis_at), (parts,), jnp.float32, least / len(cuts), high / len(cuts)))
        factor_of = factor_of * jnp.repeat(steps, extent[axis_at] // parts).reshape([-1 if axis == axis_at else 1 for axis in range(len(extent))])
    return factor_of


def scatter_about(key, dims, width, most, cuts=(), kind=jnp.bfloat16):
    loudness = levels(key, dims, cuts, -0.22, 0.18) if cuts else 1.0
    values = jax.random.normal(key, dims, jnp.float32) * width * loudness
    return jnp.minimum(jnp.maximum(values, -most), most).astype(kind)


def setup_inputs(seed: int = 0) -> dict:
    splits = jax.random.split(jax.random.key(seed), 13)
    return {
        "hidden_in": scatter_about(splits[0], (SEQ, SEQS, D), 1.0, 6.0, ((0, 8), (1, 4))),
        "rand_blocks": draw_rand_blocks(jax.random.fold_in(splits[12], 71), 0),
        "w_in": scatter_about(splits[2], (D, H, 3 * HD), D ** -0.5, 0.21875, ((0, 4), (1, 4)), jnp.float32),
        "qv_bias": scatter_about(splits[3], (2, D), 0.2, 1.2, ((1, 16),), jnp.float32),
        "w_out": scatter_about(splits[4], (D, D), (D // 64) ** -0.5, 1.75, ((0, 4), (1, 4)), jnp.float32),
        "out_bias": scatter_about(splits[5], (2, D), 0.5, 3.0, ((1, 4),), jnp.float32),
        "norm_gain": jnp.clip(1.0 + 0.18 * jax.random.normal(splits[6], (2, D), jnp.float32), 0.1, 1.9),
        "norm_bias": scatter_about(splits[7], (2, D), 0.5, 3.0, ((1, 4),), jnp.float32),
        "w_up": scatter_about(splits[8], (D, FF), D ** -0.5, 0.21875, ((0, 4), (1, 4)), jnp.float32),
        "up_bias": scatter_about(splits[9], (FF,), 0.5, 3.0, ((0, 16),), jnp.float32),
        "w_down": scatter_about(splits[10], (FF, D), (FF // 2) ** -0.5, 0.15625, ((0, 4), (1, 4)), jnp.float32),
        "cotangent": scatter_about(splits[11], (SEQ, SEQS, D), 1.0, 6.0, ((0, 8), (1, 4))),
    }


EPS = 1e-06
NEG = -1000000000.0
HIGH = lax.Precision.HIGHEST

@jax.custom_vjp
def low(v):
    return lax.optimization_barrier(v.astype(jnp.bfloat16)).astype(jnp.float32)

@jax.custom_vjp
def low_back(v):
    return v

def low_keep(v):
    return (low(v), None)

def low_pass(kept, grad):
    return (grad,)

def back_keep(v):
    return (v, None)

def back_low(kept, grad):
    return (low(grad),)
low.defvjp(low_keep, low_pass)
low_back.defvjp(back_keep, back_low)

def normalize(value, gain, shift):
    mean = lax.optimization_barrier(jnp.mean(value, axis=-1, keepdims=True))
    centred = value - mean
    variance = lax.optimization_barrier(jnp.mean(centred * centred, axis=-1, keepdims=True))
    return centred * lax.rsqrt(variance + EPS) * gain + shift

def attend(query, key, value, rand_ids):
    blocks = jnp.arange(NB).astype(jnp.int32)
    window = blocks[:, None] + jnp.arange(-1, 2).astype(jnp.int32)[None, :]
    valid = jnp.concatenate([(window >= 0) & (window < NB), jnp.ones((NB, 2 + RAND), jnp.bool_)], axis=1)
    ends = jnp.array([0, NB - 1], dtype=jnp.int32)
    chosen = jnp.concatenate([jnp.broadcast_to(jnp.clip(window, 0, NB - 1)[:, None, :], (NB, H, 3)).astype(jnp.int32), jnp.broadcast_to(ends[None, None, :], (NB, H, 2)).astype(jnp.int32), rand_ids.astype(jnp.int32)], axis=2)
    key_heads = key.reshape(NB, BLK, H, HD).transpose(2, 0, 1, 3)
    value_heads = value.reshape(NB, BLK, H, HD).transpose(2, 0, 1, 3)
    head_index = jnp.arange(H).astype(jnp.int32)[None, :, None]
    keys = key_heads[head_index, chosen]
    values = value_heads[head_index, chosen]
    query_blocks = query.reshape(NB, BLK, H, HD)
    raw = jnp.einsum('bqhd,bhjkd->bhqjk', query_blocks, keys, precision=HIGH) * HD ** (-0.5)
    scores = low_back(raw)
    scores = jnp.where(valid[:, None, None, :, None], scores, NEG)
    probs = jax.nn.softmax(scores.reshape(NB, H, BLK, (5 + RAND) * BLK), axis=-1)
    mixed = jnp.einsum('bhqk,bhkd->bqhd', low(probs), values.reshape(NB, H, (5 + RAND) * BLK, HD), precision=HIGH)
    global_query = jnp.stack([query_blocks[0], query_blocks[NB - 1]], axis=0)
    key_all = key.reshape(SEQ, H, HD)
    value_all = value.reshape(SEQ, H, HD)
    wide_raw = jnp.einsum('gqhd,khd->ghqk', global_query, key_all, precision=HIGH) * HD ** (-0.5)
    wide_probs = jax.nn.softmax(low_back(wide_raw), axis=-1)
    wide_mixed = jnp.einsum('ghqk,khd->gqhd', low(wide_probs), value_all, precision=HIGH)
    mixed = mixed.at[0].set(wide_mixed[0]).at[NB - 1].set(wide_mixed[1])
    return mixed.reshape(SEQ, H * HD)

def layer(params, tokens, rand_ids):
    w_in, qv_bias, w_out, out_bias, norm_gain, norm_bias, w_up, up_bias, w_down = [low(item) for item in params]
    projected = jnp.einsum('td,dhe->the', tokens, w_in, precision=HIGH)
    bias_pair = qv_bias.reshape(2, H, HD)
    query = low(low_back(projected[:, :, :HD] + bias_pair[0]))
    key = low(low_back(projected[:, :, HD:2 * HD]))
    value = low(low_back(projected[:, :, 2 * HD:] + bias_pair[1]))
    mixed = low(low_back(attend(query, key, value, rand_ids)))
    branch = low_back(jnp.dot(mixed, w_out, precision=HIGH) + out_bias[0])
    first = normalize(tokens + branch, norm_gain[0], norm_bias[0])
    inner = low_back(jnp.dot(low(first), w_up, precision=HIGH) + up_bias)
    active = low(jax.nn.gelu(inner, approximate=False))
    second = low_back(jnp.dot(active, w_down, precision=HIGH) + out_bias[1])
    return normalize(first + second, norm_gain[1], norm_bias[1])

def reference(hidden_in, rand_blocks, w_in, qv_bias, w_out, out_bias, norm_gain, norm_bias, w_up, up_bias, w_down, cotangent):
    params = (w_in, qv_bias, w_out, out_bias, norm_gain, norm_bias, w_up, up_bias, w_down)
    tokens = hidden_in.astype(jnp.float32).transpose(1, 0, 2)

    def whole(weights, inputs):

        def one_sequence(item):
            return layer(weights, item[0], item[1])
        return lax.map(jax.checkpoint(one_sequence), (inputs, rand_blocks))
    outputs, pullback = jax.vjp(whole, params, tokens)
    grads, token_grad = pullback(cotangent.astype(jnp.float32).transpose(1, 0, 2))
    return (outputs.transpose(1, 0, 2).astype(jnp.bfloat16), token_grad.transpose(1, 0, 2).astype(jnp.bfloat16), grads[0], grads[1], grads[2], grads[3], grads[4], grads[5], grads[6], grads[7], grads[8])
```

```python
import jax
import jax.numpy as jnp
from jax import lax
from jax.experimental import pallas as pl
from jax.experimental.pallas import tpu as pltpu
from jax.sharding import PartitionSpec as P

BLK = 64


EPS = 1e-06
NEG = -1000000000.0


def from_root(block, axis, owner):
    block = jnp.where(lax.axis_index(axis) == owner, block, jnp.zeros_like(block))
    return lax.psum(block, axis)


def extended(array, sides, width):
    for axis, dim in sides:
        size, length = (lax.axis_size(axis), array.shape[dim])
        up = [(i, (i + 1) % size) for i in range(size - 1)]
        down = [(j, i) for i, j in up]
        last = lax.slice_in_dim(array, length - width, length, axis=dim)
        leading = lax.slice_in_dim(array, 0, width, axis=dim)
        before = lax.ppermute(last, axis, up)
        after = lax.ppermute(leading, axis, down)
        array = jnp.concatenate([before, array, after], axis=dim)
    return array


def joined_2(part, axis, combine):
    gathered = jax.tree.map(lambda a: lax.all_gather(a, axis), part)

    def take(source):
        return jax.tree.map(lambda a: lax.dynamic_index_in_dim(a, source, 0, False), gathered)

    return lax.fori_loop(
        1, lax.axis_size(axis), lambda source, state: combine(state, take(source)), take(0)
    )


def norm_forward(value, gain, shift):
    mean = jnp.mean(value, axis=-1, keepdims=True)
    centred = value - mean
    inverse = lax.rsqrt(jnp.mean(centred * centred, axis=-1, keepdims=True) + EPS)
    normed = centred * inverse
    return (normed * gain + shift, normed, inverse)


def norm_backward(upper, normed, inverse, gain):
    scaled = upper * gain
    return inverse * (
        scaled
        - jnp.mean(scaled, axis=-1, keepdims=True)
        - normed * jnp.mean(scaled * normed, axis=-1, keepdims=True)
    )


def exact_gelu(value):
    return jax.nn.gelu(value, approximate=False)


def outer_sum(left, right):
    return lax.dot_general(
        left, right, (((0,), (0,)), ((), ())), preferred_element_type=jnp.float32
    )


def rows_all(value):
    return lax.all_gather(value, "tp", axis=0, tiled=True)


def rows_sum(left, right, contract):
    return lax.psum_scatter(
        lax.dot_general(
            left, right, (((1,), (contract,)), ((), ())), preferred_element_type=jnp.float32
        ),
        "tp",
        scatter_dimension=0,
        tiled=True,
    )


def spread(piece, root):
    return from_root(piece, "ctx", root)


def stats_join(first_stats, second_stats):
    top = jnp.maximum(first_stats[0], second_stats[0])
    total = first_stats[1] * jnp.exp(first_stats[0] - top) + second_stats[1] * jnp.exp(
        second_stats[0] - top
    )
    return (top, total)


def split_groups(array, steps, group):
    return array.reshape((steps, group) + array.shape[1:])


def key_set(window_pad, global_pair, random_pairs):
    per_dev = random_pairs.shape[3]
    window = jnp.stack(
        [window_pad[:, :, offset_by : offset_by + per_dev] for offset_by in range(3)], axis=3
    )
    target_shape = global_pair.shape[:2] + (per_dev,) + global_pair.shape[2:]
    global_all = jnp.broadcast_to(global_pair[:, :, None], target_shape)
    random_all = jnp.swapaxes(random_pairs, 2, 3)
    joined = jnp.concatenate([window, global_all, random_all], axis=3)
    shape = joined.shape
    return joined.reshape(shape[0], shape[1], shape[2], shape[3] * shape[4], shape[5])


def scores_of(query, keys, mask, scale):
    head_dim = query.shape[-1]
    raw = (
        jnp.einsum(
            "shpqd,shpkd->shpqk", query, keys[..., :head_dim], preferred_element_type=jnp.float32
        )
        * scale
    )
    return jnp.where(mask, raw, NEG)


def attend_group(query, window_pad, global_pair, random_pairs, mask, scale):
    head_dim = query.shape[-1]
    keys = key_set(window_pad, global_pair, random_pairs)
    scores = scores_of(query, keys, mask, scale)
    top = jnp.max(scores, axis=-1, keepdims=True)
    weights = jnp.exp(scores - top)
    total = jnp.sum(weights, axis=-1, keepdims=True)
    probs = (weights / total).astype(jnp.bfloat16)
    mixed = jnp.einsum(
        "shpqk,shpkd->shpqd", probs, keys[..., head_dim:], preferred_element_type=jnp.float32
    )
    return (mixed.astype(jnp.bfloat16), (top + jnp.log(total))[..., 0])


def attend_back(query, window_pad, global_pair, random_pairs, mask, scale, logsum, mixed_grad):
    head_dim = query.shape[-1]
    blocksize = window_pad.shape[3]
    keys = key_set(window_pad, global_pair, random_pairs)
    scores = scores_of(query, keys, mask, scale)
    probs = jnp.exp(scores - logsum[..., None])
    probs_grad = jnp.einsum(
        "shpqd,shpkd->shpqk", mixed_grad, keys[..., head_dim:], preferred_element_type=jnp.float32
    )
    inner = jnp.sum(probs * probs_grad, axis=-1, keepdims=True)
    scores_grad = (probs * (probs_grad - inner)).astype(jnp.bfloat16)
    query_grad = (
        jnp.einsum(
            "shpqk,shpkd->shpqd",
            scores_grad,
            keys[..., :head_dim],
            preferred_element_type=jnp.float32,
        )
        * scale
    )
    keys_grad = (
        jnp.einsum("shpqk,shpqd->shpkd", scores_grad, query, preferred_element_type=jnp.float32)
        * scale
    )
    values_grad = jnp.einsum(
        "shpqk,shpqd->shpkd",
        probs.astype(jnp.bfloat16),
        mixed_grad,
        preferred_element_type=jnp.float32,
    )
    pairs_grad = jnp.concatenate([keys_grad, values_grad], axis=-1)
    shape = pairs_grad.shape
    pairs_grad = pairs_grad.reshape(
        shape[0], shape[1], shape[2], shape[3] // blocksize, blocksize, shape[4]
    )
    per_dev = shape[2]
    window_grad = jnp.zeros(window_pad.shape, jnp.float32)
    for offset_by in range(3):
        window_grad = window_grad.at[:, :, offset_by : offset_by + per_dev].add(
            pairs_grad[:, :, :, offset_by]
        )
    global_grad = jnp.sum(pairs_grad[:, :, :, 3:5], axis=2)
    random_grad = jnp.swapaxes(pairs_grad[:, :, :, 5:], 2, 3)
    return (query_grad, window_grad, global_grad, random_grad)


def span_shards(
    hidden_in,
    rand_blocks,
    w_in,
    qv_bias,
    w_out,
    out_bias,
    norm_gain,
    norm_bias,
    w_up,
    up_bias,
    w_down,
    cotangent,
):
    ctx_count = lax.axis_size("ctx")
    tp_count = lax.axis_size("tp")
    ctx_place = lax.axis_index("ctx")
    part_rows, seqs, width = hidden_in.shape
    heads = w_in.shape[1]
    head_dim = w_in.shape[2] // 3
    pair_width = 2 * head_dim
    blocks_all = rand_blocks.shape[1]
    picks = rand_blocks.shape[3]
    length = part_rows * tp_count
    per_dev = length // BLK
    total_rows = length * seqs
    scale = head_dim ** (-0.5)
    group = min(seqs, max(1, 512 // length))
    steps = seqs // group
    first_owner = ctx_place == 0
    last_owner = ctx_place == ctx_count - 1
    gathered = (
        lax.all_gather(w_in.astype(jnp.bfloat16), "fsdp", axis=0, tiled=True),
        lax.all_gather(qv_bias.astype(jnp.bfloat16), "fsdp", axis=1, tiled=True),
        lax.all_gather(w_out.astype(jnp.bfloat16), "fsdp", axis=1, tiled=True),
        lax.all_gather(out_bias.astype(jnp.bfloat16), "fsdp", axis=1, tiled=True),
        lax.all_gather(norm_gain.astype(jnp.bfloat16), "fsdp", axis=1, tiled=True),
        lax.all_gather(norm_bias.astype(jnp.bfloat16), "fsdp", axis=1, tiled=True),
        lax.all_gather(w_up.astype(jnp.bfloat16), "fsdp", axis=0, tiled=True),
        lax.all_gather(up_bias.astype(jnp.bfloat16), "fsdp", axis=0, tiled=True),
        lax.all_gather(w_down.astype(jnp.bfloat16), "fsdp", axis=1, tiled=True),
    )
    input_low = gathered[0].reshape(width, heads * 3 * head_dim)
    bias_pair = gathered[1].astype(jnp.float32).reshape(2, heads, head_dim)
    output_low = gathered[2]
    bias_out = gathered[3].astype(jnp.float32)
    gains = gathered[4].astype(jnp.float32)
    shifts = gathered[5].astype(jnp.float32)
    upper_low = gathered[6]
    bias_up = gathered[7].astype(jnp.float32)
    lower_low = gathered[8]
    x_full = rows_all(hidden_in)
    x_rows = x_full.reshape(total_rows, width)
    projected = jnp.dot(x_rows, input_low, preferred_element_type=jnp.float32).reshape(
        length, seqs, heads, 3, head_dim
    )
    query = (projected[:, :, :, 0] + bias_pair[0]).astype(jnp.bfloat16)
    key = projected[:, :, :, 1].astype(jnp.bfloat16)
    value = (projected[:, :, :, 2] + bias_pair[1]).astype(jnp.bfloat16)
    query_heads = query.transpose(1, 2, 0, 3).reshape(seqs, heads, per_dev, BLK, head_dim)
    pairs = jnp.concatenate([key, value], axis=-1).transpose(1, 2, 0, 3)
    window_pad = extended(pairs, (("ctx", 2),), BLK).reshape(
        seqs, heads, per_dev + 2, BLK, pair_width
    )
    pair_blocks = pairs.reshape(seqs, heads, per_dev, BLK, pair_width)
    triple_blocks = jnp.concatenate([query_heads, pair_blocks], axis=-1)
    global_triple = jnp.stack(
        [
            spread(triple_blocks[:, :, 0], 0),
            spread(triple_blocks[:, :, per_dev - 1], ctx_count - 1),
        ],
        axis=2,
    )
    global_query = global_triple[..., :head_dim]
    global_pair = global_triple[..., head_dim:]
    key_local = pairs[..., :head_dim]
    value_local = pairs[..., head_dim:]
    wide_scores = (
        jnp.einsum("shgqd,shkd->shgqk", global_query, key_local, preferred_element_type=jnp.float32)
        * scale
    )
    wide_top = jnp.max(wide_scores, axis=-1)
    wide_total = jnp.sum(jnp.exp(wide_scores - wide_top[..., None]), axis=-1)
    all_top, all_total = joined_2((wide_top, wide_total), "ctx", stats_join)
    wide_probs = jnp.exp(wide_scores - (all_top + jnp.log(all_total))[..., None])
    wide_probs_low = wide_probs.astype(jnp.bfloat16)
    mix_low = jnp.einsum(
        "shgqk,shkd->shgqd", wide_probs_low, value_local, preferred_element_type=jnp.float32
    )
    mix_full = jnp.einsum(
        "shgqk,shkd->shgqd",
        wide_probs,
        value_local.astype(jnp.float32),
        precision=lax.Precision.HIGHEST,
    )
    mix_low, mix_full = lax.psum((mix_low, mix_full), "ctx")
    global_mixed = mix_low.astype(jnp.bfloat16)
    units = seqs * heads * picks * per_dev
    table = rand_blocks.transpose(0, 2, 3, 1).reshape(seqs, heads, picks, ctx_count, per_dev)
    table = table.transpose(0, 1, 2, 4, 3).reshape(units, ctx_count)
    mine = lax.dynamic_index_in_dim(table, ctx_place, 1, keepdims=False)
    mine_groups = mine.reshape(steps, group, heads, picks, per_dev)
    block_index = ctx_place * per_dev + jnp.arange(per_dev)
    present = jnp.concatenate(
        [
            (block_index >= 1)[:, None],
            jnp.ones((per_dev, 1), jnp.bool_),
            (block_index <= blocks_all - 2)[:, None],
            jnp.ones((per_dev, 2 + picks), jnp.bool_),
        ],
        axis=1,
    )
    mask = jnp.repeat(present, BLK, axis=1)[None, None, :, None, :]

    def random_pairs_for(block_group, id_group):
        whole = lax.all_gather(block_group, "ctx", axis=2, tiled=True)
        chosen = jax.nn.one_hot(id_group, blocks_all, dtype=jnp.bfloat16)
        return jnp.einsum(
            "shpqb,shbke->shpqke", chosen, whole, preferred_element_type=jnp.float32
        ).astype(jnp.bfloat16)

    query_groups = split_groups(query_heads, steps, group)
    pad_groups = split_groups(window_pad, steps, group)
    global_groups = split_groups(global_pair, steps, group)
    block_groups = split_groups(pair_blocks, steps, group)

    def forward_step(items):
        position, query_group, pad_group, global_group, block_group, id_group = items
        random_group = random_pairs_for(block_group, id_group)
        return attend_group(query_group, pad_group, global_group, random_group, mask, scale)

    mixed_groups, logsum_groups = lax.map(
        forward_step,
        (jnp.arange(steps), query_groups, pad_groups, global_groups, block_groups, mine_groups),
    )
    mixed_blocks = mixed_groups.reshape(seqs, heads, per_dev, BLK, head_dim)
    mixed_blocks = mixed_blocks.at[:, :, 0].set(
        jnp.where(first_owner, global_mixed[:, :, 0], mixed_blocks[:, :, 0])
    )
    mixed_blocks = mixed_blocks.at[:, :, per_dev - 1].set(
        jnp.where(last_owner, global_mixed[:, :, 1], mixed_blocks[:, :, per_dev - 1])
    )
    mixed = (
        mixed_blocks.reshape(seqs, heads, length, head_dim)
        .transpose(2, 0, 1, 3)
        .reshape(total_rows, heads * head_dim)
    )
    branch = rows_sum(mixed, output_low, 0) + bias_out[0]
    residual_in = hidden_in.reshape(part_rows * seqs, width).astype(jnp.float32)
    first, normed_one, inverse_one = norm_forward(residual_in + branch, gains[0], shifts[0])
    first_full = rows_all(first.astype(jnp.bfloat16).reshape(part_rows, seqs, width)).reshape(
        total_rows, width
    )
    inner = jnp.dot(first_full, upper_low, preferred_element_type=jnp.float32) + bias_up
    active_value, gelu_back = jax.vjp(exact_gelu, inner)
    active = active_value.astype(jnp.bfloat16)
    second = rows_sum(active, lower_low, 0) + bias_out[1]
    result, normed_two, inverse_two = norm_forward(first + second, gains[1], shifts[1])
    layer_out = result.astype(jnp.bfloat16).reshape(part_rows, seqs, width)
    upstream = cotangent.reshape(part_rows * seqs, width).astype(jnp.float32)
    second_grad = norm_backward(upstream, normed_two, inverse_two, gains[1])
    second_low = second_grad.astype(jnp.bfloat16)
    second_full = rows_all(second_low.reshape(part_rows, seqs, width)).reshape(total_rows, width)
    active_grad = lax.dot_general(
        second_full, lower_low, (((1,), (1,)), ((), ())), preferred_element_type=jnp.float32
    )
    inner_low = gelu_back(active_grad)[0].astype(jnp.bfloat16)
    first_grad = second_grad + rows_sum(inner_low, upper_low, 1)
    residual_grad = norm_backward(first_grad, normed_one, inverse_one, gains[0])
    branch_low = residual_grad.astype(jnp.bfloat16)
    branch_full = rows_all(branch_low.reshape(part_rows, seqs, width)).reshape(total_rows, width)
    mixed_grad = lax.dot_general(
        branch_full, output_low, (((1,), (1,)), ((), ())), preferred_element_type=jnp.float32
    ).astype(jnp.bfloat16)
    mixed_heads = (
        mixed_grad.reshape(length, seqs, heads, head_dim)
        .transpose(1, 2, 0, 3)
        .reshape(seqs, heads, per_dev, BLK, head_dim)
    )
    zero_block = jnp.zeros((seqs, heads, BLK, head_dim), jnp.bfloat16)
    lead_grad = jnp.where(first_owner, mixed_heads[:, :, 0], zero_block).astype(jnp.float32)
    tail_grad = jnp.where(last_owner, mixed_heads[:, :, per_dev - 1], zero_block).astype(
        jnp.float32
    )
    lead_sum, tail_sum = (
        lax.psum(lead_grad.astype(jnp.bfloat16), "ctx").astype(jnp.float32),
        lax.psum(tail_grad.astype(jnp.bfloat16), "ctx").astype(jnp.float32),
    )
    wide_grad = jnp.stack([lead_sum, tail_sum], axis=2).astype(jnp.bfloat16)
    mixed_heads = mixed_heads.at[:, :, 0].set(
        jnp.where(first_owner, zero_block, mixed_heads[:, :, 0])
    )
    mixed_heads = mixed_heads.at[:, :, per_dev - 1].set(
        jnp.where(last_owner, zero_block, mixed_heads[:, :, per_dev - 1])
    )

    def random_back(random_grad, id_group):
        chosen = jax.nn.one_hot(id_group, blocks_all, dtype=jnp.float32)
        spread_grad = jnp.einsum(
            "shpqb,shpqke->shbke", chosen, random_grad, precision=lax.Precision.HIGHEST
        )
        return lax.psum_scatter(
            spread_grad.astype(jnp.bfloat16), "ctx", scatter_dimension=2, tiled=True
        ).astype(jnp.float32)

    def backward_step(items):
        (
            position,
            query_group,
            pad_group,
            global_group,
            block_group,
            id_group,
            logsum_group,
            grad_group,
        ) = items
        random_group = random_pairs_for(block_group, id_group)
        query_grad, window_grad, global_grad, random_grad = attend_back(
            query_group,
            pad_group,
            global_group,
            random_group,
            mask,
            scale,
            logsum_group,
            grad_group,
        )
        return (query_grad, window_grad, global_grad, random_back(random_grad, id_group))

    query_grads, window_grads, global_grads, random_total = lax.map(
        backward_step,
        (
            jnp.arange(steps),
            query_groups,
            pad_groups,
            global_groups,
            block_groups,
            mine_groups,
            logsum_groups,
            split_groups(mixed_heads, steps, group),
        ),
    )
    query_grads = query_grads.reshape(seqs, heads, length, head_dim)
    window_grads = window_grads.reshape(seqs, heads, per_dev + 2, BLK, pair_width)
    global_grads = global_grads.reshape(seqs, heads, 2, BLK, pair_width)
    wide_inner = jnp.sum(wide_grad.astype(jnp.float32) * mix_full, axis=-1, keepdims=True)
    wide_probs_grad = jnp.einsum(
        "shgqd,shkd->shgqk", wide_grad, value_local, preferred_element_type=jnp.float32
    )
    wide_scores_grad = (wide_probs * (wide_probs_grad - wide_inner)).astype(jnp.bfloat16)
    wide_query_part = (
        jnp.einsum(
            "shgqk,shkd->shgqd", wide_scores_grad, key_local, preferred_element_type=jnp.float32
        )
        * scale
    )
    wide_key_grad = (
        jnp.einsum(
            "shgqk,shgqd->shkd", wide_scores_grad, global_query, preferred_element_type=jnp.float32
        )
        * scale
    )
    wide_value_grad = jnp.einsum(
        "shgqk,shgqd->shkd", wide_probs_low, wide_grad, preferred_element_type=jnp.float32
    )
    wide_pair_grad = jnp.concatenate([wide_key_grad, wide_value_grad], axis=-1).reshape(
        seqs, heads, per_dev, BLK, pair_width
    )
    rim_pair = jnp.concatenate([window_grads[:, :, 0], window_grads[:, :, per_dev + 1]], axis=2)
    rim_back = extended(rim_pair.astype(jnp.bfloat16), (("ctx", 2),), BLK).astype(rim_pair.dtype)
    local_grad = window_grads[:, :, 1 : per_dev + 1] + wide_pair_grad
    local_grad = local_grad.at[:, :, 0].add(rim_back[:, :, :BLK])
    local_grad = local_grad.at[:, :, per_dev - 1].add(rim_back[:, :, 3 * BLK :])
    global_total, wide_query = lax.psum((global_grads, wide_query_part), "ctx")
    local_grad = local_grad.at[:, :, 0].add(jnp.where(first_owner, global_total[:, :, 0], 0.0))
    local_grad = local_grad.at[:, :, per_dev - 1].add(
        jnp.where(last_owner, global_total[:, :, 1], 0.0)
    )
    query_grads = query_grads.at[:, :, :BLK].add(jnp.where(first_owner, wide_query[:, :, 0], 0.0))
    query_grads = query_grads.at[:, :, length - BLK :].add(
        jnp.where(last_owner, wide_query[:, :, 1], 0.0)
    )
    local_grad = local_grad + random_total.reshape(seqs, heads, per_dev, BLK, pair_width)
    pair_grad = local_grad.reshape(seqs, heads, length, pair_width).transpose(2, 0, 1, 3)
    query_part = query_grads.transpose(2, 0, 1, 3)
    projected_grad = jnp.concatenate([query_part, pair_grad], axis=-1).astype(jnp.bfloat16)
    projected_rows = projected_grad.reshape(total_rows, heads * 3 * head_dim)
    grad_in = (
        (residual_grad + rows_sum(projected_rows, input_low, 1))
        .astype(jnp.bfloat16)
        .reshape(part_rows, seqs, width)
    )
    input_grad = outer_sum(x_rows, projected_rows).reshape(width, heads, 3 * head_dim)
    pair_bias_grad = jnp.stack(
        [
            jnp.sum(projected_grad[..., :head_dim], axis=(0, 1), dtype=jnp.float32).reshape(-1),
            jnp.sum(projected_grad[..., 2 * head_dim :], axis=(0, 1), dtype=jnp.float32).reshape(
                -1
            ),
        ]
    )
    output_grad = outer_sum(mixed, branch_full)
    bias_grad = jnp.stack(
        [
            jnp.sum(branch_low, axis=0, dtype=jnp.float32),
            jnp.sum(second_low, axis=0, dtype=jnp.float32),
        ]
    )
    gain_grad = jnp.stack(
        [jnp.sum(first_grad * normed_one, axis=0), jnp.sum(upstream * normed_two, axis=0)]
    )
    shift_grad = jnp.stack([jnp.sum(first_grad, axis=0), jnp.sum(upstream, axis=0)])
    upper_grad = outer_sum(first_full, inner_low)
    upper_bias_grad = jnp.sum(inner_low, axis=0, dtype=jnp.float32)
    lower_grad = outer_sum(active, second_full)
    shares = (
        lax.psum_scatter(input_grad, "fsdp", scatter_dimension=0, tiled=True),
        lax.psum_scatter(pair_bias_grad, "fsdp", scatter_dimension=1, tiled=True),
        lax.psum_scatter(output_grad, "fsdp", scatter_dimension=1, tiled=True),
        lax.psum_scatter(bias_grad, "fsdp", scatter_dimension=1, tiled=True),
        lax.psum_scatter(gain_grad, "fsdp", scatter_dimension=1, tiled=True),
        lax.psum_scatter(shift_grad, "fsdp", scatter_dimension=1, tiled=True),
        lax.psum_scatter(upper_grad, "fsdp", scatter_dimension=0, tiled=True),
        lax.psum_scatter(upper_bias_grad, "fsdp", scatter_dimension=0, tiled=True),
        lax.psum_scatter(lower_grad, "fsdp", scatter_dimension=1, tiled=True),
    )
    matrices = lax.psum((shares[0], shares[1], shares[2], shares[6], shares[7], shares[8]), "ctx")
    vectors = lax.psum((shares[3], shares[4], shares[5]), ("ctx", "tp"))
    return (
        layer_out,
        grad_in,
        matrices[0],
        matrices[1],
        matrices[2],
        vectors[0],
        vectors[1],
        vectors[2],
        matrices[3],
        matrices[4],
        matrices[5],
    )


MESH = pl.DeviceIdType.MESH
BF = jnp.bfloat16
F32 = jnp.float32
NT = (((1,), (1,)), ((), ()))
NN = (((1,), (0,)), ((), ()))
TN = (((0,), (0,)), ((), ()))
VMEM_LIMIT = 58 * 2**20


def mm(left, right, dims=NN):
    return lax.dot_general(left, right, dims, preferred_element_type=F32)


class Place:
    def __init__(self):
        self.f = lax.axis_index("fsdp")
        self.c = lax.axis_index("ctx")
        self.t = lax.axis_index("tp")
        f, c, t = self.f, self.c, self.t
        self.k = k = lax.rem(f, 2)
        self.y = y = f // 2
        self.p = t + k * (3 - 2 * t)
        self.core = (f + 1 - 2 * k, c, t)
        self.xnbr = (f, 1 - c, t)
        self.ynbr = (lax.rem(f + 2, 4), c, t)
        self.zplus = (f, c, t + 1 - 2 * k)
        self.zminus = (f, c, t - 1 + 2 * k)
        self.own_core = t // 2
        self.own_slot = t + (t // 2) * (3 - 2 * t)
        self.pair = 2 * y
        self.other = 2 - 2 * y

    def swap(self, s):
        return (2 * self.y + self.c, self.k, s)

    def swap_is_self(self, s):
        return jnp.logical_and(self.k == self.c, self.t == s)


def copy_to(src, dst, send, recv, device):
    return pltpu.make_async_remote_copy(
        src_ref=src, dst_ref=dst, send_sem=send, recv_sem=recv, device_id=device, device_id_type=MESH
    )


def greet(at):
    barrier = pltpu.get_barrier_semaphore()
    sizes = [lax.axis_size(a) for a in ("fsdp", "ctx", "tp")]
    others = 0
    for i in range(sizes[0]):
        for j in range(sizes[1]):
            for m in range(sizes[2]):
                if i or j or m:
                    others += 1
                    device = (
                        lax.rem(at.f + i, sizes[0]),
                        lax.rem(at.c + j, sizes[1]),
                        lax.rem(at.t + m, sizes[2]),
                    )
                    pl.semaphore_signal(barrier, inc=1, device_id=device, device_id_type=MESH)
    pl.semaphore_wait(barrier, others)


class Gather:
    def __init__(self, at, shards, full, send, recv):
        self.at, self.shards, self.full, self.send, self.recv = at, shards, full, send, recv

    def own(self, g):
        at, full, shard = self.at, self.full[g], self.shards[g]
        half = shard.shape[0] // 2
        rows = pl.ds(pl.multiple_of(at.c * half, half), half)

        @pl.when(at.k == at.own_core)
        def _():
            full[at.own_slot, at.f, at.c] = shard[rows, :]

        @pl.when(at.k != at.own_core)
        def _():
            self.cp(g, at.own_slot, 0, shard.at[rows], full.at[at.own_slot, at.f, at.c], at.core).start()

    def cp(self, g, slot, kind, src, dst, device):
        return copy_to(src, dst, self.send.at[g, slot, kind], self.recv.at[g, slot, kind], device)

    def arrives(self, g, slot, kind, dst):
        self.cp(g, slot, kind, dst, dst, self.at.core).wait_recv()

    def ours(self, g, slot, f, c):
        return self.full[g].at[slot, pl.ds(f, 2), c]

    def step_z(self, g, turn):
        at, full = self.at, self.full[g]
        first = (at.p + 2) // 3
        slot = first if turn == 0 else 1 - first
        piece = self.ours(g, slot, at.pair, at.c)

        @pl.when(at.p == slot)
        def _():
            self.arrives(g, slot, 0, full.at[slot, at.core[0], at.c])

        @pl.when(at.p > slot)
        def _():
            self.arrives(g, slot, 1, piece)

        @pl.when(at.p < slot)
        def _():
            self.arrives(g, slot, 2, piece)

        @pl.when(jnp.logical_and(at.p >= slot, at.p < 3))
        def _():
            self.cp(g, slot, 1, piece, piece, at.zplus).start()

        @pl.when(jnp.logical_and(at.p == 1, slot == 1))
        def _():
            self.cp(g, slot, 2, piece, piece, at.zminus).start()

        self.cp(g, slot, 3, piece, piece, at.ynbr).start()
        self.cp(g, slot, 4, piece, piece, at.xnbr).start()

    def step_relay(self, g, turn):
        at, full = self.at, self.full[g]
        first = (at.p + 2) // 3
        slot = first if turn == 0 else 1 - first
        self.arrives(g, slot, 3, self.ours(g, slot, at.other, at.c))
        even = full.at[slot, at.other, at.c]
        self.cp(g, slot, 5, even, even, at.xnbr).start()
        self.arrives(g, slot, 4, self.ours(g, slot, at.pair, 1 - at.c))
        odd = full.at[slot, at.pair + 1, 1 - at.c]
        self.cp(g, slot, 6, odd, odd, at.ynbr).start()

    def step_last(self, g):
        at, full = self.at, self.full[g]
        for slot in range(2):
            self.arrives(g, slot, 5, full.at[slot, at.other, 1 - at.c])
            self.arrives(g, slot, 6, full.at[slot, at.other + 1, 1 - at.c])

    def sent(self, g):
        at, full = self.at, self.full[g]

        def left(slot, kind, src):
            self.cp(g, slot, kind, src, src, at.core).wait_send()

        @pl.when(at.k != at.own_core)
        def _():
            left(at.own_slot, 0, full.at[at.own_slot, at.f, at.c])

        for slot in range(2):
            piece = self.ours(g, slot, at.pair, at.c)

            @pl.when(jnp.logical_and(at.p >= slot, at.p < 3))
            def _():
                left(slot, 1, piece)

            if slot == 1:

                @pl.when(at.p == 1)
                def _():
                    left(slot, 2, piece)

            left(slot, 3, piece)
            left(slot, 4, piece)
            left(slot, 5, full.at[slot, at.other, at.c])
            left(slot, 6, full.at[slot, at.pair + 1, 1 - at.c])


class Swap:
    def __init__(self, at, blocks, rows, base, send, recv):
        self.at, self.blocks, self.rows, self.base, self.send, self.recv = at, blocks, rows, base, send, recv
        self.n = blocks.shape[1]

    def span(self, s, base):
        return pl.ds(pl.multiple_of(base + s * self.n, self.n), self.n)

    def start_in(self):
        at = self.at
        there = self.rows.at[self.span(at.t, self.base * at.c)]
        for s in range(4):

            @pl.when(at.swap_is_self(s))
            def _():
                self.rows[self.span(s, self.base * at.k), :] = self.blocks[s]

            @pl.when(jnp.logical_not(at.swap_is_self(s)))
            def _():
                copy_to(self.blocks.at[s], there, self.send.at[s], self.recv.at[at.t], at.swap(s)).start()

    def wait_in(self, s):
        at = self.at
        here = self.rows.at[self.span(s, self.base * at.k)]

        @pl.when(jnp.logical_not(at.swap_is_self(s)))
        def _():
            copy_to(here, here, self.send.at[s], self.recv.at[s], at.core).wait_recv()

    def start_out(self, s):
        at = self.at
        here = self.rows.at[self.span(s, self.base * at.k)]

        @pl.when(at.swap_is_self(s))
        def _():
            self.blocks[s] = self.rows[self.span(s, self.base * at.k), :]

        @pl.when(jnp.logical_not(at.swap_is_self(s)))
        def _():
            copy_to(here, self.blocks.at[at.t], self.send.at[s], self.recv.at[at.t], at.swap(s)).start()

    def wait_out(self, s):
        at = self.at

        @pl.when(jnp.logical_not(at.swap_is_self(s)))
        def _():
            copy_to(self.blocks.at[s], self.blocks.at[s], self.send.at[s], self.recv.at[s], at.core).wait_recv()

    def sent(self):
        at = self.at
        for s in range(4):

            @pl.when(jnp.logical_not(at.swap_is_self(s)))
            def _():
                copy_to(self.blocks.at[s], self.blocks.at[s], self.send.at[s], self.recv.at[s], at.core).wait_send()
QCHUNK = 256


def attend_chunk(h, q, key, query, value_t, bias, lse, mixed_t, spots):
    cols = pl.ds(pl.multiple_of(q * QCHUNK, QCHUNK), QCHUNK)
    scores = mm(key[h], query[h, cols, :], NT)
    length = scores.shape[0]
    scores = (
        scores.reshape(length // BLK, BLK, QCHUNK) + bias[h, :, cols][:, None, :]
    ).reshape(length, QCHUNK)
    top = jnp.max(scores, axis=0, keepdims=True)
    weights = jnp.exp(scores - top)
    total = jnp.sum(weights, axis=0, keepdims=True)
    probs = (weights * (1.0 / total)).astype(BF)
    lse[h, :, cols] = top + jnp.log(total)
    mixed_t[spots(h), cols] = mm(value_t[h], probs)


def forward_kernel(
    xs, cs, shard0, shard1, shard2, bias, proj_bias, proj_scale,
    x_all, up_half, full0, full1, full2, query, key, value, mixed, lse,
    value_t, mixed_t,
    xs_send, xs_recv, xc_send, xc_recv, cs_send, cs_recv, w_send, w_recv,
):
    at = Place()
    greet(at)
    gather = Gather(at, (shard0, shard1, shard2), (full0, full1, full2), w_send, w_recv)
    tokens = Swap(at, xs, x_all, 512, xs_send, xs_recv)
    grads = Swap(at, cs, up_half, 0, cs_send, cs_recv)
    part = xs.shape[1]
    tokens.start_in()
    for g in range(3):
        gather.own(g)
    gather.step_z(0, 0)
    gather.step_z(0, 1)
    gather.step_relay(0, 0)
    gather.step_relay(0, 1)

    def to_core(s, half):
        rows = x_all.at[pl.ds(pl.multiple_of(half * 512 + s * part, part), part)]
        return copy_to(rows, rows, xc_send.at[s], xc_recv.at[s], at.core)

    for s in range(4):
        tokens.wait_in(s)
        to_core(s, at.k).start()
    gather.step_z(1, 0)
    gather.step_z(1, 1)
    grads.start_in()
    for s in range(4):
        to_core(s, 1 - at.k).wait_recv()
    gather.step_last(0)

    heads = query.shape[0]
    dim = query.shape[2]
    width = x_all.shape[1]
    for slot in range(2):

        @pl.loop(0, 4)
        def _(r):
            rows = pl.ds(pl.multiple_of(r * 256, 256), 256)
            weight = full0[slot, :, :, :, 0:640].reshape(width, 640)
            got = (mm(x_all[rows, :], weight) + proj_bias[slot]) * proj_scale[...]
            for i in range(heads // 2):
                h = slot * (heads // 2) + i
                start = i * 3 * dim
                query[h, rows, :] = got[:, start : start + dim].astype(BF)
                key[h, rows, :] = got[:, start + dim : start + 2 * dim].astype(BF)
                one = got[:, start + 2 * dim : start + 3 * dim]
                value[h, rows, :] = one.astype(BF)
                value_t[h, :, rows] = one.T.astype(BF)

    gather.step_relay(1, 0)
    gather.step_relay(1, 1)
    gather.step_z(2, 0)
    gather.step_z(2, 1)
    for slot in range(2):
        mixed_t[slot * 256 : slot * 256 + dim, :] = jnp.zeros((dim, mixed_t.shape[1]), F32)

    def spots(h):
        return pl.ds(pl.multiple_of((h // 3) * 256 + (h % 3 + 1) * dim, dim), dim)

    def attend(low_head, high_head):
        @pl.loop(low_head, high_head)
        def _(h):
            @pl.loop(0, 1024 // QCHUNK)
            def _(q):
                attend_chunk(h, q, key, query, value_t, bias, lse, mixed_t, spots)

    attend(0, 2)
    gather.step_relay(2, 0)
    gather.step_relay(2, 1)
    gather.step_last(1)
    attend(2, 6)

    @pl.loop(0, 4)
    def _(r):
        rows = pl.ds(pl.multiple_of(r * 256, 256), 256)
        mixed[rows, :] = mixed_t[:, rows].T.astype(BF)

    gather.step_last(2)
    for s in range(4):
        grads.wait_in(s)
        to_core(s, at.k).wait_send()
    tokens.sent()
    grads.sent()
    for g in range(3):
        gather.sent(g)


def vmem():
    return pl.BlockSpec(memory_space=pltpu.VMEM)


def forward_call(xs, cs, shards, bias, proj_bias, proj_scale):
    width = xs.shape[2]
    length = 1024
    heads, dim = bias.shape[0], 64
    piece = (2, 4, 2, width // 8, width)
    shape = jax.ShapeDtypeStruct
    dma = pltpu.SemaphoreType.DMA
    return pl.pallas_call(
        forward_kernel,
        out_shape=(
            shape((length, width), BF),
            shape((length // 2, width), BF),
            shape(piece, BF),
            shape(piece, BF),
            shape(piece, BF),
            shape((heads, length, dim), BF),
            shape((heads, length, dim), BF),
            shape((heads, length, dim), BF),
            shape((length, 512), BF),
            shape((heads, 1, length), F32),
        ),
        in_specs=[vmem()] * 8,
        out_specs=[vmem()] * 10,
        scratch_shapes=[
            pltpu.VMEM((heads, dim, length), BF),
            pltpu.VMEM((512, length), F32),
            dma((4,)),
            dma((4,)),
            dma((4,)),
            dma((4,)),
            dma((4,)),
            dma((4,)),
            dma((3, 2, 7)),
            dma((3, 2, 7)),
        ],
        compiler_params=pltpu.CompilerParams(
            collective_id=1, has_side_effects=True, vmem_limit_bytes=VMEM_LIMIT
        ),
        name="forward",
    )(xs, cs, *shards, bias, proj_bias, proj_scale)
def joined_small(at, arrays, tp_count):
    flat = jnp.concatenate([a.astype(F32).reshape(-1) for a in arrays])
    whole = lax.all_gather(flat, ("fsdp", "tp"), axis=0)
    whole = whole.reshape(-1, tp_count, flat.shape[0])
    out, start = [], 0
    for a in arrays:
        out.append(whole[:, :, start : start + a.size].reshape(whole.shape[:2] + a.shape))
        start += a.size
    return out


def list_counts(ids, blocks):
    spots = jnp.arange(blocks)
    near = (jnp.abs(spots[:, None] - spots[None, :]) <= 1).astype(F32)
    ends = ((spots == 0) | (spots == blocks - 1)).astype(F32)
    fixed = near + ends[None, :]
    picked = jnp.sum((ids[..., None] == spots).astype(F32), axis=2)
    counts = jnp.where((ends > 0)[None, :, None], 1.0, fixed[None] + picked)
    logs = jnp.where(counts > 0, jnp.log(jnp.maximum(counts, 1.0)), -1e30)
    return jnp.repeat(logs.transpose(0, 2, 1), BLK, axis=2)


def prepare(hidden_in, rand_blocks, w_in, qv_bias, w_out, out_bias, norm_gain, norm_bias, w_up, up_bias, w_down, cotangent):
    f, c, t = (lax.axis_index(a) for a in ("fsdp", "ctx", "tp"))
    k, y = f % 2, f // 2
    tp_count = lax.axis_size("tp")
    rows, heads, wide = w_in.shape
    dim = wide // 3
    low = lambda a: lax.reduce_precision(a, 8, 7)
    qv, outs, gains, shifts, ups, rand = joined_small(
        None,
        [low(qv_bias), low(out_bias), low(norm_gain), low(norm_bias), low(up_bias), rand_blocks],
        tp_count,
    )
    slots = (k * (tp_count - 1), 1 + k * (tp_count - 3))
    pick = lambda a: jnp.stack([lax.dynamic_index_in_dim(a, s, 0, False) for s in slots])
    qv = pick(qv.transpose(1, 2, 0, 3).reshape(tp_count, 2, heads, dim))
    zero = jnp.zeros_like(qv[:, 0])
    proj_bias = jnp.stack([qv[:, 0], zero, qv[:, 1]], axis=2).reshape(2, 1, heads * wide)
    proj_bias = jnp.pad(proj_bias, ((0, 0), (0, 0), (0, dim)))
    one = jnp.ones((heads, 1, dim), F32)
    proj_scale = jnp.concatenate([one * dim**-0.5, one, one], axis=1).reshape(1, heads * wide)
    proj_scale = jnp.pad(proj_scale, ((0, 0), (0, dim)))
    whole = lambda a: a[:, 0].transpose(1, 0, 2).reshape(2, -1)
    outs, gains, shifts = whole(outs), whole(gains), whole(shifts)
    ups = pick(ups.transpose(1, 0, 2).reshape(tp_count, -1))
    ids = lax.dynamic_index_in_dim(rand, 2 * y + c, 0, False)
    ids = pick(lax.dynamic_index_in_dim(ids, t, 1, False))
    ids = ids.transpose(0, 2, 1, 3).reshape(2 * heads, ids.shape[1], ids.shape[3])
    bias = list_counts(ids, ids.shape[1])
    shard0 = jnp.concatenate([w_in.reshape(rows, heads * wide), w_out.T], axis=1).astype(BF)
    shard1 = w_up.astype(BF)
    shard2 = w_down.T.astype(BF)
    xs = hidden_in.transpose(1, 0, 2)
    cs = cotangent.transpose(1, 0, 2)
    return xs, cs, (shard0, shard1, shard2), bias, proj_bias, proj_scale, outs, gains, shifts, ups
ROWS = 256


def norm_stats(value):
    mean = jnp.mean(value, axis=-1, keepdims=True)
    centred = value - mean
    inverse = lax.rsqrt(jnp.mean(centred * centred, axis=-1, keepdims=True) + EPS)
    return centred * inverse, inverse


def gelu_both(value):
    share = 0.5 + 0.5 * lax.erf(value * 0.7071067811865476)
    density = jnp.exp(value * value * -0.5) * 0.3989422804014327
    return value * share, share + value * density


def row_sum(value):
    return jnp.sum(value, axis=0, keepdims=True)


class Cores:
    def __init__(self, at, out, back, send, recv, row_send, row_recv):
        self.at, self.out, self.back = at, out, back
        self.send, self.recv, self.row_send, self.row_recv = send, recv, row_send, row_recv

    def rows(self, half, i):
        return pl.ds(pl.multiple_of(half * 512 + i * ROWS, ROWS), ROWS)

    def part(self, stage, i):
        return copy_to(self.out.at[i], self.back.at[i], self.send.at[stage, i], self.recv.at[stage, i], self.at.core)

    def reduce(self, stage, partial, finish):
        at = self.at

        @pl.loop(0, 512 // ROWS)
        def _(i):
            self.out[i] = partial(self.rows(1 - at.k, i))
            self.part(stage, i).start()

        @pl.loop(0, 512 // ROWS)
        def _(i):
            total = partial(self.rows(at.k, i))
            self.part(stage, i).wait_recv()
            finish(i, self.rows(at.k, i), total + self.back[i])

        @pl.loop(0, 512 // ROWS)
        def _(i):
            self.part(stage, i).wait_send()

    def row(self, stage, ref, half, i):
        rows = ref.at[self.rows(half, i)]
        return copy_to(rows, rows, self.row_send.at[stage, i], self.row_recv.at[stage, i], self.at.core)

    def over_rows(self, stage, ref, work):
        at = self.at

        @pl.loop(0, 512 // ROWS)
        def _(i):
            work(self.rows(at.k, i))

        @pl.loop(0, 512 // ROWS)
        def _(i):
            self.row(stage, ref, 1 - at.k, i).wait_recv()
            work(self.rows(1 - at.k, i))

        @pl.loop(0, 512 // ROWS)
        def _(i):
            self.row(stage, ref, at.k, i).wait_send()


def flip(dst, src):
    @pl.loop(0, src.shape[0] // ROWS)
    def _(r):
        rows = pl.ds(pl.multiple_of(r * ROWS, ROWS), ROWS)
        dst[:, rows] = src[rows, :].T


def product(dst, slot, flipped, right):
    n = dst.shape[2] * dst.shape[3]

    @pl.loop(0, dst.shape[1])
    def _(r):
        rows = pl.ds(pl.multiple_of(r * n, n), n)
        got = mm(flipped[rows, :], right())
        dst[slot, r] = got.astype(BF).reshape(dst.shape[2:])


def middle_kernel(
    x_all, up_half, full0, full1, full2, mixed, outs, gains, shifts, ups,
    layer_rows, residual, mixed_grad, grad_out, grad1, grad2, small,
    part_out, part_back, first, first_b, act, slope, second_grad, second_b, branch_b, normed_one, inverse_one, flipped,
    send, recv, row_send, row_recv,
):
    at = Place()
    barrier = pltpu.get_barrier_semaphore()
    pl.semaphore_signal(barrier, inc=1, device_id=at.core, device_id_type=MESH)
    pl.semaphore_wait(barrier, 1)
    cores = Cores(at, part_out, part_back, send, recv, row_send, row_recv)
    width = x_all.shape[1]
    square = lambda full, slot: full[slot].reshape(width, width)
    out_part = lambda slot: full0[slot, :, :, :, 512:768].reshape(width, 256)
    local = lambda i: pl.ds(pl.multiple_of(i * ROWS, ROWS), ROWS)
    small[...] = jnp.zeros_like(small)

    def tally(row, value):
        small[row : row + 1, :] += row_sum(value)

    def branch_part(rows):
        return mm(mixed[rows, 0:256], out_part(0), NT) + mm(mixed[rows, 256:512], out_part(1), NT)

    def branch_done(i, rows, total):
        normed, inverse = norm_stats(x_all[rows, :].astype(F32) + (total + outs[0:1, :]))
        value = normed * gains[0:1, :] + shifts[0:1, :]
        normed_one[local(i), :] = normed
        inverse_one[local(i), :] = inverse
        first[local(i), :] = value
        first_b[rows, :] = value.astype(BF)
        cores.row(0, first_b, at.k, i).start()

    cores.reduce(0, branch_part, branch_done)

    def up(rows):
        for slot in range(2):
            inner = mm(first_b[rows, :], square(full1, slot)) + ups[slot : slot + 1, :]
            value, slope_value = gelu_both(inner)
            act[slot, rows, :] = value.astype(BF)
            slope[slot, rows, :] = slope_value.astype(BF)

    cores.over_rows(0, first_b, up)

    def second_part(rows):
        return mm(act[0, rows, :], square(full2, 0), NT) + mm(act[1, rows, :], square(full2, 1), NT)

    def second_done(i, rows, total):
        normed, inverse = norm_stats(first[local(i), :] + (total + outs[1:2, :]))
        layer_rows[local(i), :] = (normed * gains[1:2, :] + shifts[1:2, :]).astype(BF)
        upstream = up_half[local(i), :].astype(F32)
        scaled = upstream * gains[1:2, :]
        grad = inverse * (
            scaled
            - jnp.mean(scaled, axis=-1, keepdims=True)
            - normed * jnp.mean(scaled * normed, axis=-1, keepdims=True)
        )
        second_grad[local(i), :] = grad
        low = grad.astype(BF)
        second_b[rows, :] = low
        cores.row(1, second_b, at.k, i).start()
        tally(1, low.astype(F32))
        tally(3, upstream * normed)
        tally(5, upstream)

    cores.reduce(1, second_part, second_done)

    def down(rows):
        for slot in range(2):
            grad = mm(second_b[rows, :], square(full2, slot)) * slope[slot, rows, :].astype(F32)
            low = grad.astype(BF)
            slope[slot, rows, :] = low
            tally(6 + slot, low.astype(F32))

    cores.over_rows(1, second_b, down)

    def first_part(rows):
        return mm(slope[0, rows, :], square(full1, 0), NT) + mm(slope[1, rows, :], square(full1, 1), NT)

    def first_done(i, rows, total):
        grad = total + second_grad[local(i), :]
        normed = normed_one[local(i), :]
        tally(2, grad * normed)
        tally(4, grad)
        scaled = grad * gains[0:1, :]
        back = inverse_one[local(i), :] * (
            scaled
            - jnp.mean(scaled, axis=-1, keepdims=True)
            - normed * jnp.mean(scaled * normed, axis=-1, keepdims=True)
        )
        residual[local(i), :] = back
        low = back.astype(BF)
        branch_b[rows, :] = low
        cores.row(2, branch_b, at.k, i).start()
        tally(0, low.astype(F32))

    cores.reduce(2, first_part, first_done)

    def mix_back(rows):
        for slot in range(2):
            got = mm(branch_b[rows, :], out_part(slot))
            for i in range(3):
                mixed_grad[slot * 3 + i, rows, :] = got[:, 64 + 64 * i : 128 + 64 * i].astype(BF)

    cores.over_rows(2, branch_b, mix_back)

    flip(flipped, second_b)
    for slot in range(2):
        product(grad2, slot, flipped, lambda: act[slot])
    flip(flipped, first_b)
    for slot in range(2):
        product(grad1, slot, flipped, lambda: slope[slot])
    flip(flipped, branch_b)

    @pl.loop(0, 4)
    def _(r):
        rows = pl.ds(pl.multiple_of(r * 192, 192), 192)
        grad_out[rows, :] = mm(flipped[rows, :], mixed[...])


def middle_call(x_all, up_half, full0, full1, full2, mixed, outs, gains, shifts, ups):
    length, width = x_all.shape
    shape = jax.ShapeDtypeStruct
    dma = pltpu.SemaphoreType.DMA
    half = length // 2
    parts = half // ROWS
    return pl.pallas_call(
        middle_kernel,
        out_shape=(
            shape((half, width), BF),
            shape((half, width), F32),
            shape((6, length, 64), BF),
            shape((width, 512), F32),
            shape(full1.shape, BF),
            shape(full1.shape, BF),
            shape((16, width), F32),
        ),
        in_specs=[vmem()] * 10,
        out_specs=[vmem()] * 7,
        scratch_shapes=[
            pltpu.VMEM((parts, ROWS, width), F32),
            pltpu.VMEM((parts, ROWS, width), F32),
            pltpu.VMEM((half, width), F32),
            pltpu.VMEM((length, width), BF),
            pltpu.VMEM((2, length, width), BF),
            pltpu.VMEM((2, length, width), BF),
            pltpu.VMEM((half, width), F32),
            pltpu.VMEM((length, width), BF),
            pltpu.VMEM((length, width), BF),
            pltpu.VMEM((half, width), F32),
            pltpu.VMEM((half, 1), F32),
            pltpu.VMEM((width, length), BF),
            dma((3, parts)),
            dma((3, parts)),
            dma((3, parts)),
            dma((3, parts)),
        ],
        compiler_params=pltpu.CompilerParams(
            collective_id=2, has_side_effects=True, vmem_limit_bytes=VMEM_LIMIT
        ),
        name="middle",
    )(x_all, up_half, full0, full1, full2, mixed, outs, gains, shifts, ups)
class Reduce:
    def __init__(self, at, grads, work, plane, zline, final, send, recv):
        self.at, self.grads, self.work, self.plane, self.zline, self.final = at, grads, work, plane, zline, final
        self.send, self.recv = send, recv

    def cp(self, g, slot, kind, src, dst, device, recv_kind=None):
        recv_kind = kind if recv_kind is None else recv_kind
        return copy_to(src, dst, self.send.at[g, slot, kind], self.recv.at[g, slot, recv_kind], device)

    def arrives(self, g, slot, kind, dst):
        self.cp(g, slot, kind, dst, dst, self.at.core).wait_recv()

    def plane_sends(self, g, slot):
        at, grad, box = self.at, self.grads[g], self.plane.at[g, slot]
        return (
            self.cp(g, slot, 1, grad.at[slot, at.other, 1 - at.c], box.at[1], at.xnbr),
            self.cp(g, slot, 3, grad.at[slot, at.other + 1, 1 - at.c], box.at[3], at.ynbr),
            self.cp(g, slot, 0, grad.at[slot, at.pair, 1 - at.c], box.at[0], at.xnbr),
            self.cp(g, slot, 2, grad.at[slot, at.other + 1, at.c], box.at[2], at.ynbr),
        )

    def sums(self, g, slot):
        at, work, box = self.at, self.work.at[g, slot], self.plane.at[g, slot]
        return (
            self.cp(g, slot, 4, work.at[0], box.at[4], at.ynbr),
            self.cp(g, slot, 5, work.at[1], box.at[5], at.xnbr),
        )

    def plane0(self, g):
        for slot in range(2):
            for copy in self.plane_sends(g, slot):
                copy.start()

    def plane1(self, g):
        at, grad = self.at, self.grads[g]
        for slot in range(2):
            to_y, to_x = self.sums(g, slot)
            for i, kind, piece, copy in (
                (0, 1, (at.other, at.c), to_y),
                (1, 3, (at.pair + 1, 1 - at.c), to_x),
            ):
                self.arrives(g, slot, kind, self.plane.at[g, slot, kind])
                own = grad[slot, piece[0], piece[1]].astype(F32)
                self.work[g, slot, i] = (own + self.plane[g, slot, kind].astype(F32)).astype(BF)
                copy.start()

    def ours(self, g, slot):
        return self.work.at[g, slot, pl.ds(2, 2)]

    def down(self, g, slot):
        return self.cp(g, slot, 6, self.ours(g, slot), self.zline.at[g, slot, 0], self.at.zminus)

    def upward(self, g, slot):
        return self.cp(g, slot, 7, self.ours(g, slot), self.zline.at[g, slot, 1], self.at.zplus)

    def plane2(self, g):
        at, grad = self.at, self.grads[g]
        for slot in range(2):
            for kind in (0, 2, 4, 5):
                self.arrives(g, slot, kind, self.plane.at[g, slot, kind])
            for i, one, two in ((0, 0, 4), (1, 2, 5)):
                self.work[g, slot, 2 + i] = (
                    grad[slot, at.pair + i, at.c].astype(F32)
                    + (self.plane[g, slot, one].astype(F32) + self.plane[g, slot, two].astype(F32))
                ).astype(BF)

            @pl.when(at.p == 3)
            def _():
                self.down(g, slot).start()

            if slot == 1:

                @pl.when(at.p == 0)
                def _():
                    self.upward(g, slot).start()

    def add_line(self, g, slot, which):
        self.arrives(g, slot, 6 + which, self.zline.at[g, slot, which])
        for i in range(2):
            self.work[g, slot, 2 + i] = (
                self.work[g, slot, 2 + i].astype(F32) + self.zline[g, slot, which, i].astype(F32)
            ).astype(BF)

    def line(self, g, place):
        at = self.at
        for slot in range(2):
            if place < slot:
                continue

            @pl.when(at.p == place)
            def _():
                self.add_line(g, slot, 0)
                if slot == 1 and place == 1:
                    self.add_line(g, slot, 1)
                if place > slot:
                    self.down(g, slot).start()
                else:
                    self.hand_out(g, slot)

    def hands(self, g, slot):
        at, final = self.at, self.final[g]
        mine = self.work.at[g, slot, 2 + at.k]
        theirs = self.work.at[g, slot, 3 - at.k]
        return (
            self.cp(g, slot, 8, theirs, final.at[at.c], at.core, 8),
            self.cp(g, slot, 9, mine, final.at[at.c], at.xnbr, 9),
            self.cp(g, slot, 10, theirs, final.at[at.c], (at.core[0], 1 - at.c, at.t), 9),
        )

    def hand_out(self, g, slot):
        at = self.at
        for copy in self.hands(g, slot):
            copy.start()
        self.final[g][at.c] = self.work[g, slot, 2 + at.k]

    def finish(self, g, out):
        at, final = self.at, self.final[g]

        @pl.when(at.k != at.own_core)
        def _():
            self.arrives(g, at.own_slot, 8, final.at[at.c])

        self.arrives(g, at.own_slot, 9, final.at[1 - at.c])
        half = final.shape[1]
        for i in range(2):
            out[i * half : (i + 1) * half, :] = final[i].astype(F32)

    def sent(self, g):
        at = self.at
        for slot in range(2):
            for copy in (*self.plane_sends(g, slot), *self.sums(g, slot)):
                copy.wait_send()

            @pl.when(at.p > slot)
            def _():
                self.down(g, slot).wait_send()

            if slot == 1:

                @pl.when(at.p == 0)
                def _():
                    self.upward(g, slot).wait_send()

            @pl.when(at.p == slot)
            def _():
                for copy in self.hands(g, slot):
                    copy.wait_send()


def attend_back_chunk(h, q, key, query, value, key_t, bias, lse, grad, key_sum, value_sum, query_t):
    cols = pl.ds(pl.multiple_of(q * QCHUNK, QCHUNK), QCHUNK)
    some = query[h, cols, :]
    upper = grad[h, cols, :]
    scores = mm(key[h], some, NT)
    length = scores.shape[0]
    shift = bias[h, :, cols] - lse[h, :, cols]
    scores = (scores.reshape(length // BLK, BLK, QCHUNK) + shift[:, None, :]).reshape(length, QCHUNK)
    probs = jnp.exp(scores)
    probs_grad = mm(value[h], upper, NT)
    inner = jnp.sum(probs * probs_grad, axis=0, keepdims=True)
    scores_grad = (probs * (probs_grad - inner)).astype(BF)
    value_sum[...] += mm(probs.astype(BF), upper)
    key_sum[...] += mm(scores_grad, some)
    query_t[:, cols] = mm(key_t[...], scores_grad)


def backward_kernel(
    x_all, full0, grad1, grad2, grad_out, query, key, value, lse, bias, mixed_grad, residual, layer_rows, small,
    layer_blocks, grad_blocks, out0, out1, out2, small_out,
    grad0, proj_grad, key_t, key_sum, value_sum, query_t, flipped, grad_rows, part_out, part_back,
    work, plane, zline, final0, final1, final2, sum_out, sum_in,
    lo_send, lo_recv, gi_send, gi_recv, w_send, w_recv, send, recv, small_send, small_recv,
):
    at = Place()
    greet(at)
    layer = Swap(at, layer_blocks, layer_rows, 0, lo_send, lo_recv)
    inputs = Swap(at, grad_blocks, grad_rows, 0, gi_send, gi_recv)
    reduce = Reduce(at, (grad0, grad1, grad2), work, plane, zline, (final0, final1, final2), w_send, w_recv)
    cores = Cores(at, part_out, part_back, send, recv, None, None)
    width = x_all.shape[1]
    reduce.plane0(2)
    reduce.plane0(1)
    for s in range(4):
        layer.start_out(s)
    for slot in range(2):
        proj_grad[slot, :, 576:640] = jnp.zeros((1024, 64), BF)

    def attend(h):
        key_t[...] = key[h].astype(F32).T.astype(BF)
        key_sum[...] = jnp.zeros_like(key_sum)
        value_sum[...] = jnp.zeros_like(value_sum)

        @pl.loop(0, 1024 // QCHUNK)
        def _(q):
            attend_back_chunk(
                h, q, key, query, value, key_t, bias, lse, mixed_grad, key_sum, value_sum, query_t
            )

        start = (h % 3) * 192
        proj_grad[h // 3, :, start : start + 64] = (query_t[...] * 0.125).T.astype(BF)
        proj_grad[h // 3, :, start + 64 : start + 128] = key_sum[...].astype(BF)
        proj_grad[h // 3, :, start + 128 : start + 192] = value_sum[...].astype(BF)

    attend(0)
    reduce.plane1(2)
    attend(1)
    reduce.plane2(2)
    attend(2)
    reduce.line(2, 2)
    reduce.plane1(1)
    attend(3)
    reduce.line(2, 1)
    reduce.plane2(1)
    attend(4)
    reduce.line(2, 0)
    reduce.line(1, 2)
    attend(5)
    reduce.line(1, 1)

    flip(flipped, x_all)

    @pl.loop(0, 4)
    def _(r):
        rows = pl.ds(pl.multiple_of(r * 192, 192), 192)
        for slot in range(2):
            got = mm(flipped[rows, :], proj_grad[slot])
            out_part = grad_out[rows, slot * 256 : slot * 256 + 256]
            grad0[slot, r, :, :, 0:512] = got[:, 0:512].astype(BF).reshape(2, 96, 512)
            shared = got[:, 512:640] + out_part[:, 0:128]
            grad0[slot, r, :, :, 512:640] = shared.astype(BF).reshape(2, 96, 128)
            grad0[slot, r, :, :, 640:768] = out_part[:, 128:256].astype(BF).reshape(2, 96, 128)

    reduce.plane0(0)

    def in_part(rows):
        return sum(
            mm(proj_grad[slot, rows, :], full0[slot, :, :, :, 0:640].reshape(width, 640), NT)
            for slot in range(2)
        )

    def in_done(i, rows, total):
        local = pl.ds(pl.multiple_of(i * ROWS, ROWS), ROWS)
        grad_rows[local, :] = (total + residual[local, :]).astype(BF)
        for s in range(ROWS // 128):
            inputs.start_out(i * (ROWS // 128) + s)

    cores.reduce(0, in_part, in_done)
    reduce.line(1, 0)
    reduce.plane1(0)

    t = at.t
    steps = (at.xnbr, at.ynbr, (at.f, at.c, t + 1 - 2 * lax.rem(t, 2)), (at.f, at.c, lax.rem(t + 2, 4)))
    sum_out[0] = small[...]
    for slot in range(2):
        sum_out[0, 8 + slot : 9 + slot, 0:640] = row_sum(proj_grad[slot].astype(F32))
    for i, device in enumerate(steps):
        copy = copy_to(sum_out.at[i], sum_in.at[i], small_send.at[i], small_recv.at[i], device)
        copy.start()
        copy.wait_recv()
        if i < 3:
            sum_out[i + 1] = sum_out[i] + sum_in[i]
        else:
            small_out[at.k] = sum_out[i] + sum_in[i]
        copy.wait_send()
    both = copy_to(small_out.at[at.k], small_out.at[at.k], small_send.at[4], small_recv.at[4], at.core)
    both.start()

    reduce.plane2(0)
    reduce.line(0, 2)
    reduce.line(0, 1)
    reduce.line(0, 0)
    reduce.finish(2, out2)
    reduce.finish(1, out1)
    reduce.finish(0, out0)
    both.wait_send()
    copy_to(small_out.at[1 - at.k], small_out.at[1 - at.k], small_send.at[4], small_recv.at[4], at.core).wait_recv()
    for s in range(4):
        layer.wait_out(s)
        inputs.wait_out(s)
    layer.sent()
    inputs.sent()
    for g in range(3):
        reduce.sent(g)


def backward_call(x_all, full0, grad1, grad2, grad_out, query, key, value, lse, bias, mixed_grad, residual, layer_rows, small):
    length, width = x_all.shape
    half = length // 2
    shape = jax.ShapeDtypeStruct
    dma = pltpu.SemaphoreType.DMA
    fr = width // 4
    return pl.pallas_call(
        backward_kernel,
        out_shape=(
            shape((4, 128, width), BF),
            shape((4, 128, width), BF),
            shape((fr, width), F32),
            shape((fr, width), F32),
            shape((fr, width), F32),
            shape((2, 16, width), F32),
        ),
        in_specs=[vmem()] * 14,
        out_specs=[vmem()] * 6,
        scratch_shapes=[
            pltpu.VMEM(full0.shape, BF),
            pltpu.VMEM((2, length, 640), BF),
            pltpu.VMEM((64, length), BF),
            pltpu.VMEM((length, 64), F32),
            pltpu.VMEM((length, 64), F32),
            pltpu.VMEM((64, length), F32),
            pltpu.VMEM((width, length), BF),
            pltpu.VMEM((half, width), BF),
            pltpu.VMEM((half // ROWS, ROWS, width), F32),
            pltpu.VMEM((half // ROWS, ROWS, width), F32),
            pltpu.VMEM((3, 2, 4, fr // 2, width), BF),
            pltpu.VMEM((3, 2, 6, fr // 2, width), BF),
            pltpu.VMEM((3, 2, 2, 2, fr // 2, width), BF),
            pltpu.VMEM((2, fr // 2, width), BF),
            pltpu.VMEM((2, fr // 2, width), BF),
            pltpu.VMEM((2, fr // 2, width), BF),
            pltpu.VMEM((4, 16, width), F32),
            pltpu.VMEM((4, 16, width), F32),
            dma((4,)),
            dma((4,)),
            dma((4,)),
            dma((4,)),
            dma((3, 2, 11)),
            dma((3, 2, 11)),
            dma((1, half // ROWS)),
            dma((1, half // ROWS)),
            dma((5,)),
            dma((5,)),
        ],
        compiler_params=pltpu.CompilerParams(
            collective_id=3, has_side_effects=True, vmem_limit_bytes=VMEM_LIMIT
        ),
        name="backward",
    )(x_all, full0, grad1, grad2, grad_out, query, key, value, lse, bias, mixed_grad, residual, layer_rows, small)


def sequence_shards(*args):
    w_in, w_out = args[2], args[4]
    xs, cs, shards_low, bias, proj_bias, proj_scale, outs, gains, shifts, ups = prepare(*args)
    x_all, up_half, full0, full1, full2, query, key, value, mixed, lse = forward_call(
        xs, cs, shards_low, bias, proj_bias, proj_scale
    )
    layer_rows, residual, mixed_grad, grad_out, grad1, grad2, small = middle_call(
        x_all, up_half, full0, full1, full2, mixed, outs, gains, shifts, ups
    )
    layer_blocks, grad_blocks, out0, out1, out2, sums = backward_call(
        x_all, full0, grad1, grad2, grad_out, query, key, value, lse, bias, mixed_grad, residual, layer_rows, small
    )
    f, t = lax.axis_index("fsdp"), lax.axis_index("tp")
    core, slot = t // 2, t + (t // 2) * (3 - 2 * t)
    rows, heads, wide = w_in.shape
    both = sums[0] + sums[1]
    piece = lambda a: lax.dynamic_slice_in_dim(a, f * rows, rows, axis=a.ndim - 1)
    vectors = piece(both[0:6])
    used = lax.dynamic_index_in_dim(sums, core, 0, False)
    up_grad = piece(lax.dynamic_index_in_dim(used, 6 + slot, 0, False))
    proj = lax.dynamic_index_in_dim(used, 8 + slot, 0, False)[: heads * wide].reshape(heads, 3, wide // 3)
    pair_bias = jnp.stack([proj[:, 0].reshape(-1), proj[:, 2].reshape(-1)])
    pair_bias = lax.dynamic_slice_in_dim(pair_bias, f * (rows // 4), rows // 4, axis=1)
    return (
        layer_blocks.transpose(1, 0, 2),
        grad_blocks.transpose(1, 0, 2),
        out0[:, : heads * wide].reshape(rows, heads, wide),
        pair_bias,
        out0[:, heads * wide :].T,
        vectors[0:2],
        vectors[2:4],
        vectors[4:6],
        out1,
        up_grad,
        out2.T,
    )


def solution(mesh):
    placed = (
        P(("ctx", "tp"), "fsdp", None),
        P("fsdp", None, "tp", None),
        P("fsdp", "tp", None),
        P(None, ("tp", "fsdp")),
        P("tp", "fsdp"),
        P(None, "fsdp"),
        P(None, "fsdp"),
        P(None, "fsdp"),
        P("fsdp", "tp"),
        P(("tp", "fsdp")),
        P("tp", "fsdp"),
        P(("ctx", "tp"), "fsdp", None),
    )
    sizes = tuple(mesh.shape[a] for a in ("fsdp", "ctx", "tp"))

    def local(*args):
        part_rows, seqs, width = args[0].shape
        rows, heads, wide = args[2].shape
        whole = sizes == (4, 2, 4) and (part_rows, seqs, width) == (128, 4, 768)
        whole = whole and (rows, heads, wide) == (192, 3, 192) and args[8].shape == (192, 768)
        return (sequence_shards if whole else span_shards)(*args)

    return jax.shard_map(
        local,
        mesh=mesh,
        in_specs=placed,
        out_specs=(
            P(("ctx", "tp"), "fsdp", None),
            P(("ctx", "tp"), "fsdp", None),
            P("fsdp", "tp", None),
            P(None, ("tp", "fsdp")),
            P("tp", "fsdp"),
            P(None, "fsdp"),
            P(None, "fsdp"),
            P(None, "fsdp"),
            P("fsdp", "tp"),
            P(("tp", "fsdp")),
            P("tp", "fsdp"),
        ),
        check_vma=False,
    )
```

```python
import jax
import jax.numpy as jnp
from jax import lax
from jax.experimental import pallas as pl
from jax.experimental.pallas import tpu as pltpu
from jax.sharding import PartitionSpec as P

BLK = 64


EPS = 1e-06
NEG = -1000000000.0


def from_root(block, axis, owner):
    block = jnp.where(lax.axis_index(axis) == owner, block, jnp.zeros_like(block))
    return lax.psum(block, axis)


def extended(array, sides, width):
    for axis, dim in sides:
        size, length = (lax.axis_size(axis), array.shape[dim])
        up = [(i, (i + 1) % size) for i in range(size - 1)]
        down = [(j, i) for i, j in up]
        last = lax.slice_in_dim(array, length - width, length, axis=dim)
        leading = lax.slice_in_dim(array, 0, width, axis=dim)
        before = lax.ppermute(last, axis, up)
        after = lax.ppermute(leading, axis, down)
        array = jnp.concatenate([before, array, after], axis=dim)
    return array


def joined_2(part, axis, combine):
    gathered = jax.tree.map(lambda a: lax.all_gather(a, axis), part)

    def take(source):
        return jax.tree.map(lambda a: lax.dynamic_index_in_dim(a, source, 0, False), gathered)

    return lax.fori_loop(
        1, lax.axis_size(axis), lambda source, state: combine(state, take(source)), take(0)
    )


def norm_forward(value, gain, shift):
    mean = jnp.mean(value, axis=-1, keepdims=True)
    centred = value - mean
    inverse = lax.rsqrt(jnp.mean(centred * centred, axis=-1, keepdims=True) + EPS)
    normed = centred * inverse
    return (normed * gain + shift, normed, inverse)


def norm_backward(upper, normed, inverse, gain):
    scaled = upper * gain
    return inverse * (
        scaled
        - jnp.mean(scaled, axis=-1, keepdims=True)
        - normed * jnp.mean(scaled * normed, axis=-1, keepdims=True)
    )


def exact_gelu(value):
    return jax.nn.gelu(value, approximate=False)


def outer_sum(left, right):
    return lax.dot_general(
        left, right, (((0,), (0,)), ((), ())), preferred_element_type=jnp.float32
    )


def rows_all(value):
    return lax.all_gather(value, "tp", axis=0, tiled=True)


def rows_sum(left, right, contract):
    return lax.psum_scatter(
        lax.dot_general(
            left, right, (((1,), (contract,)), ((), ())), preferred_element_type=jnp.float32
        ),
        "tp",
        scatter_dimension=0,
        tiled=True,
    )


def spread(piece, root):
    return from_root(piece, "ctx", root)


def stats_join(first_stats, second_stats):
    top = jnp.maximum(first_stats[0], second_stats[0])
    total = first_stats[1] * jnp.exp(first_stats[0] - top) + second_stats[1] * jnp.exp(
        second_stats[0] - top
    )
    return (top, total)


def split_groups(array, steps, group):
    return array.reshape((steps, group) + array.shape[1:])


def key_set(window_pad, global_pair, random_pairs):
    per_dev = random_pairs.shape[3]
    window = jnp.stack(
        [window_pad[:, :, offset_by : offset_by + per_dev] for offset_by in range(3)], axis=3
    )
    target_shape = global_pair.shape[:2] + (per_dev,) + global_pair.shape[2:]
    global_all = jnp.broadcast_to(global_pair[:, :, None], target_shape)
    random_all = jnp.swapaxes(random_pairs, 2, 3)
    joined = jnp.concatenate([window, global_all, random_all], axis=3)
    shape = joined.shape
    return joined.reshape(shape[0], shape[1], shape[2], shape[3] * shape[4], shape[5])


def scores_of(query, keys, mask, scale):
    head_dim = query.shape[-1]
    raw = (
        jnp.einsum(
            "shpqd,shpkd->shpqk", query, keys[..., :head_dim], preferred_element_type=jnp.float32
        )
        * scale
    )
    return jnp.where(mask, raw, NEG)


def attend_group(query, window_pad, global_pair, random_pairs, mask, scale):
    head_dim = query.shape[-1]
    keys = key_set(window_pad, global_pair, random_pairs)
    scores = scores_of(query, keys, mask, scale)
    top = jnp.max(scores, axis=-1, keepdims=True)
    weights = jnp.exp(scores - top)
    total = jnp.sum(weights, axis=-1, keepdims=True)
    probs = (weights / total).astype(jnp.bfloat16)
    mixed = jnp.einsum(
        "shpqk,shpkd->shpqd", probs, keys[..., head_dim:], preferred_element_type=jnp.float32
    )
    return (mixed.astype(jnp.bfloat16), (top + jnp.log(total))[..., 0])


def attend_back(query, window_pad, global_pair, random_pairs, mask, scale, logsum, mixed_grad):
    head_dim = query.shape[-1]
    blocksize = window_pad.shape[3]
    keys = key_set(window_pad, global_pair, random_pairs)
    scores = scores_of(query, keys, mask, scale)
    probs = jnp.exp(scores - logsum[..., None])
    probs_grad = jnp.einsum(
        "shpqd,shpkd->shpqk", mixed_grad, keys[..., head_dim:], preferred_element_type=jnp.float32
    )
    inner = jnp.sum(probs * probs_grad, axis=-1, keepdims=True)
    scores_grad = (probs * (probs_grad - inner)).astype(jnp.bfloat16)
    query_grad = (
        jnp.einsum(
            "shpqk,shpkd->shpqd",
            scores_grad,
            keys[..., :head_dim],
            preferred_element_type=jnp.float32,
        )
        * scale
    )
    keys_grad = (
        jnp.einsum("shpqk,shpqd->shpkd", scores_grad, query, preferred_element_type=jnp.float32)
        * scale
    )
    values_grad = jnp.einsum(
        "shpqk,shpqd->shpkd",
        probs.astype(jnp.bfloat16),
        mixed_grad,
        preferred_element_type=jnp.float32,
    )
    pairs_grad = jnp.concatenate([keys_grad, values_grad], axis=-1)
    shape = pairs_grad.shape
    pairs_grad = pairs_grad.reshape(
        shape[0], shape[1], shape[2], shape[3] // blocksize, blocksize, shape[4]
    )
    per_dev = shape[2]
    window_grad = jnp.zeros(window_pad.shape, jnp.float32)
    for offset_by in range(3):
        window_grad = window_grad.at[:, :, offset_by : offset_by + per_dev].add(
            pairs_grad[:, :, :, offset_by]
        )
    global_grad = jnp.sum(pairs_grad[:, :, :, 3:5], axis=2)
    random_grad = jnp.swapaxes(pairs_grad[:, :, :, 5:], 2, 3)
    return (query_grad, window_grad, global_grad, random_grad)


def span_shards(
    hidden_in,
    rand_blocks,
    w_in,
    qv_bias,
    w_out,
    out_bias,
    norm_gain,
    norm_bias,
    w_up,
    up_bias,
    w_down,
    cotangent,
):
    ctx_count = lax.axis_size("ctx")
    tp_count = lax.axis_size("tp")
    ctx_place = lax.axis_index("ctx")
    part_rows, seqs, width = hidden_in.shape
    heads = w_in.shape[1]
    head_dim = w_in.shape[2] // 3
    pair_width = 2 * head_dim
    blocks_all = rand_blocks.shape[1]
    picks = rand_blocks.shape[3]
    length = part_rows * tp_count
    per_dev = length // BLK
    total_rows = length * seqs
    scale = head_dim ** (-0.5)
    group = min(seqs, max(1, 512 // length))
    steps = seqs // group
    first_owner = ctx_place == 0
    last_owner = ctx_place == ctx_count - 1
    gathered = (
        lax.all_gather(w_in.astype(jnp.bfloat16), "fsdp", axis=0, tiled=True),
        lax.all_gather(qv_bias.astype(jnp.bfloat16), "fsdp", axis=1, tiled=True),
        lax.all_gather(w_out.astype(jnp.bfloat16), "fsdp", axis=1, tiled=True),
        lax.all_gather(out_bias.astype(jnp.bfloat16), "fsdp", axis=1, tiled=True),
        lax.all_gather(norm_gain.astype(jnp.bfloat16), "fsdp", axis=1, tiled=True),
        lax.all_gather(norm_bias.astype(jnp.bfloat16), "fsdp", axis=1, tiled=True),
        lax.all_gather(w_up.astype(jnp.bfloat16), "fsdp", axis=0, tiled=True),
        lax.all_gather(up_bias.astype(jnp.bfloat16), "fsdp", axis=0, tiled=True),
        lax.all_gather(w_down.astype(jnp.bfloat16), "fsdp", axis=1, tiled=True),
    )
    input_low = gathered[0].reshape(width, heads * 3 * head_dim)
    bias_pair = gathered[1].astype(jnp.float32).reshape(2, heads, head_dim)
    output_low = gathered[2]
    bias_out = gathered[3].astype(jnp.float32)
    gains = gathered[4].astype(jnp.float32)
    shifts = gathered[5].astype(jnp.float32)
    upper_low = gathered[6]
    bias_up = gathered[7].astype(jnp.float32)
    lower_low = gathered[8]
    x_full = rows_all(hidden_in)
    x_rows = x_full.reshape(total_rows, width)
    projected = jnp.dot(x_rows, input_low, preferred_element_type=jnp.float32).reshape(
        length, seqs, heads, 3, head_dim
    )
    query = (projected[:, :, :, 0] + bias_pair[0]).astype(jnp.bfloat16)
    key = projected[:, :, :, 1].astype(jnp.bfloat16)
    value = (projected[:, :, :, 2] + bias_pair[1]).astype(jnp.bfloat16)
    query_heads = query.transpose(1, 2, 0, 3).reshape(seqs, heads, per_dev, BLK, head_dim)
    pairs = jnp.concatenate([key, value], axis=-1).transpose(1, 2, 0, 3)
    window_pad = extended(pairs, (("ctx", 2),), BLK).reshape(
        seqs, heads, per_dev + 2, BLK, pair_width
    )
    pair_blocks = pairs.reshape(seqs, heads, per_dev, BLK, pair_width)
    triple_blocks = jnp.concatenate([query_heads, pair_blocks], axis=-1)
    global_triple = jnp.stack(
        [
            spread(triple_blocks[:, :, 0], 0),
            spread(triple_blocks[:, :, per_dev - 1], ctx_count - 1),
        ],
        axis=2,
    )
    global_query = global_triple[..., :head_dim]
    global_pair = global_triple[..., head_dim:]
    key_local = pairs[..., :head_dim]
    value_local = pairs[..., head_dim:]
    wide_scores = (
        jnp.einsum("shgqd,shkd->shgqk", global_query, key_local, preferred_element_type=jnp.float32)
        * scale
    )
    wide_top = jnp.max(wide_scores, axis=-1)
    wide_total = jnp.sum(jnp.exp(wide_scores - wide_top[..., None]), axis=-1)
    all_top, all_total = joined_2((wide_top, wide_total), "ctx", stats_join)
    wide_probs = jnp.exp(wide_scores - (all_top + jnp.log(all_total))[..., None])
    wide_probs_low = wide_probs.astype(jnp.bfloat16)
    mix_low = jnp.einsum(
        "shgqk,shkd->shgqd", wide_probs_low, value_local, preferred_element_type=jnp.float32
    )
    mix_full = jnp.einsum(
        "shgqk,shkd->shgqd",
        wide_probs,
        value_local.astype(jnp.float32),
        precision=lax.Precision.HIGHEST,
    )
    mix_low, mix_full = lax.psum((mix_low, mix_full), "ctx")
    global_mixed = mix_low.astype(jnp.bfloat16)
    units = seqs * heads * picks * per_dev
    table = rand_blocks.transpose(0, 2, 3, 1).reshape(seqs, heads, picks, ctx_count, per_dev)
    table = table.transpose(0, 1, 2, 4, 3).reshape(units, ctx_count)
    mine = lax.dynamic_index_in_dim(table, ctx_place, 1, keepdims=False)
    mine_groups = mine.reshape(steps, group, heads, picks, per_dev)
    block_index = ctx_place * per_dev + jnp.arange(per_dev)
    present = jnp.concatenate(
        [
            (block_index >= 1)[:, None],
            jnp.ones((per_dev, 1), jnp.bool_),
            (block_index <= blocks_all - 2)[:, None],
            jnp.ones((per_dev, 2 + picks), jnp.bool_),
        ],
        axis=1,
    )
    mask = jnp.repeat(present, BLK, axis=1)[None, None, :, None, :]

    def random_pairs_for(block_group, id_group):
        whole = lax.all_gather(block_group, "ctx", axis=2, tiled=True)
        chosen = jax.nn.one_hot(id_group, blocks_all, dtype=jnp.bfloat16)
        return jnp.einsum(
            "shpqb,shbke->shpqke", chosen, whole, preferred_element_type=jnp.float32
        ).astype(jnp.bfloat16)

    query_groups = split_groups(query_heads, steps, group)
    pad_groups = split_groups(window_pad, steps, group)
    global_groups = split_groups(global_pair, steps, group)
    block_groups = split_groups(pair_blocks, steps, group)

    def forward_step(items):
        position, query_group, pad_group, global_group, block_group, id_group = items
        random_group = random_pairs_for(block_group, id_group)
        return attend_group(query_group, pad_group, global_group, random_group, mask, scale)

    mixed_groups, logsum_groups = lax.map(
        forward_step,
        (jnp.arange(steps), query_groups, pad_groups, global_groups, block_groups, mine_groups),
    )
    mixed_blocks = mixed_groups.reshape(seqs, heads, per_dev, BLK, head_dim)
    mixed_blocks = mixed_blocks.at[:, :, 0].set(
        jnp.where(first_owner, global_mixed[:, :, 0], mixed_blocks[:, :, 0])
    )
    mixed_blocks = mixed_blocks.at[:, :, per_dev - 1].set(
        jnp.where(last_owner, global_mixed[:, :, 1], mixed_blocks[:, :, per_dev - 1])
    )
    mixed = (
        mixed_blocks.reshape(seqs, heads, length, head_dim)
        .transpose(2, 0, 1, 3)
        .reshape(total_rows, heads * head_dim)
    )
    branch = rows_sum(mixed, output_low, 0) + bias_out[0]
    residual_in = hidden_in.reshape(part_rows * seqs, width).astype(jnp.float32)
    first, normed_one, inverse_one = norm_forward(residual_in + branch, gains[0], shifts[0])
    first_full = rows_all(first.astype(jnp.bfloat16).reshape(part_rows, seqs, width)).reshape(
        total_rows, width
    )
    inner = jnp.dot(first_full, upper_low, preferred_element_type=jnp.float32) + bias_up
    active_value, gelu_back = jax.vjp(exact_gelu, inner)
    active = active_value.astype(jnp.bfloat16)
    second = rows_sum(active, lower_low, 0) + bias_out[1]
    result, normed_two, inverse_two = norm_forward(first + second, gains[1], shifts[1])
    layer_out = result.astype(jnp.bfloat16).reshape(part_rows, seqs, width)
    upstream = cotangent.reshape(part_rows * seqs, width).astype(jnp.float32)
    second_grad = norm_backward(upstream, normed_two, inverse_two, gains[1])
    second_low = second_grad.astype(jnp.bfloat16)
    second_full = rows_all(second_low.reshape(part_rows, seqs, width)).reshape(total_rows, width)
    active_grad = lax.dot_general(
        second_full, lower_low, (((1,), (1,)), ((), ())), preferred_element_type=jnp.float32
    )
    inner_low = gelu_back(active_grad)[0].astype(jnp.bfloat16)
    first_grad = second_grad + rows_sum(inner_low, upper_low, 1)
    residual_grad = norm_backward(first_grad, normed_one, inverse_one, gains[0])
    branch_low = residual_grad.astype(jnp.bfloat16)
    branch_full = rows_all(branch_low.reshape(part_rows, seqs, width)).reshape(total_rows, width)
    mixed_grad = lax.dot_general(
        branch_full, output_low, (((1,), (1,)), ((), ())), preferred_element_type=jnp.float32
    ).astype(jnp.bfloat16)
    mixed_heads = (
        mixed_grad.reshape(length, seqs, heads, head_dim)
        .transpose(1, 2, 0, 3)
        .reshape(seqs, heads, per_dev, BLK, head_dim)
    )
    zero_block = jnp.zeros((seqs, heads, BLK, head_dim), jnp.bfloat16)
    lead_grad = jnp.where(first_owner, mixed_heads[:, :, 0], zero_block).astype(jnp.float32)
    tail_grad = jnp.where(last_owner, mixed_heads[:, :, per_dev - 1], zero_block).astype(
        jnp.float32
    )
    lead_sum, tail_sum = (
        lax.psum(lead_grad.astype(jnp.bfloat16), "ctx").astype(jnp.float32),
        lax.psum(tail_grad.astype(jnp.bfloat16), "ctx").astype(jnp.float32),
    )
    wide_grad = jnp.stack([lead_sum, tail_sum], axis=2).astype(jnp.bfloat16)
    mixed_heads = mixed_heads.at[:, :, 0].set(
        jnp.where(first_owner, zero_block, mixed_heads[:, :, 0])
    )
    mixed_heads = mixed_heads.at[:, :, per_dev - 1].set(
        jnp.where(last_owner, zero_block, mixed_heads[:, :, per_dev - 1])
    )

    def random_back(random_grad, id_group):
        chosen = jax.nn.one_hot(id_group, blocks_all, dtype=jnp.float32)
        spread_grad = jnp.einsum(
            "shpqb,shpqke->shbke", chosen, random_grad, precision=lax.Precision.HIGHEST
        )
        return lax.psum_scatter(
            spread_grad.astype(jnp.bfloat16), "ctx", scatter_dimension=2, tiled=True
        ).astype(jnp.float32)

    def backward_step(items):
        (
            position,
            query_group,
            pad_group,
            global_group,
            block_group,
            id_group,
            logsum_group,
            grad_group,
        ) = items
        random_group = random_pairs_for(block_group, id_group)
        query_grad, window_grad, global_grad, random_grad = attend_back(
            query_group,
            pad_group,
            global_group,
            random_group,
            mask,
            scale,
            logsum_group,
            grad_group,
        )
        return (query_grad, window_grad, global_grad, random_back(random_grad, id_group))

    query_grads, window_grads, global_grads, random_total = lax.map(
        backward_step,
        (
            jnp.arange(steps),
            query_groups,
            pad_groups,
            global_groups,
            block_groups,
            mine_groups,
            logsum_groups,
            split_groups(mixed_heads, steps, group),
        ),
    )
    query_grads = query_grads.reshape(seqs, heads, length, head_dim)
    window_grads = window_grads.reshape(seqs, heads, per_dev + 2, BLK, pair_width)
    global_grads = global_grads.reshape(seqs, heads, 2, BLK, pair_width)
    wide_inner = jnp.sum(wide_grad.astype(jnp.float32) * mix_full, axis=-1, keepdims=True)
    wide_probs_grad = jnp.einsum(
        "shgqd,shkd->shgqk", wide_grad, value_local, preferred_element_type=jnp.float32
    )
    wide_scores_grad = (wide_probs * (wide_probs_grad - wide_inner)).astype(jnp.bfloat16)
    wide_query_part = (
        jnp.einsum(
            "shgqk,shkd->shgqd", wide_scores_grad, key_local, preferred_element_type=jnp.float32
        )
        * scale
    )
    wide_key_grad = (
        jnp.einsum(
            "shgqk,shgqd->shkd", wide_scores_grad, global_query, preferred_element_type=jnp.float32
        )
        * scale
    )
    wide_value_grad = jnp.einsum(
        "shgqk,shgqd->shkd", wide_probs_low, wide_grad, preferred_element_type=jnp.float32
    )
    wide_pair_grad = jnp.concatenate([wide_key_grad, wide_value_grad], axis=-1).reshape(
        seqs, heads, per_dev, BLK, pair_width
    )
    rim_pair = jnp.concatenate([window_grads[:, :, 0], window_grads[:, :, per_dev + 1]], axis=2)
    rim_back = extended(rim_pair.astype(jnp.bfloat16), (("ctx", 2),), BLK).astype(rim_pair.dtype)
    local_grad = window_grads[:, :, 1 : per_dev + 1] + wide_pair_grad
    local_grad = local_grad.at[:, :, 0].add(rim_back[:, :, :BLK])
    local_grad = local_grad.at[:, :, per_dev - 1].add(rim_back[:, :, 3 * BLK :])
    global_total, wide_query = lax.psum((global_grads, wide_query_part), "ctx")
    local_grad = local_grad.at[:, :, 0].add(jnp.where(first_owner, global_total[:, :, 0], 0.0))
    local_grad = local_grad.at[:, :, per_dev - 1].add(
        jnp.where(last_owner, global_total[:, :, 1], 0.0)
    )
    query_grads = query_grads.at[:, :, :BLK].add(jnp.where(first_owner, wide_query[:, :, 0], 0.0))
    query_grads = query_grads.at[:, :, length - BLK :].add(
        jnp.where(last_owner, wide_query[:, :, 1], 0.0)
    )
    local_grad = local_grad + random_total.reshape(seqs, heads, per_dev, BLK, pair_width)
    pair_grad = local_grad.reshape(seqs, heads, length, pair_width).transpose(2, 0, 1, 3)
    query_part = query_grads.transpose(2, 0, 1, 3)
    projected_grad = jnp.concatenate([query_part, pair_grad], axis=-1).astype(jnp.bfloat16)
    projected_rows = projected_grad.reshape(total_rows, heads * 3 * head_dim)
    grad_in = (
        (residual_grad + rows_sum(projected_rows, input_low, 1))
        .astype(jnp.bfloat16)
        .reshape(part_rows, seqs, width)
    )
    input_grad = outer_sum(x_rows, projected_rows).reshape(width, heads, 3 * head_dim)
    pair_bias_grad = jnp.stack(
        [
            jnp.sum(projected_grad[..., :head_dim], axis=(0, 1), dtype=jnp.float32).reshape(-1),
            jnp.sum(projected_grad[..., 2 * head_dim :], axis=(0, 1), dtype=jnp.float32).reshape(
                -1
            ),
        ]
    )
    output_grad = outer_sum(mixed, branch_full)
    bias_grad = jnp.stack(
        [
            jnp.sum(branch_low, axis=0, dtype=jnp.float32),
            jnp.sum(second_low, axis=0, dtype=jnp.float32),
        ]
    )
    gain_grad = jnp.stack(
        [jnp.sum(first_grad * normed_one, axis=0), jnp.sum(upstream * normed_two, axis=0)]
    )
    shift_grad = jnp.stack([jnp.sum(first_grad, axis=0), jnp.sum(upstream, axis=0)])
    upper_grad = outer_sum(first_full, inner_low)
    upper_bias_grad = jnp.sum(inner_low, axis=0, dtype=jnp.float32)
    lower_grad = outer_sum(active, second_full)
    shares = (
        lax.psum_scatter(input_grad, "fsdp", scatter_dimension=0, tiled=True),
        lax.psum_scatter(pair_bias_grad, "fsdp", scatter_dimension=1, tiled=True),
        lax.psum_scatter(output_grad, "fsdp", scatter_dimension=1, tiled=True),
        lax.psum_scatter(bias_grad, "fsdp", scatter_dimension=1, tiled=True),
        lax.psum_scatter(gain_grad, "fsdp", scatter_dimension=1, tiled=True),
        lax.psum_scatter(shift_grad, "fsdp", scatter_dimension=1, tiled=True),
        lax.psum_scatter(upper_grad, "fsdp", scatter_dimension=0, tiled=True),
        lax.psum_scatter(upper_bias_grad, "fsdp", scatter_dimension=0, tiled=True),
        lax.psum_scatter(lower_grad, "fsdp", scatter_dimension=1, tiled=True),
    )
    matrices = lax.psum((shares[0], shares[1], shares[2], shares[6], shares[7], shares[8]), "ctx")
    vectors = lax.psum((shares[3], shares[4], shares[5]), ("ctx", "tp"))
    return (
        layer_out,
        grad_in,
        matrices[0],
        matrices[1],
        matrices[2],
        vectors[0],
        vectors[1],
        vectors[2],
        matrices[3],
        matrices[4],
        matrices[5],
    )


MESH = pl.DeviceIdType.MESH
BF = jnp.bfloat16
F32 = jnp.float32
NT = (((1,), (1,)), ((), ()))
NN = (((1,), (0,)), ((), ()))
TN = (((0,), (0,)), ((), ()))
VMEM_LIMIT = 58 * 2**20


def mm(left, right, dims=NN):
    return lax.dot_general(left, right, dims, preferred_element_type=F32)


class Place:
    def __init__(self):
        self.f = lax.axis_index("fsdp")
        self.c = lax.axis_index("ctx")
        self.t = lax.axis_index("tp")
        f, c, t = self.f, self.c, self.t
        self.k = k = lax.rem(f, 2)
        self.y = y = f // 2
        self.p = t + k * (3 - 2 * t)
        self.core = (f + 1 - 2 * k, c, t)
        self.xnbr = (f, 1 - c, t)
        self.ynbr = (lax.rem(f + 2, 4), c, t)
        self.zplus = (f, c, t + 1 - 2 * k)
        self.zminus = (f, c, t - 1 + 2 * k)
        self.own_core = t // 2
        self.own_slot = t + (t // 2) * (3 - 2 * t)
        self.pair = 2 * y
        self.other = 2 - 2 * y

    def swap(self, s):
        return (2 * self.y + self.c, self.k, s)

    def swap_is_self(self, s):
        return jnp.logical_and(self.k == self.c, self.t == s)


def copy_to(src, dst, send, recv, device):
    return pltpu.make_async_remote_copy(
        src_ref=src, dst_ref=dst, send_sem=send, recv_sem=recv, device_id=device, device_id_type=MESH
    )


def greet(at, between=lambda: None):
    barrier = pltpu.get_barrier_semaphore()
    sizes = [lax.axis_size(a) for a in ("fsdp", "ctx", "tp")]
    others = 0
    for i in range(sizes[0]):
        for j in range(sizes[1]):
            for m in range(sizes[2]):
                if i or j or m:
                    others += 1
                    device = (
                        lax.rem(at.f + i, sizes[0]),
                        lax.rem(at.c + j, sizes[1]),
                        lax.rem(at.t + m, sizes[2]),
                    )
                    pl.semaphore_signal(barrier, inc=1, device_id=device, device_id_type=MESH)
    between()
    pl.semaphore_wait(barrier, others)


class Gather:
    def __init__(self, at, shards, full, send, recv):
        self.at, self.shards, self.full, self.send, self.recv = at, shards, full, send, recv

    def own(self, g):
        at, full, shard = self.at, self.full[g], self.shards[g]
        half = shard.shape[0] // 2
        rows = pl.ds(pl.multiple_of(at.c * half, half), half)

        @pl.when(at.k == at.own_core)
        def _():
            full[at.own_slot, at.f, at.c] = shard[rows, :]

        @pl.when(at.k != at.own_core)
        def _():
            self.cp(g, at.own_slot, 0, shard.at[rows], full.at[at.own_slot, at.f, at.c], at.core).start()

    def cp(self, g, slot, kind, src, dst, device):
        return copy_to(src, dst, self.send.at[g, slot, kind], self.recv.at[g, slot, kind], device)

    def arrives(self, g, slot, kind, dst):
        self.cp(g, slot, kind, dst, dst, self.at.core).wait_recv()

    def ours(self, g, slot, f, c):
        return self.full[g].at[slot, pl.ds(f, 2), c]

    def step_z(self, g, turn):
        at, full = self.at, self.full[g]
        first = (at.p + 2) // 3
        slot = first if turn == 0 else 1 - first
        piece = self.ours(g, slot, at.pair, at.c)

        @pl.when(at.p == slot)
        def _():
            self.arrives(g, slot, 0, full.at[slot, at.core[0], at.c])

        @pl.when(at.p > slot)
        def _():
            self.arrives(g, slot, 1, piece)

        @pl.when(at.p < slot)
        def _():
            self.arrives(g, slot, 2, piece)

        @pl.when(jnp.logical_and(at.p >= slot, at.p < 3))
        def _():
            self.cp(g, slot, 1, piece, piece, at.zplus).start()

        @pl.when(jnp.logical_and(at.p == 1, slot == 1))
        def _():
            self.cp(g, slot, 2, piece, piece, at.zminus).start()

        self.cp(g, slot, 3, piece, piece, at.ynbr).start()
        self.cp(g, slot, 4, piece, piece, at.xnbr).start()

    def step_relay(self, g, turn):
        at, full = self.at, self.full[g]
        first = (at.p + 2) // 3
        slot = first if turn == 0 else 1 - first
        self.arrives(g, slot, 3, self.ours(g, slot, at.other, at.c))
        even = full.at[slot, at.other, at.c]
        self.cp(g, slot, 5, even, even, at.xnbr).start()
        self.arrives(g, slot, 4, self.ours(g, slot, at.pair, 1 - at.c))
        odd = full.at[slot, at.pair + 1, 1 - at.c]
        self.cp(g, slot, 6, odd, odd, at.ynbr).start()

    def step_last(self, g):
        at, full = self.at, self.full[g]
        for slot in range(2):
            self.arrives(g, slot, 5, full.at[slot, at.other, 1 - at.c])
            self.arrives(g, slot, 6, full.at[slot, at.other + 1, 1 - at.c])

    def sent(self, g):
        at, full = self.at, self.full[g]

        def left(slot, kind, src):
            self.cp(g, slot, kind, src, src, at.core).wait_send()

        @pl.when(at.k != at.own_core)
        def _():
            left(at.own_slot, 0, full.at[at.own_slot, at.f, at.c])

        for slot in range(2):
            piece = self.ours(g, slot, at.pair, at.c)

            @pl.when(jnp.logical_and(at.p >= slot, at.p < 3))
            def _():
                left(slot, 1, piece)

            if slot == 1:

                @pl.when(at.p == 1)
                def _():
                    left(slot, 2, piece)

            left(slot, 3, piece)
            left(slot, 4, piece)
            left(slot, 5, full.at[slot, at.other, at.c])
            left(slot, 6, full.at[slot, at.pair + 1, 1 - at.c])


class Swap:
    def __init__(self, at, blocks, rows, base, send, recv):
        self.at, self.blocks, self.rows, self.base, self.send, self.recv = at, blocks, rows, base, send, recv
        self.n = blocks.shape[1]

    def span(self, s, base):
        return pl.ds(pl.multiple_of(base + s * self.n, self.n), self.n)

    def start_in(self):
        at = self.at
        there = self.rows.at[self.span(at.t, self.base * at.c)]
        for s in range(4):

            @pl.when(at.swap_is_self(s))
            def _():
                self.rows[self.span(s, self.base * at.k), :] = self.blocks[s]

            @pl.when(jnp.logical_not(at.swap_is_self(s)))
            def _():
                copy_to(self.blocks.at[s], there, self.send.at[s], self.recv.at[at.t], at.swap(s)).start()

    def wait_in(self, s):
        at = self.at
        here = self.rows.at[self.span(s, self.base * at.k)]

        @pl.when(jnp.logical_not(at.swap_is_self(s)))
        def _():
            copy_to(here, here, self.send.at[s], self.recv.at[s], at.core).wait_recv()

    def start_out(self, s):
        at = self.at
        here = self.rows.at[self.span(s, self.base * at.k)]

        @pl.when(at.swap_is_self(s))
        def _():
            self.blocks[s] = self.rows[self.span(s, self.base * at.k), :]

        @pl.when(jnp.logical_not(at.swap_is_self(s)))
        def _():
            copy_to(here, self.blocks.at[at.t], self.send.at[s], self.recv.at[at.t], at.swap(s)).start()

    def wait_out(self, s):
        at = self.at

        @pl.when(jnp.logical_not(at.swap_is_self(s)))
        def _():
            copy_to(self.blocks.at[s], self.blocks.at[s], self.send.at[s], self.recv.at[s], at.core).wait_recv()

    def sent(self):
        at = self.at
        for s in range(4):

            @pl.when(jnp.logical_not(at.swap_is_self(s)))
            def _():
                copy_to(self.blocks.at[s], self.blocks.at[s], self.send.at[s], self.recv.at[s], at.core).wait_send()
QCHUNK = 256


def attend_chunk(h, q, key, query, value_t, bias, lse, mixed_t, spots):
    cols = pl.ds(pl.multiple_of(q * QCHUNK, QCHUNK), QCHUNK)
    scores = mm(key[h], query[h, cols, :], NT)
    length = scores.shape[0]
    scores = (
        scores.reshape(length // BLK, BLK, QCHUNK) + bias[h, :, cols][:, None, :]
    ).reshape(length, QCHUNK)
    top = jnp.max(scores, axis=0, keepdims=True)
    weights = jnp.exp(scores - top)
    total = jnp.sum(weights, axis=0, keepdims=True)
    probs = (weights * (1.0 / total)).astype(BF)
    lse[h, :, cols] = top + jnp.log(total)
    mixed_t[spots(h), cols] = mm(value_t[h], probs)


class Vectors:
    def __init__(self, at, own, vec, near, ids, picked, sems):
        self.at, self.own, self.vec, self.near, self.ids, self.picked = at, own, vec, near, ids, picked
        self.send, self.recv = sems

    def fill(self, out_bias, norm_gain, norm_bias, up_bias, qv_bias, rand):
        at = self.at
        size = out_bias.shape[1]
        for i, ref in enumerate((out_bias, norm_gain, norm_bias)):
            self.vec[at.f, 2 * i : 2 * i + 2, 0:size] = ref[...]
        self.own[0:1, 0:size] = up_bias[...]
        self.own[1:3, 0 : qv_bias.shape[1]] = qv_bias[...]
        self.ids[:, :, 0 : rand.shape[2]] = rand[...].astype(F32).astype(BF)

        @pl.when(at.k == at.own_core)
        def _():
            self.near[at.own_slot, at.f] = self.own[...]

            @pl.when(at.k == at.c)
            def _():
                self.picked[at.own_slot] = self.ids[at.t]

    def copies(self):
        at = self.at
        out = []
        box = self.vec.at[at.f]
        for i, f in enumerate((at.core[0], at.ynbr[0], lax.rem(at.core[0] + 2, 4))):
            out.append((None, copy_to(box, box, self.send.at[i], self.recv.at[at.f], (f, at.c, at.t))))
        for y in range(2):
            for t in range(4):
                f = 2 * y + at.own_core
                copy = copy_to(
                    self.own,
                    self.near.at[at.own_slot, at.f],
                    self.send.at[3 + 4 * y + t],
                    self.recv.at[4 + 4 * at.own_slot + at.f],
                    (f, at.c, t),
                )
                out.append((jnp.logical_or(f != at.f, t != at.t), copy))
        for s in range(4):
            f = at.pair + at.own_core
            copy = copy_to(
                self.ids.at[s],
                self.picked.at[at.own_slot],
                self.send.at[11 + s],
                self.recv.at[12 + at.own_slot],
                (f, at.k, s),
            )
            away = jnp.logical_or(f != at.f, s != at.t)
            out.append((jnp.logical_and(at.c == at.k, away), copy))
        return out

    def each(self, act):
        for condition, copy in self.copies():
            if condition is None:
                act(copy)
            else:
                pl.when(condition)(lambda copy=copy: act(copy))

    def start(self):
        self.each(lambda copy: copy.start())

    def sent(self):
        self.each(lambda copy: copy.wait_send())

    def wait(self):
        at = self.at

        def arrives(index, dst):
            copy_to(dst, dst, self.send.at[0], self.recv.at[index], at.core).wait_recv()

        for i in range(1, 4):
            f = lax.rem(at.f + i, 4)
            arrives(f, self.vec.at[f])
        for slot in range(2):
            ours = jnp.logical_and(at.k == at.own_core, slot == at.own_slot)
            for f in range(4):

                @pl.when(jnp.logical_not(jnp.logical_and(ours, f == at.f)))
                def _():
                    arrives(4 + 4 * slot + f, self.near.at[slot, f])

            @pl.when(jnp.logical_not(jnp.logical_and(ours, at.k == at.c)))
            def _():
                arrives(12 + slot, self.picked.at[slot])

    def unpack(self, vec_out, ups, proj_bias, row, bias):
        size = vec_out.shape[1] // 4
        low = lambda a: a.astype(BF).astype(F32)
        part = size // 4
        for f in range(4):
            vec_out[:, size * f : size * (f + 1)] = low(self.vec[f, :, 0:size])
        proj_bias[...] = jnp.zeros_like(proj_bias)
        for slot in range(2):
            for f in range(4):
                ups[slot : slot + 1, size * f : size * (f + 1)] = low(self.near[slot, f, 0:1, 0:size])
                row[slot, 0:2, part * f : part * (f + 1)] = low(self.near[slot, f, 1:3, 0:part])
            for i in range(3):
                start = i * size
                proj_bias[slot, :, start : start + 64] = row[slot, 0:1, 64 * i : 64 * i + 64]
                proj_bias[slot, :, start + 128 : start + 192] = row[slot, 1:2, 64 * i : 64 * i + 64]
        blocks, length = bias.shape[1], bias.shape[2]
        spot = lax.broadcasted_iota(jnp.int32, (blocks, length), 0)
        block = lax.broadcasted_iota(jnp.int32, (blocks, length), 1) // BLK
        number = lambda mask: jnp.where(mask, 1.0, 0.0)
        fixed = number(jnp.abs(spot - block) <= 1) + number(spot == 0) + number(spot == blocks - 1)
        edge = jnp.logical_or(block == 0, block == blocks - 1)
        spread_out = number(spot == block).astype(BF)
        here = spot.astype(F32)
        for slot in range(2):
            ids = mm(self.picked[slot], spread_out, TN)
            for i in range(3):
                counts = fixed
                for r in range(3):
                    counts = counts + number(ids[3 * i + r : 3 * i + r + 1, :] == here)
                counts = jnp.where(edge, 1.0, counts)
                bias[3 * slot + i] = jnp.where(counts > 0.5, jnp.log(jnp.maximum(counts, 1.0)), -1e30)


def forward_kernel(
    xs, cs, w_in, w_out, w_up, w_down, out_bias, norm_gain, norm_bias, up_bias, qv_bias, rand,
    x_all, up_half, full0, full1, full2, query, key, value, mixed, lse, bias, vec_out, ups,
    value_t, mixed_t, shard0, shard1, shard2, own, vec, near, ids, picked, proj_bias, bias_row,
    xs_send, xs_recv, xc_send, xc_recv, cs_send, cs_recv, w_send, w_recv, v_send, v_recv,
):
    at = Place()
    small = Vectors(at, own, vec, near, ids, picked, (v_send, v_recv))
    wide = w_in.shape[2]

    def pack():
        for h in range(3):
            shard0[:, h * wide : (h + 1) * wide] = w_in[:, h, :].astype(BF)
        shard0[:, 3 * wide : 4 * wide] = w_out[...].T.astype(BF)
        shard1[...] = w_up[...].astype(BF)
        shard2[...] = w_down[...].T.astype(BF)
        own[...] = jnp.zeros_like(own)
        ids[...] = jnp.zeros_like(ids)
        vec[at.f] = jnp.zeros(vec.shape[1:], F32)
        small.fill(out_bias, norm_gain, norm_bias, up_bias, qv_bias, rand)

    greet(at, pack)
    gather = Gather(at, (shard0, shard1, shard2), (full0, full1, full2), w_send, w_recv)
    tokens = Swap(at, xs, x_all, 512, xs_send, xs_recv)
    grads = Swap(at, cs, up_half, 0, cs_send, cs_recv)
    part = xs.shape[1]
    small.start()
    tokens.start_in()
    for g in range(3):
        gather.own(g)
    gather.step_z(0, 0)
    gather.step_z(0, 1)
    gather.step_relay(0, 0)
    gather.step_relay(0, 1)

    def to_core(s, half):
        rows = x_all.at[pl.ds(pl.multiple_of(half * 512 + s * part, part), part)]
        return copy_to(rows, rows, xc_send.at[s], xc_recv.at[s], at.core)

    for s in range(4):
        tokens.wait_in(s)
        to_core(s, at.k).start()
    gather.step_z(1, 0)
    gather.step_z(1, 1)
    grads.start_in()
    for s in range(4):
        to_core(s, 1 - at.k).wait_recv()
    gather.step_last(0)

    small.wait()
    small.unpack(vec_out, ups, proj_bias, bias_row, bias)
    heads = query.shape[0]
    dim = query.shape[2]
    width = x_all.shape[1]
    for slot in range(2):

        @pl.loop(0, 4)
        def _(r):
            rows = pl.ds(pl.multiple_of(r * 256, 256), 256)
            weight = full0[slot, :, :, :, 0:640].reshape(width, 640)
            got = mm(x_all[rows, :], weight) + proj_bias[slot]
            for i in range(heads // 2):
                h = slot * (heads // 2) + i
                start = i * 3 * dim
                query[h, rows, :] = (got[:, start : start + dim] * dim**-0.5).astype(BF)
                key[h, rows, :] = got[:, start + dim : start + 2 * dim].astype(BF)
                one = got[:, start + 2 * dim : start + 3 * dim]
                value[h, rows, :] = one.astype(BF)
                value_t[h, :, rows] = one.T.astype(BF)

    gather.step_relay(1, 0)
    gather.step_relay(1, 1)
    gather.step_z(2, 0)
    gather.step_z(2, 1)
    for slot in range(2):
        mixed_t[slot * 256 : slot * 256 + dim, :] = jnp.zeros((dim, mixed_t.shape[1]), F32)

    def spots(h):
        return pl.ds(pl.multiple_of((h // 3) * 256 + (h % 3 + 1) * dim, dim), dim)

    def attend(low_head, high_head):
        @pl.loop(low_head, high_head)
        def _(h):
            @pl.loop(0, 1024 // QCHUNK)
            def _(q):
                attend_chunk(h, q, key, query, value_t, bias, lse, mixed_t, spots)

    attend(0, 2)
    gather.step_relay(2, 0)
    gather.step_relay(2, 1)
    gather.step_last(1)
    attend(2, 6)

    @pl.loop(0, 4)
    def _(r):
        rows = pl.ds(pl.multiple_of(r * 256, 256), 256)
        mixed[rows, :] = mixed_t[:, rows].T.astype(BF)

    gather.step_last(2)
    for s in range(4):
        grads.wait_in(s)
        to_core(s, at.k).wait_send()
    small.sent()
    tokens.sent()
    grads.sent()
    for g in range(3):
        gather.sent(g)


def vmem():
    return pl.BlockSpec(memory_space=pltpu.VMEM)


def forward_call(xs, cs, w_in, w_out, w_up, w_down, out_bias, norm_gain, norm_bias, up_bias, qv_bias, rand):
    width = xs.shape[2]
    length = 1024
    heads, dim = 6, 64
    fr = width // 4
    piece = (2, 4, 2, fr // 2, width)
    shape = jax.ShapeDtypeStruct
    dma = pltpu.SemaphoreType.DMA
    return pl.pallas_call(
        forward_kernel,
        out_shape=(
            shape((length, width), BF),
            shape((length // 2, width), BF),
            shape(piece, BF),
            shape(piece, BF),
            shape(piece, BF),
            shape((heads, length, dim), BF),
            shape((heads, length, dim), BF),
            shape((heads, length, dim), BF),
            shape((length, 512), BF),
            shape((heads, 1, length), F32),
            shape((heads, length // BLK, length), F32),
            shape((8, width), F32),
            shape((2, width), F32),
        ),
        in_specs=[vmem()] * 12,
        out_specs=[vmem()] * 13,
        scratch_shapes=[
            pltpu.VMEM((heads, dim, length), BF),
            pltpu.VMEM((512, length), F32),
            pltpu.VMEM((fr, width), BF),
            pltpu.VMEM((fr, width), BF),
            pltpu.VMEM((fr, width), BF),
            pltpu.VMEM((8, 256), F32),
            pltpu.VMEM((4, 8, 256), F32),
            pltpu.VMEM((2, 4, 8, 256), F32),
            pltpu.VMEM((4, length // BLK, 128), BF),
            pltpu.VMEM((2, length // BLK, 128), BF),
            pltpu.VMEM((2, 1, 640), F32),
            pltpu.VMEM((2, 8, 256), F32),
            dma((4,)),
            dma((4,)),
            dma((4,)),
            dma((4,)),
            dma((4,)),
            dma((4,)),
            dma((3, 2, 7)),
            dma((3, 2, 7)),
            dma((15,)),
            dma((14,)),
        ],
        compiler_params=pltpu.CompilerParams(
            collective_id=1, has_side_effects=True, vmem_limit_bytes=VMEM_LIMIT
        ),
        name="forward",
    )(xs, cs, w_in, w_out, w_up, w_down, out_bias, norm_gain, norm_bias, up_bias, qv_bias, rand)
ROWS = 256


def norm_stats(value):
    mean = jnp.mean(value, axis=-1, keepdims=True)
    centred = value - mean
    inverse = lax.rsqrt(jnp.mean(centred * centred, axis=-1, keepdims=True) + EPS)
    return centred * inverse, inverse


def gelu_both(value):
    share = 0.5 + 0.5 * lax.erf(value * 0.7071067811865476)
    density = jnp.exp(value * value * -0.5) * 0.3989422804014327
    return value * share, share + value * density


def row_sum(value):
    return jnp.sum(value, axis=0, keepdims=True)


class Cores:
    def __init__(self, at, out, back, send, recv, row_send, row_recv):
        self.at, self.out, self.back = at, out, back
        self.send, self.recv, self.row_send, self.row_recv = send, recv, row_send, row_recv

    def rows(self, half, i):
        return pl.ds(pl.multiple_of(half * 512 + i * ROWS, ROWS), ROWS)

    def part(self, stage, i):
        return copy_to(self.out.at[i], self.back.at[i], self.send.at[stage, i], self.recv.at[stage, i], self.at.core)

    def reduce(self, stage, partial, finish):
        at = self.at

        @pl.loop(0, 512 // ROWS)
        def _(i):
            self.out[i] = partial(self.rows(1 - at.k, i))
            self.part(stage, i).start()

        @pl.loop(0, 512 // ROWS)
        def _(i):
            total = partial(self.rows(at.k, i))
            self.part(stage, i).wait_recv()
            finish(i, self.rows(at.k, i), total + self.back[i])

        @pl.loop(0, 512 // ROWS)
        def _(i):
            self.part(stage, i).wait_send()

    def row(self, stage, ref, half, i):
        rows = ref.at[self.rows(half, i)]
        return copy_to(rows, rows, self.row_send.at[stage, i], self.row_recv.at[stage, i], self.at.core)

    def over_rows(self, stage, ref, work):
        at = self.at

        @pl.loop(0, 512 // ROWS)
        def _(i):
            work(self.rows(at.k, i))

        @pl.loop(0, 512 // ROWS)
        def _(i):
            self.row(stage, ref, 1 - at.k, i).wait_recv()
            work(self.rows(1 - at.k, i))

        @pl.loop(0, 512 // ROWS)
        def _(i):
            self.row(stage, ref, at.k, i).wait_send()


def flip(dst, src):
    @pl.loop(0, src.shape[0] // ROWS)
    def _(r):
        rows = pl.ds(pl.multiple_of(r * ROWS, ROWS), ROWS)
        dst[:, rows] = src[rows, :].T


def product(dst, slot, flipped, right):
    n = dst.shape[2] * dst.shape[3]

    @pl.loop(0, dst.shape[1])
    def _(r):
        rows = pl.ds(pl.multiple_of(r * n, n), n)
        got = mm(flipped[rows, :], right())
        dst[slot, r] = got.astype(BF).reshape(dst.shape[2:])


def middle_kernel(
    x_all, up_half, full0, full1, full2, mixed, vectors, ups,
    layer_rows, residual, mixed_grad, grad_out, grad1, grad2, small,
    part_out, part_back, first, first_b, act, slope, second_grad, second_b, branch_b, normed_one, inverse_one, flipped,
    send, recv, row_send, row_recv,
):
    at = Place()
    barrier = pltpu.get_barrier_semaphore()
    pl.semaphore_signal(barrier, inc=1, device_id=at.core, device_id_type=MESH)
    pl.semaphore_wait(barrier, 1)
    cores = Cores(at, part_out, part_back, send, recv, row_send, row_recv)
    width = x_all.shape[1]
    square = lambda full, slot: full[slot].reshape(width, width)
    out_part = lambda slot: full0[slot, :, :, :, 512:768].reshape(width, 256)
    local = lambda i: pl.ds(pl.multiple_of(i * ROWS, ROWS), ROWS)
    small[...] = jnp.zeros_like(small)

    def tally(row, value):
        small[row : row + 1, :] += row_sum(value)

    def branch_part(rows):
        return mm(mixed[rows, 0:256], out_part(0), NT) + mm(mixed[rows, 256:512], out_part(1), NT)

    def branch_done(i, rows, total):
        normed, inverse = norm_stats(x_all[rows, :].astype(F32) + (total + vectors[0:1, :]))
        value = normed * vectors[2:3, :] + vectors[4:5, :]
        normed_one[local(i), :] = normed
        inverse_one[local(i), :] = inverse
        first[local(i), :] = value
        first_b[rows, :] = value.astype(BF)
        cores.row(0, first_b, at.k, i).start()

    cores.reduce(0, branch_part, branch_done)

    def up(rows):
        for slot in range(2):
            inner = mm(first_b[rows, :], square(full1, slot)) + ups[slot : slot + 1, :]
            value, slope_value = gelu_both(inner)
            act[slot, rows, :] = value.astype(BF)
            slope[slot, rows, :] = slope_value.astype(BF)

    cores.over_rows(0, first_b, up)

    def second_part(rows):
        return mm(act[0, rows, :], square(full2, 0), NT) + mm(act[1, rows, :], square(full2, 1), NT)

    def second_done(i, rows, total):
        normed, inverse = norm_stats(first[local(i), :] + (total + vectors[1:2, :]))
        layer_rows[local(i), :] = (normed * vectors[3:4, :] + vectors[5:6, :]).astype(BF)
        upstream = up_half[local(i), :].astype(F32)
        scaled = upstream * vectors[3:4, :]
        grad = inverse * (
            scaled
            - jnp.mean(scaled, axis=-1, keepdims=True)
            - normed * jnp.mean(scaled * normed, axis=-1, keepdims=True)
        )
        second_grad[local(i), :] = grad
        low = grad.astype(BF)
        second_b[rows, :] = low
        cores.row(1, second_b, at.k, i).start()
        tally(1, low.astype(F32))
        tally(3, upstream * normed)
        tally(5, upstream)

    cores.reduce(1, second_part, second_done)

    def down(rows):
        for slot in range(2):
            grad = mm(second_b[rows, :], square(full2, slot)) * slope[slot, rows, :].astype(F32)
            low = grad.astype(BF)
            slope[slot, rows, :] = low
            tally(6 + slot, low.astype(F32))

    cores.over_rows(1, second_b, down)

    def first_part(rows):
        return mm(slope[0, rows, :], square(full1, 0), NT) + mm(slope[1, rows, :], square(full1, 1), NT)

    def first_done(i, rows, total):
        grad = total + second_grad[local(i), :]
        normed = normed_one[local(i), :]
        tally(2, grad * normed)
        tally(4, grad)
        scaled = grad * vectors[2:3, :]
        back = inverse_one[local(i), :] * (
            scaled
            - jnp.mean(scaled, axis=-1, keepdims=True)
            - normed * jnp.mean(scaled * normed, axis=-1, keepdims=True)
        )
        residual[local(i), :] = back
        low = back.astype(BF)
        branch_b[rows, :] = low
        cores.row(2, branch_b, at.k, i).start()
        tally(0, low.astype(F32))

    cores.reduce(2, first_part, first_done)

    def mix_back(rows):
        for slot in range(2):
            got = mm(branch_b[rows, :], out_part(slot))
            for i in range(3):
                mixed_grad[slot * 3 + i, rows, :] = got[:, 64 + 64 * i : 128 + 64 * i].astype(BF)

    cores.over_rows(2, branch_b, mix_back)

    flip(flipped, second_b)
    for slot in range(2):
        product(grad2, slot, flipped, lambda: act[slot])
    flip(flipped, first_b)
    for slot in range(2):
        product(grad1, slot, flipped, lambda: slope[slot])
    flip(flipped, branch_b)

    @pl.loop(0, 4)
    def _(r):
        rows = pl.ds(pl.multiple_of(r * 192, 192), 192)
        grad_out[rows, :] = mm(flipped[rows, :], mixed[...])


def middle_call(x_all, up_half, full0, full1, full2, mixed, vectors, ups):
    length, width = x_all.shape
    shape = jax.ShapeDtypeStruct
    dma = pltpu.SemaphoreType.DMA
    half = length // 2
    parts = half // ROWS
    return pl.pallas_call(
        middle_kernel,
        out_shape=(
            shape((half, width), BF),
            shape((half, width), F32),
            shape((6, length, 64), BF),
            shape((width, 512), F32),
            shape(full1.shape, BF),
            shape(full1.shape, BF),
            shape((16, width), F32),
        ),
        in_specs=[vmem()] * 8,
        out_specs=[vmem()] * 7,
        scratch_shapes=[
            pltpu.VMEM((parts, ROWS, width), F32),
            pltpu.VMEM((parts, ROWS, width), F32),
            pltpu.VMEM((half, width), F32),
            pltpu.VMEM((length, width), BF),
            pltpu.VMEM((2, length, width), BF),
            pltpu.VMEM((2, length, width), BF),
            pltpu.VMEM((half, width), F32),
            pltpu.VMEM((length, width), BF),
            pltpu.VMEM((length, width), BF),
            pltpu.VMEM((half, width), F32),
            pltpu.VMEM((half, 1), F32),
            pltpu.VMEM((width, length), BF),
            dma((3, parts)),
            dma((3, parts)),
            dma((3, parts)),
            dma((3, parts)),
        ],
        compiler_params=pltpu.CompilerParams(
            collective_id=2, has_side_effects=True, vmem_limit_bytes=VMEM_LIMIT
        ),
        name="middle",
    )(x_all, up_half, full0, full1, full2, mixed, vectors, ups)
class Reduce:
    def __init__(self, at, grads, work, plane, zline, final, send, recv):
        self.at, self.grads, self.work, self.plane, self.zline, self.final = at, grads, work, plane, zline, final
        self.send, self.recv = send, recv

    def cp(self, g, slot, kind, src, dst, device, recv_kind=None):
        recv_kind = kind if recv_kind is None else recv_kind
        return copy_to(src, dst, self.send.at[g, slot, kind], self.recv.at[g, slot, recv_kind], device)

    def arrives(self, g, slot, kind, dst):
        self.cp(g, slot, kind, dst, dst, self.at.core).wait_recv()

    def plane_sends(self, g, slot):
        at, grad, box = self.at, self.grads[g], self.plane.at[g, slot]
        return (
            self.cp(g, slot, 1, grad.at[slot, at.other, 1 - at.c], box.at[1], at.xnbr),
            self.cp(g, slot, 3, grad.at[slot, at.other + 1, 1 - at.c], box.at[3], at.ynbr),
            self.cp(g, slot, 0, grad.at[slot, at.pair, 1 - at.c], box.at[0], at.xnbr),
            self.cp(g, slot, 2, grad.at[slot, at.other + 1, at.c], box.at[2], at.ynbr),
        )

    def sums(self, g, slot):
        at, work, box = self.at, self.work.at[g, slot], self.plane.at[g, slot]
        return (
            self.cp(g, slot, 4, work.at[0], box.at[4], at.ynbr),
            self.cp(g, slot, 5, work.at[1], box.at[5], at.xnbr),
        )

    def plane0(self, g):
        for slot in range(2):
            for copy in self.plane_sends(g, slot):
                copy.start()

    def plane1(self, g):
        at, grad = self.at, self.grads[g]
        for slot in range(2):
            to_y, to_x = self.sums(g, slot)
            for i, kind, piece, copy in (
                (0, 1, (at.other, at.c), to_y),
                (1, 3, (at.pair + 1, 1 - at.c), to_x),
            ):
                self.arrives(g, slot, kind, self.plane.at[g, slot, kind])
                own = grad[slot, piece[0], piece[1]].astype(F32)
                self.work[g, slot, i] = (own + self.plane[g, slot, kind].astype(F32)).astype(BF)
                copy.start()

    def ours(self, g, slot):
        return self.work.at[g, slot, pl.ds(2, 2)]

    def down(self, g, slot):
        return self.cp(g, slot, 6, self.ours(g, slot), self.zline.at[g, slot, 0], self.at.zminus)

    def upward(self, g, slot):
        return self.cp(g, slot, 7, self.ours(g, slot), self.zline.at[g, slot, 1], self.at.zplus)

    def plane2(self, g):
        at, grad = self.at, self.grads[g]
        for slot in range(2):
            for kind in (0, 2, 4, 5):
                self.arrives(g, slot, kind, self.plane.at[g, slot, kind])
            for i, one, two in ((0, 0, 4), (1, 2, 5)):
                self.work[g, slot, 2 + i] = (
                    grad[slot, at.pair + i, at.c].astype(F32)
                    + (self.plane[g, slot, one].astype(F32) + self.plane[g, slot, two].astype(F32))
                ).astype(BF)

            @pl.when(at.p == 3)
            def _():
                self.down(g, slot).start()

            if slot == 1:

                @pl.when(at.p == 0)
                def _():
                    self.upward(g, slot).start()

    def add_line(self, g, slot, which):
        self.arrives(g, slot, 6 + which, self.zline.at[g, slot, which])
        for i in range(2):
            self.work[g, slot, 2 + i] = (
                self.work[g, slot, 2 + i].astype(F32) + self.zline[g, slot, which, i].astype(F32)
            ).astype(BF)

    def line(self, g, place):
        at = self.at
        for slot in range(2):
            if place < slot:
                continue

            @pl.when(at.p == place)
            def _():
                self.add_line(g, slot, 0)
                if slot == 1 and place == 1:
                    self.add_line(g, slot, 1)
                if place > slot:
                    self.down(g, slot).start()
                else:
                    self.hand_out(g, slot)

    def hands(self, g, slot):
        at, final = self.at, self.final[g]
        mine = self.work.at[g, slot, 2 + at.k]
        theirs = self.work.at[g, slot, 3 - at.k]
        return (
            self.cp(g, slot, 8, theirs, final.at[at.c], at.core, 8),
            self.cp(g, slot, 9, mine, final.at[at.c], at.xnbr, 9),
            self.cp(g, slot, 10, theirs, final.at[at.c], (at.core[0], 1 - at.c, at.t), 9),
        )

    def hand_out(self, g, slot):
        at = self.at
        for copy in self.hands(g, slot):
            copy.start()
        self.final[g][at.c] = self.work[g, slot, 2 + at.k]

    def finish(self, g):
        at, final = self.at, self.final[g]

        @pl.when(at.k != at.own_core)
        def _():
            self.arrives(g, at.own_slot, 8, final.at[at.c])

        self.arrives(g, at.own_slot, 9, final.at[1 - at.c])
        return final[...].astype(F32).reshape(-1, final.shape[2])

    def sent(self, g):
        at = self.at
        for slot in range(2):
            for copy in (*self.plane_sends(g, slot), *self.sums(g, slot)):
                copy.wait_send()

            @pl.when(at.p > slot)
            def _():
                self.down(g, slot).wait_send()

            if slot == 1:

                @pl.when(at.p == 0)
                def _():
                    self.upward(g, slot).wait_send()

            @pl.when(at.p == slot)
            def _():
                for copy in self.hands(g, slot):
                    copy.wait_send()


def attend_back_chunk(h, q, key, query, value, key_t, bias, lse, grad, key_sum, value_sum, query_t):
    cols = pl.ds(pl.multiple_of(q * QCHUNK, QCHUNK), QCHUNK)
    some = query[h, cols, :]
    upper = grad[h, cols, :]
    scores = mm(key[h], some, NT)
    length = scores.shape[0]
    shift = bias[h, :, cols] - lse[h, :, cols]
    scores = (scores.reshape(length // BLK, BLK, QCHUNK) + shift[:, None, :]).reshape(length, QCHUNK)
    probs = jnp.exp(scores)
    probs_grad = mm(value[h], upper, NT)
    inner = jnp.sum(probs * probs_grad, axis=0, keepdims=True)
    scores_grad = (probs * (probs_grad - inner)).astype(BF)
    value_sum[...] += mm(probs.astype(BF), upper)
    key_sum[...] += mm(scores_grad, some)
    query_t[:, cols] = mm(key_t[...], scores_grad)


def backward_kernel(
    x_all, full0, grad1, grad2, grad_out, query, key, value, lse, bias, mixed_grad, residual, layer_rows, small,
    layer_blocks, grad_blocks, g_in, g_qv, g_out, g_outs, g_gains, g_shifts, g_up, g_ups, g_down,
    small_out, grad0, proj_grad, key_t, key_sum, value_sum, query_t, flipped, grad_rows, part_out, part_back,
    work, plane, zline, final0, final1, final2, sum_out, sum_in,
    lo_send, lo_recv, gi_send, gi_recv, w_send, w_recv, send, recv, small_send, small_recv,
):
    at = Place()
    greet(at)
    layer = Swap(at, layer_blocks, layer_rows, 0, lo_send, lo_recv)
    inputs = Swap(at, grad_blocks, grad_rows, 0, gi_send, gi_recv)
    reduce = Reduce(at, (grad0, grad1, grad2), work, plane, zline, (final0, final1, final2), w_send, w_recv)
    cores = Cores(at, part_out, part_back, send, recv, None, None)
    width = x_all.shape[1]
    reduce.plane0(2)
    reduce.plane0(1)
    for s in range(4):
        layer.start_out(s)
    for slot in range(2):
        proj_grad[slot, :, 576:640] = jnp.zeros((1024, 64), BF)

    def attend(h):
        key_t[...] = key[h].astype(F32).T.astype(BF)
        key_sum[...] = jnp.zeros_like(key_sum)
        value_sum[...] = jnp.zeros_like(value_sum)

        @pl.loop(0, 1024 // QCHUNK)
        def _(q):
            attend_back_chunk(
                h, q, key, query, value, key_t, bias, lse, mixed_grad, key_sum, value_sum, query_t
            )

        start = (h % 3) * 192
        proj_grad[h // 3, :, start : start + 64] = (query_t[...] * 0.125).T.astype(BF)
        proj_grad[h // 3, :, start + 64 : start + 128] = key_sum[...].astype(BF)
        proj_grad[h // 3, :, start + 128 : start + 192] = value_sum[...].astype(BF)

    attend(0)
    reduce.plane1(2)
    attend(1)
    reduce.plane2(2)
    attend(2)
    reduce.line(2, 2)
    reduce.plane1(1)
    attend(3)
    reduce.line(2, 1)
    reduce.plane2(1)
    attend(4)
    reduce.line(2, 0)
    reduce.line(1, 2)
    attend(5)
    reduce.line(1, 1)

    flip(flipped, x_all)

    @pl.loop(0, 4)
    def _(r):
        rows = pl.ds(pl.multiple_of(r * 192, 192), 192)
        for slot in range(2):
            got = mm(flipped[rows, :], proj_grad[slot])
            out_part = grad_out[rows, slot * 256 : slot * 256 + 256]
            grad0[slot, r, :, :, 0:512] = got[:, 0:512].astype(BF).reshape(2, 96, 512)
            shared = got[:, 512:640] + out_part[:, 0:128]
            grad0[slot, r, :, :, 512:640] = shared.astype(BF).reshape(2, 96, 128)
            grad0[slot, r, :, :, 640:768] = out_part[:, 128:256].astype(BF).reshape(2, 96, 128)

    reduce.plane0(0)

    def in_part(rows):
        return sum(
            mm(proj_grad[slot, rows, :], full0[slot, :, :, :, 0:640].reshape(width, 640), NT)
            for slot in range(2)
        )

    def in_done(i, rows, total):
        local = pl.ds(pl.multiple_of(i * ROWS, ROWS), ROWS)
        grad_rows[local, :] = (total + residual[local, :]).astype(BF)
        for s in range(ROWS // 128):
            inputs.start_out(i * (ROWS // 128) + s)

    cores.reduce(0, in_part, in_done)
    reduce.line(1, 0)
    reduce.plane1(0)

    t = at.t
    steps = (at.xnbr, at.ynbr, (at.f, at.c, t + 1 - 2 * lax.rem(t, 2)), (at.f, at.c, lax.rem(t + 2, 4)))
    sum_out[0] = small[...]
    for slot in range(2):
        sum_out[0, 8 + slot : 9 + slot, 0:640] = row_sum(proj_grad[slot].astype(F32))
    for i, device in enumerate(steps):
        copy = copy_to(sum_out.at[i], sum_in.at[i], small_send.at[i], small_recv.at[i], device)
        copy.start()
        copy.wait_recv()
        if i < 3:
            sum_out[i + 1] = sum_out[i] + sum_in[i]
        else:
            small_out[at.k] = sum_out[i] + sum_in[i]
        copy.wait_send()
    both = copy_to(small_out.at[at.k], small_out.at[at.k], small_send.at[4], small_recv.at[4], at.core)
    both.start()

    reduce.plane2(0)
    reduce.line(0, 2)
    reduce.line(0, 1)
    reduce.line(0, 0)
    g_down[...] = reduce.finish(2).T
    g_up[...] = reduce.finish(1)
    got = reduce.finish(0)
    fr = g_up.shape[0]
    for h in range(3):
        g_in[:, h, :] = got[:, h * fr : (h + 1) * fr]
    g_out[...] = got[:, 3 * fr : 4 * fr].T
    both.wait_send()
    copy_to(small_out.at[1 - at.k], small_out.at[1 - at.k], small_send.at[4], small_recv.at[4], at.core).wait_recv()
    vectors = small_out[0, 0:8, :] + small_out[1, 0:8, :]
    used = small_out.at[at.own_core]
    up_row = used[pl.ds(6 + at.own_slot, 1), :]
    proj_row = used[pl.ds(8 + at.own_slot, 1), :]
    pick = lambda j: jnp.concatenate(
        [proj_row[:, i * fr + 64 * j : i * fr + 64 * j + 64] for i in range(3)], axis=1
    )
    pair_rows = jnp.concatenate([pick(0), pick(2)], axis=0)
    part = fr // 4
    for f in range(4):

        @pl.when(at.f == f)
        def _():
            piece = vectors[:, f * fr : (f + 1) * fr]
            g_outs[...] = piece[0:2]
            g_gains[...] = piece[2:4]
            g_shifts[...] = piece[4:6]
            g_ups[...] = up_row[:, f * fr : (f + 1) * fr]
            g_qv[...] = pair_rows[:, f * part : (f + 1) * part]

    for s in range(4):
        layer.wait_out(s)
        inputs.wait_out(s)
    layer.sent()
    inputs.sent()
    for g in range(3):
        reduce.sent(g)


def backward_call(x_all, full0, grad1, grad2, grad_out, query, key, value, lse, bias, mixed_grad, residual, layer_rows, small):
    length, width = x_all.shape
    half = length // 2
    shape = jax.ShapeDtypeStruct
    dma = pltpu.SemaphoreType.DMA
    fr = width // 4
    return pl.pallas_call(
        backward_kernel,
        out_shape=(
            shape((4, 128, width), BF),
            shape((4, 128, width), BF),
            shape((fr, 3, fr), F32),
            shape((2, fr // 4), F32),
            shape((fr, fr), F32),
            shape((2, fr), F32),
            shape((2, fr), F32),
            shape((2, fr), F32),
            shape((fr, width), F32),
            shape((1, fr), F32),
            shape((width, fr), F32),
        ),
        in_specs=[vmem()] * 14,
        out_specs=[vmem()] * 11,
        scratch_shapes=[
            pltpu.VMEM((2, 16, width), F32),
            pltpu.VMEM(full0.shape, BF),
            pltpu.VMEM((2, length, 640), BF),
            pltpu.VMEM((64, length), BF),
            pltpu.VMEM((length, 64), F32),
            pltpu.VMEM((length, 64), F32),
            pltpu.VMEM((64, length), F32),
            pltpu.VMEM((width, length), BF),
            pltpu.VMEM((half, width), BF),
            pltpu.VMEM((half // ROWS, ROWS, width), F32),
            pltpu.VMEM((half // ROWS, ROWS, width), F32),
            pltpu.VMEM((3, 2, 4, fr // 2, width), BF),
            pltpu.VMEM((3, 2, 6, fr // 2, width), BF),
            pltpu.VMEM((3, 2, 2, 2, fr // 2, width), BF),
            pltpu.VMEM((2, fr // 2, width), BF),
            pltpu.VMEM((2, fr // 2, width), BF),
            pltpu.VMEM((2, fr // 2, width), BF),
            pltpu.VMEM((4, 16, width), F32),
            pltpu.VMEM((4, 16, width), F32),
            dma((4,)),
            dma((4,)),
            dma((4,)),
            dma((4,)),
            dma((3, 2, 11)),
            dma((3, 2, 11)),
            dma((1, half // ROWS)),
            dma((1, half // ROWS)),
            dma((5,)),
            dma((5,)),
        ],
        compiler_params=pltpu.CompilerParams(
            collective_id=3, has_side_effects=True, vmem_limit_bytes=VMEM_LIMIT
        ),
        name="backward",
    )(x_all, full0, grad1, grad2, grad_out, query, key, value, lse, bias, mixed_grad, residual, layer_rows, small)


def sequence_shards(hidden_in, rand_blocks, w_in, qv_bias, w_out, out_bias, norm_gain, norm_bias, w_up, up_bias, w_down, cotangent):
    xs = hidden_in.transpose(1, 0, 2)
    cs = cotangent.transpose(1, 0, 2)
    rand = rand_blocks.reshape(rand_blocks.shape[:2] + (-1,))
    x_all, up_half, full0, full1, full2, query, key, value, mixed, lse, bias, vectors, ups = forward_call(
        xs, cs, w_in, w_out, w_up, w_down, out_bias, norm_gain, norm_bias, up_bias[None], qv_bias, rand
    )
    layer_rows, residual, mixed_grad, grad_out, grad1, grad2, small = middle_call(
        x_all, up_half, full0, full1, full2, mixed, vectors, ups
    )
    layer_blocks, grad_blocks, *grads = backward_call(
        x_all, full0, grad1, grad2, grad_out, query, key, value, lse, bias, mixed_grad, residual, layer_rows, small
    )
    grads[7] = grads[7][0]
    return (layer_blocks.transpose(1, 0, 2), grad_blocks.transpose(1, 0, 2), *grads)


def solution(mesh):
    placed = (
        P(("ctx", "tp"), "fsdp", None),
        P("fsdp", None, "tp", None),
        P("fsdp", "tp", None),
        P(None, ("tp", "fsdp")),
        P("tp", "fsdp"),
        P(None, "fsdp"),
        P(None, "fsdp"),
        P(None, "fsdp"),
        P("fsdp", "tp"),
        P(("tp", "fsdp")),
        P("tp", "fsdp"),
        P(("ctx", "tp"), "fsdp", None),
    )
    sizes = tuple(mesh.shape[a] for a in ("fsdp", "ctx", "tp"))

    def local(*args):
        part_rows, seqs, width = args[0].shape
        rows, heads, wide = args[2].shape
        whole = sizes == (4, 2, 4) and (part_rows, seqs, width) == (128, 4, 768)
        whole = whole and (rows, heads, wide) == (192, 3, 192) and args[8].shape == (192, 768)
        return (sequence_shards if whole else span_shards)(*args)

    return jax.shard_map(
        local,
        mesh=mesh,
        in_specs=placed,
        out_specs=(
            P(("ctx", "tp"), "fsdp", None),
            P(("ctx", "tp"), "fsdp", None),
            P("fsdp", "tp", None),
            P(None, ("tp", "fsdp")),
            P("tp", "fsdp"),
            P(None, "fsdp"),
            P(None, "fsdp"),
            P(None, "fsdp"),
            P("fsdp", "tp"),
            P(("tp", "fsdp")),
            P("tp", "fsdp"),
        ),
        check_vma=False,
    )
```

```python
import jax
import jax.numpy as jnp
from jax import lax
from jax.experimental import pallas as pl
from jax.experimental.pallas import tpu as pltpu
from jax.sharding import PartitionSpec as P

BLK = 64


EPS = 1e-06
NEG = -1000000000.0


def from_root(block, axis, owner):
    block = jnp.where(lax.axis_index(axis) == owner, block, jnp.zeros_like(block))
    return lax.psum(block, axis)


def extended(array, sides, width):
    for axis, dim in sides:
        size, length = (lax.axis_size(axis), array.shape[dim])
        up = [(i, (i + 1) % size) for i in range(size - 1)]
        down = [(j, i) for i, j in up]
        last = lax.slice_in_dim(array, length - width, length, axis=dim)
        leading = lax.slice_in_dim(array, 0, width, axis=dim)
        before = lax.ppermute(last, axis, up)
        after = lax.ppermute(leading, axis, down)
        array = jnp.concatenate([before, array, after], axis=dim)
    return array


def joined_2(part, axis, combine):
    gathered = jax.tree.map(lambda a: lax.all_gather(a, axis), part)

    def take(source):
        return jax.tree.map(lambda a: lax.dynamic_index_in_dim(a, source, 0, False), gathered)

    return lax.fori_loop(
        1, lax.axis_size(axis), lambda source, state: combine(state, take(source)), take(0)
    )


def norm_forward(value, gain, shift):
    mean = jnp.mean(value, axis=-1, keepdims=True)
    centred = value - mean
    inverse = lax.rsqrt(jnp.mean(centred * centred, axis=-1, keepdims=True) + EPS)
    normed = centred * inverse
    return (normed * gain + shift, normed, inverse)


def norm_backward(upper, normed, inverse, gain):
    scaled = upper * gain
    return inverse * (
        scaled
        - jnp.mean(scaled, axis=-1, keepdims=True)
        - normed * jnp.mean(scaled * normed, axis=-1, keepdims=True)
    )


def exact_gelu(value):
    return jax.nn.gelu(value, approximate=False)


def outer_sum(left, right):
    return lax.dot_general(
        left, right, (((0,), (0,)), ((), ())), preferred_element_type=jnp.float32
    )


def rows_all(value):
    return lax.all_gather(value, "tp", axis=0, tiled=True)


def rows_sum(left, right, contract):
    return lax.psum_scatter(
        lax.dot_general(
            left, right, (((1,), (contract,)), ((), ())), preferred_element_type=jnp.float32
        ),
        "tp",
        scatter_dimension=0,
        tiled=True,
    )


def spread(piece, root):
    return from_root(piece, "ctx", root)


def stats_join(first_stats, second_stats):
    top = jnp.maximum(first_stats[0], second_stats[0])
    total = first_stats[1] * jnp.exp(first_stats[0] - top) + second_stats[1] * jnp.exp(
        second_stats[0] - top
    )
    return (top, total)


def split_groups(array, steps, group):
    return array.reshape((steps, group) + array.shape[1:])


def key_set(window_pad, global_pair, random_pairs):
    per_dev = random_pairs.shape[3]
    window = jnp.stack(
        [window_pad[:, :, offset_by : offset_by + per_dev] for offset_by in range(3)], axis=3
    )
    target_shape = global_pair.shape[:2] + (per_dev,) + global_pair.shape[2:]
    global_all = jnp.broadcast_to(global_pair[:, :, None], target_shape)
    random_all = jnp.swapaxes(random_pairs, 2, 3)
    joined = jnp.concatenate([window, global_all, random_all], axis=3)
    shape = joined.shape
    return joined.reshape(shape[0], shape[1], shape[2], shape[3] * shape[4], shape[5])


def scores_of(query, keys, mask, scale):
    head_dim = query.shape[-1]
    raw = (
        jnp.einsum(
            "shpqd,shpkd->shpqk", query, keys[..., :head_dim], preferred_element_type=jnp.float32
        )
        * scale
    )
    return jnp.where(mask, raw, NEG)


def attend_group(query, window_pad, global_pair, random_pairs, mask, scale):
    head_dim = query.shape[-1]
    keys = key_set(window_pad, global_pair, random_pairs)
    scores = scores_of(query, keys, mask, scale)
    top = jnp.max(scores, axis=-1, keepdims=True)
    weights = jnp.exp(scores - top)
    total = jnp.sum(weights, axis=-1, keepdims=True)
    probs = (weights / total).astype(jnp.bfloat16)
    mixed = jnp.einsum(
        "shpqk,shpkd->shpqd", probs, keys[..., head_dim:], preferred_element_type=jnp.float32
    )
    return (mixed.astype(jnp.bfloat16), (top + jnp.log(total))[..., 0])


def attend_back(query, window_pad, global_pair, random_pairs, mask, scale, logsum, mixed_grad):
    head_dim = query.shape[-1]
    blocksize = window_pad.shape[3]
    keys = key_set(window_pad, global_pair, random_pairs)
    scores = scores_of(query, keys, mask, scale)
    probs = jnp.exp(scores - logsum[..., None])
    probs_grad = jnp.einsum(
        "shpqd,shpkd->shpqk", mixed_grad, keys[..., head_dim:], preferred_element_type=jnp.float32
    )
    inner = jnp.sum(probs * probs_grad, axis=-1, keepdims=True)
    scores_grad = (probs * (probs_grad - inner)).astype(jnp.bfloat16)
    query_grad = (
        jnp.einsum(
            "shpqk,shpkd->shpqd",
            scores_grad,
            keys[..., :head_dim],
            preferred_element_type=jnp.float32,
        )
        * scale
    )
    keys_grad = (
        jnp.einsum("shpqk,shpqd->shpkd", scores_grad, query, preferred_element_type=jnp.float32)
        * scale
    )
    values_grad = jnp.einsum(
        "shpqk,shpqd->shpkd",
        probs.astype(jnp.bfloat16),
        mixed_grad,
        preferred_element_type=jnp.float32,
    )
    pairs_grad = jnp.concatenate([keys_grad, values_grad], axis=-1)
    shape = pairs_grad.shape
    pairs_grad = pairs_grad.reshape(
        shape[0], shape[1], shape[2], shape[3] // blocksize, blocksize, shape[4]
    )
    per_dev = shape[2]
    window_grad = jnp.zeros(window_pad.shape, jnp.float32)
    for offset_by in range(3):
        window_grad = window_grad.at[:, :, offset_by : offset_by + per_dev].add(
            pairs_grad[:, :, :, offset_by]
        )
    global_grad = jnp.sum(pairs_grad[:, :, :, 3:5], axis=2)
    random_grad = jnp.swapaxes(pairs_grad[:, :, :, 5:], 2, 3)
    return (query_grad, window_grad, global_grad, random_grad)


def span_shards(
    hidden_in,
    rand_blocks,
    w_in,
    qv_bias,
    w_out,
    out_bias,
    norm_gain,
    norm_bias,
    w_up,
    up_bias,
    w_down,
    cotangent,
):
    ctx_count = lax.axis_size("ctx")
    tp_count = lax.axis_size("tp")
    ctx_place = lax.axis_index("ctx")
    part_rows, seqs, width = hidden_in.shape
    heads = w_in.shape[1]
    head_dim = w_in.shape[2] // 3
    pair_width = 2 * head_dim
    blocks_all = rand_blocks.shape[1]
    picks = rand_blocks.shape[3]
    length = part_rows * tp_count
    per_dev = length // BLK
    total_rows = length * seqs
    scale = head_dim ** (-0.5)
    group = min(seqs, max(1, 512 // length))
    steps = seqs // group
    first_owner = ctx_place == 0
    last_owner = ctx_place == ctx_count - 1
    gathered = (
        lax.all_gather(w_in.astype(jnp.bfloat16), "fsdp", axis=0, tiled=True),
        lax.all_gather(qv_bias.astype(jnp.bfloat16), "fsdp", axis=1, tiled=True),
        lax.all_gather(w_out.astype(jnp.bfloat16), "fsdp", axis=1, tiled=True),
        lax.all_gather(out_bias.astype(jnp.bfloat16), "fsdp", axis=1, tiled=True),
        lax.all_gather(norm_gain.astype(jnp.bfloat16), "fsdp", axis=1, tiled=True),
        lax.all_gather(norm_bias.astype(jnp.bfloat16), "fsdp", axis=1, tiled=True),
        lax.all_gather(w_up.astype(jnp.bfloat16), "fsdp", axis=0, tiled=True),
        lax.all_gather(up_bias.astype(jnp.bfloat16), "fsdp", axis=0, tiled=True),
        lax.all_gather(w_down.astype(jnp.bfloat16), "fsdp", axis=1, tiled=True),
    )
    input_low = gathered[0].reshape(width, heads * 3 * head_dim)
    bias_pair = gathered[1].astype(jnp.float32).reshape(2, heads, head_dim)
    output_low = gathered[2]
    bias_out = gathered[3].astype(jnp.float32)
    gains = gathered[4].astype(jnp.float32)
    shifts = gathered[5].astype(jnp.float32)
    upper_low = gathered[6]
    bias_up = gathered[7].astype(jnp.float32)
    lower_low = gathered[8]
    x_full = rows_all(hidden_in)
    x_rows = x_full.reshape(total_rows, width)
    projected = jnp.dot(x_rows, input_low, preferred_element_type=jnp.float32).reshape(
        length, seqs, heads, 3, head_dim
    )
    query = (projected[:, :, :, 0] + bias_pair[0]).astype(jnp.bfloat16)
    key = projected[:, :, :, 1].astype(jnp.bfloat16)
    value = (projected[:, :, :, 2] + bias_pair[1]).astype(jnp.bfloat16)
    query_heads = query.transpose(1, 2, 0, 3).reshape(seqs, heads, per_dev, BLK, head_dim)
    pairs = jnp.concatenate([key, value], axis=-1).transpose(1, 2, 0, 3)
    window_pad = extended(pairs, (("ctx", 2),), BLK).reshape(
        seqs, heads, per_dev + 2, BLK, pair_width
    )
    pair_blocks = pairs.reshape(seqs, heads, per_dev, BLK, pair_width)
    triple_blocks = jnp.concatenate([query_heads, pair_blocks], axis=-1)
    global_triple = jnp.stack(
        [
            spread(triple_blocks[:, :, 0], 0),
            spread(triple_blocks[:, :, per_dev - 1], ctx_count - 1),
        ],
        axis=2,
    )
    global_query = global_triple[..., :head_dim]
    global_pair = global_triple[..., head_dim:]
    key_local = pairs[..., :head_dim]
    value_local = pairs[..., head_dim:]
    wide_scores = (
        jnp.einsum("shgqd,shkd->shgqk", global_query, key_local, preferred_element_type=jnp.float32)
        * scale
    )
    wide_top = jnp.max(wide_scores, axis=-1)
    wide_total = jnp.sum(jnp.exp(wide_scores - wide_top[..., None]), axis=-1)
    all_top, all_total = joined_2((wide_top, wide_total), "ctx", stats_join)
    wide_probs = jnp.exp(wide_scores - (all_top + jnp.log(all_total))[..., None])
    wide_probs_low = wide_probs.astype(jnp.bfloat16)
    mix_low = jnp.einsum(
        "shgqk,shkd->shgqd", wide_probs_low, value_local, preferred_element_type=jnp.float32
    )
    mix_full = jnp.einsum(
        "shgqk,shkd->shgqd",
        wide_probs,
        value_local.astype(jnp.float32),
        precision=lax.Precision.HIGHEST,
    )
    mix_low, mix_full = lax.psum((mix_low, mix_full), "ctx")
    global_mixed = mix_low.astype(jnp.bfloat16)
    units = seqs * heads * picks * per_dev
    table = rand_blocks.transpose(0, 2, 3, 1).reshape(seqs, heads, picks, ctx_count, per_dev)
    table = table.transpose(0, 1, 2, 4, 3).reshape(units, ctx_count)
    mine = lax.dynamic_index_in_dim(table, ctx_place, 1, keepdims=False)
    mine_groups = mine.reshape(steps, group, heads, picks, per_dev)
    block_index = ctx_place * per_dev + jnp.arange(per_dev)
    present = jnp.concatenate(
        [
            (block_index >= 1)[:, None],
            jnp.ones((per_dev, 1), jnp.bool_),
            (block_index <= blocks_all - 2)[:, None],
            jnp.ones((per_dev, 2 + picks), jnp.bool_),
        ],
        axis=1,
    )
    mask = jnp.repeat(present, BLK, axis=1)[None, None, :, None, :]

    def random_pairs_for(block_group, id_group):
        whole = lax.all_gather(block_group, "ctx", axis=2, tiled=True)
        chosen = jax.nn.one_hot(id_group, blocks_all, dtype=jnp.bfloat16)
        return jnp.einsum(
            "shpqb,shbke->shpqke", chosen, whole, preferred_element_type=jnp.float32
        ).astype(jnp.bfloat16)

    query_groups = split_groups(query_heads, steps, group)
    pad_groups = split_groups(window_pad, steps, group)
    global_groups = split_groups(global_pair, steps, group)
    block_groups = split_groups(pair_blocks, steps, group)

    def forward_step(items):
        position, query_group, pad_group, global_group, block_group, id_group = items
        random_group = random_pairs_for(block_group, id_group)
        return attend_group(query_group, pad_group, global_group, random_group, mask, scale)

    mixed_groups, logsum_groups = lax.map(
        forward_step,
        (jnp.arange(steps), query_groups, pad_groups, global_groups, block_groups, mine_groups),
    )
    mixed_blocks = mixed_groups.reshape(seqs, heads, per_dev, BLK, head_dim)
    mixed_blocks = mixed_blocks.at[:, :, 0].set(
        jnp.where(first_owner, global_mixed[:, :, 0], mixed_blocks[:, :, 0])
    )
    mixed_blocks = mixed_blocks.at[:, :, per_dev - 1].set(
        jnp.where(last_owner, global_mixed[:, :, 1], mixed_blocks[:, :, per_dev - 1])
    )
    mixed = (
        mixed_blocks.reshape(seqs, heads, length, head_dim)
        .transpose(2, 0, 1, 3)
        .reshape(total_rows, heads * head_dim)
    )
    branch = rows_sum(mixed, output_low, 0) + bias_out[0]
    residual_in = hidden_in.reshape(part_rows * seqs, width).astype(jnp.float32)
    first, normed_one, inverse_one = norm_forward(residual_in + branch, gains[0], shifts[0])
    first_full = rows_all(first.astype(jnp.bfloat16).reshape(part_rows, seqs, width)).reshape(
        total_rows, width
    )
    inner = jnp.dot(first_full, upper_low, preferred_element_type=jnp.float32) + bias_up
    active_value, gelu_back = jax.vjp(exact_gelu, inner)
    active = active_value.astype(jnp.bfloat16)
    second = rows_sum(active, lower_low, 0) + bias_out[1]
    result, normed_two, inverse_two = norm_forward(first + second, gains[1], shifts[1])
    layer_out = result.astype(jnp.bfloat16).reshape(part_rows, seqs, width)
    upstream = cotangent.reshape(part_rows * seqs, width).astype(jnp.float32)
    second_grad = norm_backward(upstream, normed_two, inverse_two, gains[1])
    second_low = second_grad.astype(jnp.bfloat16)
    second_full = rows_all(second_low.reshape(part_rows, seqs, width)).reshape(total_rows, width)
    active_grad = lax.dot_general(
        second_full, lower_low, (((1,), (1,)), ((), ())), preferred_element_type=jnp.float32
    )
    inner_low = gelu_back(active_grad)[0].astype(jnp.bfloat16)
    first_grad = second_grad + rows_sum(inner_low, upper_low, 1)
    residual_grad = norm_backward(first_grad, normed_one, inverse_one, gains[0])
    branch_low = residual_grad.astype(jnp.bfloat16)
    branch_full = rows_all(branch_low.reshape(part_rows, seqs, width)).reshape(total_rows, width)
    mixed_grad = lax.dot_general(
        branch_full, output_low, (((1,), (1,)), ((), ())), preferred_element_type=jnp.float32
    ).astype(jnp.bfloat16)
    mixed_heads = (
        mixed_grad.reshape(length, seqs, heads, head_dim)
        .transpose(1, 2, 0, 3)
        .reshape(seqs, heads, per_dev, BLK, head_dim)
    )
    zero_block = jnp.zeros((seqs, heads, BLK, head_dim), jnp.bfloat16)
    lead_grad = jnp.where(first_owner, mixed_heads[:, :, 0], zero_block).astype(jnp.float32)
    tail_grad = jnp.where(last_owner, mixed_heads[:, :, per_dev - 1], zero_block).astype(
        jnp.float32
    )
    lead_sum, tail_sum = (
        lax.psum(lead_grad.astype(jnp.bfloat16), "ctx").astype(jnp.float32),
        lax.psum(tail_grad.astype(jnp.bfloat16), "ctx").astype(jnp.float32),
    )
    wide_grad = jnp.stack([lead_sum, tail_sum], axis=2).astype(jnp.bfloat16)
    mixed_heads = mixed_heads.at[:, :, 0].set(
        jnp.where(first_owner, zero_block, mixed_heads[:, :, 0])
    )
    mixed_heads = mixed_heads.at[:, :, per_dev - 1].set(
        jnp.where(last_owner, zero_block, mixed_heads[:, :, per_dev - 1])
    )

    def random_back(random_grad, id_group):
        chosen = jax.nn.one_hot(id_group, blocks_all, dtype=jnp.float32)
        spread_grad = jnp.einsum(
            "shpqb,shpqke->shbke", chosen, random_grad, precision=lax.Precision.HIGHEST
        )
        return lax.psum_scatter(
            spread_grad.astype(jnp.bfloat16), "ctx", scatter_dimension=2, tiled=True
        ).astype(jnp.float32)

    def backward_step(items):
        (
            position,
            query_group,
            pad_group,
            global_group,
            block_group,
            id_group,
            logsum_group,
            grad_group,
        ) = items
        random_group = random_pairs_for(block_group, id_group)
        query_grad, window_grad, global_grad, random_grad = attend_back(
            query_group,
            pad_group,
            global_group,
            random_group,
            mask,
            scale,
            logsum_group,
            grad_group,
        )
        return (query_grad, window_grad, global_grad, random_back(random_grad, id_group))

    query_grads, window_grads, global_grads, random_total = lax.map(
        backward_step,
        (
            jnp.arange(steps),
            query_groups,
            pad_groups,
            global_groups,
            block_groups,
            mine_groups,
            logsum_groups,
            split_groups(mixed_heads, steps, group),
        ),
    )
    query_grads = query_grads.reshape(seqs, heads, length, head_dim)
    window_grads = window_grads.reshape(seqs, heads, per_dev + 2, BLK, pair_width)
    global_grads = global_grads.reshape(seqs, heads, 2, BLK, pair_width)
    wide_inner = jnp.sum(wide_grad.astype(jnp.float32) * mix_full, axis=-1, keepdims=True)
    wide_probs_grad = jnp.einsum(
        "shgqd,shkd->shgqk", wide_grad, value_local, preferred_element_type=jnp.float32
    )
    wide_scores_grad = (wide_probs * (wide_probs_grad - wide_inner)).astype(jnp.bfloat16)
    wide_query_part = (
        jnp.einsum(
            "shgqk,shkd->shgqd", wide_scores_grad, key_local, preferred_element_type=jnp.float32
        )
        * scale
    )
    wide_key_grad = (
        jnp.einsum(
            "shgqk,shgqd->shkd", wide_scores_grad, global_query, preferred_element_type=jnp.float32
        )
        * scale
    )
    wide_value_grad = jnp.einsum(
        "shgqk,shgqd->shkd", wide_probs_low, wide_grad, preferred_element_type=jnp.float32
    )
    wide_pair_grad = jnp.concatenate([wide_key_grad, wide_value_grad], axis=-1).reshape(
        seqs, heads, per_dev, BLK, pair_width
    )
    rim_pair = jnp.concatenate([window_grads[:, :, 0], window_grads[:, :, per_dev + 1]], axis=2)
    rim_back = extended(rim_pair.astype(jnp.bfloat16), (("ctx", 2),), BLK).astype(rim_pair.dtype)
    local_grad = window_grads[:, :, 1 : per_dev + 1] + wide_pair_grad
    local_grad = local_grad.at[:, :, 0].add(rim_back[:, :, :BLK])
    local_grad = local_grad.at[:, :, per_dev - 1].add(rim_back[:, :, 3 * BLK :])
    global_total, wide_query = lax.psum((global_grads, wide_query_part), "ctx")
    local_grad = local_grad.at[:, :, 0].add(jnp.where(first_owner, global_total[:, :, 0], 0.0))
    local_grad = local_grad.at[:, :, per_dev - 1].add(
        jnp.where(last_owner, global_total[:, :, 1], 0.0)
    )
    query_grads = query_grads.at[:, :, :BLK].add(jnp.where(first_owner, wide_query[:, :, 0], 0.0))
    query_grads = query_grads.at[:, :, length - BLK :].add(
        jnp.where(last_owner, wide_query[:, :, 1], 0.0)
    )
    local_grad = local_grad + random_total.reshape(seqs, heads, per_dev, BLK, pair_width)
    pair_grad = local_grad.reshape(seqs, heads, length, pair_width).transpose(2, 0, 1, 3)
    query_part = query_grads.transpose(2, 0, 1, 3)
    projected_grad = jnp.concatenate([query_part, pair_grad], axis=-1).astype(jnp.bfloat16)
    projected_rows = projected_grad.reshape(total_rows, heads * 3 * head_dim)
    grad_in = (
        (residual_grad + rows_sum(projected_rows, input_low, 1))
        .astype(jnp.bfloat16)
        .reshape(part_rows, seqs, width)
    )
    input_grad = outer_sum(x_rows, projected_rows).reshape(width, heads, 3 * head_dim)
    pair_bias_grad = jnp.stack(
        [
            jnp.sum(projected_grad[..., :head_dim], axis=(0, 1), dtype=jnp.float32).reshape(-1),
            jnp.sum(projected_grad[..., 2 * head_dim :], axis=(0, 1), dtype=jnp.float32).reshape(
                -1
            ),
        ]
    )
    output_grad = outer_sum(mixed, branch_full)
    bias_grad = jnp.stack(
        [
            jnp.sum(branch_low, axis=0, dtype=jnp.float32),
            jnp.sum(second_low, axis=0, dtype=jnp.float32),
        ]
    )
    gain_grad = jnp.stack(
        [jnp.sum(first_grad * normed_one, axis=0), jnp.sum(upstream * normed_two, axis=0)]
    )
    shift_grad = jnp.stack([jnp.sum(first_grad, axis=0), jnp.sum(upstream, axis=0)])
    upper_grad = outer_sum(first_full, inner_low)
    upper_bias_grad = jnp.sum(inner_low, axis=0, dtype=jnp.float32)
    lower_grad = outer_sum(active, second_full)
    shares = (
        lax.psum_scatter(input_grad, "fsdp", scatter_dimension=0, tiled=True),
        lax.psum_scatter(pair_bias_grad, "fsdp", scatter_dimension=1, tiled=True),
        lax.psum_scatter(output_grad, "fsdp", scatter_dimension=1, tiled=True),
        lax.psum_scatter(bias_grad, "fsdp", scatter_dimension=1, tiled=True),
        lax.psum_scatter(gain_grad, "fsdp", scatter_dimension=1, tiled=True),
        lax.psum_scatter(shift_grad, "fsdp", scatter_dimension=1, tiled=True),
        lax.psum_scatter(upper_grad, "fsdp", scatter_dimension=0, tiled=True),
        lax.psum_scatter(upper_bias_grad, "fsdp", scatter_dimension=0, tiled=True),
        lax.psum_scatter(lower_grad, "fsdp", scatter_dimension=1, tiled=True),
    )
    matrices = lax.psum((shares[0], shares[1], shares[2], shares[6], shares[7], shares[8]), "ctx")
    vectors = lax.psum((shares[3], shares[4], shares[5]), ("ctx", "tp"))
    return (
        layer_out,
        grad_in,
        matrices[0],
        matrices[1],
        matrices[2],
        vectors[0],
        vectors[1],
        vectors[2],
        matrices[3],
        matrices[4],
        matrices[5],
    )


MESH = pl.DeviceIdType.MESH
BF = jnp.bfloat16
F32 = jnp.float32
NT = (((1,), (1,)), ((), ()))
NN = (((1,), (0,)), ((), ()))
TN = (((0,), (0,)), ((), ()))
VMEM_LIMIT = 60 * 2**20


def mm(left, right, dims=NN):
    return lax.dot_general(left, right, dims, preferred_element_type=F32)


class Place:
    def __init__(self):
        self.f = lax.axis_index("fsdp")
        self.c = lax.axis_index("ctx")
        self.t = lax.axis_index("tp")
        f, c, t = self.f, self.c, self.t
        self.k = k = lax.rem(f, 2)
        self.y = y = f // 2
        self.p = t + k * (3 - 2 * t)
        self.core = (f + 1 - 2 * k, c, t)
        self.xnbr = (f, 1 - c, t)
        self.ynbr = (lax.rem(f + 2, 4), c, t)
        self.zplus = (f, c, t + 1 - 2 * k)
        self.zminus = (f, c, t - 1 + 2 * k)
        self.own_core = t // 2
        self.own_slot = t + (t // 2) * (3 - 2 * t)
        self.pair = 2 * y
        self.other = 2 - 2 * y

    def swap(self, s):
        return (2 * self.y + self.c, self.k, s)

    def swap_is_self(self, s):
        return jnp.logical_and(self.k == self.c, self.t == s)


def copy_to(src, dst, send, recv, device):
    return pltpu.make_async_remote_copy(
        src_ref=src, dst_ref=dst, send_sem=send, recv_sem=recv, device_id=device, device_id_type=MESH
    )


def greet(at, between=lambda: None):
    barrier = pltpu.get_barrier_semaphore()
    sizes = [lax.axis_size(a) for a in ("fsdp", "ctx", "tp")]
    others = 0
    for i in range(sizes[0]):
        for j in range(sizes[1]):
            for m in range(sizes[2]):
                if i or j or m:
                    others += 1
                    device = (
                        lax.rem(at.f + i, sizes[0]),
                        lax.rem(at.c + j, sizes[1]),
                        lax.rem(at.t + m, sizes[2]),
                    )
                    pl.semaphore_signal(barrier, inc=1, device_id=device, device_id_type=MESH)
    between()
    pl.semaphore_wait(barrier, others)


class Gather:
    def __init__(self, at, shards, full, send, recv, tall):
        self.at, self.shards, self.full, self.send, self.recv, self.tall = at, shards, full, send, recv, tall

    def own(self, g):
        at, full, shard = self.at, self.full[g], self.shards[g]
        half = shard.shape[0] // 2
        rows = pl.ds(pl.multiple_of(at.c * half, half), half)

        @pl.when(at.k == at.own_core)
        def _():
            full[at.own_slot, at.f, at.c] = shard[rows, :]

        @pl.when(at.k != at.own_core)
        def _():
            self.cp(g, at.own_slot, 0, shard.at[rows], full.at[at.own_slot, at.f, at.c], at.core).start()

    def cp(self, g, slot, kind, src, dst, device):
        return copy_to(src, dst, self.send.at[g, slot, kind], self.recv.at[g, slot, kind], device)

    def arrives(self, g, slot, kind, dst):
        self.cp(g, slot, kind, dst, dst, self.at.core).wait_recv()

    def ours(self, g, slot, f, c):
        return self.full[g].at[slot, pl.ds(f, 2), c]

    def step_z(self, g, turn):
        at, full = self.at, self.full[g]
        first = (at.p + 2) // 3
        slot = first if turn == 0 else 1 - first
        piece = self.ours(g, slot, at.pair, at.c)

        @pl.when(at.p == slot)
        def _():
            self.arrives(g, slot, 0, full.at[slot, at.core[0], at.c])

        @pl.when(at.p > slot)
        def _():
            self.arrives(g, slot, 1, piece)

        @pl.when(at.p < slot)
        def _():
            self.arrives(g, slot, 2, piece)

        @pl.when(jnp.logical_and(at.p >= slot, at.p < 3))
        def _():
            self.cp(g, slot, 1, piece, piece, at.zplus).start()

        @pl.when(jnp.logical_and(at.p == 1, slot == 1))
        def _():
            self.cp(g, slot, 2, piece, piece, at.zminus).start()

        self.cp(g, slot, 3, piece, piece, at.ynbr).start()
        self.cp(g, slot, 4, piece, piece, at.xnbr).start()

    def relays(self, g, slot):
        at, full = self.at, self.full[g]
        if g in self.tall:
            piece = self.ours(g, slot, at.pair, 1 - at.c)
            return (self.cp(g, slot, 6, piece, piece, at.ynbr),)
        even = full.at[slot, at.other, at.c]
        odd = full.at[slot, at.pair + 1, 1 - at.c]
        return self.cp(g, slot, 6, odd, odd, at.ynbr), self.cp(g, slot, 5, even, even, at.xnbr)

    def step_relay(self, g, turn):
        at = self.at
        first = (at.p + 2) // 3
        slot = first if turn == 0 else 1 - first
        copies = self.relays(g, slot)
        self.arrives(g, slot, 4, self.ours(g, slot, at.pair, 1 - at.c))
        copies[0].start()
        self.arrives(g, slot, 3, self.ours(g, slot, at.other, at.c))
        if g not in self.tall:
            copies[1].start()

    def step_last(self, g):
        at, full = self.at, self.full[g]
        for slot in range(2):
            if g in self.tall:
                self.arrives(g, slot, 6, self.ours(g, slot, at.other, 1 - at.c))
            else:
                self.arrives(g, slot, 5, full.at[slot, at.other, 1 - at.c])
                self.arrives(g, slot, 6, full.at[slot, at.other + 1, 1 - at.c])

    def sent(self, g):
        at, full = self.at, self.full[g]

        def left(slot, kind, src):
            self.cp(g, slot, kind, src, src, at.core).wait_send()

        @pl.when(at.k != at.own_core)
        def _():
            left(at.own_slot, 0, full.at[at.own_slot, at.f, at.c])

        for slot in range(2):
            piece = self.ours(g, slot, at.pair, at.c)

            @pl.when(jnp.logical_and(at.p >= slot, at.p < 3))
            def _():
                left(slot, 1, piece)

            if slot == 1:

                @pl.when(at.p == 1)
                def _():
                    left(slot, 2, piece)

            left(slot, 3, piece)
            left(slot, 4, piece)
            for copy in self.relays(g, slot):
                copy.wait_send()


class Swap:
    def __init__(self, at, blocks, rows, base, send, recv):
        self.at, self.blocks, self.rows, self.base, self.send, self.recv = at, blocks, rows, base, send, recv
        self.n = blocks.shape[1]

    def span(self, s, base):
        return pl.ds(pl.multiple_of(base + s * self.n, self.n), self.n)

    def start_in(self):
        at = self.at
        there = self.rows.at[self.span(at.t, self.base * at.c)]
        for s in range(4):

            @pl.when(at.swap_is_self(s))
            def _():
                here = self.rows.at[self.span(s, self.base * at.k)]
                pltpu.make_async_copy(self.blocks.at[s], here, self.recv.at[s]).start()

            @pl.when(jnp.logical_not(at.swap_is_self(s)))
            def _():
                copy_to(self.blocks.at[s], there, self.send.at[s], self.recv.at[at.t], at.swap(s)).start()

    def wait_in(self, s):
        at = self.at
        here = self.rows.at[self.span(s, self.base * at.k)]

        @pl.when(jnp.logical_not(at.swap_is_self(s)))
        def _():
            copy_to(here, here, self.send.at[s], self.recv.at[s], at.core).wait_recv()

        @pl.when(at.swap_is_self(s))
        def _():
            pltpu.make_async_copy(self.blocks.at[s], here, self.recv.at[s]).wait()

    def start_out(self, s):
        at = self.at
        here = self.rows.at[self.span(s, self.base * at.k)]

        @pl.when(at.swap_is_self(s))
        def _():
            pltpu.make_async_copy(here, self.blocks.at[s], self.send.at[s]).start()

        @pl.when(jnp.logical_not(at.swap_is_self(s)))
        def _():
            copy_to(here, self.blocks.at[at.t], self.send.at[s], self.recv.at[at.t], at.swap(s)).start()

    def wait_out(self, s):
        at = self.at

        @pl.when(jnp.logical_not(at.swap_is_self(s)))
        def _():
            copy_to(self.blocks.at[s], self.blocks.at[s], self.send.at[s], self.recv.at[s], at.core).wait_recv()

    def sent(self, outward=False):
        at = self.at
        for s in range(4):

            @pl.when(jnp.logical_not(at.swap_is_self(s)))
            def _():
                here = self.rows.at[self.span(s, self.base * at.k)] if outward else self.blocks.at[s]
                copy_to(here, here, self.send.at[s], self.recv.at[s], at.core).wait_send()

            if outward:

                @pl.when(at.swap_is_self(s))
                def _():
                    here = self.rows.at[self.span(s, self.base * at.k)]
                    pltpu.make_async_copy(here, self.blocks.at[s], self.send.at[s]).wait()
ROWS = 256


def norm_stats(value):
    mean = jnp.mean(value, axis=-1, keepdims=True)
    centred = value - mean
    inverse = lax.rsqrt(jnp.mean(centred * centred, axis=-1, keepdims=True) + EPS)
    return centred * inverse, inverse


def gelu_both(value):
    share = 0.5 + 0.5 * lax.erf(value * 0.7071067811865476)
    density = jnp.exp(value * value * -0.5) * 0.3989422804014327
    return value * share, share + value * density


def row_sum(value):
    return jnp.sum(value, axis=0, keepdims=True)


class Cores:
    def __init__(self, at, out, back, send, recv, row_send, row_recv):
        self.at, self.out, self.back = at, out, back
        self.send, self.recv, self.row_send, self.row_recv = send, recv, row_send, row_recv

    def rows(self, half, i):
        return pl.ds(pl.multiple_of(half * 512 + i * ROWS, ROWS), ROWS)

    def part(self, stage, i):
        return copy_to(self.out.at[i], self.back.at[i], self.send.at[stage, i], self.recv.at[stage, i], self.at.core)

    def reduce(self, stage, partial, finish):
        at = self.at

        @pl.loop(0, 512 // ROWS)
        def _(i):
            self.out[i] = partial(self.rows(1 - at.k, i))
            self.part(stage, i).start()

        @pl.loop(0, 512 // ROWS)
        def _(i):
            total = partial(self.rows(at.k, i))
            self.part(stage, i).wait_recv()
            finish(i, self.rows(at.k, i), total + self.back[i])

        @pl.loop(0, 512 // ROWS)
        def _(i):
            self.part(stage, i).wait_send()

    def row(self, stage, ref, half, i):
        rows = ref.at[self.rows(half, i)]
        return copy_to(rows, rows, self.row_send.at[stage, i], self.row_recv.at[stage, i], self.at.core)

    def over_rows(self, stage, ref, work):
        at = self.at

        @pl.loop(0, 512 // ROWS)
        def _(i):
            work(self.rows(at.k, i))

        @pl.loop(0, 512 // ROWS)
        def _(i):
            self.row(stage, ref, 1 - at.k, i).wait_recv()
            work(self.rows(1 - at.k, i))

        @pl.loop(0, 512 // ROWS)
        def _(i):
            self.row(stage, ref, at.k, i).wait_send()


def flip(dst, src):
    @pl.loop(0, src.shape[0] // ROWS)
    def _(r):
        rows = pl.ds(pl.multiple_of(r * ROWS, ROWS), ROWS)
        dst[:, rows] = src[rows, :].T


def product(dst, slot, flipped, right):
    n = dst.shape[2] * dst.shape[3]

    @pl.loop(0, dst.shape[1])
    def _(r):
        rows = pl.ds(pl.multiple_of(r * n, n), n)
        got = mm(flipped[rows, :], right())
        dst[slot, r] = got.astype(BF).reshape(dst.shape[2:])


def vmem():
    return pl.BlockSpec(memory_space=pltpu.VMEM)


QCHUNK = 256


def attend_chunk(h, q, key, query, value_t, bias, lse, mixed_t):
    cols = pl.ds(pl.multiple_of(q * QCHUNK, QCHUNK), QCHUNK)
    scores = mm(key[h], query[h, cols, :], NT)
    length = scores.shape[0]
    scores = (
        scores.reshape(length // BLK, BLK, QCHUNK) + bias[h, :, cols][:, None, :]
    ).reshape(length, QCHUNK)
    top = jnp.max(scores, axis=0, keepdims=True)
    weights = jnp.exp(scores - top)
    total = jnp.sum(weights, axis=0, keepdims=True)
    probs = (weights * (1.0 / total)).astype(BF)
    lse[h, :, cols] = top + jnp.log(total)
    mixed_t[:, cols] = mm(value_t[...], probs).astype(BF)


class Vectors:
    def __init__(self, at, own, vec, near, ids, picked, sems):
        self.at, self.own, self.vec, self.near, self.ids, self.picked = at, own, vec, near, ids, picked
        self.send, self.recv = sems

    def fill(self, out_bias, norm_gain, norm_bias, up_bias, qv_bias, rand):
        at = self.at
        size = out_bias.shape[1]
        for i, ref in enumerate((out_bias, norm_gain, norm_bias)):
            self.vec[at.f, 2 * i : 2 * i + 2, 0:size] = ref[...]
        self.own[0:1, 0:size] = up_bias[...]
        self.own[1:3, 0 : qv_bias.shape[1]] = qv_bias[...]
        for h in range(3):
            for r in range(3):
                self.ids[:, 3 * h + r, 0 : rand.shape[3]] = rand[h, r].astype(F32)

        @pl.when(at.k == at.own_core)
        def _():
            self.near[at.own_slot, at.f] = self.own[...]

            @pl.when(at.k == at.c)
            def _():
                self.picked[at.own_slot] = self.ids[at.t]

    def copies(self):
        at = self.at
        out = []
        box = self.vec.at[at.f]
        for i, f in enumerate((at.core[0], at.ynbr[0], lax.rem(at.core[0] + 2, 4))):
            out.append((None, copy_to(box, box, self.send.at[i], self.recv.at[at.f], (f, at.c, at.t))))
        for y in range(2):
            for t in range(4):
                f = 2 * y + at.own_core
                copy = copy_to(
                    self.own,
                    self.near.at[at.own_slot, at.f],
                    self.send.at[3 + 4 * y + t],
                    self.recv.at[4 + 4 * at.own_slot + at.f],
                    (f, at.c, t),
                )
                out.append((jnp.logical_or(f != at.f, t != at.t), copy))
        for s in range(4):
            f = at.pair + at.own_core
            copy = copy_to(
                self.ids.at[s],
                self.picked.at[at.own_slot],
                self.send.at[11 + s],
                self.recv.at[12 + at.own_slot],
                (f, at.k, s),
            )
            away = jnp.logical_or(f != at.f, s != at.t)
            out.append((jnp.logical_and(at.c == at.k, away), copy))
        return out

    def each(self, act):
        for condition, copy in self.copies():
            if condition is None:
                act(copy)
            else:
                pl.when(condition)(lambda copy=copy: act(copy))

    def start(self):
        self.each(lambda copy: copy.start())

    def sent(self):
        self.each(lambda copy: copy.wait_send())

    def wait(self):
        at = self.at

        def arrives(index, dst):
            copy_to(dst, dst, self.send.at[0], self.recv.at[index], at.core).wait_recv()

        for i in range(1, 4):
            f = lax.rem(at.f + i, 4)
            arrives(f, self.vec.at[f])
        for slot in range(2):
            ours = jnp.logical_and(at.k == at.own_core, slot == at.own_slot)
            for f in range(4):

                @pl.when(jnp.logical_not(jnp.logical_and(ours, f == at.f)))
                def _():
                    arrives(4 + 4 * slot + f, self.near.at[slot, f])

            @pl.when(jnp.logical_not(jnp.logical_and(ours, at.k == at.c)))
            def _():
                arrives(12 + slot, self.picked.at[slot])

    def unpack(self, vec_out, ups, proj_bias, row, bias):
        size = vec_out.shape[1] // 4
        low = lambda a: a.astype(BF).astype(F32)
        part = size // 4
        for f in range(4):
            vec_out[:, size * f : size * (f + 1)] = low(self.vec[f, :, 0:size])
        proj_bias[...] = jnp.zeros_like(proj_bias)
        for slot in range(2):
            for f in range(4):
                ups[slot : slot + 1, size * f : size * (f + 1)] = low(self.near[slot, f, 0:1, 0:size])
                row[slot, 0:2, part * f : part * (f + 1)] = low(self.near[slot, f, 1:3, 0:part])
            for i in range(3):
                start = i * size
                proj_bias[slot, :, start : start + 64] = row[slot, 0:1, 64 * i : 64 * i + 64]
                proj_bias[slot, :, start + 128 : start + 192] = row[slot, 1:2, 64 * i : 64 * i + 64]
        blocks, length = bias.shape[1], bias.shape[2]
        spot = lax.broadcasted_iota(jnp.int32, (blocks, length), 0)
        block = lax.broadcasted_iota(jnp.int32, (blocks, length), 1) // BLK
        number = lambda mask: jnp.where(mask, 1.0, 0.0)
        fixed = number(jnp.abs(spot - block) <= 1) + number(spot == 0) + number(spot == blocks - 1)
        edge = jnp.logical_or(block == 0, block == blocks - 1)
        spread_out = number(spot == block).astype(BF)
        here = spot.astype(F32)
        for slot in range(2):
            ids = mm(self.picked[slot, :, 0:blocks].astype(BF), spread_out)
            for i in range(3):
                counts = fixed
                for r in range(3):
                    counts = counts + number(ids[3 * i + r : 3 * i + r + 1, :] == here)
                counts = jnp.where(edge, 1.0, counts)
                bias[3 * slot + i] = jnp.where(counts > 0.5, jnp.log(jnp.maximum(counts, 1.0)), -1e30)


class Reduce:
    def __init__(self, at, grads, work, plane, zline, final, send, recv, tall):
        self.at, self.grads, self.work, self.plane, self.zline, self.final = at, grads, work, plane, zline, final
        self.send, self.recv, self.tall = send, recv, tall

    def cp(self, g, slot, kind, src, dst, device, recv_kind=None):
        recv_kind = kind if recv_kind is None else recv_kind
        return copy_to(src, dst, self.send.at[g, slot, kind], self.recv.at[g, slot, recv_kind], device)

    def arrives(self, g, slot, kind, dst):
        self.cp(g, slot, kind, dst, dst, self.at.core).wait_recv()

    def plane_sends(self, g, slot):
        at, grad, box = self.at, self.grads[g], self.plane.at[g, slot]
        if g in self.tall:
            two = pl.ds(at.other, 2)
            return (
                self.cp(g, slot, 0, grad.at[slot, two, 1 - at.c], box.at[0:2], at.ynbr),
                self.cp(g, slot, 1, grad.at[slot, two, at.c], box.at[2:4], at.ynbr),
            )
        return (
            self.cp(g, slot, 1, grad.at[slot, at.other, 1 - at.c], box.at[1], at.xnbr),
            self.cp(g, slot, 3, grad.at[slot, at.other + 1, 1 - at.c], box.at[3], at.ynbr),
            self.cp(g, slot, 0, grad.at[slot, at.pair, 1 - at.c], box.at[0], at.xnbr),
            self.cp(g, slot, 2, grad.at[slot, at.other + 1, at.c], box.at[2], at.ynbr),
        )

    def sums(self, g, slot):
        at, work, box = self.at, self.work.at[g, slot], self.plane.at[g, slot]
        if g in self.tall:
            return (self.cp(g, slot, 4, work.at[0:2], box.at[4:6], at.xnbr),)
        return (
            self.cp(g, slot, 4, work.at[0], box.at[4], at.ynbr),
            self.cp(g, slot, 5, work.at[1], box.at[5], at.xnbr),
        )

    def plane0(self, g, slot):
        for copy in self.plane_sends(g, slot):
            copy.start()

    def total(self, g, slot, i, piece, boxes):
        came = sum(self.plane[g, slot, b].astype(F32) for b in boxes)
        own = self.grads[g][slot, piece[0], piece[1]].astype(F32)
        self.work[g, slot, i] = (own + came).astype(BF)

    def plane1(self, g, slot):
        at = self.at
        copies = self.sums(g, slot)
        if g in self.tall:
            self.arrives(g, slot, 0, self.plane.at[g, slot, 0:2])
            for i in range(2):
                self.total(g, slot, i, (at.pair + i, 1 - at.c), (i,))
            copies[0].start()
            return
        for i, kind, piece in ((0, 1, (at.other, at.c)), (1, 3, (at.pair + 1, 1 - at.c))):
            self.arrives(g, slot, kind, self.plane.at[g, slot, kind])
            self.total(g, slot, i, piece, (kind,))
            copies[i].start()

    def ours(self, g, slot):
        return self.work.at[g, slot, pl.ds(2, 2)]

    def down(self, g, slot):
        return self.cp(g, slot, 6, self.ours(g, slot), self.zline.at[g, slot], self.at.zminus)

    def upward(self, g, slot):
        return self.cp(g, slot, 7, self.ours(g, slot), self.zline.at[g, 2], self.at.zplus)

    def plane2(self, g, slot):
        at = self.at
        if g in self.tall:
            self.arrives(g, slot, 1, self.plane.at[g, slot, 2:4])
            self.arrives(g, slot, 4, self.plane.at[g, slot, 4:6])
            boxes = ((2, 4), (3, 5))
        else:
            for kind in (0, 2, 4, 5):
                self.arrives(g, slot, kind, self.plane.at[g, slot, kind])
            boxes = ((0, 4), (2, 5))
        for i in range(2):
            self.total(g, slot, 2 + i, (at.pair + i, at.c), boxes[i])

        @pl.when(at.p == 3)
        def _():
            self.down(g, slot).start()

        if slot == 1:

            @pl.when(at.p == 0)
            def _():
                self.upward(g, slot).start()

    def add_line(self, g, slot, which):
        box = 2 if which else slot
        self.arrives(g, slot, 6 + which, self.zline.at[g, box])
        for i in range(2):
            self.work[g, slot, 2 + i] = (
                self.work[g, slot, 2 + i].astype(F32) + self.zline[g, box, i].astype(F32)
            ).astype(BF)

    def line(self, g, slot, place):
        at = self.at
        if place < slot:
            return

        @pl.when(at.p == place)
        def _():
            self.add_line(g, slot, 0)
            if slot == 1 and place == 1:
                self.add_line(g, slot, 1)
            if place > slot:
                self.down(g, slot).start()
            else:
                self.hand_out(g, slot)

    def hands(self, g, slot):
        at, final = self.at, self.final[g]
        mine = self.work.at[g, slot, 2 + at.k]
        theirs = self.work.at[g, slot, 3 - at.k]
        there = final.at[self.half(g, at.c)]
        return (
            self.cp(g, slot, 8, theirs, there, at.core, 8),
            self.cp(g, slot, 9, mine, there, at.xnbr, 9),
            self.cp(g, slot, 10, theirs, there, (at.core[0], 1 - at.c, at.t), 9),
        )

    def half(self, g, c):
        n = self.final[g].shape[0] // 2
        return pl.ds(pl.multiple_of(c * n, n), n)

    def hand_out(self, g, slot):
        at = self.at
        for copy in self.hands(g, slot):
            copy.start()
        self.final[g][self.half(g, at.c), :] = self.work[g, slot, 2 + at.k]

    def finish(self, g):
        at, final = self.at, self.final[g]

        @pl.when(at.k != at.own_core)
        def _():
            self.arrives(g, at.own_slot, 8, final.at[self.half(g, at.c)])

        self.arrives(g, at.own_slot, 9, final.at[self.half(g, 1 - at.c)])
        return final[...].astype(F32)

    def sent(self, g):
        at = self.at
        for slot in range(2):
            for copy in (*self.plane_sends(g, slot), *self.sums(g, slot)):
                copy.wait_send()

            @pl.when(at.p > slot)
            def _():
                self.down(g, slot).wait_send()

            if slot == 1:

                @pl.when(at.p == 0)
                def _():
                    self.upward(g, slot).wait_send()

            @pl.when(at.p == slot)
            def _():
                for copy in self.hands(g, slot):
                    copy.wait_send()


def attend_back_chunk(h, q, key, query, value, key_t, bias, lse, upper, key_sum, value_sum, query_t):
    cols = pl.ds(pl.multiple_of(q * QCHUNK, QCHUNK), QCHUNK)
    some = query[h, cols, :]
    upper = upper(cols)
    scores = mm(key[h], some, NT)
    length = scores.shape[0]
    shift = bias[h, :, cols] - lse[h, :, cols]
    scores = (scores.reshape(length // BLK, BLK, QCHUNK) + shift[:, None, :]).reshape(length, QCHUNK)
    probs = jnp.exp(scores)
    probs_grad = mm(value[h], upper, NT)
    inner = jnp.sum(probs * probs_grad, axis=0, keepdims=True)
    scores_grad = (probs * (probs_grad - inner)).astype(BF)
    value_sum[...] += mm(probs.astype(BF), upper)
    key_sum[...] += mm(scores_grad, some)
    query_t[:, cols] = mm(key_t[...], scores_grad)


def layer_kernel(
    xs, cs, w_in, w_out, w_up, w_down, out_bias, norm_gain, norm_bias, up_bias, qv_bias, rand,
    layer_blocks, grad_blocks, g_in, g_qv, g_out, g_outs, g_gains, g_shifts, g_up, g_ups, g_down,
    x_all, up_half, low0, low1, low2, query, key, value, mixed, lse, bias, vectors, ups,
    own, vec, near, ids, picked, proj_bias, bias_row,
    grad0, grad_out, part_out, part_back, rows_f32, normed_one, inverse_one, first_b, second_b,
    act, slope, flipped, grad_rows, key_t, key_sum, value_sum, query_t,
    work, plane, zline, final0, final1, final2, small, small_out, sum_out, sum_in,
    xs_send, xs_recv, xc_send, xc_recv, cs_send, cs_recv, p_send, p_recv, v_send, v_recv,
    lo_send, lo_recv, gi_send, gi_recv, w_send, w_recv, send, recv, row_send, row_recv, small_send, small_recv,
):
    at = Place()
    letters = Vectors(at, own, vec, near, ids, picked, (v_send, v_recv))
    finals = (final0, final1, final2)
    wide = w_in.shape[2]

    def pack():
        for h in range(3):
            final0[:, h * wide : (h + 1) * wide] = w_in[h].astype(BF)
        final0[:, 3 * wide : 4 * wide] = w_out[...].T.astype(BF)
        final1[...] = w_up[...].astype(BF)
        final2[...] = w_down[...].astype(BF)
        own[...] = jnp.zeros_like(own)
        ids[...] = jnp.zeros_like(ids)
        vec[at.f] = jnp.zeros(vec.shape[1:], F32)
        letters.fill(out_bias, norm_gain, norm_bias, up_bias, qv_bias, rand)

    greet(at, pack)
    gather = Gather(at, finals, (low0, low1, low2), p_send, p_recv, tall=(0,))
    tokens = Swap(at, xs, x_all, 512, xs_send, xs_recv)
    upstreams = Swap(at, cs, up_half, 0, cs_send, cs_recv)
    part = xs.shape[1]
    width = x_all.shape[1]
    letters.start()
    tokens.start_in()
    for g in range(3):
        gather.own(g)
    gather.step_z(0, 0)
    gather.step_z(0, 1)
    gather.step_relay(0, 0)
    gather.step_relay(0, 1)

    def to_core(s, half):
        rows = x_all.at[pl.ds(pl.multiple_of(half * 512 + s * part, part), part)]
        return copy_to(rows, rows, xc_send.at[s], xc_recv.at[s], at.core)

    for s in range(4):
        tokens.wait_in(s)
        to_core(s, at.k).start()
    gather.step_z(1, 0)
    gather.step_z(1, 1)
    upstreams.start_in()
    letters.wait()
    letters.unpack(vectors, ups, proj_bias, bias_row, bias)
    small[...] = jnp.zeros_like(small)
    for s in range(4):
        to_core(s, 1 - at.k).wait_recv()
    gather.step_last(0)

    dim = query.shape[2]
    for slot in range(2):

        @pl.loop(0, 4)
        def _(r):
            rows = pl.ds(pl.multiple_of(r * 256, 256), 256)
            weight = low0[slot, :, :, :, 0:640].reshape(width, 640)
            got = mm(x_all[rows, :], weight) + proj_bias[slot]
            for i in range(3):
                h = slot * 3 + i
                start = i * 3 * dim
                query[h, rows, :] = (got[:, start : start + dim] * dim**-0.5).astype(BF)
                key[h, rows, :] = got[:, start + dim : start + 2 * dim].astype(BF)
                one = got[:, start + 2 * dim : start + 3 * dim]
                value[h, rows, :] = one.astype(BF)
                flipped[384 + h * dim : 384 + (h + 1) * dim, rows] = one.T.astype(BF)

        if slot == 0:
            gather.step_relay(1, 0)
            gather.step_relay(1, 1)
    gather.step_z(2, 0)
    gather.step_z(2, 1)

    def attend_forward(low_head, high_head):
        @pl.loop(low_head, high_head)
        def _(h):
            @pl.loop(0, 1024 // QCHUNK)
            def _(q):
                spot = pl.ds(pl.multiple_of(h * dim, dim), dim)
                value_t = flipped.at[pl.ds(pl.multiple_of(384 + h * dim, dim), dim)]
                attend_chunk(h, q, key, query, value_t, bias, lse, flipped.at[spot])

    attend_forward(0, 3)
    gather.step_relay(2, 0)
    gather.step_relay(2, 1)
    attend_forward(3, 6)

    @pl.loop(0, 4)
    def _(r):
        rows = pl.ds(pl.multiple_of(r * 256, 256), 256)
        blank = jnp.zeros((dim, 256), BF)
        for slot in range(2):
            heads = jnp.concatenate([blank, flipped[slot * 192 : slot * 192 + 192, rows]], axis=0)
            mixed[rows, slot * 256 : slot * 256 + 256] = heads.T

    layer = Swap(at, layer_blocks, up_half, 0, lo_send, lo_recv)
    inputs = Swap(at, grad_blocks, grad_rows, 0, gi_send, gi_recv)
    reduce = Reduce(at, (grad0, low1, low2), work, plane, zline, finals, w_send, w_recv, tall=(0, 2))
    cores = Cores(at, part_out, part_back, send, recv, row_send, row_recv)
    square = lambda full, slot: full[slot].reshape(width, width)
    out_part = lambda slot: low0[slot, :, :, :, 512:768].reshape(width, 256)
    local = lambda i: pl.ds(pl.multiple_of(i * ROWS, ROWS), ROWS)

    def tally(row, value):
        small[row : row + 1, :] += row_sum(value)

    def branch_part(rows):
        return mm(mixed[rows, 0:256], out_part(0), NT) + mm(mixed[rows, 256:512], out_part(1), NT)

    def branch_done(i, rows, total):
        normed, inverse = norm_stats(x_all[rows, :].astype(F32) + (total + vectors[0:1, :]))
        value = normed * vectors[2:3, :] + vectors[4:5, :]
        normed_one[local(i), :] = normed
        inverse_one[local(i), :] = inverse
        rows_f32[local(i), :] = value
        first_b[rows, :] = value.astype(BF)
        cores.row(0, first_b, at.k, i).start()

    cores.reduce(0, branch_part, branch_done)

    def up(rows):
        for slot in range(2):
            inner = mm(first_b[rows, :], square(low1, slot)) + ups[slot : slot + 1, :]
            value, slope_value = gelu_both(inner)
            act[slot, rows, :] = value.astype(BF)
            slope[slot, rows, :] = slope_value.astype(BF)

    gather.sent(0)
    gather.step_last(1)
    gather.sent(1)
    cores.over_rows(0, first_b, up)
    gather.step_last(2)
    gather.sent(2)
    for s in range(4):
        upstreams.wait_in(s)

    def second_part(rows):
        return mm(act[0, rows, :], square(low2, 0), NT) + mm(act[1, rows, :], square(low2, 1), NT)

    def second_done(i, rows, total):
        normed, inverse = norm_stats(rows_f32[local(i), :] + (total + vectors[1:2, :]))
        layer_row = (normed * vectors[3:4, :] + vectors[5:6, :]).astype(BF)
        upstream = up_half[local(i), :].astype(F32)
        up_half[local(i), :] = layer_row
        scaled = upstream * vectors[3:4, :]
        grad = inverse * (
            scaled
            - jnp.mean(scaled, axis=-1, keepdims=True)
            - normed * jnp.mean(scaled * normed, axis=-1, keepdims=True)
        )
        rows_f32[local(i), :] = grad
        low = grad.astype(BF)
        second_b[rows, :] = low
        cores.row(1, second_b, at.k, i).start()
        tally(1, low.astype(F32))
        tally(3, upstream * normed)
        tally(5, upstream)

    cores.reduce(1, second_part, second_done)
    for s in range(4):
        layer.start_out(s)

    def down(rows):
        for slot in range(2):
            grad = mm(second_b[rows, :], square(low2, slot)) * slope[slot, rows, :].astype(F32)
            low = grad.astype(BF)
            slope[slot, rows, :] = low
            tally(6 + slot, low.astype(F32))

    cores.over_rows(1, second_b, down)
    flip(flipped, second_b)
    for slot in range(2):
        product(low2, slot, flipped, lambda: act[slot])
        reduce.plane0(2, slot)

    def first_part(rows):
        return mm(slope[0, rows, :], square(low1, 0), NT) + mm(slope[1, rows, :], square(low1, 1), NT)

    def first_done(i, rows, total):
        grad = total + rows_f32[local(i), :]
        normed = normed_one[local(i), :]
        tally(2, grad * normed)
        tally(4, grad)
        scaled = grad * vectors[2:3, :]
        back = inverse_one[local(i), :] * (
            scaled
            - jnp.mean(scaled, axis=-1, keepdims=True)
            - normed * jnp.mean(scaled * normed, axis=-1, keepdims=True)
        )
        rows_f32[local(i), :] = back
        low = back.astype(BF)
        second_b[rows, :] = low
        cores.row(2, second_b, at.k, i).start()
        tally(0, low.astype(F32))

    cores.reduce(2, first_part, first_done)
    flip(flipped, first_b)
    for slot in range(2):
        product(low1, slot, flipped, lambda: slope[slot])
        reduce.plane0(1, slot)

    mixed_grad = first_b

    def mix_back(rows):
        for slot in range(2):
            mixed_grad[rows, slot * 256 : slot * 256 + 256] = mm(second_b[rows, :], out_part(slot)).astype(BF)

    cores.over_rows(2, second_b, mix_back)
    flip(flipped, second_b)

    @pl.loop(0, 4)
    def _(r):
        rows = pl.ds(pl.multiple_of(r * 192, 192), 192)
        grad_out[rows, :] = mm(flipped[rows, :], mixed[...]).astype(BF)

    flip(flipped, x_all)
    proj_grad = act
    for slot in range(2):
        proj_grad[slot, :, 576:640] = jnp.zeros((1024, 64), BF)

    def attend(h, part):
        if part == 0:
            key_t[...] = key[h].astype(F32).T.astype(BF)
            key_sum[...] = jnp.zeros_like(key_sum)
            value_sum[...] = jnp.zeros_like(value_sum)

        @pl.loop(part * 2, part * 2 + 2)
        def _(q):
            column = (h // 3) * 256 + (h % 3 + 1) * 64
            attend_back_chunk(
                h, q, key, query, value, key_t, bias, lse,
                lambda cols: mixed_grad[cols, column : column + 64], key_sum, value_sum, query_t,
            )

        if part == 1:
            start = (h % 3) * 192
            proj_grad[h // 3, :, start : start + 64] = (query_t[...] * 0.125).T.astype(BF)
            proj_grad[h // 3, :, start + 64 : start + 128] = key_sum[...].astype(BF)
            proj_grad[h // 3, :, start + 128 : start + 192] = value_sum[...].astype(BF)

    def in_grads(slot):
        @pl.loop(0, 4)
        def _(r):
            rows = pl.ds(pl.multiple_of(r * 192, 192), 192)
            got = mm(flipped[rows, :], proj_grad[slot, :, 0:640])
            out_part = grad_out[rows, slot * 256 : slot * 256 + 256]
            grad0[slot, r, :, :, 0:512] = got[:, 0:512].astype(BF).reshape(2, 96, 512)
            shared = got[:, 512:640] + out_part[:, 0:128].astype(F32)
            grad0[slot, r, :, :, 512:640] = shared.astype(BF).reshape(2, 96, 128)
            grad0[slot, r, :, :, 640:768] = out_part[:, 128:256].reshape(2, 96, 128)

        reduce.plane0(0, slot)

    def both(step, g, *more):
        for slot in range(2):
            step(g, slot, *more)

    attend(0, 0)
    both(reduce.plane1, 2)
    attend(0, 1)
    attend(1, 0)
    both(reduce.plane2, 2)
    attend(1, 1)
    both(reduce.line, 2, 2)
    attend(2, 0)
    both(reduce.plane1, 1)
    both(reduce.line, 2, 1)
    attend(2, 1)
    both(reduce.line, 2, 0)
    in_grads(0)
    attend(3, 0)
    both(reduce.plane2, 1)
    attend(3, 1)
    both(reduce.line, 1, 2)
    attend(4, 0)
    both(reduce.line, 1, 1)
    reduce.plane1(0, 0)
    attend(4, 1)
    both(reduce.line, 1, 0)
    attend(5, 0)
    reduce.plane2(0, 0)
    attend(5, 1)
    in_grads(1)
    reduce.line(0, 0, 2)

    def in_part(rows):
        return sum(
            mm(proj_grad[slot, rows, 0:640], low0[slot, :, :, :, 0:640].reshape(width, 640), NT)
            for slot in range(2)
        )

    def in_done(i, rows, total):
        grad_rows[local(i), :] = (total + rows_f32[local(i), :]).astype(BF)
        for s in range(ROWS // 128):
            inputs.start_out(i * (ROWS // 128) + s)

    cores.reduce(3, in_part, in_done)

    t = at.t
    steps = (at.xnbr, at.ynbr, (at.f, at.c, t + 1 - 2 * lax.rem(t, 2)), (at.f, at.c, lax.rem(t + 2, 4)))
    hops = [
        copy_to(sum_out.at[i], sum_in.at[i], small_send.at[i], small_recv.at[i], device)
        for i, device in enumerate(steps)
    ]

    def small_next(i):
        hops[i].wait_recv()
        if i < 3:
            sum_out[i + 1] = sum_out[i] + sum_in[i]
            hops[i + 1].start()
        else:
            small_out[at.k] = sum_out[i] + sum_in[i]

    sum_out[0] = small[...]
    for slot in range(2):
        sum_out[0, 8 + slot : 9 + slot, 0:640] = row_sum(proj_grad[slot, :, 0:640].astype(F32))
    hops[0].start()
    reduce.line(0, 0, 1)
    reduce.plane1(0, 1)
    small_next(0)
    reduce.line(0, 0, 0)
    small_next(1)
    reduce.plane2(0, 1)
    small_next(2)
    reduce.line(0, 1, 2)
    small_next(3)
    mine = small_out.at[at.k]
    both_cores = copy_to(mine, mine, small_send.at[4], small_recv.at[4], at.core)
    both_cores.start()
    reduce.line(0, 1, 1)
    for copy in hops:
        copy.wait_send()
    g_down[...] = reduce.finish(2)
    g_up[...] = reduce.finish(1)
    got = reduce.finish(0)
    fr = g_up.shape[0]
    for h in range(3):
        g_in[h] = got[:, h * fr : (h + 1) * fr]
    g_out[...] = got[:, 3 * fr : 4 * fr].T
    both_cores.wait_send()
    copy_to(small_out.at[1 - at.k], small_out.at[1 - at.k], small_send.at[4], small_recv.at[4], at.core).wait_recv()
    sums = small_out[0, 0:8, :] + small_out[1, 0:8, :]
    used = small_out.at[at.own_core]
    up_row = used[pl.ds(6 + at.own_slot, 1), :]
    proj_row = used[pl.ds(8 + at.own_slot, 1), :]
    pick = lambda j: jnp.concatenate(
        [proj_row[:, i * fr + 64 * j : i * fr + 64 * j + 64] for i in range(3)], axis=1
    )
    pair_rows = jnp.concatenate([pick(0), pick(2)], axis=0)
    quarter = fr // 4
    for f in range(4):

        @pl.when(at.f == f)
        def _():
            piece = sums[:, f * fr : (f + 1) * fr]
            g_outs[...] = piece[0:2]
            g_gains[...] = piece[2:4]
            g_shifts[...] = piece[4:6]
            g_ups[...] = up_row[:, f * fr : (f + 1) * fr]
            g_qv[...] = pair_rows[:, f * quarter : (f + 1) * quarter]

    for s in range(4):
        layer.wait_out(s)
        inputs.wait_out(s)
    layer.sent(True)
    inputs.sent(True)
    for g in range(3):
        reduce.sent(g)
    letters.sent()
    tokens.sent()
    upstreams.sent()
    for s in range(4):
        to_core(s, at.k).wait_send()


def layer_call(xs, cs, w_in, w_out, w_up, w_down, out_bias, norm_gain, norm_bias, up_bias, qv_bias, rand):
    width = xs.shape[2]
    length, half = 1024, 512
    heads, dim = 6, 64
    blocks = length // BLK
    parts = half // ROWS
    fr = width // 4
    piece = (fr // 2, width)
    shape = jax.ShapeDtypeStruct
    dma = lambda *dims: pltpu.SemaphoreType.DMA(dims)
    low = lambda *dims: pltpu.VMEM(dims, BF)
    full = lambda *dims: pltpu.VMEM(dims, F32)
    anywhere = pl.BlockSpec(memory_space=pl.ANY)
    return pl.pallas_call(
        layer_kernel,
        out_shape=(
            shape(xs.shape, BF),
            shape(xs.shape, BF),
            shape((3, fr, fr), F32),
            shape((2, fr // 4), F32),
            shape((fr, fr), F32),
            shape((2, fr), F32),
            shape((2, fr), F32),
            shape((2, fr), F32),
            shape((fr, width), F32),
            shape((1, fr), F32),
            shape((fr, width), F32),
        ),
        in_specs=[anywhere] * 2 + [vmem()] * 10,
        out_specs=[anywhere] * 2 + [vmem()] * 9,
        scratch_shapes=[
            low(length, width),
            low(half, width),
            low(2, 4, 2, *piece),
            low(2, 4, 2, *piece),
            low(2, 4, 2, *piece),
            low(heads, length, dim),
            low(heads, length, dim),
            low(heads, length, dim),
            low(length, 512),
            full(heads, 1, length),
            full(heads, blocks, length),
            full(8, width),
            full(2, width),
            full(8, 256),
            full(4, 8, 256),
            full(2, 4, 8, 256),
            full(4, 16, 128),
            full(2, 16, 128),
            full(2, 1, 640),
            full(2, 8, 256),
            low(2, 4, 2, *piece),
            low(width, 512),
            full(parts, ROWS, width),
            full(parts, ROWS, width),
            full(half, width),
            full(half, width),
            full(half, 1),
            low(length, width),
            low(length, width),
            low(2, length, width),
            low(2, length, width),
            low(width, length),
            low(half, width),
            low(dim, length),
            full(length, dim),
            full(length, dim),
            full(dim, length),
            low(3, 2, 4, *piece),
            low(3, 2, 6, *piece),
            low(3, 3, 2, *piece),
            low(fr, width),
            low(fr, width),
            low(fr, width),
            full(16, width),
            full(2, 16, width),
            full(4, 16, width),
            full(4, 16, width),
            dma(4),
            dma(4),
            dma(4),
            dma(4),
            dma(4),
            dma(4),
            dma(3, 2, 7),
            dma(3, 2, 7),
            dma(15),
            dma(14),
            dma(4),
            dma(4),
            dma(4),
            dma(4),
            dma(3, 2, 11),
            dma(3, 2, 11),
            dma(4, parts),
            dma(4, parts),
            dma(3, parts),
            dma(3, parts),
            dma(5),
            dma(5),
        ],
        compiler_params=pltpu.CompilerParams(
            collective_id=1, has_side_effects=True, vmem_limit_bytes=VMEM_LIMIT
        ),
        name="layer",
    )(xs, cs, w_in, w_out, w_up, w_down, out_bias, norm_gain, norm_bias, up_bias, qv_bias, rand)


def sequence_shards(hidden_in, rand_blocks, w_in, qv_bias, w_out, out_bias, norm_gain, norm_bias, w_up, up_bias, w_down, cotangent):
    layer_blocks, grad_blocks, *grads = layer_call(
        hidden_in.transpose(1, 0, 2),
        cotangent.transpose(1, 0, 2),
        w_in.transpose(1, 0, 2),
        w_out,
        w_up,
        w_down.T,
        out_bias,
        norm_gain,
        norm_bias,
        up_bias[None],
        qv_bias,
        rand_blocks.transpose(2, 3, 0, 1),
    )
    grads[0] = grads[0].transpose(1, 0, 2)
    grads[7] = grads[7][0]
    grads[8] = grads[8].T
    return (layer_blocks.transpose(1, 0, 2), grad_blocks.transpose(1, 0, 2), *grads)


def solution(mesh):
    placed = (
        P(("ctx", "tp"), "fsdp", None),
        P("fsdp", None, "tp", None),
        P("fsdp", "tp", None),
        P(None, ("tp", "fsdp")),
        P("tp", "fsdp"),
        P(None, "fsdp"),
        P(None, "fsdp"),
        P(None, "fsdp"),
        P("fsdp", "tp"),
        P(("tp", "fsdp")),
        P("tp", "fsdp"),
        P(("ctx", "tp"), "fsdp", None),
    )
    sizes = tuple(mesh.shape[a] for a in ("fsdp", "ctx", "tp"))

    def local(*args):
        part_rows, seqs, width = args[0].shape
        rows, heads, wide = args[2].shape
        whole = sizes == (4, 2, 4) and (part_rows, seqs, width) == (128, 4, 768)
        whole = whole and (rows, heads, wide) == (192, 3, 192) and args[8].shape == (192, 768)
        return (sequence_shards if whole else span_shards)(*args)

    return jax.shard_map(
        local,
        mesh=mesh,
        in_specs=placed,
        out_specs=(
            P(("ctx", "tp"), "fsdp", None),
            P(("ctx", "tp"), "fsdp", None),
            P("fsdp", "tp", None),
            P(None, ("tp", "fsdp")),
            P("tp", "fsdp"),
            P(None, "fsdp"),
            P(None, "fsdp"),
            P(None, "fsdp"),
            P("fsdp", "tp"),
            P(("tp", "fsdp")),
            P("tp", "fsdp"),
        ),
        check_vma=False,
    )
```

```python
import jax
import jax.numpy as jnp
from jax import lax
from jax.experimental import pallas as pl
from jax.experimental.pallas import tpu as pltpu
from jax.sharding import PartitionSpec as P

BLK = 64


EPS = 1e-06
NEG = -1000000000.0


def from_root(block, axis, owner):
    block = jnp.where(lax.axis_index(axis) == owner, block, jnp.zeros_like(block))
    return lax.psum(block, axis)


def extended(array, sides, width):
    for axis, dim in sides:
        size, length = (lax.axis_size(axis), array.shape[dim])
        up = [(i, (i + 1) % size) for i in range(size - 1)]
        down = [(j, i) for i, j in up]
        last = lax.slice_in_dim(array, length - width, length, axis=dim)
        leading = lax.slice_in_dim(array, 0, width, axis=dim)
        before = lax.ppermute(last, axis, up)
        after = lax.ppermute(leading, axis, down)
        array = jnp.concatenate([before, array, after], axis=dim)
    return array


def joined_2(part, axis, combine):
    gathered = jax.tree.map(lambda a: lax.all_gather(a, axis), part)

    def take(source):
        return jax.tree.map(lambda a: lax.dynamic_index_in_dim(a, source, 0, False), gathered)

    return lax.fori_loop(
        1, lax.axis_size(axis), lambda source, state: combine(state, take(source)), take(0)
    )


def norm_forward(value, gain, shift):
    mean = jnp.mean(value, axis=-1, keepdims=True)
    centred = value - mean
    inverse = lax.rsqrt(jnp.mean(centred * centred, axis=-1, keepdims=True) + EPS)
    normed = centred * inverse
    return (normed * gain + shift, normed, inverse)


def norm_backward(upper, normed, inverse, gain):
    scaled = upper * gain
    return inverse * (
        scaled
        - jnp.mean(scaled, axis=-1, keepdims=True)
        - normed * jnp.mean(scaled * normed, axis=-1, keepdims=True)
    )


def exact_gelu(value):
    return jax.nn.gelu(value, approximate=False)


def outer_sum(left, right):
    return lax.dot_general(
        left, right, (((0,), (0,)), ((), ())), preferred_element_type=jnp.float32
    )


def rows_all(value):
    return lax.all_gather(value, "tp", axis=0, tiled=True)


def rows_sum(left, right, contract):
    return lax.psum_scatter(
        lax.dot_general(
            left, right, (((1,), (contract,)), ((), ())), preferred_element_type=jnp.float32
        ),
        "tp",
        scatter_dimension=0,
        tiled=True,
    )


def spread(piece, root):
    return from_root(piece, "ctx", root)


def stats_join(first_stats, second_stats):
    top = jnp.maximum(first_stats[0], second_stats[0])
    total = first_stats[1] * jnp.exp(first_stats[0] - top) + second_stats[1] * jnp.exp(
        second_stats[0] - top
    )
    return (top, total)


def split_groups(array, steps, group):
    return array.reshape((steps, group) + array.shape[1:])


def key_set(window_pad, global_pair, random_pairs):
    per_dev = random_pairs.shape[3]
    window = jnp.stack(
        [window_pad[:, :, offset_by : offset_by + per_dev] for offset_by in range(3)], axis=3
    )
    target_shape = global_pair.shape[:2] + (per_dev,) + global_pair.shape[2:]
    global_all = jnp.broadcast_to(global_pair[:, :, None], target_shape)
    random_all = jnp.swapaxes(random_pairs, 2, 3)
    joined = jnp.concatenate([window, global_all, random_all], axis=3)
    shape = joined.shape
    return joined.reshape(shape[0], shape[1], shape[2], shape[3] * shape[4], shape[5])


def scores_of(query, keys, mask, scale):
    head_dim = query.shape[-1]
    raw = (
        jnp.einsum(
            "shpqd,shpkd->shpqk", query, keys[..., :head_dim], preferred_element_type=jnp.float32
        )
        * scale
    )
    return jnp.where(mask, raw, NEG)


def attend_group(query, window_pad, global_pair, random_pairs, mask, scale):
    head_dim = query.shape[-1]
    keys = key_set(window_pad, global_pair, random_pairs)
    scores = scores_of(query, keys, mask, scale)
    top = jnp.max(scores, axis=-1, keepdims=True)
    weights = jnp.exp(scores - top)
    total = jnp.sum(weights, axis=-1, keepdims=True)
    probs = (weights / total).astype(jnp.bfloat16)
    mixed = jnp.einsum(
        "shpqk,shpkd->shpqd", probs, keys[..., head_dim:], preferred_element_type=jnp.float32
    )
    return (mixed.astype(jnp.bfloat16), (top + jnp.log(total))[..., 0])


def attend_back(query, window_pad, global_pair, random_pairs, mask, scale, logsum, mixed_grad):
    head_dim = query.shape[-1]
    blocksize = window_pad.shape[3]
    keys = key_set(window_pad, global_pair, random_pairs)
    scores = scores_of(query, keys, mask, scale)
    probs = jnp.exp(scores - logsum[..., None])
    probs_grad = jnp.einsum(
        "shpqd,shpkd->shpqk", mixed_grad, keys[..., head_dim:], preferred_element_type=jnp.float32
    )
    inner = jnp.sum(probs * probs_grad, axis=-1, keepdims=True)
    scores_grad = (probs * (probs_grad - inner)).astype(jnp.bfloat16)
    query_grad = (
        jnp.einsum(
            "shpqk,shpkd->shpqd",
            scores_grad,
            keys[..., :head_dim],
            preferred_element_type=jnp.float32,
        )
        * scale
    )
    keys_grad = (
        jnp.einsum("shpqk,shpqd->shpkd", scores_grad, query, preferred_element_type=jnp.float32)
        * scale
    )
    values_grad = jnp.einsum(
        "shpqk,shpqd->shpkd",
        probs.astype(jnp.bfloat16),
        mixed_grad,
        preferred_element_type=jnp.float32,
    )
    pairs_grad = jnp.concatenate([keys_grad, values_grad], axis=-1)
    shape = pairs_grad.shape
    pairs_grad = pairs_grad.reshape(
        shape[0], shape[1], shape[2], shape[3] // blocksize, blocksize, shape[4]
    )
    per_dev = shape[2]
    window_grad = jnp.zeros(window_pad.shape, jnp.float32)
    for offset_by in range(3):
        window_grad = window_grad.at[:, :, offset_by : offset_by + per_dev].add(
            pairs_grad[:, :, :, offset_by]
        )
    global_grad = jnp.sum(pairs_grad[:, :, :, 3:5], axis=2)
    random_grad = jnp.swapaxes(pairs_grad[:, :, :, 5:], 2, 3)
    return (query_grad, window_grad, global_grad, random_grad)


def span_shards(
    hidden_in,
    rand_blocks,
    w_in,
    qv_bias,
    w_out,
    out_bias,
    norm_gain,
    norm_bias,
    w_up,
    up_bias,
    w_down,
    cotangent,
):
    ctx_count = lax.axis_size("ctx")
    tp_count = lax.axis_size("tp")
    ctx_place = lax.axis_index("ctx")
    part_rows, seqs, width = hidden_in.shape
    heads = w_in.shape[1]
    head_dim = w_in.shape[2] // 3
    pair_width = 2 * head_dim
    blocks_all = rand_blocks.shape[1]
    picks = rand_blocks.shape[3]
    length = part_rows * tp_count
    per_dev = length // BLK
    total_rows = length * seqs
    scale = head_dim ** (-0.5)
    group = min(seqs, max(1, 512 // length))
    steps = seqs // group
    first_owner = ctx_place == 0
    last_owner = ctx_place == ctx_count - 1
    gathered = (
        lax.all_gather(w_in.astype(jnp.bfloat16), "fsdp", axis=0, tiled=True),
        lax.all_gather(qv_bias.astype(jnp.bfloat16), "fsdp", axis=1, tiled=True),
        lax.all_gather(w_out.astype(jnp.bfloat16), "fsdp", axis=1, tiled=True),
        lax.all_gather(out_bias.astype(jnp.bfloat16), "fsdp", axis=1, tiled=True),
        lax.all_gather(norm_gain.astype(jnp.bfloat16), "fsdp", axis=1, tiled=True),
        lax.all_gather(norm_bias.astype(jnp.bfloat16), "fsdp", axis=1, tiled=True),
        lax.all_gather(w_up.astype(jnp.bfloat16), "fsdp", axis=0, tiled=True),
        lax.all_gather(up_bias.astype(jnp.bfloat16), "fsdp", axis=0, tiled=True),
        lax.all_gather(w_down.astype(jnp.bfloat16), "fsdp", axis=1, tiled=True),
    )
    input_low = gathered[0].reshape(width, heads * 3 * head_dim)
    bias_pair = gathered[1].astype(jnp.float32).reshape(2, heads, head_dim)
    output_low = gathered[2]
    bias_out = gathered[3].astype(jnp.float32)
    gains = gathered[4].astype(jnp.float32)
    shifts = gathered[5].astype(jnp.float32)
    upper_low = gathered[6]
    bias_up = gathered[7].astype(jnp.float32)
    lower_low = gathered[8]
    x_full = rows_all(hidden_in)
    x_rows = x_full.reshape(total_rows, width)
    projected = jnp.dot(x_rows, input_low, preferred_element_type=jnp.float32).reshape(
        length, seqs, heads, 3, head_dim
    )
    query = (projected[:, :, :, 0] + bias_pair[0]).astype(jnp.bfloat16)
    key = projected[:, :, :, 1].astype(jnp.bfloat16)
    value = (projected[:, :, :, 2] + bias_pair[1]).astype(jnp.bfloat16)
    query_heads = query.transpose(1, 2, 0, 3).reshape(seqs, heads, per_dev, BLK, head_dim)
    pairs = jnp.concatenate([key, value], axis=-1).transpose(1, 2, 0, 3)
    window_pad = extended(pairs, (("ctx", 2),), BLK).reshape(
        seqs, heads, per_dev + 2, BLK, pair_width
    )
    pair_blocks = pairs.reshape(seqs, heads, per_dev, BLK, pair_width)
    triple_blocks = jnp.concatenate([query_heads, pair_blocks], axis=-1)
    global_triple = jnp.stack(
        [
            spread(triple_blocks[:, :, 0], 0),
            spread(triple_blocks[:, :, per_dev - 1], ctx_count - 1),
        ],
        axis=2,
    )
    global_query = global_triple[..., :head_dim]
    global_pair = global_triple[..., head_dim:]
    key_local = pairs[..., :head_dim]
    value_local = pairs[..., head_dim:]
    wide_scores = (
        jnp.einsum("shgqd,shkd->shgqk", global_query, key_local, preferred_element_type=jnp.float32)
        * scale
    )
    wide_top = jnp.max(wide_scores, axis=-1)
    wide_total = jnp.sum(jnp.exp(wide_scores - wide_top[..., None]), axis=-1)
    all_top, all_total = joined_2((wide_top, wide_total), "ctx", stats_join)
    wide_probs = jnp.exp(wide_scores - (all_top + jnp.log(all_total))[..., None])
    wide_probs_low = wide_probs.astype(jnp.bfloat16)
    mix_low = jnp.einsum(
        "shgqk,shkd->shgqd", wide_probs_low, value_local, preferred_element_type=jnp.float32
    )
    mix_full = jnp.einsum(
        "shgqk,shkd->shgqd",
        wide_probs,
        value_local.astype(jnp.float32),
        precision=lax.Precision.HIGHEST,
    )
    mix_low, mix_full = lax.psum((mix_low, mix_full), "ctx")
    global_mixed = mix_low.astype(jnp.bfloat16)
    units = seqs * heads * picks * per_dev
    table = rand_blocks.transpose(0, 2, 3, 1).reshape(seqs, heads, picks, ctx_count, per_dev)
    table = table.transpose(0, 1, 2, 4, 3).reshape(units, ctx_count)
    mine = lax.dynamic_index_in_dim(table, ctx_place, 1, keepdims=False)
    mine_groups = mine.reshape(steps, group, heads, picks, per_dev)
    block_index = ctx_place * per_dev + jnp.arange(per_dev)
    present = jnp.concatenate(
        [
            (block_index >= 1)[:, None],
            jnp.ones((per_dev, 1), jnp.bool_),
            (block_index <= blocks_all - 2)[:, None],
            jnp.ones((per_dev, 2 + picks), jnp.bool_),
        ],
        axis=1,
    )
    mask = jnp.repeat(present, BLK, axis=1)[None, None, :, None, :]

    def random_pairs_for(block_group, id_group):
        whole = lax.all_gather(block_group, "ctx", axis=2, tiled=True)
        chosen = jax.nn.one_hot(id_group, blocks_all, dtype=jnp.bfloat16)
        return jnp.einsum(
            "shpqb,shbke->shpqke", chosen, whole, preferred_element_type=jnp.float32
        ).astype(jnp.bfloat16)

    query_groups = split_groups(query_heads, steps, group)
    pad_groups = split_groups(window_pad, steps, group)
    global_groups = split_groups(global_pair, steps, group)
    block_groups = split_groups(pair_blocks, steps, group)

    def forward_step(items):
        position, query_group, pad_group, global_group, block_group, id_group = items
        random_group = random_pairs_for(block_group, id_group)
        return attend_group(query_group, pad_group, global_group, random_group, mask, scale)

    mixed_groups, logsum_groups = lax.map(
        forward_step,
        (jnp.arange(steps), query_groups, pad_groups, global_groups, block_groups, mine_groups),
    )
    mixed_blocks = mixed_groups.reshape(seqs, heads, per_dev, BLK, head_dim)
    mixed_blocks = mixed_blocks.at[:, :, 0].set(
        jnp.where(first_owner, global_mixed[:, :, 0], mixed_blocks[:, :, 0])
    )
    mixed_blocks = mixed_blocks.at[:, :, per_dev - 1].set(
        jnp.where(last_owner, global_mixed[:, :, 1], mixed_blocks[:, :, per_dev - 1])
    )
    mixed = (
        mixed_blocks.reshape(seqs, heads, length, head_dim)
        .transpose(2, 0, 1, 3)
        .reshape(total_rows, heads * head_dim)
    )
    branch = rows_sum(mixed, output_low, 0) + bias_out[0]
    residual_in = hidden_in.reshape(part_rows * seqs, width).astype(jnp.float32)
    first, normed_one, inverse_one = norm_forward(residual_in + branch, gains[0], shifts[0])
    first_full = rows_all(first.astype(jnp.bfloat16).reshape(part_rows, seqs, width)).reshape(
        total_rows, width
    )
    inner = jnp.dot(first_full, upper_low, preferred_element_type=jnp.float32) + bias_up
    active_value, gelu_back = jax.vjp(exact_gelu, inner)
    active = active_value.astype(jnp.bfloat16)
    second = rows_sum(active, lower_low, 0) + bias_out[1]
    result, normed_two, inverse_two = norm_forward(first + second, gains[1], shifts[1])
    layer_out = result.astype(jnp.bfloat16).reshape(part_rows, seqs, width)
    upstream = cotangent.reshape(part_rows * seqs, width).astype(jnp.float32)
    second_grad = norm_backward(upstream, normed_two, inverse_two, gains[1])
    second_low = second_grad.astype(jnp.bfloat16)
    second_full = rows_all(second_low.reshape(part_rows, seqs, width)).reshape(total_rows, width)
    active_grad = lax.dot_general(
        second_full, lower_low, (((1,), (1,)), ((), ())), preferred_element_type=jnp.float32
    )
    inner_low = gelu_back(active_grad)[0].astype(jnp.bfloat16)
    first_grad = second_grad + rows_sum(inner_low, upper_low, 1)
    residual_grad = norm_backward(first_grad, normed_one, inverse_one, gains[0])
    branch_low = residual_grad.astype(jnp.bfloat16)
    branch_full = rows_all(branch_low.reshape(part_rows, seqs, width)).reshape(total_rows, width)
    mixed_grad = lax.dot_general(
        branch_full, output_low, (((1,), (1,)), ((), ())), preferred_element_type=jnp.float32
    ).astype(jnp.bfloat16)
    mixed_heads = (
        mixed_grad.reshape(length, seqs, heads, head_dim)
        .transpose(1, 2, 0, 3)
        .reshape(seqs, heads, per_dev, BLK, head_dim)
    )
    zero_block = jnp.zeros((seqs, heads, BLK, head_dim), jnp.bfloat16)
    lead_grad = jnp.where(first_owner, mixed_heads[:, :, 0], zero_block).astype(jnp.float32)
    tail_grad = jnp.where(last_owner, mixed_heads[:, :, per_dev - 1], zero_block).astype(
        jnp.float32
    )
    lead_sum, tail_sum = (
        lax.psum(lead_grad.astype(jnp.bfloat16), "ctx").astype(jnp.float32),
        lax.psum(tail_grad.astype(jnp.bfloat16), "ctx").astype(jnp.float32),
    )
    wide_grad = jnp.stack([lead_sum, tail_sum], axis=2).astype(jnp.bfloat16)
    mixed_heads = mixed_heads.at[:, :, 0].set(
        jnp.where(first_owner, zero_block, mixed_heads[:, :, 0])
    )
    mixed_heads = mixed_heads.at[:, :, per_dev - 1].set(
        jnp.where(last_owner, zero_block, mixed_heads[:, :, per_dev - 1])
    )

    def random_back(random_grad, id_group):
        chosen = jax.nn.one_hot(id_group, blocks_all, dtype=jnp.float32)
        spread_grad = jnp.einsum(
            "shpqb,shpqke->shbke", chosen, random_grad, precision=lax.Precision.HIGHEST
        )
        return lax.psum_scatter(
            spread_grad.astype(jnp.bfloat16), "ctx", scatter_dimension=2, tiled=True
        ).astype(jnp.float32)

    def backward_step(items):
        (
            position,
            query_group,
            pad_group,
            global_group,
            block_group,
            id_group,
            logsum_group,
            grad_group,
        ) = items
        random_group = random_pairs_for(block_group, id_group)
        query_grad, window_grad, global_grad, random_grad = attend_back(
            query_group,
            pad_group,
            global_group,
            random_group,
            mask,
            scale,
            logsum_group,
            grad_group,
        )
        return (query_grad, window_grad, global_grad, random_back(random_grad, id_group))

    query_grads, window_grads, global_grads, random_total = lax.map(
        backward_step,
        (
            jnp.arange(steps),
            query_groups,
            pad_groups,
            global_groups,
            block_groups,
            mine_groups,
            logsum_groups,
            split_groups(mixed_heads, steps, group),
        ),
    )
    query_grads = query_grads.reshape(seqs, heads, length, head_dim)
    window_grads = window_grads.reshape(seqs, heads, per_dev + 2, BLK, pair_width)
    global_grads = global_grads.reshape(seqs, heads, 2, BLK, pair_width)
    wide_inner = jnp.sum(wide_grad.astype(jnp.float32) * mix_full, axis=-1, keepdims=True)
    wide_probs_grad = jnp.einsum(
        "shgqd,shkd->shgqk", wide_grad, value_local, preferred_element_type=jnp.float32
    )
    wide_scores_grad = (wide_probs * (wide_probs_grad - wide_inner)).astype(jnp.bfloat16)
    wide_query_part = (
        jnp.einsum(
            "shgqk,shkd->shgqd", wide_scores_grad, key_local, preferred_element_type=jnp.float32
        )
        * scale
    )
    wide_key_grad = (
        jnp.einsum(
            "shgqk,shgqd->shkd", wide_scores_grad, global_query, preferred_element_type=jnp.float32
        )
        * scale
    )
    wide_value_grad = jnp.einsum(
        "shgqk,shgqd->shkd", wide_probs_low, wide_grad, preferred_element_type=jnp.float32
    )
    wide_pair_grad = jnp.concatenate([wide_key_grad, wide_value_grad], axis=-1).reshape(
        seqs, heads, per_dev, BLK, pair_width
    )
    rim_pair = jnp.concatenate([window_grads[:, :, 0], window_grads[:, :, per_dev + 1]], axis=2)
    rim_back = extended(rim_pair.astype(jnp.bfloat16), (("ctx", 2),), BLK).astype(rim_pair.dtype)
    local_grad = window_grads[:, :, 1 : per_dev + 1] + wide_pair_grad
    local_grad = local_grad.at[:, :, 0].add(rim_back[:, :, :BLK])
    local_grad = local_grad.at[:, :, per_dev - 1].add(rim_back[:, :, 3 * BLK :])
    global_total, wide_query = lax.psum((global_grads, wide_query_part), "ctx")
    local_grad = local_grad.at[:, :, 0].add(jnp.where(first_owner, global_total[:, :, 0], 0.0))
    local_grad = local_grad.at[:, :, per_dev - 1].add(
        jnp.where(last_owner, global_total[:, :, 1], 0.0)
    )
    query_grads = query_grads.at[:, :, :BLK].add(jnp.where(first_owner, wide_query[:, :, 0], 0.0))
    query_grads = query_grads.at[:, :, length - BLK :].add(
        jnp.where(last_owner, wide_query[:, :, 1], 0.0)
    )
    local_grad = local_grad + random_total.reshape(seqs, heads, per_dev, BLK, pair_width)
    pair_grad = local_grad.reshape(seqs, heads, length, pair_width).transpose(2, 0, 1, 3)
    query_part = query_grads.transpose(2, 0, 1, 3)
    projected_grad = jnp.concatenate([query_part, pair_grad], axis=-1).astype(jnp.bfloat16)
    projected_rows = projected_grad.reshape(total_rows, heads * 3 * head_dim)
    grad_in = (
        (residual_grad + rows_sum(projected_rows, input_low, 1))
        .astype(jnp.bfloat16)
        .reshape(part_rows, seqs, width)
    )
    input_grad = outer_sum(x_rows, projected_rows).reshape(width, heads, 3 * head_dim)
    pair_bias_grad = jnp.stack(
        [
            jnp.sum(projected_grad[..., :head_dim], axis=(0, 1), dtype=jnp.float32).reshape(-1),
            jnp.sum(projected_grad[..., 2 * head_dim :], axis=(0, 1), dtype=jnp.float32).reshape(
                -1
            ),
        ]
    )
    output_grad = outer_sum(mixed, branch_full)
    bias_grad = jnp.stack(
        [
            jnp.sum(branch_low, axis=0, dtype=jnp.float32),
            jnp.sum(second_low, axis=0, dtype=jnp.float32),
        ]
    )
    gain_grad = jnp.stack(
        [jnp.sum(first_grad * normed_one, axis=0), jnp.sum(upstream * normed_two, axis=0)]
    )
    shift_grad = jnp.stack([jnp.sum(first_grad, axis=0), jnp.sum(upstream, axis=0)])
    upper_grad = outer_sum(first_full, inner_low)
    upper_bias_grad = jnp.sum(inner_low, axis=0, dtype=jnp.float32)
    lower_grad = outer_sum(active, second_full)
    shares = (
        lax.psum_scatter(input_grad, "fsdp", scatter_dimension=0, tiled=True),
        lax.psum_scatter(pair_bias_grad, "fsdp", scatter_dimension=1, tiled=True),
        lax.psum_scatter(output_grad, "fsdp", scatter_dimension=1, tiled=True),
        lax.psum_scatter(bias_grad, "fsdp", scatter_dimension=1, tiled=True),
        lax.psum_scatter(gain_grad, "fsdp", scatter_dimension=1, tiled=True),
        lax.psum_scatter(shift_grad, "fsdp", scatter_dimension=1, tiled=True),
        lax.psum_scatter(upper_grad, "fsdp", scatter_dimension=0, tiled=True),
        lax.psum_scatter(upper_bias_grad, "fsdp", scatter_dimension=0, tiled=True),
        lax.psum_scatter(lower_grad, "fsdp", scatter_dimension=1, tiled=True),
    )
    matrices = lax.psum((shares[0], shares[1], shares[2], shares[6], shares[7], shares[8]), "ctx")
    vectors = lax.psum((shares[3], shares[4], shares[5]), ("ctx", "tp"))
    return (
        layer_out,
        grad_in,
        matrices[0],
        matrices[1],
        matrices[2],
        vectors[0],
        vectors[1],
        vectors[2],
        matrices[3],
        matrices[4],
        matrices[5],
    )


MESH = pl.DeviceIdType.MESH
BF = jnp.bfloat16
F32 = jnp.float32
NT = (((1,), (1,)), ((), ()))
NN = (((1,), (0,)), ((), ()))
TN = (((0,), (0,)), ((), ()))
VMEM_LIMIT = 60 * 2**20


def mm(left, right, dims=NN):
    return lax.dot_general(left, right, dims, preferred_element_type=F32)


class Place:
    def __init__(self):
        self.f = lax.axis_index("fsdp")
        self.c = lax.axis_index("ctx")
        self.t = lax.axis_index("tp")
        f, c, t = self.f, self.c, self.t
        self.k = k = lax.rem(f, 2)
        self.y = y = f // 2
        self.p = t + k * (3 - 2 * t)
        self.core = (f + 1 - 2 * k, c, t)
        self.xnbr = (f, 1 - c, t)
        self.ynbr = (lax.rem(f + 2, 4), c, t)
        self.zplus = (f, c, t + 1 - 2 * k)
        self.zminus = (f, c, t - 1 + 2 * k)
        self.own_core = t // 2
        self.own_slot = t + (t // 2) * (3 - 2 * t)
        self.pair = 2 * y
        self.other = 2 - 2 * y

    def swap(self, s):
        return (2 * self.y + self.c, self.k, s)

    def swap_is_self(self, s):
        return jnp.logical_and(self.k == self.c, self.t == s)


def copy_to(src, dst, send, recv, device):
    return pltpu.make_async_remote_copy(
        src_ref=src, dst_ref=dst, send_sem=send, recv_sem=recv, device_id=device, device_id_type=MESH
    )


def greet(at, between=lambda: None):
    barrier = pltpu.get_barrier_semaphore()
    sizes = [lax.axis_size(a) for a in ("fsdp", "ctx", "tp")]
    others = 0
    for i in range(sizes[0]):
        for j in range(sizes[1]):
            for m in range(sizes[2]):
                if i or j or m:
                    others += 1
                    device = (
                        lax.rem(at.f + i, sizes[0]),
                        lax.rem(at.c + j, sizes[1]),
                        lax.rem(at.t + m, sizes[2]),
                    )
                    pl.semaphore_signal(barrier, inc=1, device_id=device, device_id_type=MESH)
    between()
    pl.semaphore_wait(barrier, others)


class Gather:
    def __init__(self, at, shards, full, send, recv, tall):
        self.at, self.shards, self.full, self.send, self.recv, self.tall = at, shards, full, send, recv, tall

    def own(self, g):
        at, full, shard = self.at, self.full[g], self.shards[g]
        half = shard.shape[0] // 2
        rows = pl.ds(pl.multiple_of(at.c * half, half), half)

        @pl.when(at.k == at.own_core)
        def _():
            full[at.own_slot, at.f, at.c] = shard[rows, :]

        @pl.when(at.k != at.own_core)
        def _():
            self.cp(g, at.own_slot, 0, shard.at[rows], full.at[at.own_slot, at.f, at.c], at.core).start()

    def cp(self, g, slot, kind, src, dst, device):
        return copy_to(src, dst, self.send.at[g, slot, kind], self.recv.at[g, slot, kind], device)

    def arrives(self, g, slot, kind, dst):
        self.cp(g, slot, kind, dst, dst, self.at.core).wait_recv()

    def ours(self, g, slot, f, c):
        return self.full[g].at[slot, pl.ds(f, 2), c]

    def step_z(self, g, turn):
        at, full = self.at, self.full[g]
        first = (at.p + 2) // 3
        slot = first if turn == 0 else 1 - first
        piece = self.ours(g, slot, at.pair, at.c)

        @pl.when(at.p == slot)
        def _():
            self.arrives(g, slot, 0, full.at[slot, at.core[0], at.c])

        @pl.when(at.p > slot)
        def _():
            self.arrives(g, slot, 1, piece)

        @pl.when(at.p < slot)
        def _():
            self.arrives(g, slot, 2, piece)

        @pl.when(jnp.logical_and(at.p >= slot, at.p < 3))
        def _():
            self.cp(g, slot, 1, piece, piece, at.zplus).start()

        @pl.when(jnp.logical_and(at.p == 1, slot == 1))
        def _():
            self.cp(g, slot, 2, piece, piece, at.zminus).start()

        for copy in self.ahead(g, slot):
            copy.start()

    def ahead(self, g, slot):
        at, full = self.at, self.full[g]
        if g in self.tall:
            piece = self.ours(g, slot, at.pair, at.c)
            return self.cp(g, slot, 4, piece, piece, at.xnbr), self.cp(g, slot, 3, piece, piece, at.ynbr)
        even, odd = full.at[slot, at.pair, at.c], full.at[slot, at.pair + 1, at.c]
        return self.cp(g, slot, 3, even, even, at.ynbr), self.cp(g, slot, 4, odd, odd, at.xnbr)

    def direct(self, g, slot):
        at, full = self.at, self.full[g]
        if g in self.tall:
            return ()
        even, odd = full.at[slot, at.pair, at.c], full.at[slot, at.pair + 1, at.c]
        return self.cp(g, slot, 7, even, even, at.xnbr), self.cp(g, slot, 8, odd, odd, at.ynbr)

    def relays(self, g, slot):
        at, full = self.at, self.full[g]
        if g in self.tall:
            piece = self.ours(g, slot, at.pair, 1 - at.c)
            return (self.cp(g, slot, 6, piece, piece, at.ynbr),)
        even = full.at[slot, at.other, at.c]
        odd = full.at[slot, at.pair + 1, 1 - at.c]
        return self.cp(g, slot, 6, odd, odd, at.ynbr), self.cp(g, slot, 5, even, even, at.xnbr)

    def step_relay(self, g, turn):
        at = self.at
        first = (at.p + 2) // 3
        slot = first if turn == 0 else 1 - first
        copies = self.relays(g, slot)
        full = self.full[g]
        if g in self.tall:
            self.arrives(g, slot, 4, self.ours(g, slot, at.pair, 1 - at.c))
            copies[0].start()
            return
        self.arrives(g, slot, 4, full.at[slot, at.pair + 1, 1 - at.c])
        copies[0].start()
        self.arrives(g, slot, 3, full.at[slot, at.other, at.c])
        copies[1].start()
        for copy in self.direct(g, slot):
            copy.start()

    def step_last(self, g):
        at, full = self.at, self.full[g]
        for slot in range(2):
            if g in self.tall:
                self.arrives(g, slot, 3, self.ours(g, slot, at.other, at.c))
                self.arrives(g, slot, 6, self.ours(g, slot, at.other, 1 - at.c))
            else:
                self.arrives(g, slot, 5, full.at[slot, at.other, 1 - at.c])
                self.arrives(g, slot, 6, full.at[slot, at.other + 1, 1 - at.c])
                self.arrives(g, slot, 7, full.at[slot, at.pair, 1 - at.c])
                self.arrives(g, slot, 8, full.at[slot, at.other + 1, at.c])

    def sent(self, g):
        at, full = self.at, self.full[g]

        def left(slot, kind, src):
            self.cp(g, slot, kind, src, src, at.core).wait_send()

        @pl.when(at.k != at.own_core)
        def _():
            left(at.own_slot, 0, full.at[at.own_slot, at.f, at.c])

        for slot in range(2):
            piece = self.ours(g, slot, at.pair, at.c)

            @pl.when(jnp.logical_and(at.p >= slot, at.p < 3))
            def _():
                left(slot, 1, piece)

            if slot == 1:

                @pl.when(at.p == 1)
                def _():
                    left(slot, 2, piece)

            for copy in (*self.ahead(g, slot), *self.direct(g, slot), *self.relays(g, slot)):
                copy.wait_send()


class Swap:
    def __init__(self, at, blocks, rows, base, send, recv):
        self.at, self.blocks, self.rows, self.base, self.send, self.recv = at, blocks, rows, base, send, recv
        self.n = blocks.shape[1]

    def span(self, s, base):
        return pl.ds(pl.multiple_of(base + s * self.n, self.n), self.n)

    def start_in(self):
        at = self.at
        there = self.rows.at[self.span(at.t, self.base * at.c)]
        for s in range(4):

            @pl.when(at.swap_is_self(s))
            def _():
                here = self.rows.at[self.span(s, self.base * at.k)]
                pltpu.make_async_copy(self.blocks.at[s], here, self.recv.at[s]).start()

            @pl.when(jnp.logical_not(at.swap_is_self(s)))
            def _():
                copy_to(self.blocks.at[s], there, self.send.at[s], self.recv.at[at.t], at.swap(s)).start()

    def wait_in(self, s):
        at = self.at
        here = self.rows.at[self.span(s, self.base * at.k)]

        @pl.when(jnp.logical_not(at.swap_is_self(s)))
        def _():
            copy_to(here, here, self.send.at[s], self.recv.at[s], at.core).wait_recv()

        @pl.when(at.swap_is_self(s))
        def _():
            pltpu.make_async_copy(self.blocks.at[s], here, self.recv.at[s]).wait()

    def start_out(self, s):
        at = self.at
        here = self.rows.at[self.span(s, self.base * at.k)]

        @pl.when(at.swap_is_self(s))
        def _():
            pltpu.make_async_copy(here, self.blocks.at[s], self.send.at[s]).start()

        @pl.when(jnp.logical_not(at.swap_is_self(s)))
        def _():
            copy_to(here, self.blocks.at[at.t], self.send.at[s], self.recv.at[at.t], at.swap(s)).start()

    def wait_out(self, s):
        at = self.at

        @pl.when(jnp.logical_not(at.swap_is_self(s)))
        def _():
            copy_to(self.blocks.at[s], self.blocks.at[s], self.send.at[s], self.recv.at[s], at.core).wait_recv()

    def sent(self, outward=False):
        at = self.at
        for s in range(4):

            @pl.when(jnp.logical_not(at.swap_is_self(s)))
            def _():
                here = self.rows.at[self.span(s, self.base * at.k)] if outward else self.blocks.at[s]
                copy_to(here, here, self.send.at[s], self.recv.at[s], at.core).wait_send()

            if outward:

                @pl.when(at.swap_is_self(s))
                def _():
                    here = self.rows.at[self.span(s, self.base * at.k)]
                    pltpu.make_async_copy(here, self.blocks.at[s], self.send.at[s]).wait()
ROWS = 256


def norm_stats(value):
    mean = jnp.mean(value, axis=-1, keepdims=True)
    centred = value - mean
    inverse = lax.rsqrt(jnp.mean(centred * centred, axis=-1, keepdims=True) + EPS)
    return centred * inverse, inverse


def gelu_both(value):
    share = 0.5 + 0.5 * lax.erf(value * 0.7071067811865476)
    density = jnp.exp(value * value * -0.5) * 0.3989422804014327
    return value * share, share + value * density


def row_sum(value):
    return jnp.sum(value, axis=0, keepdims=True)


class Cores:
    def __init__(self, at, out, back, send, recv, row_send, row_recv):
        self.at, self.out, self.back = at, out, back
        self.send, self.recv, self.row_send, self.row_recv = send, recv, row_send, row_recv

    def rows(self, half, i):
        return pl.ds(pl.multiple_of(half * 512 + i * ROWS, ROWS), ROWS)

    def part(self, stage, i):
        return copy_to(self.out.at[i], self.back.at[i], self.send.at[stage, i], self.recv.at[stage, i], self.at.core)

    def reduce(self, stage, partial, finish, between=lambda: None):
        at = self.at

        @pl.loop(0, 512 // ROWS)
        def _(i):
            self.out[i] = partial(self.rows(1 - at.k, i))
            self.part(stage, i).start()

        between()

        @pl.loop(0, 512 // ROWS)
        def _(i):
            total = partial(self.rows(at.k, i))
            self.part(stage, i).wait_recv()
            finish(i, self.rows(at.k, i), total + self.back[i])

        @pl.loop(0, 512 // ROWS)
        def _(i):
            self.part(stage, i).wait_send()

    def row(self, stage, ref, half, i):
        rows = ref.at[self.rows(half, i)]
        return copy_to(rows, rows, self.row_send.at[stage, i], self.row_recv.at[stage, i], self.at.core)

    def over_rows(self, stage, ref, work):
        at = self.at

        @pl.loop(0, 512 // ROWS)
        def _(i):
            work(self.rows(at.k, i))

        @pl.loop(0, 512 // ROWS)
        def _(i):
            self.row(stage, ref, 1 - at.k, i).wait_recv()
            work(self.rows(1 - at.k, i))

        @pl.loop(0, 512 // ROWS)
        def _(i):
            self.row(stage, ref, at.k, i).wait_send()


def flip(dst, src):
    @pl.loop(0, src.shape[0] // ROWS)
    def _(r):
        rows = pl.ds(pl.multiple_of(r * ROWS, ROWS), ROWS)
        dst[:, rows] = src[rows, :].T


def product(dst, slot, flipped, right):
    n = dst.shape[2] * dst.shape[3]

    @pl.loop(0, dst.shape[1])
    def _(r):
        rows = pl.ds(pl.multiple_of(r * n, n), n)
        got = mm(flipped[rows, :], right())
        dst[slot, r] = got.astype(BF).reshape(dst.shape[2:])


def vmem():
    return pl.BlockSpec(memory_space=pltpu.VMEM)


QCHUNK = 512


def attend_chunk(h, q, key, query, value_t, bias, lse, mixed_t):
    cols = pl.ds(pl.multiple_of(q * QCHUNK, QCHUNK), QCHUNK)
    scores = mm(key[h], query[h, cols, :], NT)
    length = scores.shape[0]
    scores = (
        scores.reshape(length // BLK, BLK, QCHUNK) + bias[h, :, cols][:, None, :]
    ).reshape(length, QCHUNK)
    top = jnp.max(scores, axis=0, keepdims=True)
    weights = jnp.exp(scores - top)
    total = jnp.sum(weights, axis=0, keepdims=True)
    probs = (weights * (1.0 / total)).astype(BF)
    lse[h, :, cols] = top + jnp.log(total)
    mixed_t[:, cols] = mm(value_t[...], probs).astype(BF)


class Vectors:
    def __init__(self, at, own, vec, near, ids, picked, sems):
        self.at, self.own, self.vec, self.near, self.ids, self.picked = at, own, vec, near, ids, picked
        self.send, self.recv = sems

    def fill(self, out_bias, norm_gain, norm_bias, up_bias, qv_bias, rand):
        at = self.at
        size = out_bias.shape[1]
        for i, ref in enumerate((out_bias, norm_gain, norm_bias)):
            self.vec[at.f, 2 * i : 2 * i + 2, 0:size] = ref[...]
        self.own[0:1, 0:size] = up_bias[...]
        self.own[1:3, 0 : qv_bias.shape[1]] = qv_bias[...]
        for h in range(3):
            for r in range(3):
                self.ids[:, 3 * h + r, 0 : rand.shape[3]] = rand[h, r].astype(F32)

        @pl.when(at.k == at.own_core)
        def _():
            self.near[at.own_slot, at.f] = self.own[...]

            @pl.when(at.k == at.c)
            def _():
                self.picked[at.own_slot] = self.ids[at.t]

    def copies(self):
        at = self.at
        out = []
        box = self.vec.at[at.f]
        for i, f in enumerate((at.core[0], at.ynbr[0], lax.rem(at.core[0] + 2, 4))):
            out.append((None, copy_to(box, box, self.send.at[i], self.recv.at[at.f], (f, at.c, at.t))))
        for y in range(2):
            for t in range(4):
                f = 2 * y + at.own_core
                copy = copy_to(
                    self.own,
                    self.near.at[at.own_slot, at.f],
                    self.send.at[3 + 4 * y + t],
                    self.recv.at[4 + 4 * at.own_slot + at.f],
                    (f, at.c, t),
                )
                out.append((jnp.logical_or(f != at.f, t != at.t), copy))
        for s in range(4):
            f = at.pair + at.own_core
            copy = copy_to(
                self.ids.at[s],
                self.picked.at[at.own_slot],
                self.send.at[11 + s],
                self.recv.at[12 + at.own_slot],
                (f, at.k, s),
            )
            away = jnp.logical_or(f != at.f, s != at.t)
            out.append((jnp.logical_and(at.c == at.k, away), copy))
        return out

    def each(self, act):
        for condition, copy in self.copies():
            if condition is None:
                act(copy)
            else:
                pl.when(condition)(lambda copy=copy: act(copy))

    def start(self):
        self.each(lambda copy: copy.start())

    def sent(self):
        self.each(lambda copy: copy.wait_send())

    def wait(self):
        at = self.at

        def arrives(index, dst):
            copy_to(dst, dst, self.send.at[0], self.recv.at[index], at.core).wait_recv()

        for i in range(1, 4):
            f = lax.rem(at.f + i, 4)
            arrives(f, self.vec.at[f])
        for slot in range(2):
            ours = jnp.logical_and(at.k == at.own_core, slot == at.own_slot)
            for f in range(4):

                @pl.when(jnp.logical_not(jnp.logical_and(ours, f == at.f)))
                def _():
                    arrives(4 + 4 * slot + f, self.near.at[slot, f])

            @pl.when(jnp.logical_not(jnp.logical_and(ours, at.k == at.c)))
            def _():
                arrives(12 + slot, self.picked.at[slot])

    def unpack(self, vec_out, ups, proj_bias, row, bias):
        size = vec_out.shape[1] // 4
        low = lambda a: a.astype(BF).astype(F32)
        part = size // 4
        for f in range(4):
            vec_out[:, size * f : size * (f + 1)] = low(self.vec[f, :, 0:size])
        proj_bias[...] = jnp.zeros_like(proj_bias)
        for slot in range(2):
            for f in range(4):
                ups[slot : slot + 1, size * f : size * (f + 1)] = low(self.near[slot, f, 0:1, 0:size])
                row[slot, 0:2, part * f : part * (f + 1)] = low(self.near[slot, f, 1:3, 0:part])
            for i in range(3):
                start = i * size
                proj_bias[slot, :, start : start + 64] = row[slot, 0:1, 64 * i : 64 * i + 64]
                proj_bias[slot, :, start + 128 : start + 192] = row[slot, 1:2, 64 * i : 64 * i + 64]
        blocks, length = bias.shape[1], bias.shape[2]
        spot = lax.broadcasted_iota(jnp.int32, (blocks, length), 0)
        block = lax.broadcasted_iota(jnp.int32, (blocks, length), 1) // BLK
        number = lambda mask: jnp.where(mask, 1.0, 0.0)
        fixed = number(jnp.abs(spot - block) <= 1) + number(spot == 0) + number(spot == blocks - 1)
        edge = jnp.logical_or(block == 0, block == blocks - 1)
        spread_out = number(spot == block).astype(BF)
        here = spot.astype(F32)
        for slot in range(2):
            ids = mm(self.picked[slot, :, 0:blocks].astype(BF), spread_out)
            for i in range(3):
                counts = fixed
                for r in range(3):
                    counts = counts + number(ids[3 * i + r : 3 * i + r + 1, :] == here)
                counts = jnp.where(edge, 1.0, counts)
                bias[3 * slot + i] = jnp.where(counts > 0.5, jnp.log(jnp.maximum(counts, 1.0)), -1e30)


class Reduce:
    def __init__(self, at, grads, work, plane, zline, final, send, recv):
        self.at, self.grads, self.work, self.plane, self.zline, self.final = at, grads, work, plane, zline, final
        self.send, self.recv = send, recv

    def cp(self, g, slot, kind, src, dst, device, recv_kind=None):
        recv_kind = kind if recv_kind is None else recv_kind
        return copy_to(src, dst, self.send.at[g, slot, kind], self.recv.at[g, slot, recv_kind], device)

    def arrives(self, g, slot, kind, dst):
        self.cp(g, slot, kind, dst, dst, self.at.core).wait_recv()

    def plane_sends(self, g, slot):
        at, grad, box = self.at, self.grads[g], self.plane.at[g, slot]
        return (
            self.cp(g, slot, 1, grad.at[slot, at.other, 1 - at.c], box.at[1], at.xnbr),
            self.cp(g, slot, 3, grad.at[slot, at.other + 1, 1 - at.c], box.at[3], at.ynbr),
            self.cp(g, slot, 0, grad.at[slot, at.pair, 1 - at.c], box.at[0], at.xnbr),
            self.cp(g, slot, 2, grad.at[slot, at.other + 1, at.c], box.at[2], at.ynbr),
        )

    def sums(self, g, slot):
        at, work, box = self.at, self.work.at[g, slot], self.plane.at[g, slot]
        return (
            self.cp(g, slot, 4, work.at[0], box.at[4], at.ynbr),
            self.cp(g, slot, 5, work.at[1], box.at[5], at.xnbr),
        )

    def plane0(self, g, slot):
        for copy in self.plane_sends(g, slot)[:2]:
            copy.start()

    def total(self, g, slot, i, piece, boxes):
        came = sum(self.plane[g, slot, b].astype(F32) for b in boxes)
        own = self.grads[g][slot, piece[0], piece[1]].astype(F32)
        self.work[g, slot, i] = (own + came).astype(BF)

    def plane1(self, g, slot):
        at = self.at
        copies = self.sums(g, slot)
        for i, kind, piece in ((0, 1, (at.other, at.c)), (1, 3, (at.pair + 1, 1 - at.c))):
            self.arrives(g, slot, kind, self.plane.at[g, slot, kind])
            self.total(g, slot, i, piece, (kind,))
            copies[i].start()
        for copy in self.plane_sends(g, slot)[2:]:
            copy.start()

    def ours(self, g, slot):
        return self.work.at[g, slot, pl.ds(2, 2)]

    def down(self, g, slot):
        return self.cp(g, slot, 6, self.ours(g, slot), self.zline.at[g, slot], self.at.zminus)

    def upward(self, g, slot):
        return self.cp(g, slot, 7, self.ours(g, slot), self.zline.at[g, 2], self.at.zplus)

    def plane2(self, g, slot):
        at = self.at
        for kind in (0, 2, 4, 5):
            self.arrives(g, slot, kind, self.plane.at[g, slot, kind])
        boxes = ((0, 4), (2, 5))
        for i in range(2):
            self.total(g, slot, 2 + i, (at.pair + i, at.c), boxes[i])

        @pl.when(at.p == 3)
        def _():
            self.down(g, slot).start()

        if slot == 1:

            @pl.when(at.p == 0)
            def _():
                self.upward(g, slot).start()

    def add_line(self, g, slot, which):
        box = 2 if which else slot
        self.arrives(g, slot, 6 + which, self.zline.at[g, box])
        for i in range(2):
            self.work[g, slot, 2 + i] = (
                self.work[g, slot, 2 + i].astype(F32) + self.zline[g, box, i].astype(F32)
            ).astype(BF)

    def line(self, g, slot, place):
        at = self.at
        if place < slot:
            return

        @pl.when(at.p == place)
        def _():
            self.add_line(g, slot, 0)
            if slot == 1 and place == 1:
                self.add_line(g, slot, 1)
            if place > slot:
                self.down(g, slot).start()
            else:
                self.hand_out(g, slot)

    def hands(self, g, slot):
        at, final = self.at, self.final[g]
        mine = self.work.at[g, slot, 2 + at.k]
        theirs = self.work.at[g, slot, 3 - at.k]
        there = final.at[self.half(g, at.c)]
        return (
            self.cp(g, slot, 8, theirs, there, at.core, 8),
            self.cp(g, slot, 9, mine, there, at.xnbr, 9),
            self.cp(g, slot, 10, theirs, there, (at.core[0], 1 - at.c, at.t), 9),
        )

    def half(self, g, c):
        n = self.final[g].shape[0] // 2
        return pl.ds(pl.multiple_of(c * n, n), n)

    def hand_out(self, g, slot):
        at = self.at
        for copy in self.hands(g, slot):
            copy.start()
        self.final[g][self.half(g, at.c), :] = self.work[g, slot, 2 + at.k]

    def finish(self, g):
        at, final = self.at, self.final[g]

        @pl.when(at.k != at.own_core)
        def _():
            self.arrives(g, at.own_slot, 8, final.at[self.half(g, at.c)])

        self.arrives(g, at.own_slot, 9, final.at[self.half(g, 1 - at.c)])
        return final[...].astype(F32)

    def sent(self, g):
        at = self.at
        for slot in range(2):
            for copy in (*self.plane_sends(g, slot), *self.sums(g, slot)):
                copy.wait_send()

            @pl.when(at.p > slot)
            def _():
                self.down(g, slot).wait_send()

            if slot == 1:

                @pl.when(at.p == 0)
                def _():
                    self.upward(g, slot).wait_send()

            @pl.when(at.p == slot)
            def _():
                for copy in self.hands(g, slot):
                    copy.wait_send()


def attend_back_chunk(h, q, key, query, value, key_t, bias, lse, upper, key_sum, value_sum, query_t):
    cols = pl.ds(pl.multiple_of(q * QCHUNK, QCHUNK), QCHUNK)
    some = query[h, cols, :]
    upper = upper(cols)
    scores = mm(key[h], some, NT)
    length = scores.shape[0]
    shift = bias[h, :, cols] - lse[h, :, cols]
    scores = (scores.reshape(length // BLK, BLK, QCHUNK) + shift[:, None, :]).reshape(length, QCHUNK)
    probs = jnp.exp(scores)
    probs_grad = mm(value[h], upper, NT)
    inner = jnp.sum(probs * probs_grad, axis=0, keepdims=True)
    scores_grad = (probs * (probs_grad - inner)).astype(BF)
    value_sum[...] += mm(probs.astype(BF), upper)
    key_sum[...] += mm(scores_grad, some)
    query_t[:, cols] = mm(key_t[...], scores_grad)


def layer_kernel(
    xs, cs, w_in, w_out, w_up, w_down, out_bias, norm_gain, norm_bias, up_bias, qv_bias, rand,
    layer_blocks, grad_blocks, g_in, g_qv, g_out, g_outs, g_gains, g_shifts, g_up, g_ups, g_down,
    x_all, up_half, low0, low1, low2, query, key, value, mixed, lse, bias, vectors, ups,
    own, vec, near, ids, picked, proj_bias, bias_row,
    grad0, grad_out, part_out, part_back, rows_f32, normed_one, inverse_one, first_b, second_b,
    act, slope, flipped, grad_rows, key_t, key_sum, value_sum, query_t,
    work, plane, zline, final0, final1, final2, small, small_out, sum_out, sum_in,
    xs_send, xs_recv, xc_send, xc_recv, cs_send, cs_recv, p_send, p_recv, v_send, v_recv,
    lo_send, lo_recv, gi_send, gi_recv, w_send, w_recv, send, recv, row_send, row_recv, small_send, small_recv,
):
    at = Place()
    letters = Vectors(at, own, vec, near, ids, picked, (v_send, v_recv))
    finals = (final0, final1, final2)
    wide = w_in.shape[2]

    def pack():
        for h in range(3):
            final0[:, h * wide : (h + 1) * wide] = w_in[h].astype(BF)
        final0[:, 3 * wide : 4 * wide] = w_out[...].T.astype(BF)
        final1[...] = w_up[...].astype(BF)
        final2[...] = w_down[...].astype(BF)
        own[...] = jnp.zeros_like(own)
        ids[...] = jnp.zeros_like(ids)
        vec[at.f] = jnp.zeros(vec.shape[1:], F32)
        letters.fill(out_bias, norm_gain, norm_bias, up_bias, qv_bias, rand)

    greet(at, pack)
    gather = Gather(at, finals, (low0, low1, low2), p_send, p_recv, tall=(1,))
    tokens = Swap(at, xs, x_all, 512, xs_send, xs_recv)
    upstreams = Swap(at, cs, up_half, 0, cs_send, cs_recv)
    part = xs.shape[1]
    width = x_all.shape[1]
    letters.start()
    for g in range(3):
        gather.own(g)
    gather.step_z(0, 0)
    gather.step_z(0, 1)
    tokens.start_in()
    gather.step_relay(0, 0)
    gather.step_relay(0, 1)

    def to_core(s, half):
        rows = x_all.at[pl.ds(pl.multiple_of(half * 512 + s * part, part), part)]
        return copy_to(rows, rows, xc_send.at[s], xc_recv.at[s], at.core)

    for s in range(4):
        tokens.wait_in(s)
        to_core(s, at.k).start()
    gather.step_z(1, 0)
    gather.step_z(1, 1)
    letters.wait()
    letters.unpack(vectors, ups, proj_bias, bias_row, bias)
    small[...] = jnp.zeros_like(small)
    for s in range(4):
        to_core(s, 1 - at.k).wait_recv()
    gather.step_last(0)

    dim = query.shape[2]
    for slot in range(2):

        @pl.loop(0, 4)
        def _(r):
            rows = pl.ds(pl.multiple_of(r * 256, 256), 256)
            weight = low0[slot, :, :, :, 0:640].reshape(width, 640)
            got = mm(x_all[rows, :], weight) + proj_bias[slot]
            for i in range(3):
                h = slot * 3 + i
                start = i * 3 * dim
                query[h, rows, :] = (got[:, start : start + dim] * dim**-0.5).astype(BF)
                key[h, rows, :] = got[:, start + dim : start + 2 * dim].astype(BF)
                one = got[:, start + 2 * dim : start + 3 * dim]
                value[h, rows, :] = one.astype(BF)
                flipped[384 + h * dim : 384 + (h + 1) * dim, rows] = one.T.astype(BF)

        if slot == 0:
            gather.step_z(2, 0)
            gather.step_z(2, 1)
            upstreams.start_in()
    gather.step_relay(1, 0)
    gather.step_relay(1, 1)

    def attend_forward(low_head, high_head):
        @pl.loop(low_head, high_head)
        def _(h):
            @pl.loop(0, 1024 // QCHUNK)
            def _(q):
                spot = pl.ds(pl.multiple_of(h * dim, dim), dim)
                value_t = flipped.at[pl.ds(pl.multiple_of(384 + h * dim, dim), dim)]
                attend_chunk(h, q, key, query, value_t, bias, lse, flipped.at[spot])

    attend_forward(0, 3)
    gather.step_relay(2, 0)
    gather.step_relay(2, 1)
    attend_forward(3, 6)

    @pl.loop(0, 4)
    def _(r):
        rows = pl.ds(pl.multiple_of(r * 256, 256), 256)
        blank = jnp.zeros((dim, 256), BF)
        for slot in range(2):
            heads = jnp.concatenate([blank, flipped[slot * 192 : slot * 192 + 192, rows]], axis=0)
            mixed[rows, slot * 256 : slot * 256 + 256] = heads.T

    layer = Swap(at, layer_blocks, up_half, 0, lo_send, lo_recv)
    inputs = Swap(at, grad_blocks, grad_rows, 0, gi_send, gi_recv)
    reduce = Reduce(at, (grad0, low1, low2), work, plane, zline, finals, w_send, w_recv)
    cores = Cores(at, part_out, part_back, send, recv, row_send, row_recv)
    square = lambda full, slot: full[slot].reshape(width, width)
    out_part = lambda slot: low0[slot, :, :, :, 512:768].reshape(width, 256)
    local = lambda i: pl.ds(pl.multiple_of(i * ROWS, ROWS), ROWS)

    def tally(row, value):
        small[row : row + 1, :] += row_sum(value)

    def branch_part(rows):
        return mm(mixed[rows, 0:256], out_part(0), NT) + mm(mixed[rows, 256:512], out_part(1), NT)

    def branch_done(i, rows, total):
        normed, inverse = norm_stats(x_all[rows, :].astype(F32) + (total + vectors[0:1, :]))
        value = normed * vectors[2:3, :] + vectors[4:5, :]
        normed_one[local(i), :] = normed
        inverse_one[local(i), :] = inverse
        rows_f32[local(i), :] = value
        first_b[rows, :] = value.astype(BF)
        cores.row(0, first_b, at.k, i).start()

    cores.reduce(0, branch_part, branch_done)

    def up(rows):
        for slot in range(2):
            inner = mm(first_b[rows, :], square(low1, slot)) + ups[slot : slot + 1, :]
            value, slope_value = gelu_both(inner)
            act[slot, rows, :] = value.astype(BF)
            slope[slot, rows, :] = slope_value.astype(BF)

    gather.sent(0)
    gather.step_last(1)
    gather.sent(1)
    cores.over_rows(0, first_b, up)
    gather.step_last(2)
    gather.sent(2)
    for s in range(4):
        upstreams.wait_in(s)

    def second_part(rows):
        return mm(act[0, rows, :], square(low2, 0), NT) + mm(act[1, rows, :], square(low2, 1), NT)

    def second_done(i, rows, total):
        normed, inverse = norm_stats(rows_f32[local(i), :] + (total + vectors[1:2, :]))
        layer_row = (normed * vectors[3:4, :] + vectors[5:6, :]).astype(BF)
        upstream = up_half[local(i), :].astype(F32)
        up_half[local(i), :] = layer_row
        scaled = upstream * vectors[3:4, :]
        grad = inverse * (
            scaled
            - jnp.mean(scaled, axis=-1, keepdims=True)
            - normed * jnp.mean(scaled * normed, axis=-1, keepdims=True)
        )
        rows_f32[local(i), :] = grad
        low = grad.astype(BF)
        second_b[rows, :] = low
        cores.row(1, second_b, at.k, i).start()
        tally(1, low.astype(F32))
        tally(3, upstream * normed)
        tally(5, upstream)

    cores.reduce(1, second_part, second_done)

    def down(rows):
        for slot in range(2):
            grad = mm(second_b[rows, :], square(low2, slot)) * slope[slot, rows, :].astype(F32)
            low = grad.astype(BF)
            slope[slot, rows, :] = low
            tally(6 + slot, low.astype(F32))

    cores.over_rows(1, second_b, down)
    flip(flipped, second_b)
    for slot in range(2):
        product(low2, slot, flipped, lambda: act[slot])
        reduce.plane0(2, slot)

    def first_part(rows):
        return mm(slope[0, rows, :], square(low1, 0), NT) + mm(slope[1, rows, :], square(low1, 1), NT)

    def first_done(i, rows, total):
        grad = total + rows_f32[local(i), :]
        normed = normed_one[local(i), :]
        tally(2, grad * normed)
        tally(4, grad)
        scaled = grad * vectors[2:3, :]
        back = inverse_one[local(i), :] * (
            scaled
            - jnp.mean(scaled, axis=-1, keepdims=True)
            - normed * jnp.mean(scaled * normed, axis=-1, keepdims=True)
        )
        rows_f32[local(i), :] = back
        low = back.astype(BF)
        second_b[rows, :] = low
        cores.row(2, second_b, at.k, i).start()
        tally(0, low.astype(F32))

    cores.reduce(2, first_part, first_done)
    for slot in range(2):
        reduce.plane1(2, slot)
    flip(flipped, first_b)
    for slot in range(2):
        product(low1, slot, flipped, lambda: slope[slot])
        reduce.plane0(1, slot)

    mixed_grad = first_b

    def mix_back(rows):
        for slot in range(2):
            mixed_grad[rows, slot * 256 : slot * 256 + 256] = mm(second_b[rows, :], out_part(slot)).astype(BF)

    cores.over_rows(2, second_b, mix_back)
    flip(flipped, second_b)

    @pl.loop(0, 4)
    def _(r):
        rows = pl.ds(pl.multiple_of(r * 192, 192), 192)
        grad_out[rows, :] = mm(flipped[rows, :], mixed[...]).astype(BF)

    flip(flipped, x_all)
    proj_grad = act
    for slot in range(2):
        proj_grad[slot, :, 576:640] = jnp.zeros((1024, 64), BF)

    def attend(h, part):
        if part == 0:
            key_t[...] = key[h].astype(F32).T.astype(BF)
            key_sum[...] = jnp.zeros_like(key_sum)
            value_sum[...] = jnp.zeros_like(value_sum)

        @pl.loop(part * (512 // QCHUNK), (part + 1) * (512 // QCHUNK))
        def _(q):
            column = (h // 3) * 256 + (h % 3 + 1) * 64
            attend_back_chunk(
                h, q, key, query, value, key_t, bias, lse,
                lambda cols: mixed_grad[cols, column : column + 64], key_sum, value_sum, query_t,
            )

        if part == 1:
            start = (h % 3) * 192
            proj_grad[h // 3, :, start : start + 64] = (query_t[...] * 0.125).T.astype(BF)
            proj_grad[h // 3, :, start + 64 : start + 128] = key_sum[...].astype(BF)
            proj_grad[h // 3, :, start + 128 : start + 192] = value_sum[...].astype(BF)

    def in_grads(slot):
        @pl.loop(0, 4)
        def _(r):
            rows = pl.ds(pl.multiple_of(r * 192, 192), 192)
            got = mm(flipped[rows, :], proj_grad[slot, :, 0:640])
            out_part = grad_out[rows, slot * 256 : slot * 256 + 256]
            grad0[slot, r, :, :, 0:512] = got[:, 0:512].astype(BF).reshape(2, 96, 512)
            shared = got[:, 512:640] + out_part[:, 0:128].astype(F32)
            grad0[slot, r, :, :, 512:640] = shared.astype(BF).reshape(2, 96, 128)
            grad0[slot, r, :, :, 640:768] = out_part[:, 128:256].reshape(2, 96, 128)

        reduce.plane0(0, slot)

    def both(step, g, *more):
        for slot in range(2):
            step(g, slot, *more)

    attend(0, 0)
    attend(0, 1)
    both(reduce.plane2, 2)
    attend(1, 0)
    both(reduce.plane1, 1)
    attend(1, 1)
    both(reduce.line, 2, 2)
    attend(2, 0)
    both(reduce.line, 2, 1)
    attend(2, 1)
    in_grads(0)
    attend(3, 0)
    both(reduce.line, 2, 0)
    attend(3, 1)
    both(reduce.plane2, 1)
    attend(4, 0)
    reduce.plane1(0, 0)
    attend(4, 1)
    both(reduce.line, 1, 2)
    for s in range(4):
        layer.start_out(s)
    attend(5, 0)
    both(reduce.line, 1, 1)
    reduce.plane2(0, 0)
    attend(5, 1)
    both(reduce.line, 1, 0)
    in_grads(1)

    t = at.t
    steps = (at.xnbr, at.ynbr, (at.f, at.c, t + 1 - 2 * lax.rem(t, 2)), (at.f, at.c, lax.rem(t + 2, 4)))
    hops = [
        copy_to(sum_out.at[i], sum_in.at[i], small_send.at[i], small_recv.at[i], device)
        for i, device in enumerate(steps)
    ]

    def small_next(i):
        hops[i].wait_recv()
        if i < 3:
            sum_out[i + 1] = sum_out[i] + sum_in[i]
            hops[i + 1].start()
        else:
            small_out[at.k] = sum_out[i] + sum_in[i]

    sum_out[0] = small[...]
    for slot in range(2):
        sum_out[0, 8 + slot : 9 + slot, 0:640] = row_sum(proj_grad[slot, :, 0:640].astype(F32))
    hops[0].start()
    reduce.line(0, 0, 2)

    def in_part(rows):
        return sum(
            mm(proj_grad[slot, rows, 0:640], low0[slot, :, :, :, 0:640].reshape(width, 640), NT)
            for slot in range(2)
        )

    def in_done(i, rows, total):
        grad_rows[local(i), :] = (total + rows_f32[local(i), :]).astype(BF)
        for s in range(ROWS // 128):
            inputs.start_out(i * (ROWS // 128) + s)

    def between():
        small_next(0)
        reduce.plane1(0, 1)
        reduce.line(0, 0, 1)

    cores.reduce(3, in_part, in_done, between)
    small_next(1)
    reduce.line(0, 0, 0)
    reduce.plane2(0, 1)
    small_next(2)
    reduce.line(0, 1, 2)
    small_next(3)
    mine = small_out.at[at.k]
    both_cores = copy_to(mine, mine, small_send.at[4], small_recv.at[4], at.core)
    both_cores.start()
    reduce.line(0, 1, 1)
    for copy in hops:
        copy.wait_send()
    g_down[...] = reduce.finish(2)
    g_up[...] = reduce.finish(1)
    got = reduce.finish(0)
    fr = g_up.shape[0]
    for h in range(3):
        g_in[h] = got[:, h * fr : (h + 1) * fr]
    g_out[...] = got[:, 3 * fr : 4 * fr].T
    both_cores.wait_send()
    copy_to(small_out.at[1 - at.k], small_out.at[1 - at.k], small_send.at[4], small_recv.at[4], at.core).wait_recv()
    sums = small_out[0, 0:8, :] + small_out[1, 0:8, :]
    used = small_out.at[at.own_core]
    up_row = used[pl.ds(6 + at.own_slot, 1), :]
    proj_row = used[pl.ds(8 + at.own_slot, 1), :]
    pick = lambda j: jnp.concatenate(
        [proj_row[:, i * fr + 64 * j : i * fr + 64 * j + 64] for i in range(3)], axis=1
    )
    pair_rows = jnp.concatenate([pick(0), pick(2)], axis=0)
    quarter = fr // 4
    for f in range(4):

        @pl.when(at.f == f)
        def _():
            piece = sums[:, f * fr : (f + 1) * fr]
            g_outs[...] = piece[0:2]
            g_gains[...] = piece[2:4]
            g_shifts[...] = piece[4:6]
            g_ups[...] = up_row[:, f * fr : (f + 1) * fr]
            g_qv[...] = pair_rows[:, f * quarter : (f + 1) * quarter]

    for s in range(4):
        layer.wait_out(s)
        inputs.wait_out(s)
    layer.sent(True)
    inputs.sent(True)
    for g in range(3):
        reduce.sent(g)
    letters.sent()
    tokens.sent()
    upstreams.sent()
    for s in range(4):
        to_core(s, at.k).wait_send()


def layer_call(xs, cs, w_in, w_out, w_up, w_down, out_bias, norm_gain, norm_bias, up_bias, qv_bias, rand):
    width = xs.shape[2]
    length, half = 1024, 512
    heads, dim = 6, 64
    blocks = length // BLK
    parts = half // ROWS
    fr = width // 4
    piece = (fr // 2, width)
    shape = jax.ShapeDtypeStruct
    dma = lambda *dims: pltpu.SemaphoreType.DMA(dims)
    low = lambda *dims: pltpu.VMEM(dims, BF)
    full = lambda *dims: pltpu.VMEM(dims, F32)
    anywhere = pl.BlockSpec(memory_space=pl.ANY)
    return pl.pallas_call(
        layer_kernel,
        out_shape=(
            shape(xs.shape, BF),
            shape(xs.shape, BF),
            shape((3, fr, fr), F32),
            shape((2, fr // 4), F32),
            shape((fr, fr), F32),
            shape((2, fr), F32),
            shape((2, fr), F32),
            shape((2, fr), F32),
            shape((fr, width), F32),
            shape((1, fr), F32),
            shape((fr, width), F32),
        ),
        in_specs=[anywhere] * 2 + [vmem()] * 10,
        out_specs=[anywhere] * 2 + [vmem()] * 9,
        scratch_shapes=[
            low(length, width),
            low(half, width),
            low(2, 4, 2, *piece),
            low(2, 4, 2, *piece),
            low(2, 4, 2, *piece),
            low(heads, length, dim),
            low(heads, length, dim),
            low(heads, length, dim),
            low(length, 512),
            full(heads, 1, length),
            full(heads, blocks, length),
            full(8, width),
            full(2, width),
            full(8, 256),
            full(4, 8, 256),
            full(2, 4, 8, 256),
            full(4, 16, 128),
            full(2, 16, 128),
            full(2, 1, 640),
            full(2, 8, 256),
            low(2, 4, 2, *piece),
            low(width, 512),
            full(parts, ROWS, width),
            full(parts, ROWS, width),
            full(half, width),
            full(half, width),
            full(half, 1),
            low(length, width),
            low(length, width),
            low(2, length, width),
            low(2, length, width),
            low(width, length),
            low(half, width),
            low(dim, length),
            full(length, dim),
            full(length, dim),
            full(dim, length),
            low(3, 2, 4, *piece),
            low(3, 2, 6, *piece),
            low(3, 3, 2, *piece),
            low(fr, width),
            low(fr, width),
            low(fr, width),
            full(16, width),
            full(2, 16, width),
            full(4, 16, width),
            full(4, 16, width),
            dma(4),
            dma(4),
            dma(4),
            dma(4),
            dma(4),
            dma(4),
            dma(3, 2, 9),
            dma(3, 2, 9),
            dma(15),
            dma(14),
            dma(4),
            dma(4),
            dma(4),
            dma(4),
            dma(3, 2, 11),
            dma(3, 2, 11),
            dma(4, parts),
            dma(4, parts),
            dma(3, parts),
            dma(3, parts),
            dma(5),
            dma(5),
        ],
        compiler_params=pltpu.CompilerParams(
            collective_id=1, has_side_effects=True, vmem_limit_bytes=VMEM_LIMIT
        ),
        name="layer",
    )(xs, cs, w_in, w_out, w_up, w_down, out_bias, norm_gain, norm_bias, up_bias, qv_bias, rand)


def copy_kernel(*refs):
    half = len(refs) // 2
    for src, dst in zip(refs[:half], refs[half:]):
        dst[...] = src[...]


def copied(arrays):
    return pl.pallas_call(
        copy_kernel,
        out_shape=[jax.ShapeDtypeStruct(a.shape, a.dtype) for a in arrays],
        in_specs=[vmem()] * len(arrays),
        out_specs=[vmem()] * len(arrays),
        name="results",
    )(*arrays)


def sequence_shards(hidden_in, rand_blocks, w_in, qv_bias, w_out, out_bias, norm_gain, norm_bias, w_up, up_bias, w_down, cotangent):
    layer_blocks, grad_blocks, *grads = layer_call(
        hidden_in.transpose(1, 0, 2),
        cotangent.transpose(1, 0, 2),
        w_in.transpose(1, 0, 2),
        w_out,
        w_up,
        w_down.T,
        out_bias,
        norm_gain,
        norm_bias,
        up_bias[None],
        qv_bias,
        rand_blocks.transpose(2, 3, 0, 1),
    )
    grads = list(copied(grads))
    grads[0] = grads[0].transpose(1, 0, 2)
    grads[7] = grads[7][0]
    grads[8] = grads[8].T
    return (layer_blocks.transpose(1, 0, 2), grad_blocks.transpose(1, 0, 2), *grads)


def solution(mesh):
    placed = (
        P(("ctx", "tp"), "fsdp", None),
        P("fsdp", None, "tp", None),
        P("fsdp", "tp", None),
        P(None, ("tp", "fsdp")),
        P("tp", "fsdp"),
        P(None, "fsdp"),
        P(None, "fsdp"),
        P(None, "fsdp"),
        P("fsdp", "tp"),
        P(("tp", "fsdp")),
        P("tp", "fsdp"),
        P(("ctx", "tp"), "fsdp", None),
    )
    sizes = tuple(mesh.shape[a] for a in ("fsdp", "ctx", "tp"))

    def local(*args):
        part_rows, seqs, width = args[0].shape
        rows, heads, wide = args[2].shape
        whole = sizes == (4, 2, 4) and (part_rows, seqs, width) == (128, 4, 768)
        whole = whole and (rows, heads, wide) == (192, 3, 192) and args[8].shape == (192, 768)
        return (sequence_shards if whole else span_shards)(*args)

    return jax.shard_map(
        local,
        mesh=mesh,
        in_specs=placed,
        out_specs=(
            P(("ctx", "tp"), "fsdp", None),
            P(("ctx", "tp"), "fsdp", None),
            P("fsdp", "tp", None),
            P(None, ("tp", "fsdp")),
            P("tp", "fsdp"),
            P(None, "fsdp"),
            P(None, "fsdp"),
            P(None, "fsdp"),
            P("fsdp", "tp"),
            P(("tp", "fsdp")),
            P("tp", "fsdp"),
        ),
        check_vma=False,
    )
```

```python
import jax
import jax.numpy as jnp
from jax import lax
from jax.experimental import pallas as pl
from jax.experimental.pallas import tpu as pltpu
from jax.sharding import PartitionSpec as P

BLK = 64


EPS = 1e-06
NEG = -1000000000.0


def from_root(block, axis, owner):
    block = jnp.where(lax.axis_index(axis) == owner, block, jnp.zeros_like(block))
    return lax.psum(block, axis)


def extended(array, sides, width):
    for axis, dim in sides:
        size, length = (lax.axis_size(axis), array.shape[dim])
        up = [(i, (i + 1) % size) for i in range(size - 1)]
        down = [(j, i) for i, j in up]
        last = lax.slice_in_dim(array, length - width, length, axis=dim)
        leading = lax.slice_in_dim(array, 0, width, axis=dim)
        before = lax.ppermute(last, axis, up)
        after = lax.ppermute(leading, axis, down)
        array = jnp.concatenate([before, array, after], axis=dim)
    return array


def joined_2(part, axis, combine):
    gathered = jax.tree.map(lambda a: lax.all_gather(a, axis), part)

    def take(source):
        return jax.tree.map(lambda a: lax.dynamic_index_in_dim(a, source, 0, False), gathered)

    return lax.fori_loop(
        1, lax.axis_size(axis), lambda source, state: combine(state, take(source)), take(0)
    )


def norm_forward(value, gain, shift):
    mean = jnp.mean(value, axis=-1, keepdims=True)
    centred = value - mean
    inverse = lax.rsqrt(jnp.mean(centred * centred, axis=-1, keepdims=True) + EPS)
    normed = centred * inverse
    return (normed * gain + shift, normed, inverse)


def norm_backward(upper, normed, inverse, gain):
    scaled = upper * gain
    return inverse * (
        scaled
        - jnp.mean(scaled, axis=-1, keepdims=True)
        - normed * jnp.mean(scaled * normed, axis=-1, keepdims=True)
    )


def exact_gelu(value):
    return jax.nn.gelu(value, approximate=False)


def outer_sum(left, right):
    return lax.dot_general(
        left, right, (((0,), (0,)), ((), ())), preferred_element_type=jnp.float32
    )


def rows_all(value):
    return lax.all_gather(value, "tp", axis=0, tiled=True)


def rows_sum(left, right, contract):
    return lax.psum_scatter(
        lax.dot_general(
            left, right, (((1,), (contract,)), ((), ())), preferred_element_type=jnp.float32
        ),
        "tp",
        scatter_dimension=0,
        tiled=True,
    )


def spread(piece, root):
    return from_root(piece, "ctx", root)


def stats_join(first_stats, second_stats):
    top = jnp.maximum(first_stats[0], second_stats[0])
    total = first_stats[1] * jnp.exp(first_stats[0] - top) + second_stats[1] * jnp.exp(
        second_stats[0] - top
    )
    return (top, total)


def split_groups(array, steps, group):
    return array.reshape((steps, group) + array.shape[1:])


def key_set(window_pad, global_pair, random_pairs):
    per_dev = random_pairs.shape[3]
    window = jnp.stack(
        [window_pad[:, :, offset_by : offset_by + per_dev] for offset_by in range(3)], axis=3
    )
    target_shape = global_pair.shape[:2] + (per_dev,) + global_pair.shape[2:]
    global_all = jnp.broadcast_to(global_pair[:, :, None], target_shape)
    random_all = jnp.swapaxes(random_pairs, 2, 3)
    joined = jnp.concatenate([window, global_all, random_all], axis=3)
    shape = joined.shape
    return joined.reshape(shape[0], shape[1], shape[2], shape[3] * shape[4], shape[5])


def scores_of(query, keys, mask, scale):
    head_dim = query.shape[-1]
    raw = (
        jnp.einsum(
            "shpqd,shpkd->shpqk", query, keys[..., :head_dim], preferred_element_type=jnp.float32
        )
        * scale
    )
    return jnp.where(mask, raw, NEG)


def attend_group(query, window_pad, global_pair, random_pairs, mask, scale):
    head_dim = query.shape[-1]
    keys = key_set(window_pad, global_pair, random_pairs)
    scores = scores_of(query, keys, mask, scale)
    top = jnp.max(scores, axis=-1, keepdims=True)
    weights = jnp.exp(scores - top)
    total = jnp.sum(weights, axis=-1, keepdims=True)
    probs = (weights / total).astype(jnp.bfloat16)
    mixed = jnp.einsum(
        "shpqk,shpkd->shpqd", probs, keys[..., head_dim:], preferred_element_type=jnp.float32
    )
    return (mixed.astype(jnp.bfloat16), (top + jnp.log(total))[..., 0])


def attend_back(query, window_pad, global_pair, random_pairs, mask, scale, logsum, mixed_grad):
    head_dim = query.shape[-1]
    blocksize = window_pad.shape[3]
    keys = key_set(window_pad, global_pair, random_pairs)
    scores = scores_of(query, keys, mask, scale)
    probs = jnp.exp(scores - logsum[..., None])
    probs_grad = jnp.einsum(
        "shpqd,shpkd->shpqk", mixed_grad, keys[..., head_dim:], preferred_element_type=jnp.float32
    )
    inner = jnp.sum(probs * probs_grad, axis=-1, keepdims=True)
    scores_grad = (probs * (probs_grad - inner)).astype(jnp.bfloat16)
    query_grad = (
        jnp.einsum(
            "shpqk,shpkd->shpqd",
            scores_grad,
            keys[..., :head_dim],
            preferred_element_type=jnp.float32,
        )
        * scale
    )
    keys_grad = (
        jnp.einsum("shpqk,shpqd->shpkd", scores_grad, query, preferred_element_type=jnp.float32)
        * scale
    )
    values_grad = jnp.einsum(
        "shpqk,shpqd->shpkd",
        probs.astype(jnp.bfloat16),
        mixed_grad,
        preferred_element_type=jnp.float32,
    )
    pairs_grad = jnp.concatenate([keys_grad, values_grad], axis=-1)
    shape = pairs_grad.shape
    pairs_grad = pairs_grad.reshape(
        shape[0], shape[1], shape[2], shape[3] // blocksize, blocksize, shape[4]
    )
    per_dev = shape[2]
    window_grad = jnp.zeros(window_pad.shape, jnp.float32)
    for offset_by in range(3):
        window_grad = window_grad.at[:, :, offset_by : offset_by + per_dev].add(
            pairs_grad[:, :, :, offset_by]
        )
    global_grad = jnp.sum(pairs_grad[:, :, :, 3:5], axis=2)
    random_grad = jnp.swapaxes(pairs_grad[:, :, :, 5:], 2, 3)
    return (query_grad, window_grad, global_grad, random_grad)


def span_shards(
    hidden_in,
    rand_blocks,
    w_in,
    qv_bias,
    w_out,
    out_bias,
    norm_gain,
    norm_bias,
    w_up,
    up_bias,
    w_down,
    cotangent,
):
    ctx_count = lax.axis_size("ctx")
    tp_count = lax.axis_size("tp")
    ctx_place = lax.axis_index("ctx")
    part_rows, seqs, width = hidden_in.shape
    heads = w_in.shape[1]
    head_dim = w_in.shape[2] // 3
    pair_width = 2 * head_dim
    blocks_all = rand_blocks.shape[1]
    picks = rand_blocks.shape[3]
    length = part_rows * tp_count
    per_dev = length // BLK
    total_rows = length * seqs
    scale = head_dim ** (-0.5)
    group = min(seqs, max(1, 512 // length))
    steps = seqs // group
    first_owner = ctx_place == 0
    last_owner = ctx_place == ctx_count - 1
    gathered = (
        lax.all_gather(w_in.astype(jnp.bfloat16), "fsdp", axis=0, tiled=True),
        lax.all_gather(qv_bias.astype(jnp.bfloat16), "fsdp", axis=1, tiled=True),
        lax.all_gather(w_out.astype(jnp.bfloat16), "fsdp", axis=1, tiled=True),
        lax.all_gather(out_bias.astype(jnp.bfloat16), "fsdp", axis=1, tiled=True),
        lax.all_gather(norm_gain.astype(jnp.bfloat16), "fsdp", axis=1, tiled=True),
        lax.all_gather(norm_bias.astype(jnp.bfloat16), "fsdp", axis=1, tiled=True),
        lax.all_gather(w_up.astype(jnp.bfloat16), "fsdp", axis=0, tiled=True),
        lax.all_gather(up_bias.astype(jnp.bfloat16), "fsdp", axis=0, tiled=True),
        lax.all_gather(w_down.astype(jnp.bfloat16), "fsdp", axis=1, tiled=True),
    )
    input_low = gathered[0].reshape(width, heads * 3 * head_dim)
    bias_pair = gathered[1].astype(jnp.float32).reshape(2, heads, head_dim)
    output_low = gathered[2]
    bias_out = gathered[3].astype(jnp.float32)
    gains = gathered[4].astype(jnp.float32)
    shifts = gathered[5].astype(jnp.float32)
    upper_low = gathered[6]
    bias_up = gathered[7].astype(jnp.float32)
    lower_low = gathered[8]
    x_full = rows_all(hidden_in)
    x_rows = x_full.reshape(total_rows, width)
    projected = jnp.dot(x_rows, input_low, preferred_element_type=jnp.float32).reshape(
        length, seqs, heads, 3, head_dim
    )
    query = (projected[:, :, :, 0] + bias_pair[0]).astype(jnp.bfloat16)
    key = projected[:, :, :, 1].astype(jnp.bfloat16)
    value = (projected[:, :, :, 2] + bias_pair[1]).astype(jnp.bfloat16)
    query_heads = query.transpose(1, 2, 0, 3).reshape(seqs, heads, per_dev, BLK, head_dim)
    pairs = jnp.concatenate([key, value], axis=-1).transpose(1, 2, 0, 3)
    window_pad = extended(pairs, (("ctx", 2),), BLK).reshape(
        seqs, heads, per_dev + 2, BLK, pair_width
    )
    pair_blocks = pairs.reshape(seqs, heads, per_dev, BLK, pair_width)
    triple_blocks = jnp.concatenate([query_heads, pair_blocks], axis=-1)
    global_triple = jnp.stack(
        [
            spread(triple_blocks[:, :, 0], 0),
            spread(triple_blocks[:, :, per_dev - 1], ctx_count - 1),
        ],
        axis=2,
    )
    global_query = global_triple[..., :head_dim]
    global_pair = global_triple[..., head_dim:]
    key_local = pairs[..., :head_dim]
    value_local = pairs[..., head_dim:]
    wide_scores = (
        jnp.einsum("shgqd,shkd->shgqk", global_query, key_local, preferred_element_type=jnp.float32)
        * scale
    )
    wide_top = jnp.max(wide_scores, axis=-1)
    wide_total = jnp.sum(jnp.exp(wide_scores - wide_top[..., None]), axis=-1)
    all_top, all_total = joined_2((wide_top, wide_total), "ctx", stats_join)
    wide_probs = jnp.exp(wide_scores - (all_top + jnp.log(all_total))[..., None])
    wide_probs_low = wide_probs.astype(jnp.bfloat16)
    mix_low = jnp.einsum(
        "shgqk,shkd->shgqd", wide_probs_low, value_local, preferred_element_type=jnp.float32
    )
    mix_full = jnp.einsum(
        "shgqk,shkd->shgqd",
        wide_probs,
        value_local.astype(jnp.float32),
        precision=lax.Precision.HIGHEST,
    )
    mix_low, mix_full = lax.psum((mix_low, mix_full), "ctx")
    global_mixed = mix_low.astype(jnp.bfloat16)
    units = seqs * heads * picks * per_dev
    table = rand_blocks.transpose(0, 2, 3, 1).reshape(seqs, heads, picks, ctx_count, per_dev)
    table = table.transpose(0, 1, 2, 4, 3).reshape(units, ctx_count)
    mine = lax.dynamic_index_in_dim(table, ctx_place, 1, keepdims=False)
    mine_groups = mine.reshape(steps, group, heads, picks, per_dev)
    block_index = ctx_place * per_dev + jnp.arange(per_dev)
    present = jnp.concatenate(
        [
            (block_index >= 1)[:, None],
            jnp.ones((per_dev, 1), jnp.bool_),
            (block_index <= blocks_all - 2)[:, None],
            jnp.ones((per_dev, 2 + picks), jnp.bool_),
        ],
        axis=1,
    )
    mask = jnp.repeat(present, BLK, axis=1)[None, None, :, None, :]

    def random_pairs_for(block_group, id_group):
        whole = lax.all_gather(block_group, "ctx", axis=2, tiled=True)
        chosen = jax.nn.one_hot(id_group, blocks_all, dtype=jnp.bfloat16)
        return jnp.einsum(
            "shpqb,shbke->shpqke", chosen, whole, preferred_element_type=jnp.float32
        ).astype(jnp.bfloat16)

    query_groups = split_groups(query_heads, steps, group)
    pad_groups = split_groups(window_pad, steps, group)
    global_groups = split_groups(global_pair, steps, group)
    block_groups = split_groups(pair_blocks, steps, group)

    def forward_step(items):
        position, query_group, pad_group, global_group, block_group, id_group = items
        random_group = random_pairs_for(block_group, id_group)
        return attend_group(query_group, pad_group, global_group, random_group, mask, scale)

    mixed_groups, logsum_groups = lax.map(
        forward_step,
        (jnp.arange(steps), query_groups, pad_groups, global_groups, block_groups, mine_groups),
    )
    mixed_blocks = mixed_groups.reshape(seqs, heads, per_dev, BLK, head_dim)
    mixed_blocks = mixed_blocks.at[:, :, 0].set(
        jnp.where(first_owner, global_mixed[:, :, 0], mixed_blocks[:, :, 0])
    )
    mixed_blocks = mixed_blocks.at[:, :, per_dev - 1].set(
        jnp.where(last_owner, global_mixed[:, :, 1], mixed_blocks[:, :, per_dev - 1])
    )
    mixed = (
        mixed_blocks.reshape(seqs, heads, length, head_dim)
        .transpose(2, 0, 1, 3)
        .reshape(total_rows, heads * head_dim)
    )
    branch = rows_sum(mixed, output_low, 0) + bias_out[0]
    residual_in = hidden_in.reshape(part_rows * seqs, width).astype(jnp.float32)
    first, normed_one, inverse_one = norm_forward(residual_in + branch, gains[0], shifts[0])
    first_full = rows_all(first.astype(jnp.bfloat16).reshape(part_rows, seqs, width)).reshape(
        total_rows, width
    )
    inner = jnp.dot(first_full, upper_low, preferred_element_type=jnp.float32) + bias_up
    active_value, gelu_back = jax.vjp(exact_gelu, inner)
    active = active_value.astype(jnp.bfloat16)
    second = rows_sum(active, lower_low, 0) + bias_out[1]
    result, normed_two, inverse_two = norm_forward(first + second, gains[1], shifts[1])
    layer_out = result.astype(jnp.bfloat16).reshape(part_rows, seqs, width)
    upstream = cotangent.reshape(part_rows * seqs, width).astype(jnp.float32)
    second_grad = norm_backward(upstream, normed_two, inverse_two, gains[1])
    second_low = second_grad.astype(jnp.bfloat16)
    second_full = rows_all(second_low.reshape(part_rows, seqs, width)).reshape(total_rows, width)
    active_grad = lax.dot_general(
        second_full, lower_low, (((1,), (1,)), ((), ())), preferred_element_type=jnp.float32
    )
    inner_low = gelu_back(active_grad)[0].astype(jnp.bfloat16)
    first_grad = second_grad + rows_sum(inner_low, upper_low, 1)
    residual_grad = norm_backward(first_grad, normed_one, inverse_one, gains[0])
    branch_low = residual_grad.astype(jnp.bfloat16)
    branch_full = rows_all(branch_low.reshape(part_rows, seqs, width)).reshape(total_rows, width)
    mixed_grad = lax.dot_general(
        branch_full, output_low, (((1,), (1,)), ((), ())), preferred_element_type=jnp.float32
    ).astype(jnp.bfloat16)
    mixed_heads = (
        mixed_grad.reshape(length, seqs, heads, head_dim)
        .transpose(1, 2, 0, 3)
        .reshape(seqs, heads, per_dev, BLK, head_dim)
    )
    zero_block = jnp.zeros((seqs, heads, BLK, head_dim), jnp.bfloat16)
    lead_grad = jnp.where(first_owner, mixed_heads[:, :, 0], zero_block).astype(jnp.float32)
    tail_grad = jnp.where(last_owner, mixed_heads[:, :, per_dev - 1], zero_block).astype(
        jnp.float32
    )
    lead_sum, tail_sum = (
        lax.psum(lead_grad.astype(jnp.bfloat16), "ctx").astype(jnp.float32),
        lax.psum(tail_grad.astype(jnp.bfloat16), "ctx").astype(jnp.float32),
    )
    wide_grad = jnp.stack([lead_sum, tail_sum], axis=2).astype(jnp.bfloat16)
    mixed_heads = mixed_heads.at[:, :, 0].set(
        jnp.where(first_owner, zero_block, mixed_heads[:, :, 0])
    )
    mixed_heads = mixed_heads.at[:, :, per_dev - 1].set(
        jnp.where(last_owner, zero_block, mixed_heads[:, :, per_dev - 1])
    )

    def random_back(random_grad, id_group):
        chosen = jax.nn.one_hot(id_group, blocks_all, dtype=jnp.float32)
        spread_grad = jnp.einsum(
            "shpqb,shpqke->shbke", chosen, random_grad, precision=lax.Precision.HIGHEST
        )
        return lax.psum_scatter(
            spread_grad.astype(jnp.bfloat16), "ctx", scatter_dimension=2, tiled=True
        ).astype(jnp.float32)

    def backward_step(items):
        (
            position,
            query_group,
            pad_group,
            global_group,
            block_group,
            id_group,
            logsum_group,
            grad_group,
        ) = items
        random_group = random_pairs_for(block_group, id_group)
        query_grad, window_grad, global_grad, random_grad = attend_back(
            query_group,
            pad_group,
            global_group,
            random_group,
            mask,
            scale,
            logsum_group,
            grad_group,
        )
        return (query_grad, window_grad, global_grad, random_back(random_grad, id_group))

    query_grads, window_grads, global_grads, random_total = lax.map(
        backward_step,
        (
            jnp.arange(steps),
            query_groups,
            pad_groups,
            global_groups,
            block_groups,
            mine_groups,
            logsum_groups,
            split_groups(mixed_heads, steps, group),
        ),
    )
    query_grads = query_grads.reshape(seqs, heads, length, head_dim)
    window_grads = window_grads.reshape(seqs, heads, per_dev + 2, BLK, pair_width)
    global_grads = global_grads.reshape(seqs, heads, 2, BLK, pair_width)
    wide_inner = jnp.sum(wide_grad.astype(jnp.float32) * mix_full, axis=-1, keepdims=True)
    wide_probs_grad = jnp.einsum(
        "shgqd,shkd->shgqk", wide_grad, value_local, preferred_element_type=jnp.float32
    )
    wide_scores_grad = (wide_probs * (wide_probs_grad - wide_inner)).astype(jnp.bfloat16)
    wide_query_part = (
        jnp.einsum(
            "shgqk,shkd->shgqd", wide_scores_grad, key_local, preferred_element_type=jnp.float32
        )
        * scale
    )
    wide_key_grad = (
        jnp.einsum(
            "shgqk,shgqd->shkd", wide_scores_grad, global_query, preferred_element_type=jnp.float32
        )
        * scale
    )
    wide_value_grad = jnp.einsum(
        "shgqk,shgqd->shkd", wide_probs_low, wide_grad, preferred_element_type=jnp.float32
    )
    wide_pair_grad = jnp.concatenate([wide_key_grad, wide_value_grad], axis=-1).reshape(
        seqs, heads, per_dev, BLK, pair_width
    )
    rim_pair = jnp.concatenate([window_grads[:, :, 0], window_grads[:, :, per_dev + 1]], axis=2)
    rim_back = extended(rim_pair.astype(jnp.bfloat16), (("ctx", 2),), BLK).astype(rim_pair.dtype)
    local_grad = window_grads[:, :, 1 : per_dev + 1] + wide_pair_grad
    local_grad = local_grad.at[:, :, 0].add(rim_back[:, :, :BLK])
    local_grad = local_grad.at[:, :, per_dev - 1].add(rim_back[:, :, 3 * BLK :])
    global_total, wide_query = lax.psum((global_grads, wide_query_part), "ctx")
    local_grad = local_grad.at[:, :, 0].add(jnp.where(first_owner, global_total[:, :, 0], 0.0))
    local_grad = local_grad.at[:, :, per_dev - 1].add(
        jnp.where(last_owner, global_total[:, :, 1], 0.0)
    )
    query_grads = query_grads.at[:, :, :BLK].add(jnp.where(first_owner, wide_query[:, :, 0], 0.0))
    query_grads = query_grads.at[:, :, length - BLK :].add(
        jnp.where(last_owner, wide_query[:, :, 1], 0.0)
    )
    local_grad = local_grad + random_total.reshape(seqs, heads, per_dev, BLK, pair_width)
    pair_grad = local_grad.reshape(seqs, heads, length, pair_width).transpose(2, 0, 1, 3)
    query_part = query_grads.transpose(2, 0, 1, 3)
    projected_grad = jnp.concatenate([query_part, pair_grad], axis=-1).astype(jnp.bfloat16)
    projected_rows = projected_grad.reshape(total_rows, heads * 3 * head_dim)
    grad_in = (
        (residual_grad + rows_sum(projected_rows, input_low, 1))
        .astype(jnp.bfloat16)
        .reshape(part_rows, seqs, width)
    )
    input_grad = outer_sum(x_rows, projected_rows).reshape(width, heads, 3 * head_dim)
    pair_bias_grad = jnp.stack(
        [
            jnp.sum(projected_grad[..., :head_dim], axis=(0, 1), dtype=jnp.float32).reshape(-1),
            jnp.sum(projected_grad[..., 2 * head_dim :], axis=(0, 1), dtype=jnp.float32).reshape(
                -1
            ),
        ]
    )
    output_grad = outer_sum(mixed, branch_full)
    bias_grad = jnp.stack(
        [
            jnp.sum(branch_low, axis=0, dtype=jnp.float32),
            jnp.sum(second_low, axis=0, dtype=jnp.float32),
        ]
    )
    gain_grad = jnp.stack(
        [jnp.sum(first_grad * normed_one, axis=0), jnp.sum(upstream * normed_two, axis=0)]
    )
    shift_grad = jnp.stack([jnp.sum(first_grad, axis=0), jnp.sum(upstream, axis=0)])
    upper_grad = outer_sum(first_full, inner_low)
    upper_bias_grad = jnp.sum(inner_low, axis=0, dtype=jnp.float32)
    lower_grad = outer_sum(active, second_full)
    shares = (
        lax.psum_scatter(input_grad, "fsdp", scatter_dimension=0, tiled=True),
        lax.psum_scatter(pair_bias_grad, "fsdp", scatter_dimension=1, tiled=True),
        lax.psum_scatter(output_grad, "fsdp", scatter_dimension=1, tiled=True),
        lax.psum_scatter(bias_grad, "fsdp", scatter_dimension=1, tiled=True),
        lax.psum_scatter(gain_grad, "fsdp", scatter_dimension=1, tiled=True),
        lax.psum_scatter(shift_grad, "fsdp", scatter_dimension=1, tiled=True),
        lax.psum_scatter(upper_grad, "fsdp", scatter_dimension=0, tiled=True),
        lax.psum_scatter(upper_bias_grad, "fsdp", scatter_dimension=0, tiled=True),
        lax.psum_scatter(lower_grad, "fsdp", scatter_dimension=1, tiled=True),
    )
    matrices = lax.psum((shares[0], shares[1], shares[2], shares[6], shares[7], shares[8]), "ctx")
    vectors = lax.psum((shares[3], shares[4], shares[5]), ("ctx", "tp"))
    return (
        layer_out,
        grad_in,
        matrices[0],
        matrices[1],
        matrices[2],
        vectors[0],
        vectors[1],
        vectors[2],
        matrices[3],
        matrices[4],
        matrices[5],
    )


MESH = pl.DeviceIdType.MESH
BF = jnp.bfloat16
F32 = jnp.float32
NT = (((1,), (1,)), ((), ()))
NN = (((1,), (0,)), ((), ()))
TN = (((0,), (0,)), ((), ()))
VMEM_LIMIT = 60 * 2**20


def mm(left, right, dims=NN):
    return lax.dot_general(left, right, dims, preferred_element_type=F32)


class Place:
    def __init__(self):
        self.f = lax.axis_index("fsdp")
        self.c = lax.axis_index("ctx")
        self.t = lax.axis_index("tp")
        f, c, t = self.f, self.c, self.t
        self.k = k = lax.rem(f, 2)
        self.y = y = f // 2
        self.p = t + k * (3 - 2 * t)
        self.core = (f + 1 - 2 * k, c, t)
        self.xnbr = (f, 1 - c, t)
        self.ynbr = (lax.rem(f + 2, 4), c, t)
        self.zplus = (f, c, t + 1 - 2 * k)
        self.zminus = (f, c, t - 1 + 2 * k)
        self.own_core = t // 2
        self.own_slot = t + (t // 2) * (3 - 2 * t)
        self.pair = 2 * y
        self.other = 2 - 2 * y

    def swap(self, s):
        return (2 * self.y + self.c, self.k, s)

    def swap_is_self(self, s):
        return jnp.logical_and(self.k == self.c, self.t == s)


def copy_to(src, dst, send, recv, device):
    return pltpu.make_async_remote_copy(
        src_ref=src, dst_ref=dst, send_sem=send, recv_sem=recv, device_id=device, device_id_type=MESH
    )


def greet(at, between=lambda: None):
    barrier = pltpu.get_barrier_semaphore()
    sizes = [lax.axis_size(a) for a in ("fsdp", "ctx", "tp")]
    others = 0
    for i in range(sizes[0]):
        for j in range(sizes[1]):
            for m in range(sizes[2]):
                if i or j or m:
                    others += 1
                    device = (
                        lax.rem(at.f + i, sizes[0]),
                        lax.rem(at.c + j, sizes[1]),
                        lax.rem(at.t + m, sizes[2]),
                    )
                    pl.semaphore_signal(barrier, inc=1, device_id=device, device_id_type=MESH)
    between()
    pl.semaphore_wait(barrier, others)


class Gather:
    def __init__(self, at, shards, full, send, recv, tall):
        self.at, self.shards, self.full, self.send, self.recv, self.tall = at, shards, full, send, recv, tall

    def own(self, g):
        at, full, shard = self.at, self.full[g], self.shards[g]
        half = shard.shape[0] // 2
        rows = pl.ds(pl.multiple_of(at.c * half, half), half)

        @pl.when(at.k == at.own_core)
        def _():
            full[at.own_slot, at.f, at.c] = shard[rows, :]

        @pl.when(at.k != at.own_core)
        def _():
            self.cp(g, at.own_slot, 0, shard.at[rows], full.at[at.own_slot, at.f, at.c], at.core).start()

    def cp(self, g, slot, kind, src, dst, device):
        return copy_to(src, dst, self.send.at[g, slot, kind], self.recv.at[g, slot, kind], device)

    def arrives(self, g, slot, kind, dst):
        self.cp(g, slot, kind, dst, dst, self.at.core).wait_recv()

    def ours(self, g, slot, f, c):
        return self.full[g].at[slot, pl.ds(f, 2), c]

    def step_z(self, g, turn):
        at, full = self.at, self.full[g]
        first = (at.p + 2) // 3
        slot = first if turn == 0 else 1 - first
        piece = self.ours(g, slot, at.pair, at.c)

        @pl.when(at.p == slot)
        def _():
            self.arrives(g, slot, 0, full.at[slot, at.core[0], at.c])

        @pl.when(at.p > slot)
        def _():
            self.arrives(g, slot, 1, piece)

        @pl.when(at.p < slot)
        def _():
            self.arrives(g, slot, 2, piece)

        @pl.when(jnp.logical_and(at.p >= slot, at.p < 3))
        def _():
            self.cp(g, slot, 1, piece, piece, at.zplus).start()

        @pl.when(jnp.logical_and(at.p == 1, slot == 1))
        def _():
            self.cp(g, slot, 2, piece, piece, at.zminus).start()

        for copy in self.ahead(g, slot):
            copy.start()

    def ahead(self, g, slot):
        at, full = self.at, self.full[g]
        if g in self.tall:
            piece = self.ours(g, slot, at.pair, at.c)
            return self.cp(g, slot, 4, piece, piece, at.xnbr), self.cp(g, slot, 3, piece, piece, at.ynbr)
        even, odd = full.at[slot, at.pair, at.c], full.at[slot, at.pair + 1, at.c]
        return self.cp(g, slot, 3, even, even, at.ynbr), self.cp(g, slot, 4, odd, odd, at.xnbr)

    def direct(self, g, slot):
        at, full = self.at, self.full[g]
        if g in self.tall:
            return ()
        even, odd = full.at[slot, at.pair, at.c], full.at[slot, at.pair + 1, at.c]
        return self.cp(g, slot, 7, even, even, at.xnbr), self.cp(g, slot, 8, odd, odd, at.ynbr)

    def relays(self, g, slot):
        at, full = self.at, self.full[g]
        if g in self.tall:
            piece = self.ours(g, slot, at.pair, 1 - at.c)
            return (self.cp(g, slot, 6, piece, piece, at.ynbr),)
        even = full.at[slot, at.other, at.c]
        odd = full.at[slot, at.pair + 1, 1 - at.c]
        return self.cp(g, slot, 6, odd, odd, at.ynbr), self.cp(g, slot, 5, even, even, at.xnbr)

    def step_relay(self, g, turn):
        at = self.at
        first = (at.p + 2) // 3
        slot = first if turn == 0 else 1 - first
        copies = self.relays(g, slot)
        full = self.full[g]
        if g in self.tall:
            self.arrives(g, slot, 4, self.ours(g, slot, at.pair, 1 - at.c))
            copies[0].start()
            return
        self.arrives(g, slot, 4, full.at[slot, at.pair + 1, 1 - at.c])
        copies[0].start()
        self.arrives(g, slot, 3, full.at[slot, at.other, at.c])
        copies[1].start()
        for copy in self.direct(g, slot):
            copy.start()

    def step_last(self, g):
        at, full = self.at, self.full[g]
        for slot in range(2):
            if g in self.tall:
                self.arrives(g, slot, 3, self.ours(g, slot, at.other, at.c))
                self.arrives(g, slot, 6, self.ours(g, slot, at.other, 1 - at.c))
            else:
                self.arrives(g, slot, 5, full.at[slot, at.other, 1 - at.c])
                self.arrives(g, slot, 6, full.at[slot, at.other + 1, 1 - at.c])
                self.arrives(g, slot, 7, full.at[slot, at.pair, 1 - at.c])
                self.arrives(g, slot, 8, full.at[slot, at.other + 1, at.c])

    def sent(self, g):
        at, full = self.at, self.full[g]

        def left(slot, kind, src):
            self.cp(g, slot, kind, src, src, at.core).wait_send()

        @pl.when(at.k != at.own_core)
        def _():
            left(at.own_slot, 0, full.at[at.own_slot, at.f, at.c])

        for slot in range(2):
            piece = self.ours(g, slot, at.pair, at.c)

            @pl.when(jnp.logical_and(at.p >= slot, at.p < 3))
            def _():
                left(slot, 1, piece)

            if slot == 1:

                @pl.when(at.p == 1)
                def _():
                    left(slot, 2, piece)

            for copy in (*self.ahead(g, slot), *self.direct(g, slot), *self.relays(g, slot)):
                copy.wait_send()


class Swap:
    def __init__(self, at, blocks, rows, base, send, recv):
        self.at, self.blocks, self.rows, self.base, self.send, self.recv = at, blocks, rows, base, send, recv
        self.n = blocks.shape[1]

    def span(self, s, base):
        return pl.ds(pl.multiple_of(base + s * self.n, self.n), self.n)

    def start_in(self):
        at = self.at
        there = self.rows.at[self.span(at.t, self.base * at.c)]
        for s in range(4):

            @pl.when(at.swap_is_self(s))
            def _():
                here = self.rows.at[self.span(s, self.base * at.k)]
                pltpu.make_async_copy(self.blocks.at[s], here, self.recv.at[s]).start()

            @pl.when(jnp.logical_not(at.swap_is_self(s)))
            def _():
                copy_to(self.blocks.at[s], there, self.send.at[s], self.recv.at[at.t], at.swap(s)).start()

    def wait_in(self, s):
        at = self.at
        here = self.rows.at[self.span(s, self.base * at.k)]

        @pl.when(jnp.logical_not(at.swap_is_self(s)))
        def _():
            copy_to(here, here, self.send.at[s], self.recv.at[s], at.core).wait_recv()

        @pl.when(at.swap_is_self(s))
        def _():
            pltpu.make_async_copy(self.blocks.at[s], here, self.recv.at[s]).wait()

    def start_out(self, s):
        at = self.at
        here = self.rows.at[self.span(s, self.base * at.k)]

        @pl.when(at.swap_is_self(s))
        def _():
            pltpu.make_async_copy(here, self.blocks.at[s], self.send.at[s]).start()

        @pl.when(jnp.logical_not(at.swap_is_self(s)))
        def _():
            copy_to(here, self.blocks.at[at.t], self.send.at[s], self.recv.at[at.t], at.swap(s)).start()

    def wait_out(self, s):
        at = self.at

        @pl.when(jnp.logical_not(at.swap_is_self(s)))
        def _():
            copy_to(self.blocks.at[s], self.blocks.at[s], self.send.at[s], self.recv.at[s], at.core).wait_recv()

    def sent(self, outward=False):
        at = self.at
        for s in range(4):

            @pl.when(jnp.logical_not(at.swap_is_self(s)))
            def _():
                here = self.rows.at[self.span(s, self.base * at.k)] if outward else self.blocks.at[s]
                copy_to(here, here, self.send.at[s], self.recv.at[s], at.core).wait_send()

            if outward:

                @pl.when(at.swap_is_self(s))
                def _():
                    here = self.rows.at[self.span(s, self.base * at.k)]
                    pltpu.make_async_copy(here, self.blocks.at[s], self.send.at[s]).wait()
ROWS = 256


def norm_stats(value):
    mean = jnp.mean(value, axis=-1, keepdims=True)
    centred = value - mean
    inverse = lax.rsqrt(jnp.mean(centred * centred, axis=-1, keepdims=True) + EPS)
    return centred * inverse, inverse


def gelu_both(value):
    share = 0.5 + 0.5 * lax.erf(value * 0.7071067811865476)
    density = jnp.exp(value * value * -0.5) * 0.3989422804014327
    return value * share, share + value * density


def row_sum(value):
    return jnp.sum(value, axis=0, keepdims=True)


class Cores:
    def __init__(self, at, out, back, send, recv, row_send, row_recv):
        self.at, self.out, self.back = at, out, back
        self.send, self.recv, self.row_send, self.row_recv = send, recv, row_send, row_recv

    def rows(self, half, i):
        return pl.ds(pl.multiple_of(half * 512 + i * ROWS, ROWS), ROWS)

    def part(self, stage, i):
        return copy_to(self.out.at[i], self.back.at[i], self.send.at[stage, i], self.recv.at[stage, i], self.at.core)

    def reduce(self, stage, partial, finish, between=lambda: None):
        at = self.at

        @pl.loop(0, 512 // ROWS)
        def _(i):
            self.out[i] = partial(self.rows(1 - at.k, i))
            self.part(stage, i).start()

        between()

        @pl.loop(0, 512 // ROWS)
        def _(i):
            total = partial(self.rows(at.k, i))
            self.part(stage, i).wait_recv()
            finish(i, self.rows(at.k, i), total + self.back[i])

        @pl.loop(0, 512 // ROWS)
        def _(i):
            self.part(stage, i).wait_send()

    def row(self, stage, ref, half, i):
        rows = ref.at[self.rows(half, i)]
        return copy_to(rows, rows, self.row_send.at[stage, i], self.row_recv.at[stage, i], self.at.core)

    def over_rows(self, stage, ref, work):
        at = self.at

        @pl.loop(0, 512 // ROWS)
        def _(i):
            work(self.rows(at.k, i))

        @pl.loop(0, 512 // ROWS)
        def _(i):
            self.row(stage, ref, 1 - at.k, i).wait_recv()
            work(self.rows(1 - at.k, i))

        @pl.loop(0, 512 // ROWS)
        def _(i):
            self.row(stage, ref, at.k, i).wait_send()


def flip(dst, src):
    @pl.loop(0, src.shape[0] // ROWS)
    def _(r):
        rows = pl.ds(pl.multiple_of(r * ROWS, ROWS), ROWS)
        dst[:, rows] = src[rows, :].T


def product(dst, slot, flipped, right):
    n = dst.shape[2] * dst.shape[3]

    @pl.loop(0, dst.shape[1])
    def _(r):
        rows = pl.ds(pl.multiple_of(r * n, n), n)
        got = mm(flipped[rows, :], right())
        dst[slot, r] = got.astype(BF).reshape(dst.shape[2:])


def vmem():
    return pl.BlockSpec(memory_space=pltpu.VMEM)


QCHUNK = 512


def attend_chunk(h, q, key, query, value_t, bias, lse, mixed_t):
    cols = pl.ds(pl.multiple_of(q * QCHUNK, QCHUNK), QCHUNK)
    scores = mm(key[h], query[h, cols, :], NT)
    length = scores.shape[0]
    scores = (
        scores.reshape(length // BLK, BLK, QCHUNK) + bias[h, :, cols][:, None, :]
    ).reshape(length, QCHUNK)
    top = jnp.max(scores, axis=0, keepdims=True)
    weights = jnp.exp(scores - top)
    total = jnp.sum(weights, axis=0, keepdims=True)
    probs = (weights * (1.0 / total)).astype(BF)
    lse[h, :, cols] = top + jnp.log(total)
    mixed_t[:, cols] = mm(value_t[...], probs).astype(BF)


class Vectors:
    def __init__(self, at, own, vec, near, ids, picked, sems):
        self.at, self.own, self.vec, self.near, self.ids, self.picked = at, own, vec, near, ids, picked
        self.send, self.recv = sems

    def fill(self, out_bias, norm_gain, norm_bias, up_bias, qv_bias, rand):
        at = self.at
        size = out_bias.shape[1]
        for i, ref in enumerate((out_bias, norm_gain, norm_bias)):
            self.vec[at.f, 2 * i : 2 * i + 2, 0:size] = ref[...]
        self.own[0:1, 0:size] = up_bias[...]
        self.own[1:3, 0 : qv_bias.shape[1]] = qv_bias[...]
        for h in range(3):
            for r in range(3):
                self.ids[:, 3 * h + r, 0 : rand.shape[3]] = rand[h, r].astype(F32)

        @pl.when(at.k == at.own_core)
        def _():
            self.near[at.own_slot, at.f] = self.own[...]

            @pl.when(at.k == at.c)
            def _():
                self.picked[at.own_slot] = self.ids[at.t]

    def copies(self):
        at = self.at
        out = []
        box = self.vec.at[at.f]
        for i, f in enumerate((at.core[0], at.ynbr[0], lax.rem(at.core[0] + 2, 4))):
            out.append((None, copy_to(box, box, self.send.at[i], self.recv.at[at.f], (f, at.c, at.t))))
        for y in range(2):
            for t in range(4):
                f = 2 * y + at.own_core
                copy = copy_to(
                    self.own,
                    self.near.at[at.own_slot, at.f],
                    self.send.at[3 + 4 * y + t],
                    self.recv.at[4 + 4 * at.own_slot + at.f],
                    (f, at.c, t),
                )
                out.append((jnp.logical_or(f != at.f, t != at.t), copy))
        for s in range(4):
            f = at.pair + at.own_core
            copy = copy_to(
                self.ids.at[s],
                self.picked.at[at.own_slot],
                self.send.at[11 + s],
                self.recv.at[12 + at.own_slot],
                (f, at.k, s),
            )
            away = jnp.logical_or(f != at.f, s != at.t)
            out.append((jnp.logical_and(at.c == at.k, away), copy))
        return out

    def each(self, act):
        for condition, copy in self.copies():
            if condition is None:
                act(copy)
            else:
                pl.when(condition)(lambda copy=copy: act(copy))

    def start(self):
        self.each(lambda copy: copy.start())

    def sent(self):
        self.each(lambda copy: copy.wait_send())

    def wait(self):
        at = self.at

        def arrives(index, dst):
            copy_to(dst, dst, self.send.at[0], self.recv.at[index], at.core).wait_recv()

        for i in range(1, 4):
            f = lax.rem(at.f + i, 4)
            arrives(f, self.vec.at[f])
        for slot in range(2):
            ours = jnp.logical_and(at.k == at.own_core, slot == at.own_slot)
            for f in range(4):

                @pl.when(jnp.logical_not(jnp.logical_and(ours, f == at.f)))
                def _():
                    arrives(4 + 4 * slot + f, self.near.at[slot, f])

            @pl.when(jnp.logical_not(jnp.logical_and(ours, at.k == at.c)))
            def _():
                arrives(12 + slot, self.picked.at[slot])

    def unpack(self, vec_out, ups, proj_bias, row, bias):
        size = vec_out.shape[1] // 4
        low = lambda a: a.astype(BF).astype(F32)
        part = size // 4
        for f in range(4):
            vec_out[:, size * f : size * (f + 1)] = low(self.vec[f, :, 0:size])
        proj_bias[...] = jnp.zeros_like(proj_bias)
        for slot in range(2):
            for f in range(4):
                ups[slot : slot + 1, size * f : size * (f + 1)] = low(self.near[slot, f, 0:1, 0:size])
                row[slot, 0:2, part * f : part * (f + 1)] = low(self.near[slot, f, 1:3, 0:part])
            for i in range(3):
                start = i * size
                proj_bias[slot, :, start : start + 64] = row[slot, 0:1, 64 * i : 64 * i + 64]
                proj_bias[slot, :, start + 128 : start + 192] = row[slot, 1:2, 64 * i : 64 * i + 64]
        blocks, length = bias.shape[1], bias.shape[2]
        spot = lax.broadcasted_iota(jnp.int32, (blocks, length), 0)
        block = lax.broadcasted_iota(jnp.int32, (blocks, length), 1) // BLK
        number = lambda mask: jnp.where(mask, 1.0, 0.0)
        fixed = number(jnp.abs(spot - block) <= 1) + number(spot == 0) + number(spot == blocks - 1)
        edge = jnp.logical_or(block == 0, block == blocks - 1)
        spread_out = number(spot == block).astype(BF)
        here = spot.astype(F32)
        for slot in range(2):
            ids = mm(self.picked[slot, :, 0:blocks].astype(BF), spread_out)
            for i in range(3):
                counts = fixed
                for r in range(3):
                    counts = counts + number(ids[3 * i + r : 3 * i + r + 1, :] == here)
                counts = jnp.where(edge, 1.0, counts)
                bias[3 * slot + i] = jnp.where(counts > 0.5, jnp.log(jnp.maximum(counts, 1.0)), -1e30)


class Reduce:
    def __init__(self, at, grads, work, plane, zline, final, send, recv):
        self.at, self.grads, self.work, self.plane, self.zline, self.final = at, grads, work, plane, zline, final
        self.send, self.recv = send, recv

    def cp(self, g, slot, kind, src, dst, device, recv_kind=None):
        recv_kind = kind if recv_kind is None else recv_kind
        return copy_to(src, dst, self.send.at[g, slot, kind], self.recv.at[g, slot, recv_kind], device)

    def arrives(self, g, slot, kind, dst):
        self.cp(g, slot, kind, dst, dst, self.at.core).wait_recv()

    def plane_sends(self, g, slot):
        at, grad, box = self.at, self.grads[g], self.plane[g].at[slot]
        return (
            self.cp(g, slot, 1, grad.at[slot, at.other, 1 - at.c], box.at[1], at.xnbr),
            self.cp(g, slot, 3, grad.at[slot, at.other + 1, 1 - at.c], box.at[3], at.ynbr),
            self.cp(g, slot, 0, grad.at[slot, at.pair, 1 - at.c], box.at[0], at.xnbr),
            self.cp(g, slot, 2, grad.at[slot, at.other + 1, at.c], box.at[2], at.ynbr),
        )

    def sums(self, g, slot):
        at, work, box = self.at, self.work[g].at[slot], self.plane[g].at[slot]
        return (
            self.cp(g, slot, 4, work.at[0], box.at[4], at.ynbr),
            self.cp(g, slot, 5, work.at[1], box.at[5], at.xnbr),
        )

    def plane0(self, g, slot):
        for copy in self.plane_sends(g, slot)[:2]:
            copy.start()

    def total(self, g, slot, i, piece, boxes):
        came = sum(self.plane[g][slot, b].astype(F32) for b in boxes)
        own = self.grads[g][slot, piece[0], piece[1]].astype(F32)
        self.work[g][slot, i] = (own + came).astype(BF)

    def plane1(self, g, slot):
        at = self.at
        copies = self.sums(g, slot)
        for i, kind, piece in ((0, 1, (at.other, at.c)), (1, 3, (at.pair + 1, 1 - at.c))):
            self.arrives(g, slot, kind, self.plane[g].at[slot, kind])
            self.total(g, slot, i, piece, (kind,))
            copies[i].start()
        for copy in self.plane_sends(g, slot)[2:]:
            copy.start()

    def ours(self, g, slot):
        return self.work[g].at[slot, pl.ds(2, 2)]

    def down(self, g, slot):
        return self.cp(g, slot, 6, self.ours(g, slot), self.zline[g].at[slot], self.at.zminus)

    def upward(self, g, slot):
        return self.cp(g, slot, 7, self.ours(g, slot), self.zline[g].at[2], self.at.zplus)

    def plane2(self, g, slot):
        at = self.at
        for kind in (0, 2, 4, 5):
            self.arrives(g, slot, kind, self.plane[g].at[slot, kind])
        boxes = ((0, 4), (2, 5))
        for i in range(2):
            self.total(g, slot, 2 + i, (at.pair + i, at.c), boxes[i])

        @pl.when(at.p == 3)
        def _():
            self.down(g, slot).start()

        if slot == 1:

            @pl.when(at.p == 0)
            def _():
                self.upward(g, slot).start()

    def add_line(self, g, slot, which):
        box = 2 if which else slot
        self.arrives(g, slot, 6 + which, self.zline[g].at[box])
        for i in range(2):
            self.work[g][slot, 2 + i] = (
                self.work[g][slot, 2 + i].astype(F32) + self.zline[g][box, i].astype(F32)
            ).astype(BF)

    def line(self, g, slot, place):
        at = self.at
        if place < slot:
            return

        @pl.when(at.p == place)
        def _():
            self.add_line(g, slot, 0)
            if slot == 1 and place == 1:
                self.add_line(g, slot, 1)
            if place > slot:
                self.down(g, slot).start()
            else:
                self.hand_out(g, slot)

    def hands(self, g, slot):
        at, final = self.at, self.final[g]
        mine = self.work[g].at[slot, 2 + at.k]
        theirs = self.work[g].at[slot, 3 - at.k]
        there = final.at[self.half(g, at.c)]
        return (
            self.cp(g, slot, 8, theirs, there, at.core, 8),
            self.cp(g, slot, 9, mine, there, at.xnbr, 9),
            self.cp(g, slot, 10, theirs, there, (at.core[0], 1 - at.c, at.t), 9),
        )

    def half(self, g, c):
        n = self.final[g].shape[0] // 2
        return pl.ds(pl.multiple_of(c * n, n), n)

    def hand_out(self, g, slot):
        at = self.at
        for copy in self.hands(g, slot):
            copy.start()
        self.final[g][self.half(g, at.c), :] = self.work[g][slot, 2 + at.k]

    def finish(self, g):
        at, final = self.at, self.final[g]

        @pl.when(at.k != at.own_core)
        def _():
            self.arrives(g, at.own_slot, 8, final.at[self.half(g, at.c)])

        self.arrives(g, at.own_slot, 9, final.at[self.half(g, 1 - at.c)])
        return final[...].astype(F32)

    def sent(self, g):
        at = self.at
        for slot in range(2):
            for copy in (*self.plane_sends(g, slot), *self.sums(g, slot)):
                copy.wait_send()

            @pl.when(at.p > slot)
            def _():
                self.down(g, slot).wait_send()

            if slot == 1:

                @pl.when(at.p == 0)
                def _():
                    self.upward(g, slot).wait_send()

            @pl.when(at.p == slot)
            def _():
                for copy in self.hands(g, slot):
                    copy.wait_send()


def attend_back_chunk(h, q, key, query, value, key_t, bias, lse, upper, key_sum, value_sum, query_t):
    cols = pl.ds(pl.multiple_of(q * QCHUNK, QCHUNK), QCHUNK)
    some = query[h, cols, :]
    upper = upper(cols)
    scores = mm(key[h], some, NT)
    length = scores.shape[0]
    shift = bias[h, :, cols] - lse[h, :, cols]
    scores = (scores.reshape(length // BLK, BLK, QCHUNK) + shift[:, None, :]).reshape(length, QCHUNK)
    probs = jnp.exp(scores)
    probs_grad = mm(value[h], upper, NT)
    inner = jnp.sum(probs * probs_grad, axis=0, keepdims=True)
    scores_grad = (probs * (probs_grad - inner)).astype(BF)
    value_sum[...] += mm(probs.astype(BF), upper)
    key_sum[...] += mm(scores_grad, some)
    query_t[:, cols] = mm(key_t[...], scores_grad)


def layer_kernel(
    xs, cs, w_in, w_out, w_up, w_down, out_bias, norm_gain, norm_bias, up_bias, qv_bias, rand,
    layer_blocks, grad_blocks, g_in, g_qv, g_out, g_outs, g_gains, g_shifts, g_up, g_ups, g_down,
    x_all, up_half, low0, low1, low2, query, key, value, mixed, lse, bias, vectors, ups,
    own, vec, near, ids, picked, proj_bias, bias_row,
    grad0, grad_out, part_out, part_back, rows_f32, normed_one, inverse_one, first_b, second_b,
    act, slope, flipped, grad_rows, key_t, key_sum, value_sum, query_t,
    work, plane, zline, final0, final1, final2, small, small_out, sum_out, sum_in,
    xs_send, xs_recv, xc_send, xc_recv, cs_send, cs_recv, p_send, p_recv, v_send, v_recv,
    lo_send, lo_recv, gi_send, gi_recv, w_send, w_recv, send, recv, row_send, row_recv, small_send, small_recv,
):
    at = Place()
    letters = Vectors(at, own, vec, near, ids, picked, (v_send, v_recv))
    finals = (final0, final1, final2)
    wide = w_in.shape[2]

    def pack():
        for h in range(3):
            final0[:, h * wide : (h + 1) * wide] = w_in[h].astype(BF)
        final0[:, 3 * wide : 4 * wide] = w_out[...].T.astype(BF)
        final1[...] = w_up[...].astype(BF)
        final2[...] = w_down[...].astype(BF)
        own[...] = jnp.zeros_like(own)
        ids[...] = jnp.zeros_like(ids)
        vec[at.f] = jnp.zeros(vec.shape[1:], F32)
        letters.fill(out_bias, norm_gain, norm_bias, up_bias, qv_bias, rand)

    greet(at, pack)
    gather = Gather(at, finals, (low0, low1, low2), p_send, p_recv, tall=(1,))
    tokens = Swap(at, xs, x_all, 512, xs_send, xs_recv)
    upstreams = Swap(at, cs, up_half, 0, cs_send, cs_recv)
    part = xs.shape[1]
    width = x_all.shape[1]
    letters.start()
    for g in range(3):
        gather.own(g)
    gather.step_z(0, 0)
    gather.step_z(0, 1)
    tokens.start_in()
    gather.step_relay(0, 0)
    gather.step_relay(0, 1)

    def to_core(s, half):
        rows = x_all.at[pl.ds(pl.multiple_of(half * 512 + s * part, part), part)]
        return copy_to(rows, rows, xc_send.at[s], xc_recv.at[s], at.core)

    for s in range(4):
        tokens.wait_in(s)
        to_core(s, at.k).start()
    gather.step_z(1, 0)
    gather.step_z(1, 1)
    letters.wait()
    letters.unpack(vectors, ups, proj_bias, bias_row, bias)
    small[...] = jnp.zeros_like(small)
    for s in range(4):
        to_core(s, 1 - at.k).wait_recv()
    gather.step_last(0)

    dim = query.shape[2]
    for slot in range(2):

        @pl.loop(0, 4)
        def _(r):
            rows = pl.ds(pl.multiple_of(r * 256, 256), 256)
            weight = low0[slot, :, :, :, 0:640].reshape(width, 640)
            got = mm(x_all[rows, :], weight) + proj_bias[slot]
            for i in range(3):
                h = slot * 3 + i
                start = i * 3 * dim
                query[h, rows, :] = (got[:, start : start + dim] * dim**-0.5).astype(BF)
                key[h, rows, :] = got[:, start + dim : start + 2 * dim].astype(BF)
                one = got[:, start + 2 * dim : start + 3 * dim]
                value[h, rows, :] = one.astype(BF)
                flipped[384 + h * dim : 384 + (h + 1) * dim, rows] = one.T.astype(BF)

        if slot == 0:
            gather.step_z(2, 0)
            gather.step_z(2, 1)
    gather.step_relay(1, 0)
    gather.step_relay(1, 1)

    def attend_forward(low_head, high_head):
        @pl.loop(low_head, high_head)
        def _(h):
            @pl.loop(0, 1024 // QCHUNK)
            def _(q):
                spot = pl.ds(pl.multiple_of(h * dim, dim), dim)
                value_t = flipped.at[pl.ds(pl.multiple_of(384 + h * dim, dim), dim)]
                attend_chunk(h, q, key, query, value_t, bias, lse, flipped.at[spot])

    attend_forward(0, 3)
    gather.step_relay(2, 0)
    gather.step_relay(2, 1)
    upstreams.start_in()
    attend_forward(3, 6)

    @pl.loop(0, 4)
    def _(r):
        rows = pl.ds(pl.multiple_of(r * 256, 256), 256)
        blank = jnp.zeros((dim, 256), BF)
        for slot in range(2):
            heads = jnp.concatenate([blank, flipped[slot * 192 : slot * 192 + 192, rows]], axis=0)
            mixed[rows, slot * 256 : slot * 256 + 256] = heads.T

    layer = Swap(at, layer_blocks, up_half, 0, lo_send, lo_recv)
    inputs = Swap(at, grad_blocks, grad_rows, 0, gi_send, gi_recv)
    low_half, high_half = pl.ds(0, width // 2), pl.ds(width // 2, width // 2)
    views = lambda ref, *dims: (ref.at[0, *dims, low_half], ref.at[1], ref.at[2], ref.at[0, *dims, high_half])
    every = lambda ref: [pl.ds(0, n) for n in ref.shape[1:-1]]
    reduce = Reduce(
        at,
        (grad0.at[..., low_half], low1, low2, grad0.at[..., high_half]),
        *(views(ref, *every(ref)) for ref in (work, plane, zline)),
        (final0.at[:, low_half], final1, final2, final0.at[:, high_half]),
        w_send,
        w_recv,
    )
    cores = Cores(at, part_out, part_back, send, recv, row_send, row_recv)
    square = lambda full, slot: full[slot].reshape(width, width)
    out_part = lambda slot: low0[slot, :, :, :, 512:768].reshape(width, 256)
    local = lambda i: pl.ds(pl.multiple_of(i * ROWS, ROWS), ROWS)

    def tally(row, value):
        small[row : row + 1, :] += row_sum(value)

    def branch_part(rows):
        return mm(mixed[rows, 0:256], out_part(0), NT) + mm(mixed[rows, 256:512], out_part(1), NT)

    def branch_done(i, rows, total):
        normed, inverse = norm_stats(x_all[rows, :].astype(F32) + (total + vectors[0:1, :]))
        value = normed * vectors[2:3, :] + vectors[4:5, :]
        normed_one[local(i), :] = normed
        inverse_one[local(i), :] = inverse
        rows_f32[local(i), :] = value
        first_b[rows, :] = value.astype(BF)
        cores.row(0, first_b, at.k, i).start()

    cores.reduce(0, branch_part, branch_done)

    def up(rows):
        for slot in range(2):
            inner = mm(first_b[rows, :], square(low1, slot)) + ups[slot : slot + 1, :]
            value, slope_value = gelu_both(inner)
            act[slot, rows, :] = value.astype(BF)
            slope[slot, rows, :] = slope_value.astype(BF)

    gather.sent(0)
    gather.step_last(1)
    gather.sent(1)
    cores.over_rows(0, first_b, up)
    gather.step_last(2)
    gather.sent(2)
    for s in range(4):
        upstreams.wait_in(s)

    def second_part(rows):
        return mm(act[0, rows, :], square(low2, 0), NT) + mm(act[1, rows, :], square(low2, 1), NT)

    def second_done(i, rows, total):
        normed, inverse = norm_stats(rows_f32[local(i), :] + (total + vectors[1:2, :]))
        layer_row = (normed * vectors[3:4, :] + vectors[5:6, :]).astype(BF)
        upstream = up_half[local(i), :].astype(F32)
        up_half[local(i), :] = layer_row
        scaled = upstream * vectors[3:4, :]
        grad = inverse * (
            scaled
            - jnp.mean(scaled, axis=-1, keepdims=True)
            - normed * jnp.mean(scaled * normed, axis=-1, keepdims=True)
        )
        rows_f32[local(i), :] = grad
        low = grad.astype(BF)
        second_b[rows, :] = low
        cores.row(1, second_b, at.k, i).start()
        tally(1, low.astype(F32))
        tally(3, upstream * normed)
        tally(5, upstream)

    cores.reduce(1, second_part, second_done)
    for s in range(4):
        layer.start_out(s)

    def down(rows):
        for slot in range(2):
            grad = mm(second_b[rows, :], square(low2, slot)) * slope[slot, rows, :].astype(F32)
            low = grad.astype(BF)
            slope[slot, rows, :] = low
            tally(6 + slot, low.astype(F32))

    cores.over_rows(1, second_b, down)
    flip(flipped, second_b)
    for slot in range(2):
        product(low2, slot, flipped, lambda: act[slot])
        reduce.plane0(2, slot)

    def first_part(rows):
        return mm(slope[0, rows, :], square(low1, 0), NT) + mm(slope[1, rows, :], square(low1, 1), NT)

    def first_done(i, rows, total):
        grad = total + rows_f32[local(i), :]
        normed = normed_one[local(i), :]
        tally(2, grad * normed)
        tally(4, grad)
        scaled = grad * vectors[2:3, :]
        back = inverse_one[local(i), :] * (
            scaled
            - jnp.mean(scaled, axis=-1, keepdims=True)
            - normed * jnp.mean(scaled * normed, axis=-1, keepdims=True)
        )
        rows_f32[local(i), :] = back
        low = back.astype(BF)
        second_b[rows, :] = low
        cores.row(2, second_b, at.k, i).start()
        tally(0, low.astype(F32))

    cores.reduce(2, first_part, first_done)
    for slot in range(2):
        reduce.plane1(2, slot)
    flip(flipped, first_b)
    for slot in range(2):
        product(low1, slot, flipped, lambda: slope[slot])
        reduce.plane0(1, slot)

    mixed_grad = first_b

    def mix_back(rows):
        for slot in range(2):
            mixed_grad[rows, slot * 256 : slot * 256 + 256] = mm(second_b[rows, :], out_part(slot)).astype(BF)

    cores.over_rows(2, second_b, mix_back)
    flip(flipped, second_b)

    @pl.loop(0, 4)
    def _(r):
        rows = pl.ds(pl.multiple_of(r * 192, 192), 192)
        grad_out[rows, :] = mm(flipped[rows, :], mixed[...]).astype(BF)

    flip(flipped, x_all)
    proj_grad = act
    for slot in range(2):
        proj_grad[slot, :, 576:640] = jnp.zeros((1024, 64), BF)

    def attend(h, part):
        if part == 0:
            key_t[...] = key[h].astype(F32).T.astype(BF)
            key_sum[...] = jnp.zeros_like(key_sum)
            value_sum[...] = jnp.zeros_like(value_sum)

        @pl.loop(part * (512 // QCHUNK), (part + 1) * (512 // QCHUNK))
        def _(q):
            column = (h // 3) * 256 + (h % 3 + 1) * 64
            attend_back_chunk(
                h, q, key, query, value, key_t, bias, lse,
                lambda cols: mixed_grad[cols, column : column + 64], key_sum, value_sum, query_t,
            )

        if part == 1:
            start = (h % 3) * 192
            proj_grad[h // 3, :, start : start + 64] = (query_t[...] * 0.125).T.astype(BF)
            proj_grad[h // 3, :, start + 64 : start + 128] = key_sum[...].astype(BF)
            proj_grad[h // 3, :, start + 128 : start + 192] = value_sum[...].astype(BF)

    def in_grads(slot, g):
        @pl.loop(0, 4)
        def _(r):
            rows = pl.ds(pl.multiple_of(r * 192, 192), 192)
            if g == 0:
                got = mm(flipped[rows, :], proj_grad[slot, :, 0:384])
                grad0[slot, r, :, :, 0:384] = got.astype(BF).reshape(2, 96, 384)
            else:
                got = mm(flipped[rows, :], proj_grad[slot, :, 384:640])
                out_part = grad_out[rows, slot * 256 : slot * 256 + 256]
                grad0[slot, r, :, :, 384:512] = got[:, 0:128].astype(BF).reshape(2, 96, 128)
                shared = got[:, 128:256] + out_part[:, 0:128].astype(F32)
                grad0[slot, r, :, :, 512:640] = shared.astype(BF).reshape(2, 96, 128)
                grad0[slot, r, :, :, 640:768] = out_part[:, 128:256].reshape(2, 96, 128)

        reduce.plane0(g, slot)

    def both(step, g, *more):
        for slot in range(2):
            step(g, slot, *more)

    def halves(step, slot, *more):
        for g in (0, 3):
            step(g, slot, *more)

    attend(0, 0)
    attend(0, 1)
    both(reduce.plane2, 2)
    attend(1, 0)
    both(reduce.plane1, 1)
    attend(1, 1)
    both(reduce.line, 2, 2)
    attend(2, 0)
    both(reduce.line, 2, 1)
    attend(2, 1)
    in_grads(0, 0)
    in_grads(0, 3)
    attend(3, 0)
    both(reduce.line, 2, 0)
    attend(3, 1)
    both(reduce.plane2, 1)
    attend(4, 0)
    halves(reduce.plane1, 0)
    attend(4, 1)
    in_grads(1, 0)
    both(reduce.line, 1, 2)
    attend(5, 0)
    both(reduce.line, 1, 1)
    halves(reduce.plane2, 0)
    attend(5, 1)
    in_grads(1, 3)
    reduce.plane1(0, 1)
    both(reduce.line, 1, 0)

    t = at.t
    steps = (at.xnbr, at.ynbr, (at.f, at.c, t + 1 - 2 * lax.rem(t, 2)), (at.f, at.c, lax.rem(t + 2, 4)))
    hops = [
        copy_to(sum_out.at[i], sum_in.at[i], small_send.at[i], small_recv.at[i], device)
        for i, device in enumerate(steps)
    ]

    def small_next(i):
        hops[i].wait_recv()
        if i < 3:
            sum_out[i + 1] = sum_out[i] + sum_in[i]
            hops[i + 1].start()
        else:
            small_out[at.k] = sum_out[i] + sum_in[i]

    sum_out[0] = small[...]
    for slot in range(2):
        sum_out[0, 8 + slot : 9 + slot, 0:640] = row_sum(proj_grad[slot, :, 0:640].astype(F32))
    hops[0].start()
    halves(reduce.line, 0, 2)

    def in_part(rows):
        return sum(
            mm(proj_grad[slot, rows, 0:640], low0[slot, :, :, :, 0:640].reshape(width, 640), NT)
            for slot in range(2)
        )

    def in_done(i, rows, total):
        grad_rows[local(i), :] = (total + rows_f32[local(i), :]).astype(BF)
        for s in range(ROWS // 128):
            inputs.start_out(i * (ROWS // 128) + s)

    def between():
        small_next(0)
        reduce.plane1(3, 1)
        halves(reduce.line, 0, 1)
        reduce.plane2(0, 1)

    cores.reduce(3, in_part, in_done, between)
    small_next(1)
    reduce.line(0, 1, 2)
    halves(reduce.line, 0, 0)
    reduce.plane2(3, 1)
    small_next(2)
    reduce.line(0, 1, 1)
    reduce.line(3, 1, 2)
    small_next(3)
    mine = small_out.at[at.k]
    both_cores = copy_to(mine, mine, small_send.at[4], small_recv.at[4], at.core)
    both_cores.start()
    reduce.line(3, 1, 1)
    for copy in hops:
        copy.wait_send()
    g_down[...] = reduce.finish(2)
    g_up[...] = reduce.finish(1)
    reduce.finish(0)
    reduce.finish(3)
    got = final0[...].astype(F32)
    fr = g_up.shape[0]
    for h in range(3):
        g_in[h] = got[:, h * fr : (h + 1) * fr]
    g_out[...] = got[:, 3 * fr : 4 * fr].T
    both_cores.wait_send()
    copy_to(small_out.at[1 - at.k], small_out.at[1 - at.k], small_send.at[4], small_recv.at[4], at.core).wait_recv()
    sums = small_out[0, 0:8, :] + small_out[1, 0:8, :]
    used = small_out.at[at.own_core]
    up_row = used[pl.ds(6 + at.own_slot, 1), :]
    proj_row = used[pl.ds(8 + at.own_slot, 1), :]
    pick = lambda j: jnp.concatenate(
        [proj_row[:, i * fr + 64 * j : i * fr + 64 * j + 64] for i in range(3)], axis=1
    )
    pair_rows = jnp.concatenate([pick(0), pick(2)], axis=0)
    quarter = fr // 4
    for f in range(4):

        @pl.when(at.f == f)
        def _():
            piece = sums[:, f * fr : (f + 1) * fr]
            g_outs[...] = piece[0:2]
            g_gains[...] = piece[2:4]
            g_shifts[...] = piece[4:6]
            g_ups[...] = up_row[:, f * fr : (f + 1) * fr]
            g_qv[...] = pair_rows[:, f * quarter : (f + 1) * quarter]

    for s in range(4):
        layer.wait_out(s)
        inputs.wait_out(s)
    layer.sent(True)
    inputs.sent(True)
    for g in range(4):
        reduce.sent(g)
    letters.sent()
    tokens.sent()
    upstreams.sent()
    for s in range(4):
        to_core(s, at.k).wait_send()


def layer_call(xs, cs, w_in, w_out, w_up, w_down, out_bias, norm_gain, norm_bias, up_bias, qv_bias, rand):
    width = xs.shape[2]
    length, half = 1024, 512
    heads, dim = 6, 64
    blocks = length // BLK
    parts = half // ROWS
    fr = width // 4
    piece = (fr // 2, width)
    shape = jax.ShapeDtypeStruct
    dma = lambda *dims: pltpu.SemaphoreType.DMA(dims)
    low = lambda *dims: pltpu.VMEM(dims, BF)
    full = lambda *dims: pltpu.VMEM(dims, F32)
    anywhere = pl.BlockSpec(memory_space=pl.ANY)
    return pl.pallas_call(
        layer_kernel,
        out_shape=(
            shape(xs.shape, BF),
            shape(xs.shape, BF),
            shape((3, fr, fr), F32),
            shape((2, fr // 4), F32),
            shape((fr, fr), F32),
            shape((2, fr), F32),
            shape((2, fr), F32),
            shape((2, fr), F32),
            shape((fr, width), F32),
            shape((1, fr), F32),
            shape((fr, width), F32),
        ),
        in_specs=[anywhere] * 2 + [vmem()] * 10,
        out_specs=[anywhere] * 2 + [vmem()] * 9,
        scratch_shapes=[
            low(length, width),
            low(half, width),
            low(2, 4, 2, *piece),
            low(2, 4, 2, *piece),
            low(2, 4, 2, *piece),
            low(heads, length, dim),
            low(heads, length, dim),
            low(heads, length, dim),
            low(length, 512),
            full(heads, 1, length),
            full(heads, blocks, length),
            full(8, width),
            full(2, width),
            full(8, 256),
            full(4, 8, 256),
            full(2, 4, 8, 256),
            full(4, 16, 128),
            full(2, 16, 128),
            full(2, 1, 640),
            full(2, 8, 256),
            low(2, 4, 2, *piece),
            low(width, 512),
            full(parts, ROWS, width),
            full(parts, ROWS, width),
            full(half, width),
            full(half, width),
            full(half, 1),
            low(length, width),
            low(length, width),
            low(2, length, width),
            low(2, length, width),
            low(width, length),
            low(half, width),
            low(dim, length),
            full(length, dim),
            full(length, dim),
            full(dim, length),
            low(3, 2, 4, *piece),
            low(3, 2, 6, *piece),
            low(3, 3, 2, *piece),
            low(fr, width),
            low(fr, width),
            low(fr, width),
            full(16, width),
            full(2, 16, width),
            full(4, 16, width),
            full(4, 16, width),
            dma(4),
            dma(4),
            dma(4),
            dma(4),
            dma(4),
            dma(4),
            dma(3, 2, 9),
            dma(3, 2, 9),
            dma(15),
            dma(14),
            dma(4),
            dma(4),
            dma(4),
            dma(4),
            dma(4, 2, 11),
            dma(4, 2, 11),
            dma(4, parts),
            dma(4, parts),
            dma(3, parts),
            dma(3, parts),
            dma(5),
            dma(5),
        ],
        compiler_params=pltpu.CompilerParams(
            collective_id=1, has_side_effects=True, vmem_limit_bytes=VMEM_LIMIT
        ),
        name="layer",
    )(xs, cs, w_in, w_out, w_up, w_down, out_bias, norm_gain, norm_bias, up_bias, qv_bias, rand)


def sequence_shards(hidden_in, rand_blocks, w_in, qv_bias, w_out, out_bias, norm_gain, norm_bias, w_up, up_bias, w_down, cotangent):
    layer_blocks, grad_blocks, *grads = layer_call(
        hidden_in.transpose(1, 0, 2),
        cotangent.transpose(1, 0, 2),
        w_in.transpose(1, 0, 2),
        w_out,
        w_up,
        w_down.T,
        out_bias,
        norm_gain,
        norm_bias,
        up_bias[None],
        qv_bias,
        rand_blocks.transpose(2, 3, 0, 1),
    )
    grads[0] = grads[0].transpose(1, 0, 2)
    grads[7] = grads[7][0]
    grads[8] = grads[8].T
    return (layer_blocks.transpose(1, 0, 2), grad_blocks.transpose(1, 0, 2), *grads)


def solution(mesh):
    placed = (
        P(("ctx", "tp"), "fsdp", None),
        P("fsdp", None, "tp", None),
        P("fsdp", "tp", None),
        P(None, ("tp", "fsdp")),
        P("tp", "fsdp"),
        P(None, "fsdp"),
        P(None, "fsdp"),
        P(None, "fsdp"),
        P("fsdp", "tp"),
        P(("tp", "fsdp")),
        P("tp", "fsdp"),
        P(("ctx", "tp"), "fsdp", None),
    )
    sizes = tuple(mesh.shape[a] for a in ("fsdp", "ctx", "tp"))

    def local(*args):
        part_rows, seqs, width = args[0].shape
        rows, heads, wide = args[2].shape
        whole = sizes == (4, 2, 4) and (part_rows, seqs, width) == (128, 4, 768)
        whole = whole and (rows, heads, wide) == (192, 3, 192) and args[8].shape == (192, 768)
        return (sequence_shards if whole else span_shards)(*args)

    return jax.shard_map(
        local,
        mesh=mesh,
        in_specs=placed,
        out_specs=(
            P(("ctx", "tp"), "fsdp", None),
            P(("ctx", "tp"), "fsdp", None),
            P("fsdp", "tp", None),
            P(None, ("tp", "fsdp")),
            P("tp", "fsdp"),
            P(None, "fsdp"),
            P(None, "fsdp"),
            P(None, "fsdp"),
            P("fsdp", "tp"),
            P(("tp", "fsdp")),
            P("tp", "fsdp"),
        ),
        check_vma=False,
    )
```

```python
import jax
import jax.numpy as jnp
from jax import lax
from jax.experimental import pallas as pl
from jax.experimental.pallas import tpu as pltpu
from jax.sharding import PartitionSpec as P

BLK = 64


EPS = 1e-06
NEG = -1000000000.0


def from_root(block, axis, owner):
    block = jnp.where(lax.axis_index(axis) == owner, block, jnp.zeros_like(block))
    return lax.psum(block, axis)


def extended(array, sides, width):
    for axis, dim in sides:
        size, length = (lax.axis_size(axis), array.shape[dim])
        up = [(i, (i + 1) % size) for i in range(size - 1)]
        down = [(j, i) for i, j in up]
        last = lax.slice_in_dim(array, length - width, length, axis=dim)
        leading = lax.slice_in_dim(array, 0, width, axis=dim)
        before = lax.ppermute(last, axis, up)
        after = lax.ppermute(leading, axis, down)
        array = jnp.concatenate([before, array, after], axis=dim)
    return array


def joined_2(part, axis, combine):
    gathered = jax.tree.map(lambda a: lax.all_gather(a, axis), part)

    def take(source):
        return jax.tree.map(lambda a: lax.dynamic_index_in_dim(a, source, 0, False), gathered)

    return lax.fori_loop(
        1, lax.axis_size(axis), lambda source, state: combine(state, take(source)), take(0)
    )


def norm_forward(value, gain, shift):
    mean = jnp.mean(value, axis=-1, keepdims=True)
    centred = value - mean
    inverse = lax.rsqrt(jnp.mean(centred * centred, axis=-1, keepdims=True) + EPS)
    normed = centred * inverse
    return (normed * gain + shift, normed, inverse)


def norm_backward(upper, normed, inverse, gain):
    scaled = upper * gain
    return inverse * (
        scaled
        - jnp.mean(scaled, axis=-1, keepdims=True)
        - normed * jnp.mean(scaled * normed, axis=-1, keepdims=True)
    )


def exact_gelu(value):
    return jax.nn.gelu(value, approximate=False)


def outer_sum(left, right):
    return lax.dot_general(
        left, right, (((0,), (0,)), ((), ())), preferred_element_type=jnp.float32
    )


def rows_all(value):
    return lax.all_gather(value, "tp", axis=0, tiled=True)


def rows_sum(left, right, contract):
    return lax.psum_scatter(
        lax.dot_general(
            left, right, (((1,), (contract,)), ((), ())), preferred_element_type=jnp.float32
        ),
        "tp",
        scatter_dimension=0,
        tiled=True,
    )


def spread(piece, root):
    return from_root(piece, "ctx", root)


def stats_join(first_stats, second_stats):
    top = jnp.maximum(first_stats[0], second_stats[0])
    total = first_stats[1] * jnp.exp(first_stats[0] - top) + second_stats[1] * jnp.exp(
        second_stats[0] - top
    )
    return (top, total)


def split_groups(array, steps, group):
    return array.reshape((steps, group) + array.shape[1:])


def key_set(window_pad, global_pair, random_pairs):
    per_dev = random_pairs.shape[3]
    window = jnp.stack(
        [window_pad[:, :, offset_by : offset_by + per_dev] for offset_by in range(3)], axis=3
    )
    target_shape = global_pair.shape[:2] + (per_dev,) + global_pair.shape[2:]
    global_all = jnp.broadcast_to(global_pair[:, :, None], target_shape)
    random_all = jnp.swapaxes(random_pairs, 2, 3)
    joined = jnp.concatenate([window, global_all, random_all], axis=3)
    shape = joined.shape
    return joined.reshape(shape[0], shape[1], shape[2], shape[3] * shape[4], shape[5])


def scores_of(query, keys, mask, scale):
    head_dim = query.shape[-1]
    raw = (
        jnp.einsum(
            "shpqd,shpkd->shpqk", query, keys[..., :head_dim], preferred_element_type=jnp.float32
        )
        * scale
    )
    return jnp.where(mask, raw, NEG)


def attend_group(query, window_pad, global_pair, random_pairs, mask, scale):
    head_dim = query.shape[-1]
    keys = key_set(window_pad, global_pair, random_pairs)
    scores = scores_of(query, keys, mask, scale)
    top = jnp.max(scores, axis=-1, keepdims=True)
    weights = jnp.exp(scores - top)
    total = jnp.sum(weights, axis=-1, keepdims=True)
    probs = (weights / total).astype(jnp.bfloat16)
    mixed = jnp.einsum(
        "shpqk,shpkd->shpqd", probs, keys[..., head_dim:], preferred_element_type=jnp.float32
    )
    return (mixed.astype(jnp.bfloat16), (top + jnp.log(total))[..., 0])


def attend_back(query, window_pad, global_pair, random_pairs, mask, scale, logsum, mixed_grad):
    head_dim = query.shape[-1]
    blocksize = window_pad.shape[3]
    keys = key_set(window_pad, global_pair, random_pairs)
    scores = scores_of(query, keys, mask, scale)
    probs = jnp.exp(scores - logsum[..., None])
    probs_grad = jnp.einsum(
        "shpqd,shpkd->shpqk", mixed_grad, keys[..., head_dim:], preferred_element_type=jnp.float32
    )
    inner = jnp.sum(probs * probs_grad, axis=-1, keepdims=True)
    scores_grad = (probs * (probs_grad - inner)).astype(jnp.bfloat16)
    query_grad = (
        jnp.einsum(
            "shpqk,shpkd->shpqd",
            scores_grad,
            keys[..., :head_dim],
            preferred_element_type=jnp.float32,
        )
        * scale
    )
    keys_grad = (
        jnp.einsum("shpqk,shpqd->shpkd", scores_grad, query, preferred_element_type=jnp.float32)
        * scale
    )
    values_grad = jnp.einsum(
        "shpqk,shpqd->shpkd",
        probs.astype(jnp.bfloat16),
        mixed_grad,
        preferred_element_type=jnp.float32,
    )
    pairs_grad = jnp.concatenate([keys_grad, values_grad], axis=-1)
    shape = pairs_grad.shape
    pairs_grad = pairs_grad.reshape(
        shape[0], shape[1], shape[2], shape[3] // blocksize, blocksize, shape[4]
    )
    per_dev = shape[2]
    window_grad = jnp.zeros(window_pad.shape, jnp.float32)
    for offset_by in range(3):
        window_grad = window_grad.at[:, :, offset_by : offset_by + per_dev].add(
            pairs_grad[:, :, :, offset_by]
        )
    global_grad = jnp.sum(pairs_grad[:, :, :, 3:5], axis=2)
    random_grad = jnp.swapaxes(pairs_grad[:, :, :, 5:], 2, 3)
    return (query_grad, window_grad, global_grad, random_grad)


def span_shards(
    hidden_in,
    rand_blocks,
    w_in,
    qv_bias,
    w_out,
    out_bias,
    norm_gain,
    norm_bias,
    w_up,
    up_bias,
    w_down,
    cotangent,
):
    ctx_count = lax.axis_size("ctx")
    tp_count = lax.axis_size("tp")
    ctx_place = lax.axis_index("ctx")
    part_rows, seqs, width = hidden_in.shape
    heads = w_in.shape[1]
    head_dim = w_in.shape[2] // 3
    pair_width = 2 * head_dim
    blocks_all = rand_blocks.shape[1]
    picks = rand_blocks.shape[3]
    length = part_rows * tp_count
    per_dev = length // BLK
    total_rows = length * seqs
    scale = head_dim ** (-0.5)
    group = min(seqs, max(1, 512 // length))
    steps = seqs // group
    first_owner = ctx_place == 0
    last_owner = ctx_place == ctx_count - 1
    gathered = (
        lax.all_gather(w_in.astype(jnp.bfloat16), "fsdp", axis=0, tiled=True),
        lax.all_gather(qv_bias.astype(jnp.bfloat16), "fsdp", axis=1, tiled=True),
        lax.all_gather(w_out.astype(jnp.bfloat16), "fsdp", axis=1, tiled=True),
        lax.all_gather(out_bias.astype(jnp.bfloat16), "fsdp", axis=1, tiled=True),
        lax.all_gather(norm_gain.astype(jnp.bfloat16), "fsdp", axis=1, tiled=True),
        lax.all_gather(norm_bias.astype(jnp.bfloat16), "fsdp", axis=1, tiled=True),
        lax.all_gather(w_up.astype(jnp.bfloat16), "fsdp", axis=0, tiled=True),
        lax.all_gather(up_bias.astype(jnp.bfloat16), "fsdp", axis=0, tiled=True),
        lax.all_gather(w_down.astype(jnp.bfloat16), "fsdp", axis=1, tiled=True),
    )
    input_low = gathered[0].reshape(width, heads * 3 * head_dim)
    bias_pair = gathered[1].astype(jnp.float32).reshape(2, heads, head_dim)
    output_low = gathered[2]
    bias_out = gathered[3].astype(jnp.float32)
    gains = gathered[4].astype(jnp.float32)
    shifts = gathered[5].astype(jnp.float32)
    upper_low = gathered[6]
    bias_up = gathered[7].astype(jnp.float32)
    lower_low = gathered[8]
    x_full = rows_all(hidden_in)
    x_rows = x_full.reshape(total_rows, width)
    projected = jnp.dot(x_rows, input_low, preferred_element_type=jnp.float32).reshape(
        length, seqs, heads, 3, head_dim
    )
    query = (projected[:, :, :, 0] + bias_pair[0]).astype(jnp.bfloat16)
    key = projected[:, :, :, 1].astype(jnp.bfloat16)
    value = (projected[:, :, :, 2] + bias_pair[1]).astype(jnp.bfloat16)
    query_heads = query.transpose(1, 2, 0, 3).reshape(seqs, heads, per_dev, BLK, head_dim)
    pairs = jnp.concatenate([key, value], axis=-1).transpose(1, 2, 0, 3)
    window_pad = extended(pairs, (("ctx", 2),), BLK).reshape(
        seqs, heads, per_dev + 2, BLK, pair_width
    )
    pair_blocks = pairs.reshape(seqs, heads, per_dev, BLK, pair_width)
    triple_blocks = jnp.concatenate([query_heads, pair_blocks], axis=-1)
    global_triple = jnp.stack(
        [
            spread(triple_blocks[:, :, 0], 0),
            spread(triple_blocks[:, :, per_dev - 1], ctx_count - 1),
        ],
        axis=2,
    )
    global_query = global_triple[..., :head_dim]
    global_pair = global_triple[..., head_dim:]
    key_local = pairs[..., :head_dim]
    value_local = pairs[..., head_dim:]
    wide_scores = (
        jnp.einsum("shgqd,shkd->shgqk", global_query, key_local, preferred_element_type=jnp.float32)
        * scale
    )
    wide_top = jnp.max(wide_scores, axis=-1)
    wide_total = jnp.sum(jnp.exp(wide_scores - wide_top[..., None]), axis=-1)
    all_top, all_total = joined_2((wide_top, wide_total), "ctx", stats_join)
    wide_probs = jnp.exp(wide_scores - (all_top + jnp.log(all_total))[..., None])
    wide_probs_low = wide_probs.astype(jnp.bfloat16)
    mix_low = jnp.einsum(
        "shgqk,shkd->shgqd", wide_probs_low, value_local, preferred_element_type=jnp.float32
    )
    mix_full = jnp.einsum(
        "shgqk,shkd->shgqd",
        wide_probs,
        value_local.astype(jnp.float32),
        precision=lax.Precision.HIGHEST,
    )
    mix_low, mix_full = lax.psum((mix_low, mix_full), "ctx")
    global_mixed = mix_low.astype(jnp.bfloat16)
    units = seqs * heads * picks * per_dev
    table = rand_blocks.transpose(0, 2, 3, 1).reshape(seqs, heads, picks, ctx_count, per_dev)
    table = table.transpose(0, 1, 2, 4, 3).reshape(units, ctx_count)
    mine = lax.dynamic_index_in_dim(table, ctx_place, 1, keepdims=False)
    mine_groups = mine.reshape(steps, group, heads, picks, per_dev)
    block_index = ctx_place * per_dev + jnp.arange(per_dev)
    present = jnp.concatenate(
        [
            (block_index >= 1)[:, None],
            jnp.ones((per_dev, 1), jnp.bool_),
            (block_index <= blocks_all - 2)[:, None],
            jnp.ones((per_dev, 2 + picks), jnp.bool_),
        ],
        axis=1,
    )
    mask = jnp.repeat(present, BLK, axis=1)[None, None, :, None, :]

    def random_pairs_for(block_group, id_group):
        whole = lax.all_gather(block_group, "ctx", axis=2, tiled=True)
        chosen = jax.nn.one_hot(id_group, blocks_all, dtype=jnp.bfloat16)
        return jnp.einsum(
            "shpqb,shbke->shpqke", chosen, whole, preferred_element_type=jnp.float32
        ).astype(jnp.bfloat16)

    query_groups = split_groups(query_heads, steps, group)
    pad_groups = split_groups(window_pad, steps, group)
    global_groups = split_groups(global_pair, steps, group)
    block_groups = split_groups(pair_blocks, steps, group)

    def forward_step(items):
        position, query_group, pad_group, global_group, block_group, id_group = items
        random_group = random_pairs_for(block_group, id_group)
        return attend_group(query_group, pad_group, global_group, random_group, mask, scale)

    mixed_groups, logsum_groups = lax.map(
        forward_step,
        (jnp.arange(steps), query_groups, pad_groups, global_groups, block_groups, mine_groups),
    )
    mixed_blocks = mixed_groups.reshape(seqs, heads, per_dev, BLK, head_dim)
    mixed_blocks = mixed_blocks.at[:, :, 0].set(
        jnp.where(first_owner, global_mixed[:, :, 0], mixed_blocks[:, :, 0])
    )
    mixed_blocks = mixed_blocks.at[:, :, per_dev - 1].set(
        jnp.where(last_owner, global_mixed[:, :, 1], mixed_blocks[:, :, per_dev - 1])
    )
    mixed = (
        mixed_blocks.reshape(seqs, heads, length, head_dim)
        .transpose(2, 0, 1, 3)
        .reshape(total_rows, heads * head_dim)
    )
    branch = rows_sum(mixed, output_low, 0) + bias_out[0]
    residual_in = hidden_in.reshape(part_rows * seqs, width).astype(jnp.float32)
    first, normed_one, inverse_one = norm_forward(residual_in + branch, gains[0], shifts[0])
    first_full = rows_all(first.astype(jnp.bfloat16).reshape(part_rows, seqs, width)).reshape(
        total_rows, width
    )
    inner = jnp.dot(first_full, upper_low, preferred_element_type=jnp.float32) + bias_up
    active_value, gelu_back = jax.vjp(exact_gelu, inner)
    active = active_value.astype(jnp.bfloat16)
    second = rows_sum(active, lower_low, 0) + bias_out[1]
    result, normed_two, inverse_two = norm_forward(first + second, gains[1], shifts[1])
    layer_out = result.astype(jnp.bfloat16).reshape(part_rows, seqs, width)
    upstream = cotangent.reshape(part_rows * seqs, width).astype(jnp.float32)
    second_grad = norm_backward(upstream, normed_two, inverse_two, gains[1])
    second_low = second_grad.astype(jnp.bfloat16)
    second_full = rows_all(second_low.reshape(part_rows, seqs, width)).reshape(total_rows, width)
    active_grad = lax.dot_general(
        second_full, lower_low, (((1,), (1,)), ((), ())), preferred_element_type=jnp.float32
    )
    inner_low = gelu_back(active_grad)[0].astype(jnp.bfloat16)
    first_grad = second_grad + rows_sum(inner_low, upper_low, 1)
    residual_grad = norm_backward(first_grad, normed_one, inverse_one, gains[0])
    branch_low = residual_grad.astype(jnp.bfloat16)
    branch_full = rows_all(branch_low.reshape(part_rows, seqs, width)).reshape(total_rows, width)
    mixed_grad = lax.dot_general(
        branch_full, output_low, (((1,), (1,)), ((), ())), preferred_element_type=jnp.float32
    ).astype(jnp.bfloat16)
    mixed_heads = (
        mixed_grad.reshape(length, seqs, heads, head_dim)
        .transpose(1, 2, 0, 3)
        .reshape(seqs, heads, per_dev, BLK, head_dim)
    )
    zero_block = jnp.zeros((seqs, heads, BLK, head_dim), jnp.bfloat16)
    lead_grad = jnp.where(first_owner, mixed_heads[:, :, 0], zero_block).astype(jnp.float32)
    tail_grad = jnp.where(last_owner, mixed_heads[:, :, per_dev - 1], zero_block).astype(
        jnp.float32
    )
    lead_sum, tail_sum = (
        lax.psum(lead_grad.astype(jnp.bfloat16), "ctx").astype(jnp.float32),
        lax.psum(tail_grad.astype(jnp.bfloat16), "ctx").astype(jnp.float32),
    )
    wide_grad = jnp.stack([lead_sum, tail_sum], axis=2).astype(jnp.bfloat16)
    mixed_heads = mixed_heads.at[:, :, 0].set(
        jnp.where(first_owner, zero_block, mixed_heads[:, :, 0])
    )
    mixed_heads = mixed_heads.at[:, :, per_dev - 1].set(
        jnp.where(last_owner, zero_block, mixed_heads[:, :, per_dev - 1])
    )

    def random_back(random_grad, id_group):
        chosen = jax.nn.one_hot(id_group, blocks_all, dtype=jnp.float32)
        spread_grad = jnp.einsum(
            "shpqb,shpqke->shbke", chosen, random_grad, precision=lax.Precision.HIGHEST
        )
        return lax.psum_scatter(
            spread_grad.astype(jnp.bfloat16), "ctx", scatter_dimension=2, tiled=True
        ).astype(jnp.float32)

    def backward_step(items):
        (
            position,
            query_group,
            pad_group,
            global_group,
            block_group,
            id_group,
            logsum_group,
            grad_group,
        ) = items
        random_group = random_pairs_for(block_group, id_group)
        query_grad, window_grad, global_grad, random_grad = attend_back(
            query_group,
            pad_group,
            global_group,
            random_group,
            mask,
            scale,
            logsum_group,
            grad_group,
        )
        return (query_grad, window_grad, global_grad, random_back(random_grad, id_group))

    query_grads, window_grads, global_grads, random_total = lax.map(
        backward_step,
        (
            jnp.arange(steps),
            query_groups,
            pad_groups,
            global_groups,
            block_groups,
            mine_groups,
            logsum_groups,
            split_groups(mixed_heads, steps, group),
        ),
    )
    query_grads = query_grads.reshape(seqs, heads, length, head_dim)
    window_grads = window_grads.reshape(seqs, heads, per_dev + 2, BLK, pair_width)
    global_grads = global_grads.reshape(seqs, heads, 2, BLK, pair_width)
    wide_inner = jnp.sum(wide_grad.astype(jnp.float32) * mix_full, axis=-1, keepdims=True)
    wide_probs_grad = jnp.einsum(
        "shgqd,shkd->shgqk", wide_grad, value_local, preferred_element_type=jnp.float32
    )
    wide_scores_grad = (wide_probs * (wide_probs_grad - wide_inner)).astype(jnp.bfloat16)
    wide_query_part = (
        jnp.einsum(
            "shgqk,shkd->shgqd", wide_scores_grad, key_local, preferred_element_type=jnp.float32
        )
        * scale
    )
    wide_key_grad = (
        jnp.einsum(
            "shgqk,shgqd->shkd", wide_scores_grad, global_query, preferred_element_type=jnp.float32
        )
        * scale
    )
    wide_value_grad = jnp.einsum(
        "shgqk,shgqd->shkd", wide_probs_low, wide_grad, preferred_element_type=jnp.float32
    )
    wide_pair_grad = jnp.concatenate([wide_key_grad, wide_value_grad], axis=-1).reshape(
        seqs, heads, per_dev, BLK, pair_width
    )
    rim_pair = jnp.concatenate([window_grads[:, :, 0], window_grads[:, :, per_dev + 1]], axis=2)
    rim_back = extended(rim_pair.astype(jnp.bfloat16), (("ctx", 2),), BLK).astype(rim_pair.dtype)
    local_grad = window_grads[:, :, 1 : per_dev + 1] + wide_pair_grad
    local_grad = local_grad.at[:, :, 0].add(rim_back[:, :, :BLK])
    local_grad = local_grad.at[:, :, per_dev - 1].add(rim_back[:, :, 3 * BLK :])
    global_total, wide_query = lax.psum((global_grads, wide_query_part), "ctx")
    local_grad = local_grad.at[:, :, 0].add(jnp.where(first_owner, global_total[:, :, 0], 0.0))
    local_grad = local_grad.at[:, :, per_dev - 1].add(
        jnp.where(last_owner, global_total[:, :, 1], 0.0)
    )
    query_grads = query_grads.at[:, :, :BLK].add(jnp.where(first_owner, wide_query[:, :, 0], 0.0))
    query_grads = query_grads.at[:, :, length - BLK :].add(
        jnp.where(last_owner, wide_query[:, :, 1], 0.0)
    )
    local_grad = local_grad + random_total.reshape(seqs, heads, per_dev, BLK, pair_width)
    pair_grad = local_grad.reshape(seqs, heads, length, pair_width).transpose(2, 0, 1, 3)
    query_part = query_grads.transpose(2, 0, 1, 3)
    projected_grad = jnp.concatenate([query_part, pair_grad], axis=-1).astype(jnp.bfloat16)
    projected_rows = projected_grad.reshape(total_rows, heads * 3 * head_dim)
    grad_in = (
        (residual_grad + rows_sum(projected_rows, input_low, 1))
        .astype(jnp.bfloat16)
        .reshape(part_rows, seqs, width)
    )
    input_grad = outer_sum(x_rows, projected_rows).reshape(width, heads, 3 * head_dim)
    pair_bias_grad = jnp.stack(
        [
            jnp.sum(projected_grad[..., :head_dim], axis=(0, 1), dtype=jnp.float32).reshape(-1),
            jnp.sum(projected_grad[..., 2 * head_dim :], axis=(0, 1), dtype=jnp.float32).reshape(
                -1
            ),
        ]
    )
    output_grad = outer_sum(mixed, branch_full)
    bias_grad = jnp.stack(
        [
            jnp.sum(branch_low, axis=0, dtype=jnp.float32),
            jnp.sum(second_low, axis=0, dtype=jnp.float32),
        ]
    )
    gain_grad = jnp.stack(
        [jnp.sum(first_grad * normed_one, axis=0), jnp.sum(upstream * normed_two, axis=0)]
    )
    shift_grad = jnp.stack([jnp.sum(first_grad, axis=0), jnp.sum(upstream, axis=0)])
    upper_grad = outer_sum(first_full, inner_low)
    upper_bias_grad = jnp.sum(inner_low, axis=0, dtype=jnp.float32)
    lower_grad = outer_sum(active, second_full)
    shares = (
        lax.psum_scatter(input_grad, "fsdp", scatter_dimension=0, tiled=True),
        lax.psum_scatter(pair_bias_grad, "fsdp", scatter_dimension=1, tiled=True),
        lax.psum_scatter(output_grad, "fsdp", scatter_dimension=1, tiled=True),
        lax.psum_scatter(bias_grad, "fsdp", scatter_dimension=1, tiled=True),
        lax.psum_scatter(gain_grad, "fsdp", scatter_dimension=1, tiled=True),
        lax.psum_scatter(shift_grad, "fsdp", scatter_dimension=1, tiled=True),
        lax.psum_scatter(upper_grad, "fsdp", scatter_dimension=0, tiled=True),
        lax.psum_scatter(upper_bias_grad, "fsdp", scatter_dimension=0, tiled=True),
        lax.psum_scatter(lower_grad, "fsdp", scatter_dimension=1, tiled=True),
    )
    matrices = lax.psum((shares[0], shares[1], shares[2], shares[6], shares[7], shares[8]), "ctx")
    vectors = lax.psum((shares[3], shares[4], shares[5]), ("ctx", "tp"))
    return (
        layer_out,
        grad_in,
        matrices[0],
        matrices[1],
        matrices[2],
        vectors[0],
        vectors[1],
        vectors[2],
        matrices[3],
        matrices[4],
        matrices[5],
    )


MESH = pl.DeviceIdType.MESH
BF = jnp.bfloat16
F32 = jnp.float32
NT = (((1,), (1,)), ((), ()))
NN = (((1,), (0,)), ((), ()))
TN = (((0,), (0,)), ((), ()))
VMEM_LIMIT = 60 * 2**20


def mm(left, right, dims=NN):
    return lax.dot_general(left, right, dims, preferred_element_type=F32)


class Place:
    def __init__(self):
        self.f = lax.axis_index("fsdp")
        self.c = lax.axis_index("ctx")
        self.t = lax.axis_index("tp")
        f, c, t = self.f, self.c, self.t
        self.k = k = lax.rem(f, 2)
        self.y = y = f // 2
        self.p = t + k * (3 - 2 * t)
        self.core = (f + 1 - 2 * k, c, t)
        self.xnbr = (f, 1 - c, t)
        self.ynbr = (lax.rem(f + 2, 4), c, t)
        self.zplus = (f, c, t + 1 - 2 * k)
        self.zminus = (f, c, t - 1 + 2 * k)
        self.own_core = t // 2
        self.own_slot = t + (t // 2) * (3 - 2 * t)
        self.pair = 2 * y
        self.other = 2 - 2 * y

    def swap(self, s):
        return (2 * self.y + self.c, self.k, s)

    def swap_is_self(self, s):
        return jnp.logical_and(self.k == self.c, self.t == s)


def copy_to(src, dst, send, recv, device):
    return pltpu.make_async_remote_copy(
        src_ref=src, dst_ref=dst, send_sem=send, recv_sem=recv, device_id=device, device_id_type=MESH
    )


def greet(at, between=lambda: None):
    barrier = pltpu.get_barrier_semaphore()
    sizes = [lax.axis_size(a) for a in ("fsdp", "ctx", "tp")]
    others = 0
    for i in range(sizes[0]):
        for j in range(sizes[1]):
            for m in range(sizes[2]):
                if i or j or m:
                    others += 1
                    device = (
                        lax.rem(at.f + i, sizes[0]),
                        lax.rem(at.c + j, sizes[1]),
                        lax.rem(at.t + m, sizes[2]),
                    )
                    pl.semaphore_signal(barrier, inc=1, device_id=device, device_id_type=MESH)
    between()
    pl.semaphore_wait(barrier, others)


class Gather:
    def __init__(self, at, shards, full, send, recv, tall):
        self.at, self.shards, self.full, self.send, self.recv, self.tall = at, shards, full, send, recv, tall

    def own(self, g):
        at, full, shard = self.at, self.full[g], self.shards[g]
        half = shard.shape[0] // 2
        rows = pl.ds(pl.multiple_of(at.c * half, half), half)

        @pl.when(at.k == at.own_core)
        def _():
            full[at.own_slot, at.f, at.c] = shard[rows, :]

        @pl.when(at.k != at.own_core)
        def _():
            self.cp(g, at.own_slot, 0, shard.at[rows], full.at[at.own_slot, at.f, at.c], at.core).start()

    def cp(self, g, slot, kind, src, dst, device):
        return copy_to(src, dst, self.send.at[g, slot, kind], self.recv.at[g, slot, kind], device)

    def arrives(self, g, slot, kind, dst):
        self.cp(g, slot, kind, dst, dst, self.at.core).wait_recv()

    def ours(self, g, slot, f, c):
        return self.full[g].at[slot, pl.ds(f, 2), c]

    def step_z(self, g, turn):
        at, full = self.at, self.full[g]
        first = (at.p + 2) // 3
        slot = first if turn == 0 else 1 - first
        piece = self.ours(g, slot, at.pair, at.c)

        @pl.when(at.p == slot)
        def _():
            self.arrives(g, slot, 0, full.at[slot, at.core[0], at.c])

        @pl.when(at.p > slot)
        def _():
            self.arrives(g, slot, 1, piece)

        @pl.when(at.p < slot)
        def _():
            self.arrives(g, slot, 2, piece)

        @pl.when(jnp.logical_and(at.p >= slot, at.p < 3))
        def _():
            self.cp(g, slot, 1, piece, piece, at.zplus).start()

        @pl.when(jnp.logical_and(at.p == 1, slot == 1))
        def _():
            self.cp(g, slot, 2, piece, piece, at.zminus).start()

        for copy in self.ahead(g, slot):
            copy.start()

    def ahead(self, g, slot):
        at, full = self.at, self.full[g]
        if g in self.tall:
            piece = self.ours(g, slot, at.pair, at.c)
            return self.cp(g, slot, 4, piece, piece, at.xnbr), self.cp(g, slot, 3, piece, piece, at.ynbr)
        even, odd = full.at[slot, at.pair, at.c], full.at[slot, at.pair + 1, at.c]
        return self.cp(g, slot, 3, even, even, at.ynbr), self.cp(g, slot, 4, odd, odd, at.xnbr)

    def direct(self, g, slot):
        at, full = self.at, self.full[g]
        if g in self.tall:
            return ()
        even, odd = full.at[slot, at.pair, at.c], full.at[slot, at.pair + 1, at.c]
        return self.cp(g, slot, 7, even, even, at.xnbr), self.cp(g, slot, 8, odd, odd, at.ynbr)

    def relays(self, g, slot):
        at, full = self.at, self.full[g]
        if g in self.tall:
            piece = self.ours(g, slot, at.pair, 1 - at.c)
            return (self.cp(g, slot, 6, piece, piece, at.ynbr),)
        even = full.at[slot, at.other, at.c]
        odd = full.at[slot, at.pair + 1, 1 - at.c]
        return self.cp(g, slot, 6, odd, odd, at.ynbr), self.cp(g, slot, 5, even, even, at.xnbr)

    def step_relay(self, g, turn):
        at = self.at
        first = (at.p + 2) // 3
        slot = first if turn == 0 else 1 - first
        copies = self.relays(g, slot)
        full = self.full[g]
        if g in self.tall:
            self.arrives(g, slot, 4, self.ours(g, slot, at.pair, 1 - at.c))
            copies[0].start()
            return
        self.arrives(g, slot, 4, full.at[slot, at.pair + 1, 1 - at.c])
        copies[0].start()
        self.arrives(g, slot, 3, full.at[slot, at.other, at.c])
        copies[1].start()
        for copy in self.direct(g, slot):
            copy.start()

    def step_last(self, g):
        at, full = self.at, self.full[g]
        for slot in range(2):
            if g in self.tall:
                self.arrives(g, slot, 3, self.ours(g, slot, at.other, at.c))
                self.arrives(g, slot, 6, self.ours(g, slot, at.other, 1 - at.c))
            else:
                self.arrives(g, slot, 5, full.at[slot, at.other, 1 - at.c])
                self.arrives(g, slot, 6, full.at[slot, at.other + 1, 1 - at.c])
                self.arrives(g, slot, 7, full.at[slot, at.pair, 1 - at.c])
                self.arrives(g, slot, 8, full.at[slot, at.other + 1, at.c])

    def sent(self, g):
        at, full = self.at, self.full[g]

        def left(slot, kind, src):
            self.cp(g, slot, kind, src, src, at.core).wait_send()

        @pl.when(at.k != at.own_core)
        def _():
            left(at.own_slot, 0, full.at[at.own_slot, at.f, at.c])

        for slot in range(2):
            piece = self.ours(g, slot, at.pair, at.c)

            @pl.when(jnp.logical_and(at.p >= slot, at.p < 3))
            def _():
                left(slot, 1, piece)

            if slot == 1:

                @pl.when(at.p == 1)
                def _():
                    left(slot, 2, piece)

            for copy in (*self.ahead(g, slot), *self.direct(g, slot), *self.relays(g, slot)):
                copy.wait_send()


class Swap:
    def __init__(self, at, blocks, rows, base, send, recv):
        self.at, self.blocks, self.rows, self.base, self.send, self.recv = at, blocks, rows, base, send, recv
        self.n = blocks.shape[1]

    def span(self, s, base):
        return pl.ds(pl.multiple_of(base + s * self.n, self.n), self.n)

    def start_in(self):
        at = self.at
        there = self.rows.at[self.span(at.t, self.base * at.c)]
        for s in range(4):

            @pl.when(at.swap_is_self(s))
            def _():
                here = self.rows.at[self.span(s, self.base * at.k)]
                pltpu.make_async_copy(self.blocks.at[s], here, self.recv.at[s]).start()

            @pl.when(jnp.logical_not(at.swap_is_self(s)))
            def _():
                copy_to(self.blocks.at[s], there, self.send.at[s], self.recv.at[at.t], at.swap(s)).start()

    def wait_in(self, s):
        at = self.at
        here = self.rows.at[self.span(s, self.base * at.k)]

        @pl.when(jnp.logical_not(at.swap_is_self(s)))
        def _():
            copy_to(here, here, self.send.at[s], self.recv.at[s], at.core).wait_recv()

        @pl.when(at.swap_is_self(s))
        def _():
            pltpu.make_async_copy(self.blocks.at[s], here, self.recv.at[s]).wait()

    def start_out(self, s):
        at = self.at
        here = self.rows.at[self.span(s, self.base * at.k)]

        @pl.when(at.swap_is_self(s))
        def _():
            pltpu.make_async_copy(here, self.blocks.at[s], self.send.at[s]).start()

        @pl.when(jnp.logical_not(at.swap_is_self(s)))
        def _():
            copy_to(here, self.blocks.at[at.t], self.send.at[s], self.recv.at[at.t], at.swap(s)).start()

    def wait_out(self, s):
        at = self.at

        @pl.when(jnp.logical_not(at.swap_is_self(s)))
        def _():
            copy_to(self.blocks.at[s], self.blocks.at[s], self.send.at[s], self.recv.at[s], at.core).wait_recv()

    def sent(self, outward=False):
        at = self.at
        for s in range(4):

            @pl.when(jnp.logical_not(at.swap_is_self(s)))
            def _():
                here = self.rows.at[self.span(s, self.base * at.k)] if outward else self.blocks.at[s]
                copy_to(here, here, self.send.at[s], self.recv.at[s], at.core).wait_send()

            if outward:

                @pl.when(at.swap_is_self(s))
                def _():
                    here = self.rows.at[self.span(s, self.base * at.k)]
                    pltpu.make_async_copy(here, self.blocks.at[s], self.send.at[s]).wait()
ROWS = 256


def norm_stats(value):
    mean = jnp.mean(value, axis=-1, keepdims=True)
    centred = value - mean
    inverse = lax.rsqrt(jnp.mean(centred * centred, axis=-1, keepdims=True) + EPS)
    return centred * inverse, inverse


def gelu_both(value):
    share = 0.5 + 0.5 * lax.erf(value * 0.7071067811865476)
    density = jnp.exp(value * value * -0.5) * 0.3989422804014327
    return value * share, share + value * density


def row_sum(value):
    return jnp.sum(value, axis=0, keepdims=True)


class Cores:
    def __init__(self, at, out, back, send, recv, row_send, row_recv):
        self.at, self.out, self.back = at, out, back
        self.send, self.recv, self.row_send, self.row_recv = send, recv, row_send, row_recv

    def rows(self, half, i):
        return pl.ds(pl.multiple_of(half * 512 + i * ROWS, ROWS), ROWS)

    def part(self, stage, i):
        return copy_to(self.out.at[i], self.back.at[i], self.send.at[stage, i], self.recv.at[stage, i], self.at.core)

    def reduce(self, stage, partial, finish, between=lambda: None):
        at = self.at

        @pl.loop(0, 512 // ROWS)
        def _(i):
            self.out[i] = partial(self.rows(1 - at.k, i))
            self.part(stage, i).start()

        between()

        @pl.loop(0, 512 // ROWS)
        def _(i):
            total = partial(self.rows(at.k, i))
            self.part(stage, i).wait_recv()
            finish(i, self.rows(at.k, i), total + self.back[i])

        @pl.loop(0, 512 // ROWS)
        def _(i):
            self.part(stage, i).wait_send()

    def row(self, stage, ref, half, i):
        rows = ref.at[self.rows(half, i)]
        return copy_to(rows, rows, self.row_send.at[stage, i], self.row_recv.at[stage, i], self.at.core)

    def over_rows(self, stage, ref, work):
        at = self.at

        @pl.loop(0, 512 // ROWS)
        def _(i):
            work(self.rows(at.k, i))

        @pl.loop(0, 512 // ROWS)
        def _(i):
            self.row(stage, ref, 1 - at.k, i).wait_recv()
            work(self.rows(1 - at.k, i))

        @pl.loop(0, 512 // ROWS)
        def _(i):
            self.row(stage, ref, at.k, i).wait_send()


def flip(dst, src):
    @pl.loop(0, src.shape[0] // ROWS)
    def _(r):
        rows = pl.ds(pl.multiple_of(r * ROWS, ROWS), ROWS)
        dst[:, rows] = src[rows, :].T


def product(dst, slot, flipped, right):
    n = dst.shape[2] * dst.shape[3]

    @pl.loop(0, dst.shape[1])
    def _(r):
        rows = pl.ds(pl.multiple_of(r * n, n), n)
        got = mm(flipped[rows, :], right())
        dst[slot, r] = got.astype(BF).reshape(dst.shape[2:])


def vmem():
    return pl.BlockSpec(memory_space=pltpu.VMEM)


QCHUNK = 512


def attend_chunk(h, q, key, query, value_t, bias, lse, mixed_t):
    cols = pl.ds(pl.multiple_of(q * QCHUNK, QCHUNK), QCHUNK)
    scores = mm(key[h], query[h, cols, :], NT)
    length = scores.shape[0]
    scores = (
        scores.reshape(length // BLK, BLK, QCHUNK) + bias[h, :, cols][:, None, :]
    ).reshape(length, QCHUNK)
    top = jnp.max(scores, axis=0, keepdims=True)
    weights = jnp.exp(scores - top)
    total = jnp.sum(weights, axis=0, keepdims=True)
    probs = (weights * (1.0 / total)).astype(BF)
    lse[h, :, cols] = top + jnp.log(total)
    mixed_t[:, cols] = mm(value_t[...], probs).astype(BF)


class Vectors:
    def __init__(self, at, own, vec, near, ids, picked, sems):
        self.at, self.own, self.vec, self.near, self.ids, self.picked = at, own, vec, near, ids, picked
        self.send, self.recv = sems

    def fill(self, out_bias, norm_gain, norm_bias, up_bias, qv_bias, rand):
        at = self.at
        size = out_bias.shape[1]
        for i, ref in enumerate((out_bias, norm_gain, norm_bias)):
            self.vec[at.f, 2 * i : 2 * i + 2, 0:size] = ref[...]
        self.own[0:1, 0:size] = up_bias[...]
        self.own[1:3, 0 : qv_bias.shape[1]] = qv_bias[...]
        for h in range(3):
            for r in range(3):
                self.ids[:, 3 * h + r, 0 : rand.shape[3]] = rand[h, r].astype(F32)

        @pl.when(at.k == at.own_core)
        def _():
            self.near[at.own_slot, at.f] = self.own[...]

            @pl.when(at.k == at.c)
            def _():
                self.picked[at.own_slot] = self.ids[at.t]

    def copies(self):
        at = self.at
        out = []
        box = self.vec.at[at.f]
        for i, f in enumerate((at.core[0], at.ynbr[0], lax.rem(at.core[0] + 2, 4))):
            out.append((None, copy_to(box, box, self.send.at[i], self.recv.at[at.f], (f, at.c, at.t))))
        for y in range(2):
            for t in range(4):
                f = 2 * y + at.own_core
                copy = copy_to(
                    self.own,
                    self.near.at[at.own_slot, at.f],
                    self.send.at[3 + 4 * y + t],
                    self.recv.at[4 + 4 * at.own_slot + at.f],
                    (f, at.c, t),
                )
                out.append((jnp.logical_or(f != at.f, t != at.t), copy))
        for s in range(4):
            f = at.pair + at.own_core
            copy = copy_to(
                self.ids.at[s],
                self.picked.at[at.own_slot],
                self.send.at[11 + s],
                self.recv.at[12 + at.own_slot],
                (f, at.k, s),
            )
            away = jnp.logical_or(f != at.f, s != at.t)
            out.append((jnp.logical_and(at.c == at.k, away), copy))
        return out

    def each(self, act):
        for condition, copy in self.copies():
            if condition is None:
                act(copy)
            else:
                pl.when(condition)(lambda copy=copy: act(copy))

    def start(self):
        self.each(lambda copy: copy.start())

    def sent(self):
        self.each(lambda copy: copy.wait_send())

    def wait(self):
        at = self.at

        def arrives(index, dst):
            copy_to(dst, dst, self.send.at[0], self.recv.at[index], at.core).wait_recv()

        for i in range(1, 4):
            f = lax.rem(at.f + i, 4)
            arrives(f, self.vec.at[f])
        for slot in range(2):
            ours = jnp.logical_and(at.k == at.own_core, slot == at.own_slot)
            for f in range(4):

                @pl.when(jnp.logical_not(jnp.logical_and(ours, f == at.f)))
                def _():
                    arrives(4 + 4 * slot + f, self.near.at[slot, f])

            @pl.when(jnp.logical_not(jnp.logical_and(ours, at.k == at.c)))
            def _():
                arrives(12 + slot, self.picked.at[slot])

    def unpack(self, vec_out, ups, proj_bias, row, bias):
        size = vec_out.shape[1] // 4
        low = lambda a: a.astype(BF).astype(F32)
        part = size // 4
        for f in range(4):
            vec_out[:, size * f : size * (f + 1)] = low(self.vec[f, :, 0:size])
        proj_bias[...] = jnp.zeros_like(proj_bias)
        for slot in range(2):
            for f in range(4):
                ups[slot : slot + 1, size * f : size * (f + 1)] = low(self.near[slot, f, 0:1, 0:size])
                row[slot, 0:2, part * f : part * (f + 1)] = low(self.near[slot, f, 1:3, 0:part])
            for i in range(3):
                start = i * size
                proj_bias[slot, :, start : start + 64] = row[slot, 0:1, 64 * i : 64 * i + 64]
                proj_bias[slot, :, start + 128 : start + 192] = row[slot, 1:2, 64 * i : 64 * i + 64]
        blocks, length = bias.shape[1], bias.shape[2]
        spot = lax.broadcasted_iota(jnp.int32, (blocks, length), 0)
        block = lax.broadcasted_iota(jnp.int32, (blocks, length), 1) // BLK
        number = lambda mask: jnp.where(mask, 1.0, 0.0)
        fixed = number(jnp.abs(spot - block) <= 1) + number(spot == 0) + number(spot == blocks - 1)
        edge = jnp.logical_or(block == 0, block == blocks - 1)
        spread_out = number(spot == block).astype(BF)
        here = spot.astype(F32)
        for slot in range(2):
            ids = mm(self.picked[slot, :, 0:blocks].astype(BF), spread_out)
            for i in range(3):
                counts = fixed
                for r in range(3):
                    counts = counts + number(ids[3 * i + r : 3 * i + r + 1, :] == here)
                counts = jnp.where(edge, 1.0, counts)
                bias[3 * slot + i] = jnp.where(counts > 0.5, jnp.log(jnp.maximum(counts, 1.0)), -1e30)


class Reduce:
    def __init__(self, at, grads, work, plane, zline, final, send, recv):
        self.at, self.grads, self.work, self.plane, self.zline, self.final = at, grads, work, plane, zline, final
        self.send, self.recv = send, recv

    def cp(self, g, slot, kind, src, dst, device, recv_kind=None):
        recv_kind = kind if recv_kind is None else recv_kind
        return copy_to(src, dst, self.send.at[g, slot, kind], self.recv.at[g, slot, recv_kind], device)

    def arrives(self, g, slot, kind, dst):
        self.cp(g, slot, kind, dst, dst, self.at.core).wait_recv()

    def plane_sends(self, g, slot):
        at, grad, box = self.at, self.grads[g], self.plane[g].at[slot]
        return (
            self.cp(g, slot, 1, grad.at[slot, at.other, 1 - at.c], box.at[1], at.xnbr),
            self.cp(g, slot, 3, grad.at[slot, at.other + 1, 1 - at.c], box.at[3], at.ynbr),
            self.cp(g, slot, 0, grad.at[slot, at.pair, 1 - at.c], box.at[0], at.xnbr),
            self.cp(g, slot, 2, grad.at[slot, at.other + 1, at.c], box.at[2], at.ynbr),
        )

    def sums(self, g, slot):
        at, work, box = self.at, self.work[g].at[slot], self.plane[g].at[slot]
        return (
            self.cp(g, slot, 4, work.at[0], box.at[4], at.ynbr),
            self.cp(g, slot, 5, work.at[1], box.at[5], at.xnbr),
        )

    def plane0(self, g, slot):
        for copy in self.plane_sends(g, slot)[:2]:
            copy.start()

    def total(self, g, slot, i, piece, boxes):
        came = sum(self.plane[g][slot, b].astype(F32) for b in boxes)
        own = self.grads[g][slot, piece[0], piece[1]].astype(F32)
        self.work[g][slot, i] = (own + came).astype(BF)

    def plane1(self, g, slot):
        at = self.at
        copies = self.sums(g, slot)
        for i, kind, piece in ((0, 1, (at.other, at.c)), (1, 3, (at.pair + 1, 1 - at.c))):
            self.arrives(g, slot, kind, self.plane[g].at[slot, kind])
            self.total(g, slot, i, piece, (kind,))
            copies[i].start()
        for copy in self.plane_sends(g, slot)[2:]:
            copy.start()

    def ours(self, g, slot):
        return self.work[g].at[slot, pl.ds(2, 2)]

    def down(self, g, slot):
        return self.cp(g, slot, 6, self.ours(g, slot), self.zline[g].at[slot], self.at.zminus)

    def upward(self, g, slot):
        return self.cp(g, slot, 7, self.ours(g, slot), self.zline[g].at[2], self.at.zplus)

    def plane2(self, g, slot):
        at = self.at
        for kind in (0, 2, 4, 5):
            self.arrives(g, slot, kind, self.plane[g].at[slot, kind])
        boxes = ((0, 4), (2, 5))
        for i in range(2):
            self.total(g, slot, 2 + i, (at.pair + i, at.c), boxes[i])

        @pl.when(at.p == 3)
        def _():
            self.down(g, slot).start()

        if slot == 1:

            @pl.when(at.p == 0)
            def _():
                self.upward(g, slot).start()

    def add_line(self, g, slot, which):
        box = 2 if which else slot
        self.arrives(g, slot, 6 + which, self.zline[g].at[box])
        for i in range(2):
            self.work[g][slot, 2 + i] = (
                self.work[g][slot, 2 + i].astype(F32) + self.zline[g][box, i].astype(F32)
            ).astype(BF)

    def line(self, g, slot, place):
        at = self.at
        if place < slot:
            return

        @pl.when(at.p == place)
        def _():
            self.add_line(g, slot, 0)
            if slot == 1 and place == 1:
                self.add_line(g, slot, 1)
            if place > slot:
                self.down(g, slot).start()
            else:
                self.hand_out(g, slot)

    def hands(self, g, slot):
        at, final = self.at, self.final[g]
        mine = self.work[g].at[slot, 2 + at.k]
        theirs = self.work[g].at[slot, 3 - at.k]
        there = final.at[self.half(g, at.c)]
        return (
            self.cp(g, slot, 8, theirs, there, at.core, 8),
            self.cp(g, slot, 9, mine, there, at.xnbr, 9),
            self.cp(g, slot, 10, theirs, there, (at.core[0], 1 - at.c, at.t), 9),
        )

    def half(self, g, c):
        n = self.final[g].shape[0] // 2
        return pl.ds(pl.multiple_of(c * n, n), n)

    def hand_out(self, g, slot):
        at = self.at
        for copy in self.hands(g, slot):
            copy.start()
        self.final[g][self.half(g, at.c), :] = self.work[g][slot, 2 + at.k]

    def finish(self, g):
        at, final = self.at, self.final[g]

        @pl.when(at.k != at.own_core)
        def _():
            self.arrives(g, at.own_slot, 8, final.at[self.half(g, at.c)])

        self.arrives(g, at.own_slot, 9, final.at[self.half(g, 1 - at.c)])
        return final[...].astype(F32)

    def sent(self, g):
        at = self.at
        for slot in range(2):
            for copy in (*self.plane_sends(g, slot), *self.sums(g, slot)):
                copy.wait_send()

            @pl.when(at.p > slot)
            def _():
                self.down(g, slot).wait_send()

            if slot == 1:

                @pl.when(at.p == 0)
                def _():
                    self.upward(g, slot).wait_send()

            @pl.when(at.p == slot)
            def _():
                for copy in self.hands(g, slot):
                    copy.wait_send()


def attend_back_chunk(h, q, key, query, value, key_t, bias, lse, upper, key_sum, value_sum, query_t):
    cols = pl.ds(pl.multiple_of(q * QCHUNK, QCHUNK), QCHUNK)
    some = query[h, cols, :]
    upper = upper(cols)
    scores = mm(key[h], some, NT)
    length = scores.shape[0]
    shift = bias[h, :, cols] - lse[h, :, cols]
    scores = (scores.reshape(length // BLK, BLK, QCHUNK) + shift[:, None, :]).reshape(length, QCHUNK)
    probs = jnp.exp(scores)
    probs_grad = mm(value[h], upper, NT)
    inner = jnp.sum(probs * probs_grad, axis=0, keepdims=True)
    scores_grad = (probs * (probs_grad - inner)).astype(BF)
    value_sum[...] += mm(probs.astype(BF), upper)
    key_sum[...] += mm(scores_grad, some)
    query_t[:, cols] = mm(key_t[...], scores_grad)


def layer_kernel(
    xs, cs, w_in, w_out, w_up, w_down, out_bias, norm_gain, norm_bias, up_bias, qv_bias, rand,
    layer_blocks, grad_blocks, g_in, g_qv, g_out, g_outs, g_gains, g_shifts, g_up, g_ups, g_down,
    x_all, up_half, low0, low1, low2, query, key, value, mixed, lse, bias, vectors, ups,
    own, vec, near, ids, picked, proj_bias, bias_row,
    grad0, grad_out, part_out, part_back, rows_f32, normed_one, inverse_one, first_b, second_b,
    act, slope, flipped, grad_rows, key_t, key_sum, value_sum, query_t,
    work, plane, zline, final0, final1, final2, small, small_out, sum_out, sum_in,
    xs_send, xs_recv, xc_send, xc_recv, cs_send, cs_recv, p_send, p_recv, v_send, v_recv,
    lo_send, lo_recv, gi_send, gi_recv, w_send, w_recv, send, recv, row_send, row_recv, small_send, small_recv,
):
    at = Place()
    letters = Vectors(at, own, vec, near, ids, picked, (v_send, v_recv))
    finals = (final0, final1, final2)
    wide = w_in.shape[2]

    def pack():
        for h in range(3):
            final0[:, h * wide : (h + 1) * wide] = w_in[h].astype(BF)
        final0[:, 3 * wide : 4 * wide] = w_out[...].T.astype(BF)
        final1[...] = w_up[...].astype(BF)
        final2[...] = w_down[...].astype(BF)
        own[...] = jnp.zeros_like(own)
        ids[...] = jnp.zeros_like(ids)
        vec[at.f] = jnp.zeros(vec.shape[1:], F32)
        letters.fill(out_bias, norm_gain, norm_bias, up_bias, qv_bias, rand)

    greet(at, pack)
    gather = Gather(at, finals, (low0, low1, low2), p_send, p_recv, tall=(1,))
    tokens = Swap(at, xs, x_all, 512, xs_send, xs_recv)
    upstreams = Swap(at, cs, up_half, 0, cs_send, cs_recv)
    part = xs.shape[1]
    width = x_all.shape[1]
    letters.start()
    for g in range(3):
        gather.own(g)
    gather.step_z(0, 0)
    gather.step_z(0, 1)
    tokens.start_in()
    gather.step_relay(0, 0)
    gather.step_relay(0, 1)

    def to_core(s, half):
        rows = x_all.at[pl.ds(pl.multiple_of(half * 512 + s * part, part), part)]
        return copy_to(rows, rows, xc_send.at[s], xc_recv.at[s], at.core)

    for s in range(4):
        tokens.wait_in(s)
        to_core(s, at.k).start()
    gather.step_z(1, 0)
    gather.step_z(1, 1)
    letters.wait()
    letters.unpack(vectors, ups, proj_bias, bias_row, bias)
    small[...] = jnp.zeros_like(small)
    for s in range(4):
        to_core(s, 1 - at.k).wait_recv()
    gather.step_last(0)

    dim = query.shape[2]
    for slot in range(2):

        @pl.loop(0, 4)
        def _(r):
            rows = pl.ds(pl.multiple_of(r * 256, 256), 256)
            weight = low0[slot, :, :, :, 0:640].reshape(width, 640)
            got = mm(x_all[rows, :], weight) + proj_bias[slot]
            for i in range(3):
                h = slot * 3 + i
                start = i * 3 * dim
                query[h, rows, :] = (got[:, start : start + dim] * dim**-0.5).astype(BF)
                key[h, rows, :] = got[:, start + dim : start + 2 * dim].astype(BF)
                one = got[:, start + 2 * dim : start + 3 * dim]
                value[h, rows, :] = one.astype(BF)
                flipped[384 + h * dim : 384 + (h + 1) * dim, rows] = one.T.astype(BF)

        if slot == 0:
            gather.step_z(2, 0)
            gather.step_z(2, 1)
    gather.step_relay(1, 0)
    gather.step_relay(1, 1)

    def attend_forward(low_head, high_head):
        @pl.loop(low_head, high_head)
        def _(h):
            @pl.loop(0, 1024 // QCHUNK)
            def _(q):
                spot = pl.ds(pl.multiple_of(h * dim, dim), dim)
                value_t = flipped.at[pl.ds(pl.multiple_of(384 + h * dim, dim), dim)]
                attend_chunk(h, q, key, query, value_t, bias, lse, flipped.at[spot])

    attend_forward(0, 3)
    gather.step_relay(2, 0)
    gather.step_relay(2, 1)
    upstreams.start_in()
    attend_forward(3, 6)

    @pl.loop(0, 4)
    def _(r):
        rows = pl.ds(pl.multiple_of(r * 256, 256), 256)
        blank = jnp.zeros((dim, 256), BF)
        for slot in range(2):
            heads = jnp.concatenate([blank, flipped[slot * 192 : slot * 192 + 192, rows]], axis=0)
            mixed[rows, slot * 256 : slot * 256 + 256] = heads.T

    layer = Swap(at, layer_blocks, up_half, 0, lo_send, lo_recv)
    inputs = Swap(at, grad_blocks, grad_rows, 0, gi_send, gi_recv)
    low_half, high_half = pl.ds(0, width // 2), pl.ds(width // 2, width // 2)
    views = lambda ref, *dims: (ref.at[0, *dims, low_half], ref.at[1], ref.at[2], ref.at[0, *dims, high_half])
    every = lambda ref: [pl.ds(0, n) for n in ref.shape[1:-1]]
    reduce = Reduce(
        at,
        (grad0.at[..., low_half], low1, low2, grad0.at[..., high_half]),
        *(views(ref, *every(ref)) for ref in (work, plane, zline)),
        (final0.at[:, low_half], final1, final2, final0.at[:, high_half]),
        w_send,
        w_recv,
    )
    cores = Cores(at, part_out, part_back, send, recv, row_send, row_recv)
    square = lambda full, slot: full[slot].reshape(width, width)
    out_part = lambda slot: low0[slot, :, :, :, 512:768].reshape(width, 256)
    local = lambda i: pl.ds(pl.multiple_of(i * ROWS, ROWS), ROWS)

    def tally(row, value):
        small[row : row + 1, :] += row_sum(value)

    def branch_part(rows):
        return mm(mixed[rows, 0:256], out_part(0), NT) + mm(mixed[rows, 256:512], out_part(1), NT)

    def branch_done(i, rows, total):
        normed, inverse = norm_stats(x_all[rows, :].astype(F32) + (total + vectors[0:1, :]))
        value = normed * vectors[2:3, :] + vectors[4:5, :]
        normed_one[local(i), :] = normed
        inverse_one[local(i), :] = inverse
        rows_f32[local(i), :] = value
        first_b[rows, :] = value.astype(BF)
        cores.row(0, first_b, at.k, i).start()

    cores.reduce(0, branch_part, branch_done)

    def up(rows):
        for slot in range(2):
            inner = mm(first_b[rows, :], square(low1, slot)) + ups[slot : slot + 1, :]
            value, slope_value = gelu_both(inner)
            act[slot, rows, :] = value.astype(BF)
            slope[slot, rows, :] = slope_value.astype(BF)

    gather.sent(0)
    gather.step_last(1)
    gather.sent(1)
    cores.over_rows(0, first_b, up)
    gather.step_last(2)
    gather.sent(2)
    for s in range(4):
        upstreams.wait_in(s)

    def second_part(rows):
        return mm(act[0, rows, :], square(low2, 0), NT) + mm(act[1, rows, :], square(low2, 1), NT)

    def second_done(i, rows, total):
        normed, inverse = norm_stats(rows_f32[local(i), :] + (total + vectors[1:2, :]))
        layer_row = (normed * vectors[3:4, :] + vectors[5:6, :]).astype(BF)
        upstream = up_half[local(i), :].astype(F32)
        up_half[local(i), :] = layer_row
        scaled = upstream * vectors[3:4, :]
        grad = inverse * (
            scaled
            - jnp.mean(scaled, axis=-1, keepdims=True)
            - normed * jnp.mean(scaled * normed, axis=-1, keepdims=True)
        )
        rows_f32[local(i), :] = grad
        low = grad.astype(BF)
        second_b[rows, :] = low
        cores.row(1, second_b, at.k, i).start()
        tally(1, low.astype(F32))
        tally(3, upstream * normed)
        tally(5, upstream)

    cores.reduce(1, second_part, second_done)
    for s in range(4):
        layer.start_out(s)

    def down(rows):
        for slot in range(2):
            grad = mm(second_b[rows, :], square(low2, slot)) * slope[slot, rows, :].astype(F32)
            low = grad.astype(BF)
            slope[slot, rows, :] = low
            tally(6 + slot, low.astype(F32))

    cores.over_rows(1, second_b, down)
    flip(flipped, second_b)
    for slot in range(2):
        product(low2, slot, flipped, lambda: act[slot])
        reduce.plane0(2, slot)

    def first_part(rows):
        return mm(slope[0, rows, :], square(low1, 0), NT) + mm(slope[1, rows, :], square(low1, 1), NT)

    def first_done(i, rows, total):
        grad = total + rows_f32[local(i), :]
        normed = normed_one[local(i), :]
        tally(2, grad * normed)
        tally(4, grad)
        scaled = grad * vectors[2:3, :]
        back = inverse_one[local(i), :] * (
            scaled
            - jnp.mean(scaled, axis=-1, keepdims=True)
            - normed * jnp.mean(scaled * normed, axis=-1, keepdims=True)
        )
        rows_f32[local(i), :] = back
        low = back.astype(BF)
        second_b[rows, :] = low
        cores.row(2, second_b, at.k, i).start()
        tally(0, low.astype(F32))

    cores.reduce(2, first_part, first_done)
    for slot in range(2):
        reduce.plane1(2, slot)
    flip(flipped, first_b)
    for slot in range(2):
        product(low1, slot, flipped, lambda: slope[slot])
        reduce.plane0(1, slot)

    mixed_grad = first_b

    def mix_back(rows):
        for slot in range(2):
            mixed_grad[rows, slot * 256 : slot * 256 + 256] = mm(second_b[rows, :], out_part(slot)).astype(BF)

    cores.over_rows(2, second_b, mix_back)
    flip(flipped, second_b)

    @pl.loop(0, 4)
    def _(r):
        rows = pl.ds(pl.multiple_of(r * 192, 192), 192)
        grad_out[rows, :] = mm(flipped[rows, :], mixed[...]).astype(BF)

    flip(flipped, x_all)
    proj_grad = act
    for slot in range(2):
        proj_grad[slot, :, 576:640] = jnp.zeros((1024, 64), BF)

    def attend(h):
        key_t[...] = key[h].astype(F32).T.astype(BF)
        key_sum[...] = jnp.zeros_like(key_sum)
        value_sum[...] = jnp.zeros_like(value_sum)

        @pl.loop(0, 1024 // QCHUNK)
        def _(q):
            column = (h // 3) * 256 + (h % 3 + 1) * 64
            attend_back_chunk(
                h, q, key, query, value, key_t, bias, lse,
                lambda cols: mixed_grad[cols, column : column + 64], key_sum, value_sum, query_t,
            )

        start = (h % 3) * 192
        proj_grad[h // 3, :, start : start + 64] = (query_t[...] * 0.125).T.astype(BF)
        proj_grad[h // 3, :, start + 64 : start + 128] = key_sum[...].astype(BF)
        proj_grad[h // 3, :, start + 128 : start + 192] = value_sum[...].astype(BF)

    def in_grads(slot, g):
        @pl.loop(0, 4)
        def _(r):
            rows = pl.ds(pl.multiple_of(r * 192, 192), 192)
            if g == 0:
                got = mm(flipped[rows, :], proj_grad[slot, :, 0:384])
                grad0[slot, r, :, :, 0:384] = got.astype(BF).reshape(2, 96, 384)
            else:
                got = mm(flipped[rows, :], proj_grad[slot, :, 384:640])
                out_part = grad_out[rows, slot * 256 : slot * 256 + 256]
                grad0[slot, r, :, :, 384:512] = got[:, 0:128].astype(BF).reshape(2, 96, 128)
                shared = got[:, 128:256] + out_part[:, 0:128].astype(F32)
                grad0[slot, r, :, :, 512:640] = shared.astype(BF).reshape(2, 96, 128)
                grad0[slot, r, :, :, 640:768] = out_part[:, 128:256].reshape(2, 96, 128)

        reduce.plane0(g, slot)

    def both(step, g, *more):
        for slot in range(2):
            step(g, slot, *more)

    def halves(step, slot, *more):
        for g in (0, 3):
            step(g, slot, *more)

    attend(0)
    both(reduce.plane2, 2)
    attend(1)
    both(reduce.plane1, 1)
    both(reduce.line, 2, 2)
    attend(2)
    both(reduce.line, 2, 1)
    in_grads(0, 0)
    in_grads(0, 3)
    attend(3)
    both(reduce.line, 2, 0)
    both(reduce.plane2, 1)
    attend(4)
    halves(reduce.plane1, 0)
    in_grads(1, 0)
    both(reduce.line, 1, 2)
    attend(5)
    in_grads(1, 3)
    both(reduce.line, 1, 1)
    halves(reduce.plane2, 0)
    reduce.plane1(0, 1)
    both(reduce.line, 1, 0)

    t = at.t
    steps = (at.xnbr, at.ynbr, (at.f, at.c, t + 1 - 2 * lax.rem(t, 2)), (at.f, at.c, lax.rem(t + 2, 4)))
    hops = [
        copy_to(sum_out.at[i], sum_in.at[i], small_send.at[i], small_recv.at[i], device)
        for i, device in enumerate(steps)
    ]

    def small_next(i):
        hops[i].wait_recv()
        if i < 3:
            sum_out[i + 1] = sum_out[i] + sum_in[i]
            hops[i + 1].start()
        else:
            small_out[at.k] = sum_out[i] + sum_in[i]

    sum_out[0] = small[...]
    for slot in range(2):
        sum_out[0, 8 + slot : 9 + slot, 0:640] = row_sum(proj_grad[slot, :, 0:640].astype(F32))
    hops[0].start()
    halves(reduce.line, 0, 2)

    def in_part(rows):
        return sum(
            mm(proj_grad[slot, rows, 0:640], low0[slot, :, :, :, 0:640].reshape(width, 640), NT)
            for slot in range(2)
        )

    def in_done(i, rows, total):
        grad_rows[local(i), :] = (total + rows_f32[local(i), :]).astype(BF)
        for s in range(ROWS // 128):
            inputs.start_out(i * (ROWS // 128) + s)

    def between():
        small_next(0)
        reduce.plane1(3, 1)
        halves(reduce.line, 0, 1)
        reduce.plane2(0, 1)

    cores.reduce(3, in_part, in_done, between)
    small_next(1)
    reduce.line(0, 1, 2)
    halves(reduce.line, 0, 0)
    reduce.plane2(3, 1)
    small_next(2)
    reduce.line(0, 1, 1)
    reduce.line(3, 1, 2)
    small_next(3)
    mine = small_out.at[at.k]
    both_cores = copy_to(mine, mine, small_send.at[4], small_recv.at[4], at.core)
    both_cores.start()
    reduce.line(3, 1, 1)
    for copy in hops:
        copy.wait_send()
    g_down[...] = reduce.finish(2)
    g_up[...] = reduce.finish(1)
    reduce.finish(0)
    reduce.finish(3)
    got = final0[...].astype(F32)
    fr = g_up.shape[0]
    for h in range(3):
        g_in[h] = got[:, h * fr : (h + 1) * fr]
    g_out[...] = got[:, 3 * fr : 4 * fr].T
    both_cores.wait_send()
    copy_to(small_out.at[1 - at.k], small_out.at[1 - at.k], small_send.at[4], small_recv.at[4], at.core).wait_recv()
    sums = small_out[0, 0:8, :] + small_out[1, 0:8, :]
    used = small_out.at[at.own_core]
    up_row = used[pl.ds(6 + at.own_slot, 1), :]
    proj_row = used[pl.ds(8 + at.own_slot, 1), :]
    pick = lambda j: jnp.concatenate(
        [proj_row[:, i * fr + 64 * j : i * fr + 64 * j + 64] for i in range(3)], axis=1
    )
    pair_rows = jnp.concatenate([pick(0), pick(2)], axis=0)
    quarter = fr // 4
    for f in range(4):

        @pl.when(at.f == f)
        def _():
            piece = sums[:, f * fr : (f + 1) * fr]
            g_outs[...] = piece[0:2]
            g_gains[...] = piece[2:4]
            g_shifts[...] = piece[4:6]
            g_ups[...] = up_row[:, f * fr : (f + 1) * fr]
            g_qv[...] = pair_rows[:, f * quarter : (f + 1) * quarter]

    for s in range(4):
        layer.wait_out(s)
        inputs.wait_out(s)
    layer.sent(True)
    inputs.sent(True)
    for g in range(4):
        reduce.sent(g)
    letters.sent()
    tokens.sent()
    upstreams.sent()
    for s in range(4):
        to_core(s, at.k).wait_send()


def layer_call(xs, cs, w_in, w_out, w_up, w_down, out_bias, norm_gain, norm_bias, up_bias, qv_bias, rand):
    width = xs.shape[2]
    length, half = 1024, 512
    heads, dim = 6, 64
    blocks = length // BLK
    parts = half // ROWS
    fr = width // 4
    piece = (fr // 2, width)
    shape = jax.ShapeDtypeStruct
    dma = lambda *dims: pltpu.SemaphoreType.DMA(dims)
    low = lambda *dims: pltpu.VMEM(dims, BF)
    full = lambda *dims: pltpu.VMEM(dims, F32)
    anywhere = pl.BlockSpec(memory_space=pl.ANY)
    return pl.pallas_call(
        layer_kernel,
        out_shape=(
            shape(xs.shape, BF),
            shape(xs.shape, BF),
            shape((3, fr, fr), F32),
            shape((2, fr // 4), F32),
            shape((fr, fr), F32),
            shape((2, fr), F32),
            shape((2, fr), F32),
            shape((2, fr), F32),
            shape((fr, width), F32),
            shape((1, fr), F32),
            shape((fr, width), F32),
        ),
        in_specs=[anywhere] * 2 + [vmem()] * 10,
        out_specs=[anywhere] * 2 + [vmem()] * 9,
        scratch_shapes=[
            low(length, width),
            low(half, width),
            low(2, 4, 2, *piece),
            low(2, 4, 2, *piece),
            low(2, 4, 2, *piece),
            low(heads, length, dim),
            low(heads, length, dim),
            low(heads, length, dim),
            low(length, 512),
            full(heads, 1, length),
            full(heads, blocks, length),
            full(8, width),
            full(2, width),
            full(8, 256),
            full(4, 8, 256),
            full(2, 4, 8, 256),
            full(4, 16, 128),
            full(2, 16, 128),
            full(2, 1, 640),
            full(2, 8, 256),
            low(2, 4, 2, *piece),
            low(width, 512),
            full(parts, ROWS, width),
            full(parts, ROWS, width),
            full(half, width),
            full(half, width),
            full(half, 1),
            low(length, width),
            low(length, width),
            low(2, length, width),
            low(2, length, width),
            low(width, length),
            low(half, width),
            low(dim, length),
            full(length, dim),
            full(length, dim),
            full(dim, length),
            low(3, 2, 4, *piece),
            low(3, 2, 6, *piece),
            low(3, 3, 2, *piece),
            low(fr, width),
            low(fr, width),
            low(fr, width),
            full(16, width),
            full(2, 16, width),
            full(4, 16, width),
            full(4, 16, width),
            dma(4),
            dma(4),
            dma(4),
            dma(4),
            dma(4),
            dma(4),
            dma(3, 2, 9),
            dma(3, 2, 9),
            dma(15),
            dma(14),
            dma(4),
            dma(4),
            dma(4),
            dma(4),
            dma(4, 2, 11),
            dma(4, 2, 11),
            dma(4, parts),
            dma(4, parts),
            dma(3, parts),
            dma(3, parts),
            dma(5),
            dma(5),
        ],
        compiler_params=pltpu.CompilerParams(
            collective_id=1, has_side_effects=True, vmem_limit_bytes=VMEM_LIMIT
        ),
        name="layer",
    )(xs, cs, w_in, w_out, w_up, w_down, out_bias, norm_gain, norm_bias, up_bias, qv_bias, rand)


def copy_kernel(*refs):
    half = len(refs) // 2
    for src, dst in zip(refs[:half], refs[half:]):
        dst[...] = src[...]


def copied(arrays):
    return pl.pallas_call(
        copy_kernel,
        out_shape=[jax.ShapeDtypeStruct(a.shape, a.dtype) for a in arrays],
        in_specs=[vmem()] * len(arrays),
        out_specs=[vmem()] * len(arrays),
        name="results",
    )(*arrays)


def sequence_shards(hidden_in, rand_blocks, w_in, qv_bias, w_out, out_bias, norm_gain, norm_bias, w_up, up_bias, w_down, cotangent):
    layer_blocks, grad_blocks, *grads = layer_call(
        hidden_in.transpose(1, 0, 2),
        cotangent.transpose(1, 0, 2),
        w_in.transpose(1, 0, 2),
        w_out,
        w_up,
        w_down.T,
        out_bias,
        norm_gain,
        norm_bias,
        up_bias[None],
        qv_bias,
        rand_blocks.transpose(2, 3, 0, 1),
    )
    grads = list(copied(grads))
    grads[0] = grads[0].transpose(1, 0, 2)
    grads[7] = grads[7][0]
    grads[8] = grads[8].T
    return (layer_blocks.transpose(1, 0, 2), grad_blocks.transpose(1, 0, 2), *grads)


def solution(mesh):
    placed = (
        P(("ctx", "tp"), "fsdp", None),
        P("fsdp", None, "tp", None),
        P("fsdp", "tp", None),
        P(None, ("tp", "fsdp")),
        P("tp", "fsdp"),
        P(None, "fsdp"),
        P(None, "fsdp"),
        P(None, "fsdp"),
        P("fsdp", "tp"),
        P(("tp", "fsdp")),
        P("tp", "fsdp"),
        P(("ctx", "tp"), "fsdp", None),
    )
    sizes = tuple(mesh.shape[a] for a in ("fsdp", "ctx", "tp"))

    def local(*args):
        part_rows, seqs, width = args[0].shape
        rows, heads, wide = args[2].shape
        whole = sizes == (4, 2, 4) and (part_rows, seqs, width) == (128, 4, 768)
        whole = whole and (rows, heads, wide) == (192, 3, 192) and args[8].shape == (192, 768)
        return (sequence_shards if whole else span_shards)(*args)

    return jax.shard_map(
        local,
        mesh=mesh,
        in_specs=placed,
        out_specs=(
            P(("ctx", "tp"), "fsdp", None),
            P(("ctx", "tp"), "fsdp", None),
            P("fsdp", "tp", None),
            P(None, ("tp", "fsdp")),
            P("tp", "fsdp"),
            P(None, "fsdp"),
            P(None, "fsdp"),
            P(None, "fsdp"),
            P("fsdp", "tp"),
            P(("tp", "fsdp")),
            P("tp", "fsdp"),
        ),
        check_vma=False,
    )
```
